32 devices in a mesh: dp: 4 (over y, x), ctx: 8 (over z, core).
Axes of the slice: x: 2, y: 2, z: 4, core: 2. Of those that a mesh axis runs over, the one named last changes fastest.
Arguments:
- q_nope: bfloat16 [4, 1024, 8192], P('dp', 'ctx'), may hold values from -6 to 6
- q_rope: bfloat16 [4, 1024, 4096], P('dp', 'ctx'), may hold values from -6 to 6
- grad_out: bfloat16 [4, 1024, 8192], P('dp', 'ctx'), may hold values from -6 to 6
- log_total: float32 [4, 64, 1024], P('dp', None, 'ctx'), may hold values from 5 to 6.5
- kv_latent: bfloat16 [4, 1024, 320], P('dp', 'ctx'), may hold values from -6 to 6
- up_weight: bfloat16 [256, 16384], P('ctx'), may hold values from -0.375 to 0.375
- selected: int32 [4, 16, 3], P('dp', 'ctx'), may hold values from -1 to 14, as said below
- offered: int32 [4, 8, 4], P('dp'), may hold values from 0 to 1, as said below
Outputs:
- grad_q_nope: bfloat16 [4, 1024, 8192], P('dp', 'ctx')
- grad_q_rope: bfloat16 [4, 1024, 4096], P('dp', 'ctx')
- grad_latent: float32 [4, 1024, 320], P('dp', 'ctx')
- grad_weight: float32 [256, 16384], P('ctx')
The draws below stay inside these ranges and needn't reach their ends.
Inputs may be any that keep to these rules, and one draw needn't show every extreme that they name: offered[b, s, m] is a block number within group s's 128/64 blocks; in matching m group s offers it to group s + m + 1. `selected`: each list holds distinct global block ids, then -1 entries; every id is an earlier block of the query block's own group or a block offered to that group in one of the four matchings; a query block that is not the first of its group always lists the block just before it.
All inputs are finite; a program needn't handle non-finite values.
Results may differ from the reference program's by a relative error of at most 0.0028.
The reference program's roundings to bfloat16 on the way count: a program that leaves them out, or rounds other values in their place, can miss the bound.
Values may be sent and summed in bfloat16 or wider, within the bound.
No kernel may reach another device: no remote copies, remote signals or barrier semaphores. Data moves between devices by JAX's collectives and lax.ppermute only.
A program may use at most 192 MiB of HBM per device.

```python
import jax
import jax.numpy as jnp
from jax import lax

H = 64
LAT = 256
ROPE = 64
NOPE = 128
VDIM = 128
BLOCK = 64
TOPK = 3
TOK_DEV = 128
LENGTH = 1024
BATCH = 4
NQB = 16
N_CTX = 8


partner_offsets = (1, 2, 3, 4)


def build_plan(key):
    per_block = TOK_DEV // BLOCK
    plan_key = jax.random.fold_in(key, 11)
    pick_key = jax.random.fold_in(key, 12)
    offered = jax.random.randint(plan_key, (BATCH, N_CTX, 4), 0, per_block, dtype=jnp.int32)
    offered = offered.at[:, 0, 0].set(0).at[:, 0, 1].set(per_block - 1)
    blocks = jnp.arange(NQB, dtype=jnp.int32)
    group_of = blocks // per_block
    within = blocks % per_block
    earlier = jnp.arange(per_block - 1, dtype=jnp.int32)
    own_ids = group_of[:, None] * per_block + earlier[None, :]
    own_valid = earlier[None, :] < within[:, None]
    own_first = earlier[None, :] == within[:, None] - 1
    offered_ids = []
    offered_valid = []
    for matching, offset in enumerate(partner_offsets):
        source = group_of - offset
        sender = jnp.maximum(source, 0)
        offered_ids.append(sender[None, :] * per_block + offered[:, sender, matching])
        offered_valid.append(jnp.broadcast_to((source >= 0)[None, :], (BATCH, NQB)))
    candidates = jnp.concatenate([jnp.broadcast_to(own_ids[None], (BATCH, NQB, per_block - 1)), jnp.stack(offered_ids, axis=-1)], axis=-1)
    usable = jnp.concatenate([jnp.broadcast_to(own_valid[None], (BATCH, NQB, per_block - 1)), jnp.stack(offered_valid, axis=-1)], axis=-1)
    leading = jnp.concatenate([jnp.broadcast_to(own_first[None], (BATCH, NQB, per_block - 1)), jnp.zeros((BATCH, NQB, 4), dtype=bool)], axis=-1)
    columns = candidates.shape[-1]
    noise_draw = jax.random.randint(pick_key, candidates.shape, 0, 1 << 20, dtype=jnp.int32)
    ranking_key = noise_draw * 64 + jnp.arange(columns, dtype=jnp.int32)
    ranking_key = jnp.where(leading, -1, jnp.where(usable, ranking_key, 1 << 30))
    ranking = jnp.argsort(ranking_key, axis=-1)[..., :TOPK]
    chosen = jnp.take_along_axis(candidates, ranking, axis=-1)
    chosen_valid = jnp.take_along_axis(usable, ranking, axis=-1)
    selected = jnp.where(chosen_valid, chosen, -1).astype(jnp.int32)
    return (offered, selected)


def draw_offered(key, part):
    return build_plan(key)[0]


def draw_selected(key, part):
    return build_plan(key)[1]


def block_levels(key, dims, cuts, low, top_value):
    loudness, own = 1.0, jax.random.fold_in(key, 6)
    for axis_at, shards_of in cuts:
        steps = jnp.exp(jax.random.uniform(jax.random.fold_in(own, axis_at), (shards_of,), jnp.float32, low / len(cuts), top_value / len(cuts)))
        loudness = loudness * jnp.repeat(steps, dims[axis_at] // shards_of).reshape([-1 if axis == axis_at else 1 for axis in range(len(dims))])
    return loudness


def scatter_about(key, shape, spread, limit, cuts=(), held_as=jnp.bfloat16):
    gain = block_levels(key, shape, cuts, -0.22, 0.18) if cuts else 1.0
    entries = jax.random.normal(key, shape, jnp.float32) * spread * gain
    return jnp.minimum(jnp.maximum(entries, -limit), limit).astype(held_as)


def setup_inputs(seed: int = 0) -> dict:
    splits = jax.random.split(jax.random.key(seed), 9)
    q_nope = scatter_about(splits[0], (BATCH, LENGTH, H * NOPE), 1.0, 6.0, ((0, 4), (1, 8)))
    q_rope = scatter_about(splits[1], (BATCH, LENGTH, H * ROPE), 1.0, 6.0, ((0, 4), (1, 8)))
    grad_out = scatter_about(splits[2], (BATCH, LENGTH, H * VDIM), 1.0, 6.0, ((0, 4), (1, 8)))
    log_total = jnp.clip(5.0 + 1.5 * jax.random.uniform(splits[3], (BATCH, H, LENGTH), jnp.float32) ** block_levels(splits[3], (BATCH, H, LENGTH), ((0, 4), (2, 8)), -0.2, 0.2), 5.0, 6.5)
    kv_latent = scatter_about(splits[4], (BATCH, LENGTH, LAT + ROPE), 1.0, 6.0, ((0, 4), (1, 8)))
    up_weight = scatter_about(splits[5], (LAT, H * (NOPE + VDIM)), LAT ** -0.5, 0.375, ((0, 8),))
    selected = draw_selected(jax.random.fold_in(splits[8], 71), 0)
    offered = draw_offered(jax.random.fold_in(splits[8], 71), 0)
    return {"q_nope": q_nope, "q_rope": q_rope, "grad_out": grad_out, "log_total": log_total, "kv_latent": kv_latent, "up_weight": up_weight, "selected": selected, "offered": offered}


partner_offsets = (1, 2, 3, 4)

def allowed_mask(selection, key_ids, first_query):
    query_ids = first_query + jnp.arange(selection.shape[0], dtype=jnp.int32)
    same_block = key_ids[None, :] == query_ids[:, None]
    picked = jnp.any(selection[:, :, None] == key_ids[None, None, :], axis=1) & (key_ids >= 0)[None, :]
    inner = jnp.arange(BLOCK, dtype=jnp.int32)
    causal = inner[:, None] >= inner[None, :]
    block_mask = picked[:, None, :, None] | same_block[:, None, :, None] & causal[None, :, None, :]
    return block_mask.reshape(selection.shape[0] * BLOCK, key_ids.shape[0] * BLOCK)

def head_backward(queries, rope_queries, out_grads, totals, key_part, value_part, rope_keys, allowed):
    softmax_scale = 1.0 / jnp.sqrt(jnp.float32(NOPE + ROPE))
    queries32 = queries.astype(jnp.float32)
    rope32 = rope_queries.astype(jnp.float32)
    grads32 = out_grads.astype(jnp.float32)
    keys32 = key_part.astype(jnp.float32)
    values32 = value_part.astype(jnp.float32)
    ropek32 = rope_keys.astype(jnp.float32)
    scores = (jnp.einsum('qhd,khd->hqk', queries32, keys32) + jnp.einsum('qhd,kd->hqk', rope32, ropek32)) * softmax_scale
    probabilities = jnp.where(allowed[None], jnp.exp(scores - totals[:, :, None]), jnp.float32(0.0))
    prob_grads = jnp.einsum('qhd,khd->hqk', grads32, values32)
    row_dot = lax.optimization_barrier(jnp.sum(probabilities * prob_grads, axis=2, keepdims=True))
    score_grads = (probabilities * (prob_grads - row_dot)).astype(jnp.bfloat16).astype(jnp.float32)
    probs_low = probabilities.astype(jnp.bfloat16).astype(jnp.float32)
    grad_nope = (jnp.einsum('hqk,khd->qhd', score_grads, keys32) * softmax_scale).astype(jnp.bfloat16)
    grad_rope = (jnp.einsum('hqk,kd->qhd', score_grads, ropek32) * softmax_scale).astype(jnp.bfloat16)
    key_grad = jnp.einsum('hqk,qhd->khd', score_grads, queries32) * softmax_scale
    value_grad = jnp.einsum('hqk,qhd->khd', probs_low, grads32)
    both_grads = jnp.concatenate([key_grad, value_grad], axis=2).astype(jnp.bfloat16)
    rope_grad = jnp.einsum('hqk,qhd->kd', score_grads, rope32) * softmax_scale
    return (grad_nope, grad_rope, both_grads, rope_grad)

def group_backward(queries, rope_queries, out_grads, totals, candidates, weight, allowed):
    latent_cols = candidates[:, :LAT]
    rope_keys = candidates[:, LAT:]
    expanded = jnp.dot(latent_cols, weight, preferred_element_type=jnp.float32).astype(jnp.bfloat16)
    query_len = queries.shape[0]
    key_len = candidates.shape[0]
    head_count = totals.shape[0]
    per_group = 8 if head_count % 8 == 0 else head_count
    groups = head_count // per_group

    def regroup(array, width, length):
        return array.reshape(length, groups, per_group, width).transpose(1, 0, 2, 3)
    both_parts = regroup(expanded, NOPE + VDIM, key_len)
    items = (regroup(queries, NOPE, query_len), regroup(rope_queries, ROPE, query_len), regroup(out_grads, VDIM, query_len), totals.reshape(groups, per_group, query_len), both_parts[..., :NOPE], both_parts[..., NOPE:])

    def one_heads(entry):
        return head_backward(entry[0], entry[1], entry[2], entry[3], entry[4], entry[5], rope_keys, allowed)
    results = lax.map(one_heads, items)
    grad_nope = results[0].transpose(1, 0, 2, 3).reshape(query_len, head_count * NOPE)
    grad_rope = results[1].transpose(1, 0, 2, 3).reshape(query_len, head_count * ROPE)
    key_grads = results[2].transpose(1, 0, 2, 3).reshape(key_len, head_count * (NOPE + VDIM))
    rope_part = lax.optimization_barrier(jnp.sum(results[3], axis=0))
    latent_grad = jnp.dot(key_grads, weight.T, preferred_element_type=jnp.float32)
    cand_grad = jnp.concatenate([latent_grad, rope_part], axis=1)
    return (grad_nope, grad_rope, key_grads, cand_grad)

def reference(q_nope, q_rope, grad_out, log_total, kv_latent, up_weight, selected, offered):
    per_block = TOK_DEV // BLOCK

    def one_sequence(weight_sum, inputs):
        queries, rope_queries, out_grads, totals, latent_rows, selection, offer_plan = inputs

        def one_group(state_pair, group_index):
            grad_rows, weight_acc = state_pair
            begin_row = (group_index * TOK_DEV).astype(jnp.int32)
            pieces = [lax.dynamic_slice_in_dim(latent_rows, begin_row, TOK_DEV, 0)]
            piece_ids = [group_index * per_block + jnp.arange(per_block, dtype=jnp.int32)]
            first_rows = []
            usable_list = []
            for matching, offset in enumerate(partner_offsets):
                source = group_index - offset
                usable = source >= 0
                sender = jnp.maximum(source, 0)
                block_index = offer_plan[sender, matching]
                first_row = (sender * TOK_DEV + block_index * BLOCK).astype(jnp.int32)
                block_rows = lax.dynamic_slice_in_dim(latent_rows, first_row, BLOCK, 0)
                pieces.append(jnp.where(usable, block_rows, jnp.zeros_like(block_rows)))
                piece_ids.append(jnp.where(usable, sender * per_block + block_index, -1).astype(jnp.int32)[None])
                first_rows.append(first_row)
                usable_list.append(usable)
            candidates = jnp.concatenate(pieces, axis=0)
            key_ids = jnp.concatenate(piece_ids, axis=0)
            own_selection = lax.dynamic_slice_in_dim(selection, (group_index * per_block).astype(jnp.int32), per_block, 0)
            allowed = allowed_mask(own_selection, key_ids, group_index * per_block)
            grad_nope, grad_rope, key_grads, cand_grad = group_backward(lax.dynamic_slice_in_dim(queries, begin_row, TOK_DEV, 0), lax.dynamic_slice_in_dim(rope_queries, begin_row, TOK_DEV, 0), lax.dynamic_slice_in_dim(out_grads, begin_row, TOK_DEV, 0), lax.dynamic_slice_in_dim(totals, begin_row, TOK_DEV, 1), candidates, up_weight, allowed)
            own_now = lax.dynamic_slice_in_dim(grad_rows, begin_row, TOK_DEV, 0)
            grad_rows = lax.dynamic_update_slice_in_dim(grad_rows, own_now + cand_grad[:TOK_DEV], begin_row, 0)
            for matching in range(4):
                returned = cand_grad[TOK_DEV + matching * BLOCK:TOK_DEV + (matching + 1) * BLOCK]
                returned = jnp.where(usable_list[matching], returned, jnp.zeros_like(returned))
                current = lax.dynamic_slice_in_dim(grad_rows, first_rows[matching], BLOCK, 0)
                grad_rows = lax.dynamic_update_slice_in_dim(grad_rows, current + returned, first_rows[matching], 0)
            weight_acc = weight_acc + lax.dot_general(candidates[:, :LAT], key_grads, (((0,), (0,)), ((), ())), preferred_element_type=jnp.float32)
            return ((grad_rows, weight_acc), (grad_nope, grad_rope))
        zero_rows = jnp.zeros((LENGTH, LAT + ROPE), jnp.float32)
        (grad_rows, weight_sum), (nope_parts, rope_parts) = lax.scan(one_group, (zero_rows, weight_sum), jnp.arange(N_CTX, dtype=jnp.int32))
        return (weight_sum, (nope_parts.reshape(LENGTH, H * NOPE), rope_parts.reshape(LENGTH, H * ROPE), grad_rows))
    weight_zero = jnp.zeros((LAT, H * (NOPE + VDIM)), jnp.float32)
    weight_sum, (grad_nope, grad_rope, grad_rows) = lax.scan(one_sequence, weight_zero, (q_nope, q_rope, grad_out, log_total, kv_latent, selected, offered))
    return (grad_nope, grad_rope, grad_rows, weight_sum)
```

```python
import functools

import jax
import jax.numpy as jnp
from jax import lax
from jax.experimental import pallas as pl
from jax.experimental.pallas import tpu as pltpu
from jax.sharding import PartitionSpec as P

LAT = 256
ROPE = 64
NOPE = 128
VDIM = 128
BLOCK = 64

partner_offsets = (1, 2, 3, 4)
HIDDEN = -1e30
KERNEL_BYTES = 12 * 1024 * 1024
INPUT_BYTES = 56 * 1024 * 1024


def from_behind(value, axis, steps):
    count = lax.axis_size(axis)
    initial, last = (max(0, -steps), min(count, count - steps))
    return lax.ppermute(value, axis, [(source, source + steps) for source in range(initial, last)])


def exchange(value, axis, bits):
    count = lax.axis_size(axis)
    return lax.ppermute(value, axis, [(source, source ^ bits) for source in range(count)])


def after(value, *earlier):
    return lax.optimization_barrier((value, *earlier))[0]


def dot(left, right, left_dim, right_dim):
    return lax.dot_general(
        left,
        right,
        (((left_dim,), (right_dim,)), ((), ())),
        preferred_element_type=jnp.float32,
    )


def heads_kernel(
    place,
    q_own, rope_own, out_own, tot_own,
    q_sib, rope_sib, out_sib, tot_sib,
    weight, cand, cand_t, rope_keys, bias,
    *rest,
    earlier,
):
    gq_own, gr_own, sib_grads, *weight_grads, lat_sum, rope_sum = rest[earlier:]
    scale = 1.0 / jnp.sqrt(jnp.float32(NOPE + ROPE))
    rows = cand.shape[0] // 2
    half = weight_grads[0].shape[0]
    part = pl.program_id(0) * (len(weight_grads) // 2) // pl.num_programs(0)
    sib_q, sib_rope = sib_grads.at[:, : 2 * NOPE], sib_grads.at[:, 2 * NOPE :]
    lane_half = lax.broadcasted_iota(jnp.int32, (rows, 2 * ROPE), 1) // ROPE

    @pl.when(pl.program_id(0) == 0)
    def _():
        lat_sum[...] = jnp.zeros_like(lat_sum)
        rope_sum[...] = jnp.zeros_like(rope_sum)

    groups = (
        (q_own, rope_own, out_own, tot_own, gq_own, gr_own),
        (q_sib, rope_sib, out_sib, tot_sib, sib_q, sib_rope),
    )
    rope_grads = [None, None]
    for head in range(2):
        columns = pl.ds(head * (NOPE + VDIM), NOPE + VDIM)
        head_weight = weight[:, columns]
        expanded = dot(cand[...], head_weight, 1, 0).astype(jnp.bfloat16)
        both_grads = []
        for side, (q_ref, rope_ref, out_ref, tot_ref, gq_ref, gr_ref) in enumerate(groups):
            own_rows = slice(side * rows, (side + 1) * rows)
            here = pl.ds(head * NOPE, NOPE)
            rope_part = jnp.where(
                lane_half == head, rope_keys[own_rows, :], jnp.zeros((), jnp.bfloat16)
            )
            keys = jnp.concatenate([expanded[own_rows, :NOPE], rope_part], axis=1)
            values = expanded[own_rows, NOPE:]
            queries = jnp.concatenate([q_ref[:, here], rope_ref[...]], axis=1)
            out_grads = out_ref[:, here]
            scores = dot(keys, queries, 1, 1) * scale
            probs = jnp.exp(scores - tot_ref[0, head : head + 1, :] + bias[own_rows, :])
            prob_grads = dot(values, out_grads, 1, 1)
            row_dot = jnp.sum(probs * prob_grads, axis=0, keepdims=True)
            score_grads = (probs * (prob_grads - row_dot)).astype(jnp.bfloat16)
            query_grad = dot(score_grads, keys, 0, 0) * scale
            gq_ref[:, here] = query_grad[:, :NOPE].astype(jnp.bfloat16)
            if head == 0:
                rope_grads[side] = query_grad[:, NOPE:]
            else:
                gr_ref[...] = (rope_grads[side] + query_grad[:, NOPE:]).astype(jnp.bfloat16)
            key_grad = dot(score_grads, queries, 1, 0) * scale
            value_grad = dot(probs.astype(jnp.bfloat16), out_grads, 1, 0)
            rope_sum[own_rows, :] += jnp.where(lane_half == head, key_grad[:, NOPE:], 0.0)
            both_grads.append(
                jnp.concatenate([key_grad[:, :NOPE], value_grad], axis=1).astype(jnp.bfloat16)
            )
        key_grads = jnp.concatenate(both_grads, axis=0)
        lat_sum[...] += dot(key_grads, head_weight, 1, 1)
        weight_grad = dot(cand_t[...], key_grads, 1, 0)
        for at in range(len(weight_grads) // 2):

            @pl.when(part == at)
            def _():
                weight_grads[2 * at][:, columns] = weight_grad[:half]
                weight_grads[2 * at + 1][:, columns] = weight_grad[half:]


def chunk_backward(place, own, packed, totals, weight, shared, earlier, sizes, parts):
    q_own, rope_own, out_own = own
    tot_own, tot_sib = totals
    cand, cand_t, rope_keys, bias = shared
    tokens = q_own.shape[0]
    chunks, pairs = sizes
    wide, narrow = 2 * NOPE, 2 * ROPE
    span = pairs * (2 * wide + narrow)
    mine = lambda p, place: (place[0] * 2 + place[1]) * pairs + p
    theirs = lambda p, place: place[0] * pairs + p
    part_pairs = pairs // parts

    def part_block(part):
        return lambda p, place: (0, jnp.clip(p - part * part_pairs, 0, part_pairs - 1))

    whole = lambda array: pl.BlockSpec(array.shape, lambda p, place: (0, 0))
    in_specs = [
        pl.BlockSpec((tokens, wide), lambda p, place: (0, mine(p, place))),
        pl.BlockSpec((tokens, narrow), lambda p, place: (0, mine(p, place))),
        pl.BlockSpec((tokens, wide), lambda p, place: (0, mine(p, place))),
        pl.BlockSpec((1, 2, tokens), lambda p, place: (mine(p, place), 0, 0)),
        pl.BlockSpec((tokens, wide), lambda p, place: (0, place[0] * (span // wide) + p)),
        pl.BlockSpec(
            (tokens, narrow),
            lambda p, place: (0, place[0] * (span // narrow) + pairs * wide // narrow + p),
        ),
        pl.BlockSpec(
            (tokens, wide),
            lambda p, place: (0, place[0] * (span // wide) + pairs * (wide + narrow) // wide + p),
        ),
        pl.BlockSpec((1, 2, tokens), lambda p, place: (theirs(p, place), 0, 0)),
        pl.BlockSpec((LAT, 2 * (NOPE + VDIM)), lambda p, place: (0, p)),
        whole(cand),
        whole(cand_t),
        whole(rope_keys),
        whole(bias),
    ]
    operands = [q_own, rope_own, out_own, tot_own, packed, packed, packed, tot_sib, weight]
    operands += [cand, cand_t, rope_keys, bias]
    aliases = {}
    if earlier is not None:
        for index, array in enumerate(earlier):
            aliases[1 + len(operands)] = index
            in_specs.append(pl.BlockSpec(memory_space=pl.ANY))
            operands.append(array)
    columns = weight.shape[1]
    bf16, f32 = jnp.bfloat16, jnp.float32
    out_shape = [
        jax.ShapeDtypeStruct(q_own.shape, bf16),
        jax.ShapeDtypeStruct(rope_own.shape, bf16),
        jax.ShapeDtypeStruct((tokens, chunks * pairs * (wide + narrow)), bf16),
        *[jax.ShapeDtypeStruct((LAT // 2, columns // parts), f32)] * (2 * parts),
        jax.ShapeDtypeStruct((cand.shape[0], LAT), f32),
        jax.ShapeDtypeStruct((cand.shape[0], narrow), f32),
    ]
    out_specs = [
        pl.BlockSpec((tokens, wide), lambda p, place: (0, mine(p, place))),
        pl.BlockSpec((tokens, narrow), lambda p, place: (0, mine(p, place))),
        pl.BlockSpec((tokens, wide + narrow), lambda p, place: (0, theirs(p, place))),
        *[
            pl.BlockSpec((LAT // 2, 2 * (NOPE + VDIM)), part_block(part // 2))
            for part in range(2 * parts)
        ],
        pl.BlockSpec((cand.shape[0], LAT), lambda p, place: (0, 0)),
        pl.BlockSpec((cand.shape[0], narrow), lambda p, place: (0, 0)),
    ]
    return pl.pallas_call(
        functools.partial(heads_kernel, earlier=len(aliases)),
        grid_spec=pltpu.PrefetchScalarGridSpec(
            num_scalar_prefetch=1, grid=(pairs,), in_specs=in_specs, out_specs=out_specs
        ),
        out_shape=out_shape,
        input_output_aliases=aliases,
        compiler_params=pltpu.CompilerParams(vmem_limit_bytes=KERNEL_BYTES),
        cost_estimate=pl.CostEstimate(
            flops=pairs * 1_000_000_000, bytes_accessed=pairs * 3_000_000, transcendentals=0
        ),
        name="heads_backward",
    )(place, *operands)


def place_kernel(place, received, q_in, rope_in, q_out, rope_out):
    wide, narrow = 2 * NOPE, 2 * ROPE
    for pair in range(q_out.shape[1] // wide):
        start = pair * (wide + narrow)
        q_out[:, pair * wide : (pair + 1) * wide] = received[:, start : start + wide]
        rope_out[:, pair * narrow : (pair + 1) * narrow] = received[
            :, start + wide : start + wide + narrow
        ]


def place_columns(place, received, q_full, rope_full, chunks):
    tokens = q_full.shape[0]
    q_cols, rope_cols = q_full.shape[1] // chunks // 2, rope_full.shape[1] // chunks // 2
    put = lambda c, place: (0, c * 2 + 1 - place[1])
    return pl.pallas_call(
        place_kernel,
        grid_spec=pltpu.PrefetchScalarGridSpec(
            num_scalar_prefetch=1,
            grid=(chunks,),
            in_specs=[
                pl.BlockSpec((tokens, q_cols + rope_cols), lambda c, place: (0, c)),
                pl.BlockSpec(memory_space=pl.ANY),
                pl.BlockSpec(memory_space=pl.ANY),
            ],
            out_specs=[
                pl.BlockSpec((tokens, q_cols), put),
                pl.BlockSpec((tokens, rope_cols), put),
            ],
        ),
        out_shape=[
            jax.ShapeDtypeStruct(q_full.shape, q_full.dtype),
            jax.ShapeDtypeStruct(rope_full.shape, rope_full.dtype),
        ],
        input_output_aliases={2: 0, 3: 1},
        compiler_params=pltpu.CompilerParams(vmem_limit_bytes=KERNEL_BYTES),
        cost_estimate=pl.CostEstimate(flops=0, bytes_accessed=4_000_000, transcendentals=0),
        name="place_columns",
    )(place, received, q_full, rope_full)


def stack_kernel(*refs, arrangement):
    outs = refs[len(refs) - len(arrangement) :]
    for out, sources in zip(outs, arrangement):
        row = 0
        for index, block in sources:
            piece = refs[index]
            columns = slice(block * out.shape[1], (block + 1) * out.shape[1])
            out[row : row + piece.shape[0], :] = piece[:, columns]
            row += piece.shape[0]


def stack(inputs, arrangement, columns):
    whole = lambda shape: pl.BlockSpec(shape, lambda: (0, 0))
    shapes = [(sum(inputs[i].shape[0] for i, _ in sources), columns) for sources in arrangement]
    return pl.pallas_call(
        functools.partial(stack_kernel, arrangement=arrangement),
        in_specs=[whole(array.shape) for array in inputs],
        out_specs=[whole(shape) for shape in shapes],
        out_shape=[jax.ShapeDtypeStruct(shape, inputs[0].dtype) for shape in shapes],
        compiler_params=pltpu.CompilerParams(vmem_limit_bytes=KERNEL_BYTES),
        cost_estimate=pl.CostEstimate(flops=0, bytes_accessed=2_000_000, transcendentals=0),
        name="stack",
    )(*inputs)


def leave_kernel(place, *refs):
    *inputs, leaving, near, distant = refs
    staying, half = (near, distant), len(inputs) // 2
    width = inputs[0].shape[1]
    for at in range(half):
        leaving[:, at * width : (at + 1) * width] = inputs[at][...]
        staying[at][...] = inputs[half + at][...]


def weight_parts(place, up_weight, chunks, far):
    rows = up_weight.shape[0]
    width = up_weight.shape[1] // chunks // 2

    def column_block(t, other):
        def block(i, place):
            return (0, (place[0] ^ t) * 2 + (1 - place[1] if other else place[1]))

        return pl.BlockSpec((rows, width), block)

    return pl.pallas_call(
        leave_kernel,
        grid_spec=pltpu.PrefetchScalarGridSpec(
            num_scalar_prefetch=1,
            grid=(1,),
            in_specs=[column_block(t, other) for other in (True, False) for t in (0, far)],
            out_specs=[pl.BlockSpec((rows, 2 * width), lambda i, place: (0, 0))]
            + [pl.BlockSpec((rows, width), lambda i, place: (0, 0))] * 2,
        ),
        out_shape=[jax.ShapeDtypeStruct((rows, 2 * width), up_weight.dtype)]
        + [jax.ShapeDtypeStruct((rows, width), up_weight.dtype)] * 2,
        compiler_params=pltpu.CompilerParams(vmem_limit_bytes=INPUT_BYTES),
        cost_estimate=pl.CostEstimate(flops=0, bytes_accessed=1_000_000, transcendentals=0),
        name="weight_parts",
    )(place, *[up_weight] * 4)


def lay_kernel(place, *refs):
    *pieces, out = refs
    width = out.shape[1] // 4
    for step in range(len(pieces) // 2):
        early, late = pieces[2 * step], pieces[2 * step + 1]

        @pl.when(pl.program_id(0) == step)
        def _():
            for which in range(2):
                source = slice(which * width, (which + 1) * width)
                out[:, 2 * which * width : (2 * which + 1) * width] = early[:, source]
                out[:, (2 * which + 1) * width : (2 * which + 2) * width] = late[:, source]


def lay_out(place, pieces):
    rows, columns = pieces[0].shape
    count = len(pieces) // 2
    return pl.pallas_call(
        lay_kernel,
        grid_spec=pltpu.PrefetchScalarGridSpec(
            num_scalar_prefetch=1,
            grid=(count,),
            in_specs=[pl.BlockSpec((rows, columns), lambda t, place: (0, 0))] * len(pieces),
            out_specs=pl.BlockSpec((rows, 2 * columns), lambda t, place: (0, place[0] ^ t)),
        ),
        out_shape=jax.ShapeDtypeStruct((rows, count * 2 * columns), pieces[0].dtype),
        compiler_params=pltpu.CompilerParams(vmem_limit_bytes=KERNEL_BYTES),
        cost_estimate=pl.CostEstimate(flops=0, bytes_accessed=4_000_000, transcendentals=0),
        name="lay_out",
    )(place, *pieces)


def pack_kernel(place, q_ref, rope_ref, out_ref, packed):
    q_cols, rope_cols = q_ref.shape[1], rope_ref.shape[1]
    packed[:, :q_cols] = q_ref[...]
    packed[:, q_cols : q_cols + rope_cols] = rope_ref[...]
    packed[:, q_cols + rope_cols :] = out_ref[...]


def pack_columns(place, arrays, chunks):
    tokens = arrays[0].shape[0]
    widths = [array.shape[1] // chunks // 2 for array in arrays]
    theirs = lambda c, place: (0, c * 2 + 1 - place[1])
    return pl.pallas_call(
        pack_kernel,
        grid_spec=pltpu.PrefetchScalarGridSpec(
            num_scalar_prefetch=1,
            grid=(chunks,),
            in_specs=[pl.BlockSpec((tokens, width), theirs) for width in widths],
            out_specs=pl.BlockSpec((tokens, sum(widths)), lambda c, place: (0, c)),
        ),
        out_shape=jax.ShapeDtypeStruct((tokens, chunks * sum(widths)), arrays[0].dtype),
        compiler_params=pltpu.CompilerParams(vmem_limit_bytes=INPUT_BYTES),
        cost_estimate=pl.CostEstimate(flops=0, bytes_accessed=5_000_000, transcendentals=0),
        name="pack_columns",
    )(place, *arrays)


def halving_order(count):
    bits = count.bit_length() - 1
    partners = []
    for place in range(count):
        partner = place & 1
        for bit in range(1, bits):
            partner |= ((place >> (bits - bit)) & 1) << bit
        partners.append(partner)
    return partners


def channel_order(ctx, lat_block):
    channel = lax.broadcasted_iota(jnp.int32, (LAT, LAT), 0)
    place = lax.broadcasted_iota(jnp.int32, (LAT, LAT), 1)
    count = LAT // lat_block
    bits = count.bit_length() - 1
    block = place // lat_block
    partner = block & 1
    for bit in range(1, bits):
        partner |= ((block >> (bits - bit)) & 1) << bit
    return channel == (ctx ^ partner) * lat_block + place % lat_block


def collect_kernel(plan, own, sib, cand, cand_t, rope_keys, bias, *, blocks, lat_block):
    pieces = []
    key_at = lax.broadcasted_iota(jnp.int32, (BLOCK, 2 * BLOCK), 0)
    query = lax.broadcasted_iota(jnp.int32, (BLOCK, 2 * BLOCK), 1)
    per_side = len(blocks) // 2
    for block, other in enumerate(blocks):
        rows_ref = sib if other else own
        start = pl.multiple_of(plan[1 + block], 16)
        rows = rows_ref[pl.ds(start, BLOCK), :]
        usable = plan[1 + len(blocks) + block]
        pieces.append(jnp.where(usable > 0, rows, jnp.zeros_like(rows)))
        side, at = divmod(block, per_side)
        kinds = (sib if side else own)[2 * BLOCK : 2 * BLOCK + 16, :][:1].astype(jnp.float32)
        kind = jnp.where(
            query < BLOCK, kinds[:, 2 * at : 2 * at + 1], kinds[:, 2 * at + 1 : 2 * at + 2]
        )
        allowed = (kind > 1.5) | (kind > 0.5) & (key_at <= query % BLOCK)
        bias[block * BLOCK : (block + 1) * BLOCK, :] = jnp.where(allowed, 0.0, HIDDEN)
    both = jnp.concatenate(pieces, axis=0)
    order = channel_order(plan[0], lat_block).astype(jnp.bfloat16)
    latent = both[:, :LAT]
    cand[...] = dot(latent, order, 1, 0).astype(jnp.bfloat16)
    cand_t[...] = dot(order, latent, 0, 1).astype(jnp.bfloat16)
    twice = lax.broadcasted_iota(jnp.int32, (ROPE, 2 * ROPE), 0)
    twice = twice == lax.broadcasted_iota(jnp.int32, (ROPE, 2 * ROPE), 1) % ROPE
    rope_keys[...] = dot(both[:, LAT:], twice.astype(jnp.bfloat16), 1, 0).astype(jnp.bfloat16)


def collect(plan, own, sib, blocks, lat_block):
    rows = len(blocks) * BLOCK
    bf16 = jnp.bfloat16
    shapes = [((rows, LAT), bf16), ((LAT, rows), bf16), ((rows, 2 * ROPE), bf16)]
    shapes.append(((rows, 2 * BLOCK), jnp.float32))
    whole = lambda shape: pl.BlockSpec(shape, lambda i, plan: (0, 0))
    return pl.pallas_call(
        functools.partial(collect_kernel, blocks=blocks, lat_block=lat_block),
        grid_spec=pltpu.PrefetchScalarGridSpec(
            num_scalar_prefetch=1,
            grid=(1,),
            in_specs=[whole(own.shape), whole(sib.shape)],
            out_specs=[whole(shape) for shape, _ in shapes],
        ),
        out_shape=[jax.ShapeDtypeStruct(shape, dtype) for shape, dtype in shapes],
        compiler_params=pltpu.CompilerParams(vmem_limit_bytes=KERNEL_BYTES),
        cost_estimate=pl.CostEstimate(
            flops=250_000_000, bytes_accessed=3_000_000, transcendentals=0
        ),
        name="collect",
    )(plan, own, sib)


def spread_kernel(plan, *refs, blocks, lat_block):
    *sums, own, sib = refs
    count = len(sums) // 2
    latent, rope = sums[0][...], sums[count][...]
    for index in range(1, count):
        latent, rope = latent + sums[index][...], rope + sums[count + index][...]
    order = channel_order(plan[0], lat_block).astype(jnp.float32)
    latent = lax.dot_general(
        latent,
        order,
        (((1,), (1,)), ((), ())),
        precision=lax.Precision.HIGHEST,
        preferred_element_type=jnp.float32,
    )
    rows = jnp.concatenate([latent, rope[:, :ROPE] + rope[:, ROPE:]], axis=1)
    own[...] = jnp.zeros_like(own)
    sib[...] = jnp.zeros_like(sib)
    for block, other in enumerate(blocks):
        here = pl.ds(pl.multiple_of(plan[1 + block], 16), BLOCK)
        target = sib if other else own
        target[here, :] += rows[block * BLOCK : (block + 1) * BLOCK]


def spread(plan, latents, ropes, rows, blocks, lat_block):
    shape = (rows, LAT + ROPE)
    sums = [*latents, *ropes]
    return pl.pallas_call(
        functools.partial(spread_kernel, blocks=blocks, lat_block=lat_block),
        grid_spec=pltpu.PrefetchScalarGridSpec(
            num_scalar_prefetch=1,
            grid=(1,),
            in_specs=[pl.BlockSpec(array.shape, lambda i, plan: (0, 0)) for array in sums],
            out_specs=[pl.BlockSpec(shape, lambda i, plan: (0, 0))] * 2,
        ),
        out_shape=[jax.ShapeDtypeStruct(shape, jnp.float32)] * 2,
        compiler_params=pltpu.CompilerParams(vmem_limit_bytes=KERNEL_BYTES),
        cost_estimate=pl.CostEstimate(
            flops=700_000_000, bytes_accessed=6_000_000, transcendentals=0
        ),
        name="spread",
    )(plan, *sums)


def halve(value, axis, bit):
    half = value.shape[0] // 2
    return value[:half] + exchange(value[half:], axis, bit)


def shards(q_nope, q_rope, grad_out, log_total, kv_latent, up_weight, selected, offered):
    n_dp, n_ctx = lax.axis_size("dp"), lax.axis_size("ctx")
    dp, ctx = lax.axis_index("dp"), lax.axis_index("ctx")
    core = ctx % 2
    group_len = kv_latent.shape[1]
    per_block = group_len // BLOCK
    heads = log_total.shape[1]
    part_heads = heads // n_dp // 2
    pairs = part_heads // 2
    part_cols = part_heads * (NOPE + VDIM)
    far = n_dp - 1
    lat_block = up_weight.shape[0]

    place = jnp.stack([dp, core]).astype(jnp.int32)

    leaving, *staying = weight_parts(place, up_weight, n_dp, far)
    crossed = exchange(leaving, "ctx", 1)
    crossed, q_nope, q_rope, grad_out, log_total, kv_latent = lax.optimization_barrier(
        (crossed, q_nope, q_rope, grad_out, log_total, kv_latent)
    )
    chip_rows = stack(
        [*staying, crossed], (((0, 0), (2, 0)), ((1, 0), (2, 1))), part_cols
    )
    chip_rows, q_nope, q_rope, grad_out, log_total, kv_latent = lax.optimization_barrier(
        (chip_rows, q_nope, q_rope, grad_out, log_total, kv_latent)
    )
    queries, rope_queries, out_grads = q_nope[0], q_rope[0], grad_out[0]

    packed = exchange(
        pack_columns(place, (queries, rope_queries, out_grads), n_dp), "ctx", 1
    )
    totals = log_total[0].reshape(n_dp, 2, pairs, 2, group_len)
    tot_sib = exchange(lax.dynamic_index_in_dim(totals, 1 - core, 1, keepdims=False), "ctx", 1)
    totals = (
        totals.reshape(n_dp * 2 * pairs, 2, group_len),
        tot_sib.reshape(n_dp * pairs, 2, group_len),
    )

    offer_plan = offered[0]
    span = group_len + 16
    blocks, starts, usables = [], [], []
    for side in range(2):
        group = ctx ^ side
        offsets = [0] * per_block + list(partner_offsets)
        blocks += [(offset + side) % 2 for offset in offsets]
        source = jnp.stack([group - offset for offset in offsets])
        sender = jnp.maximum(source, 0)
        inner = jnp.concatenate(
            [
                jnp.arange(per_block, dtype=jnp.int32),
                offer_plan[sender[per_block:], jnp.arange(len(partner_offsets))],
            ]
        )
        usable = source >= 0
        behind = ctx // 2 - sender // 2
        starts.append(jnp.where(usable, behind * span + inner * BLOCK, 0))
        usables.append(usable)
        if side == 0:
            ids = jnp.where(usable, sender * per_block + inner, -1)
            query_ids = group * per_block + jnp.arange(per_block, dtype=jnp.int32)
            picked = jnp.any(selected[0][None, :, :] == ids[:, None, None], axis=2)
            picked = picked & (ids >= 0)[:, None]
            same = ids[:, None] == query_ids[None, :]
            kinds = jnp.where(picked, 2.0, jnp.where(same, 1.0, 0.0)).reshape(1, -1)
    plan = jnp.concatenate([ctx[None], *starts, *usables]).astype(jnp.int32)
    kinds = jnp.pad(kinds.astype(jnp.bfloat16), ((0, 15), (0, LAT + ROPE - kinds.shape[1])))
    bundle = jnp.concatenate([kv_latent[0], kinds], axis=0)
    bundles = [bundle, from_behind(bundle, "ctx", 2), from_behind(bundle, "ctx", 4)]
    own_bundles = stack(bundles, (((0, 0), (1, 0), (2, 0)),), LAT + ROPE)[0]
    sib_bundles = exchange(own_bundles, "ctx", 1)
    shared = collect(plan, own_bundles, sib_bundles, tuple(blocks), lat_block)

    partners = halving_order(n_ctx)[::2]
    weights = {}
    for order, t in enumerate((0, far)):
        at_step = {0: chip_rows[order]}
        if order:
            at_step[0] = after(at_step[0], packed, tot_sib, sib_bundles)
        for step in range(4, n_ctx, 4):
            at_step[step] = exchange(at_step[0], "ctx", step)
        for step in range(2, n_ctx, 4):
            at_step[step] = exchange(at_step[step - 2], "ctx", 2)
        pieces = [at_step[partner] for partner in partners]
        weights[t] = stack(
            pieces, (tuple((index, 0) for index in range(len(pieces))),), part_cols
        )[0]
    for t in range(1, far):
        weights[t] = exchange(weights[0], "dp", t)

    earlier = None
    weight_grads, latents, ropes = {}, [], []
    for t in [0, far] + list(range(1, far)):
        split = 1 if t in (0, far) else 2
        rest = chunk_backward(
            jnp.stack([dp ^ t, core]).astype(jnp.int32),
            (queries, rope_queries, out_grads),
            packed,
            totals,
            weights[t],
            shared,
            earlier,
            (n_dp, pairs),
            split,
        )
        earlier, rest = rest[:3], rest[3:]
        weight_grads[t] = (rest[0 : 2 * split : 2], rest[1 : 2 * split : 2])
        latents.append(rest[-2])
        ropes.append(rest[-1])

    q_full, rope_full, sib_grads = earlier
    received = exchange(sib_grads, "ctx", 1)
    grad_nope, grad_rope = place_columns(place, received, q_full, rope_full, n_dp)

    own_grads, sib_grads = spread(plan, latents, ropes, 3 * span, tuple(blocks), lat_block)
    grad_rows = own_grads + exchange(sib_grads, "ctx", 1)
    by_chip = [grad_rows[at * span : at * span + group_len] for at in range(3)]
    grad_rows = by_chip[0]
    for chips in (1, 2):
        grad_rows = grad_rows + from_behind(by_chip[chips], "ctx", -2 * chips)

    bits = [1 << b for b in range(n_dp.bit_length() - 1)]
    half_cols = part_cols // 2
    sums = []
    for side, order in enumerate((bits, bits[::-1])):
        parts = {t: list(weight_grads[t][side]) for t in weight_grads}
        for bit in order:
            arrived = {}
            for t in sorted((t for t in parts if t & bit), reverse=True):
                arrived[t ^ bit] = [exchange(part, "dp", bit) for part in parts[t]]
            summed = {}
            for t, more in arrived.items():
                mine = parts[t]
                pieces = []
                for half in range(2):
                    columns = slice(half * half_cols, (half + 1) * half_cols)
                    pieces.append(
                        (mine[half] if len(mine) == 2 else mine[0][:, columns])
                        + (more[half] if len(more) == 2 else more[0][:, columns])
                    )
                summed[t] = pieces
            parts = summed
        sums.append(parts[0])

    ctx_bits = [1 << b for b in range(1, n_ctx.bit_length() - 1)]
    finished = []
    for half in range(2):
        rows = sums[0][half] + exchange(sums[1][half], "ctx", ctx_bits[0])
        for bit in ctx_bits[1:]:
            rows = halve(rows, "ctx", bit)
        kept, crossed = rows[:lat_block], exchange(rows[lat_block:], "ctx", 1)
        piece = jnp.where(
            core == 0,
            jnp.concatenate([kept, crossed], axis=1),
            jnp.concatenate([crossed, kept], axis=1),
        )
        finished.append([piece] + [exchange(piece, "dp", t) for t in range(1, n_dp)])
    grad_weight = lay_out(place, [piece for both in zip(*finished) for piece in both])
    return (grad_nope[None], grad_rope[None], grad_rows[None], grad_weight)


def solution(mesh):
    in_specs = (
        P("dp", "ctx", None),
        P("dp", "ctx", None),
        P("dp", "ctx", None),
        P("dp", None, "ctx"),
        P("dp", "ctx", None),
        P("ctx", None),
        P("dp", "ctx", None),
        P("dp", None, None),
    )
    out_specs = (P("dp", "ctx", None), P("dp", "ctx", None), P("dp", "ctx", None), P("ctx", None))
    return jax.shard_map(shards, mesh=mesh, in_specs=in_specs, out_specs=out_specs, check_vma=False)
```

```python
import functools

import jax
import jax.numpy as jnp
from jax import lax
from jax.experimental import pallas as pl
from jax.experimental.pallas import tpu as pltpu
from jax.sharding import PartitionSpec as P

LAT = 256
ROPE = 64
NOPE = 128
VDIM = 128
BLOCK = 64

partner_offsets = (1, 2, 3, 4)
HIDDEN = -1e30
KERNEL_BYTES = 12 * 1024 * 1024
INPUT_BYTES = 56 * 1024 * 1024


def from_behind(value, axis, steps):
    count = lax.axis_size(axis)
    initial, last = (max(0, -steps), min(count, count - steps))
    return lax.ppermute(value, axis, [(source, source + steps) for source in range(initial, last)])


def exchange(value, axis, bits):
    count = lax.axis_size(axis)
    return lax.ppermute(value, axis, [(source, source ^ bits) for source in range(count)])


def after(value, *earlier):
    return lax.optimization_barrier((value, *earlier))[0]


def dot(left, right, left_dim, right_dim):
    return lax.dot_general(
        left,
        right,
        (((left_dim,), (right_dim,)), ((), ())),
        preferred_element_type=jnp.float32,
    )


def heads_kernel(
    place,
    q_own, rope_own, out_own, tot_own,
    q_sib, rope_sib, out_sib, tot_sib,
    weight, cand, cand_t, rope_keys, bias,
    *rest,
    earlier,
):
    gq_own, gr_own, sib_grads, *weight_grads, lat_sum, rope_sum = rest[earlier:]
    scale = 1.0 / jnp.sqrt(jnp.float32(NOPE + ROPE))
    rows = cand.shape[0] // 2
    half = weight_grads[0].shape[0]
    sib_q, sib_rope = sib_grads.at[:, : 2 * NOPE], sib_grads.at[:, 2 * NOPE :]
    lane_half = lax.broadcasted_iota(jnp.int32, (rows, 2 * ROPE), 1) // ROPE

    @pl.when(pl.program_id(0) == 0)
    def _():
        lat_sum[...] = jnp.zeros_like(lat_sum)
        rope_sum[...] = jnp.zeros_like(rope_sum)

    groups = (
        (q_own, rope_own, out_own, tot_own, gq_own, gr_own),
        (q_sib, rope_sib, out_sib, tot_sib, sib_q, sib_rope),
    )
    rope_grads = [None, None]
    for head in range(2):
        columns = pl.ds(head * (NOPE + VDIM), NOPE + VDIM)
        head_weight = weight[:, columns]
        expanded = dot(cand[...], head_weight, 1, 0).astype(jnp.bfloat16)
        both_grads = []
        for side, (q_ref, rope_ref, out_ref, tot_ref, gq_ref, gr_ref) in enumerate(groups):
            own_rows = slice(side * rows, (side + 1) * rows)
            here = pl.ds(head * NOPE, NOPE)
            rope_part = jnp.where(
                lane_half == head, rope_keys[own_rows, :], jnp.zeros((), jnp.bfloat16)
            )
            keys = jnp.concatenate([expanded[own_rows, :NOPE], rope_part], axis=1)
            values = expanded[own_rows, NOPE:]
            queries = jnp.concatenate([q_ref[:, here], rope_ref[...]], axis=1)
            out_grads = out_ref[:, here]
            scores = dot(keys, queries, 1, 1) * scale
            probs = jnp.exp(scores - tot_ref[0, head : head + 1, :] + bias[own_rows, :])
            prob_grads = dot(values, out_grads, 1, 1)
            row_dot = jnp.sum(probs * prob_grads, axis=0, keepdims=True)
            score_grads = (probs * (prob_grads - row_dot)).astype(jnp.bfloat16)
            query_grad = dot(score_grads, keys, 0, 0) * scale
            gq_ref[:, here] = query_grad[:, :NOPE].astype(jnp.bfloat16)
            if head == 0:
                rope_grads[side] = query_grad[:, NOPE:]
            else:
                gr_ref[...] = (rope_grads[side] + query_grad[:, NOPE:]).astype(jnp.bfloat16)
            key_grad = dot(score_grads, queries, 1, 0) * scale
            value_grad = dot(probs.astype(jnp.bfloat16), out_grads, 1, 0)
            rope_sum[own_rows, :] += jnp.where(lane_half == head, key_grad[:, NOPE:], 0.0)
            both_grads.append(
                jnp.concatenate([key_grad[:, :NOPE], value_grad], axis=1).astype(jnp.bfloat16)
            )
        key_grads = jnp.concatenate(both_grads, axis=0)
        lat_sum[...] += dot(key_grads, head_weight, 1, 1)
        weight_grad = dot(cand_t[...], key_grads, 1, 0)
        weight_grads[0][:, columns] = weight_grad[:half]
        weight_grads[1][:, columns] = weight_grad[half:]


def chunk_backward(place, t, unit, own, packed, totals, weight, shared, earlier, sizes):
    q_own, rope_own, out_own = own
    tot_own, tot_sib = totals
    cand, cand_t, rope_keys, bias = shared
    tokens = q_own.shape[0]
    chunks, pairs = sizes
    wide, narrow = 2 * NOPE, 2 * ROPE
    span = pairs * (2 * wide + narrow)
    first, count = unit
    mine = lambda p, place: (place[1 + t] * 2 + place[0]) * pairs + first + p
    theirs = lambda p, place: place[1 + t] * pairs + first + p
    whole = lambda array: pl.BlockSpec(array.shape, lambda p, place: (0, 0))
    in_specs = [
        pl.BlockSpec((tokens, wide), lambda p, place: (0, mine(p, place))),
        pl.BlockSpec((tokens, narrow), lambda p, place: (0, mine(p, place))),
        pl.BlockSpec((tokens, wide), lambda p, place: (0, mine(p, place))),
        pl.BlockSpec((1, 2, tokens), lambda p, place: (mine(p, place), 0, 0)),
        pl.BlockSpec((tokens, wide), lambda p, place: (0, place[1 + t] * (span // wide) + first + p)),
        pl.BlockSpec(
            (tokens, narrow),
            lambda p, place: (0, place[1 + t] * (span // narrow) + pairs * wide // narrow + first + p),
        ),
        pl.BlockSpec(
            (tokens, wide),
            lambda p, place: (0, place[1 + t] * (span // wide) + pairs * (wide + narrow) // wide + first + p),
        ),
        pl.BlockSpec((1, 2, tokens), lambda p, place: (theirs(p, place), 0, 0)),
        pl.BlockSpec((LAT, 2 * (NOPE + VDIM)), lambda p, place: (0, first + p)),
        whole(cand),
        whole(cand_t),
        whole(rope_keys),
        whole(bias),
    ]
    operands = [q_own, rope_own, out_own, tot_own, packed, packed, packed, tot_sib, weight]
    operands += [cand, cand_t, rope_keys, bias]
    aliases = {}
    if earlier is not None:
        for index, array in enumerate(earlier):
            aliases[1 + len(operands)] = index
            in_specs.append(pl.BlockSpec(memory_space=pl.ANY))
            operands.append(array)
    columns = 2 * (NOPE + VDIM) * count
    bf16, f32 = jnp.bfloat16, jnp.float32
    out_shape = [
        jax.ShapeDtypeStruct(q_own.shape, bf16),
        jax.ShapeDtypeStruct(rope_own.shape, bf16),
        jax.ShapeDtypeStruct((tokens, chunks * pairs * (wide + narrow)), bf16),
        *[jax.ShapeDtypeStruct((LAT // 2, columns), f32)] * 2,
        jax.ShapeDtypeStruct((cand.shape[0], LAT), f32),
        jax.ShapeDtypeStruct((cand.shape[0], narrow), f32),
    ]
    out_specs = [
        pl.BlockSpec((tokens, wide), lambda p, place: (0, mine(p, place))),
        pl.BlockSpec((tokens, narrow), lambda p, place: (0, mine(p, place))),
        pl.BlockSpec((tokens, wide + narrow), lambda p, place: (0, theirs(p, place))),
        *[pl.BlockSpec((LAT // 2, 2 * (NOPE + VDIM)), lambda p, place: (0, p))] * 2,
        pl.BlockSpec((cand.shape[0], LAT), lambda p, place: (0, 0)),
        pl.BlockSpec((cand.shape[0], narrow), lambda p, place: (0, 0)),
    ]
    return pl.pallas_call(
        functools.partial(heads_kernel, earlier=len(aliases)),
        grid_spec=pltpu.PrefetchScalarGridSpec(
            num_scalar_prefetch=1, grid=(count,), in_specs=in_specs, out_specs=out_specs
        ),
        out_shape=out_shape,
        input_output_aliases=aliases,
        compiler_params=pltpu.CompilerParams(vmem_limit_bytes=KERNEL_BYTES),
        cost_estimate=pl.CostEstimate(
            flops=count * 100_000_000, bytes_accessed=count * 300_000, transcendentals=0
        ),
        name="heads_backward",
    )(place, *operands)


def place_kernel(place, received, q_in, rope_in, q_out, rope_out):
    wide, narrow = 2 * NOPE, 2 * ROPE
    for pair in range(q_out.shape[1] // wide):
        start = pair * (wide + narrow)
        q_out[:, pair * wide : (pair + 1) * wide] = received[:, start : start + wide]
        rope_out[:, pair * narrow : (pair + 1) * narrow] = received[
            :, start + wide : start + wide + narrow
        ]


def place_columns(place, received, q_full, rope_full, chunks):
    tokens = q_full.shape[0]
    q_cols, rope_cols = q_full.shape[1] // chunks // 2, rope_full.shape[1] // chunks // 2
    put = lambda c, place: (0, c * 2 + 1 - place[0])
    return pl.pallas_call(
        place_kernel,
        grid_spec=pltpu.PrefetchScalarGridSpec(
            num_scalar_prefetch=1,
            grid=(chunks,),
            in_specs=[
                pl.BlockSpec((tokens, q_cols + rope_cols), lambda c, place: (0, c)),
                pl.BlockSpec(memory_space=pl.ANY),
                pl.BlockSpec(memory_space=pl.ANY),
            ],
            out_specs=[
                pl.BlockSpec((tokens, q_cols), put),
                pl.BlockSpec((tokens, rope_cols), put),
            ],
        ),
        out_shape=[
            jax.ShapeDtypeStruct(q_full.shape, q_full.dtype),
            jax.ShapeDtypeStruct(rope_full.shape, rope_full.dtype),
        ],
        input_output_aliases={2: 0, 3: 1},
        compiler_params=pltpu.CompilerParams(vmem_limit_bytes=KERNEL_BYTES),
        cost_estimate=pl.CostEstimate(flops=0, bytes_accessed=4_000_000, transcendentals=0),
        name="place_columns",
    )(place, received, q_full, rope_full)


def stack_kernel(*refs, arrangement):
    outs = refs[len(refs) - len(arrangement) :]
    for out, sources in zip(outs, arrangement):
        row = 0
        for index, block in sources:
            piece = refs[index]
            columns = slice(block * out.shape[1], (block + 1) * out.shape[1])
            out[row : row + piece.shape[0], :] = piece[:, columns]
            row += piece.shape[0]


def stack(inputs, arrangement, columns):
    whole = lambda shape: pl.BlockSpec(shape, lambda: (0, 0))
    shapes = [(sum(inputs[i].shape[0] for i, _ in sources), columns) for sources in arrangement]
    return pl.pallas_call(
        functools.partial(stack_kernel, arrangement=arrangement),
        in_specs=[whole(array.shape) for array in inputs],
        out_specs=[whole(shape) for shape in shapes],
        out_shape=[jax.ShapeDtypeStruct(shape, inputs[0].dtype) for shape in shapes],
        compiler_params=pltpu.CompilerParams(vmem_limit_bytes=KERNEL_BYTES),
        cost_estimate=pl.CostEstimate(flops=0, bytes_accessed=2_000_000, transcendentals=0),
        name="stack",
    )(*inputs)


def leave_kernel(place, *refs):
    *inputs, leaving, near, distant = refs
    staying, half = (near, distant), len(inputs) // 2
    width = inputs[0].shape[1]
    for at in range(half):
        leaving[:, at * width : (at + 1) * width] = inputs[at][...]
        staying[at][...] = inputs[half + at][...]


def weight_parts(place, up_weight, chunks, far):
    rows = up_weight.shape[0]
    width = up_weight.shape[1] // chunks // 2

    def column_block(t, other):
        def block(i, place):
            return (0, place[1 + t] * 2 + (1 - place[0] if other else place[0]))

        return pl.BlockSpec((rows, width), block)

    return pl.pallas_call(
        leave_kernel,
        grid_spec=pltpu.PrefetchScalarGridSpec(
            num_scalar_prefetch=1,
            grid=(1,),
            in_specs=[column_block(t, other) for other in (True, False) for t in (0, far)],
            out_specs=[pl.BlockSpec((rows, 2 * width), lambda i, place: (0, 0))]
            + [pl.BlockSpec((rows, width), lambda i, place: (0, 0))] * 2,
        ),
        out_shape=[jax.ShapeDtypeStruct((rows, 2 * width), up_weight.dtype)]
        + [jax.ShapeDtypeStruct((rows, width), up_weight.dtype)] * 2,
        compiler_params=pltpu.CompilerParams(vmem_limit_bytes=INPUT_BYTES),
        cost_estimate=pl.CostEstimate(flops=0, bytes_accessed=1_000_000, transcendentals=0),
        name="weight_parts",
    )(place, *[up_weight] * 4)


def lay_kernel(place, *refs):
    *pieces, out = refs
    width = out.shape[1] // 4
    for step in range(len(pieces) // 2):
        early, late = pieces[2 * step], pieces[2 * step + 1]

        @pl.when(pl.program_id(0) == step)
        def _():
            for which in range(2):
                source = slice(which * width, (which + 1) * width)
                out[:, 2 * which * width : (2 * which + 1) * width] = early[:, source]
                out[:, (2 * which + 1) * width : (2 * which + 2) * width] = late[:, source]


def lay_out(place, pieces):
    rows, columns = pieces[0].shape
    count = len(pieces) // 2
    return pl.pallas_call(
        lay_kernel,
        grid_spec=pltpu.PrefetchScalarGridSpec(
            num_scalar_prefetch=1,
            grid=(count,),
            in_specs=[pl.BlockSpec((rows, columns), lambda t, place: (0, 0))] * len(pieces),
            out_specs=pl.BlockSpec((rows, 2 * columns), lambda t, place: (0, place[1 + t])),
        ),
        out_shape=jax.ShapeDtypeStruct((rows, count * 2 * columns), pieces[0].dtype),
        compiler_params=pltpu.CompilerParams(vmem_limit_bytes=KERNEL_BYTES),
        cost_estimate=pl.CostEstimate(flops=0, bytes_accessed=4_000_000, transcendentals=0),
        name="lay_out",
    )(place, *pieces)


def piece_kernel(place, kept, crossed, out):
    width = kept.shape[1]

    @pl.when(place[0] == 0)
    def _():
        out[:, :width] = kept[...]
        out[:, width:] = crossed[...]

    @pl.when(place[0] != 0)
    def _():
        out[:, :width] = crossed[...]
        out[:, width:] = kept[...]


def join_cores(place, kept, crossed):
    rows, columns = kept.shape
    return pl.pallas_call(
        piece_kernel,
        grid_spec=pltpu.PrefetchScalarGridSpec(
            num_scalar_prefetch=1,
            grid=(1,),
            in_specs=[pl.BlockSpec((rows, columns), lambda i, place: (0, 0))] * 2,
            out_specs=pl.BlockSpec((rows, 2 * columns), lambda i, place: (0, 0)),
        ),
        out_shape=jax.ShapeDtypeStruct((rows, 2 * columns), kept.dtype),
        compiler_params=pltpu.CompilerParams(vmem_limit_bytes=KERNEL_BYTES),
        cost_estimate=pl.CostEstimate(flops=0, bytes_accessed=500_000, transcendentals=0),
        name="join_cores",
    )(place, kept, crossed)


def pack_kernel(place, q_ref, rope_ref, out_ref, packed):
    q_cols, rope_cols = q_ref.shape[1], rope_ref.shape[1]
    packed[:, :q_cols] = q_ref[...]
    packed[:, q_cols : q_cols + rope_cols] = rope_ref[...]
    packed[:, q_cols + rope_cols :] = out_ref[...]


def pack_columns(place, arrays, chunks):
    tokens = arrays[0].shape[0]
    widths = [array.shape[1] // chunks // 2 for array in arrays]
    theirs = lambda c, place: (0, c * 2 + 1 - place[0])
    return pl.pallas_call(
        pack_kernel,
        grid_spec=pltpu.PrefetchScalarGridSpec(
            num_scalar_prefetch=1,
            grid=(chunks,),
            in_specs=[pl.BlockSpec((tokens, width), theirs) for width in widths],
            out_specs=pl.BlockSpec((tokens, sum(widths)), lambda c, place: (0, c)),
        ),
        out_shape=jax.ShapeDtypeStruct((tokens, chunks * sum(widths)), arrays[0].dtype),
        compiler_params=pltpu.CompilerParams(vmem_limit_bytes=INPUT_BYTES),
        cost_estimate=pl.CostEstimate(flops=0, bytes_accessed=5_000_000, transcendentals=0),
        name="pack_columns",
    )(place, *arrays)


def halving_order(count):
    bits = count.bit_length() - 1
    partners = []
    for place in range(count):
        partner = place & 1
        for bit in range(1, bits):
            partner |= ((place >> (bits - bit)) & 1) << bit
        partners.append(partner)
    return partners


def channel_order(ctx, lat_block):
    channel = lax.broadcasted_iota(jnp.int32, (LAT, LAT), 0)
    place = lax.broadcasted_iota(jnp.int32, (LAT, LAT), 1)
    count = LAT // lat_block
    bits = count.bit_length() - 1
    block = place // lat_block
    partner = block & 1
    for bit in range(1, bits):
        partner |= ((block >> (bits - bit)) & 1) << bit
    return channel == (ctx ^ partner) * lat_block + place % lat_block


def collect_kernel(plan, own, sib, cand, cand_t, rope_keys, bias, *, blocks, lat_block):
    pieces = []
    key_at = lax.broadcasted_iota(jnp.int32, (BLOCK, 2 * BLOCK), 0)
    query = lax.broadcasted_iota(jnp.int32, (BLOCK, 2 * BLOCK), 1)
    per_side = len(blocks) // 2
    for block, other in enumerate(blocks):
        rows_ref = sib if other else own
        start = pl.multiple_of(plan[1 + block], 16)
        rows = rows_ref[pl.ds(start, BLOCK), :]
        usable = plan[1 + len(blocks) + block]
        pieces.append(jnp.where(usable > 0, rows, jnp.zeros_like(rows)))
        side, at = divmod(block, per_side)
        kinds = (sib if side else own)[2 * BLOCK : 2 * BLOCK + 16, :][:1].astype(jnp.float32)
        kind = jnp.where(
            query < BLOCK, kinds[:, 2 * at : 2 * at + 1], kinds[:, 2 * at + 1 : 2 * at + 2]
        )
        allowed = (kind > 1.5) | (kind > 0.5) & (key_at <= query % BLOCK)
        bias[block * BLOCK : (block + 1) * BLOCK, :] = jnp.where(allowed, 0.0, HIDDEN)
    both = jnp.concatenate(pieces, axis=0)
    order = channel_order(plan[0], lat_block).astype(jnp.bfloat16)
    latent = both[:, :LAT]
    cand[...] = dot(latent, order, 1, 0).astype(jnp.bfloat16)
    cand_t[...] = dot(order, latent, 0, 1).astype(jnp.bfloat16)
    twice = lax.broadcasted_iota(jnp.int32, (ROPE, 2 * ROPE), 0)
    twice = twice == lax.broadcasted_iota(jnp.int32, (ROPE, 2 * ROPE), 1) % ROPE
    rope_keys[...] = dot(both[:, LAT:], twice.astype(jnp.bfloat16), 1, 0).astype(jnp.bfloat16)


def collect(plan, own, sib, blocks, lat_block):
    rows = len(blocks) * BLOCK
    bf16 = jnp.bfloat16
    shapes = [((rows, LAT), bf16), ((LAT, rows), bf16), ((rows, 2 * ROPE), bf16)]
    shapes.append(((rows, 2 * BLOCK), jnp.float32))
    whole = lambda shape: pl.BlockSpec(shape, lambda i, plan: (0, 0))
    return pl.pallas_call(
        functools.partial(collect_kernel, blocks=blocks, lat_block=lat_block),
        grid_spec=pltpu.PrefetchScalarGridSpec(
            num_scalar_prefetch=1,
            grid=(1,),
            in_specs=[whole(own.shape), whole(sib.shape)],
            out_specs=[whole(shape) for shape, _ in shapes],
        ),
        out_shape=[jax.ShapeDtypeStruct(shape, dtype) for shape, dtype in shapes],
        compiler_params=pltpu.CompilerParams(vmem_limit_bytes=KERNEL_BYTES),
        cost_estimate=pl.CostEstimate(
            flops=250_000_000, bytes_accessed=3_000_000, transcendentals=0
        ),
        name="collect",
    )(plan, own, sib)


def spread_kernel(plan, *refs, blocks, lat_block):
    *sums, own, sib = refs
    count = len(sums) // 2
    latent, rope = sums[0][...], sums[count][...]
    for index in range(1, count):
        latent, rope = latent + sums[index][...], rope + sums[count + index][...]
    order = channel_order(plan[0], lat_block).astype(jnp.float32)
    latent = lax.dot_general(
        latent,
        order,
        (((1,), (1,)), ((), ())),
        precision=lax.Precision.HIGHEST,
        preferred_element_type=jnp.float32,
    )
    rows = jnp.concatenate([latent, rope[:, :ROPE] + rope[:, ROPE:]], axis=1)
    own[...] = jnp.zeros_like(own)
    sib[...] = jnp.zeros_like(sib)
    for block, other in enumerate(blocks):
        here = pl.ds(pl.multiple_of(plan[1 + block], 16), BLOCK)
        target = sib if other else own
        target[here, :] += rows[block * BLOCK : (block + 1) * BLOCK]


def spread(plan, latents, ropes, rows, blocks, lat_block):
    shape = (rows, LAT + ROPE)
    sums = [*latents, *ropes]
    return pl.pallas_call(
        functools.partial(spread_kernel, blocks=blocks, lat_block=lat_block),
        grid_spec=pltpu.PrefetchScalarGridSpec(
            num_scalar_prefetch=1,
            grid=(1,),
            in_specs=[pl.BlockSpec(array.shape, lambda i, plan: (0, 0)) for array in sums],
            out_specs=[pl.BlockSpec(shape, lambda i, plan: (0, 0))] * 2,
        ),
        out_shape=[jax.ShapeDtypeStruct(shape, jnp.float32)] * 2,
        compiler_params=pltpu.CompilerParams(vmem_limit_bytes=KERNEL_BYTES),
        cost_estimate=pl.CostEstimate(
            flops=700_000_000, bytes_accessed=6_000_000, transcendentals=0
        ),
        name="spread",
    )(plan, *sums)


def halve(value, axis, bit):
    half = value.shape[0] // 2
    return value[:half] + exchange(value[half:], axis, bit)


def shards(q_nope, q_rope, grad_out, log_total, kv_latent, up_weight, selected, offered):
    n_dp, n_ctx = lax.axis_size("dp"), lax.axis_size("ctx")
    dp, ctx = lax.axis_index("dp"), lax.axis_index("ctx")
    core = ctx % 2
    group_len = kv_latent.shape[1]
    per_block = group_len // BLOCK
    heads = log_total.shape[1]
    part_heads = heads // n_dp // 2
    pairs = part_heads // 2
    part_cols = part_heads * (NOPE + VDIM)
    far = n_dp - 1
    lat_block = up_weight.shape[0]

    place = jnp.stack([core] + [dp ^ t for t in range(n_dp)]).astype(jnp.int32)

    leaving, *staying = weight_parts(place, up_weight, n_dp, far)
    crossed = exchange(leaving, "ctx", 1)
    chip_rows = stack(
        [*staying, crossed], (((0, 0), (2, 0)), ((1, 0), (2, 1))), part_cols
    )
    chip_rows, place, selected, offered, q_nope, q_rope, grad_out, log_total, kv_latent = (
        lax.optimization_barrier(
            (chip_rows, place, selected, offered, q_nope, q_rope, grad_out, log_total, kv_latent)
        )
    )
    partners = halving_order(n_ctx)[::2]

    def over_chips(start):
        at_step = {0: start}
        for step in range(2, n_ctx, 4):
            at_step[step] = exchange(at_step[step - 2], "ctx", 2)
            if step + 2 < n_ctx:
                at_step[step + 2] = exchange(start, "ctx", step + 2)
        return [at_step[partner] for partner in partners], at_step[n_ctx - 2]

    def joined(pieces):
        return stack(pieces, (tuple((index, 0) for index in range(len(pieces))),), part_cols)[0]

    near_pieces, last = over_chips(chip_rows[0])
    weights = {0: joined(near_pieces)}
    weights[far] = joined(over_chips(after(chip_rows[1], last))[0])
    for t in range(1, far):
        weights[t] = exchange(weights[0], "dp", t)
    queries, rope_queries, out_grads = q_nope[0], q_rope[0], grad_out[0]

    packed = exchange(
        pack_columns(place, (queries, rope_queries, out_grads), n_dp), "ctx", 1
    )
    totals = log_total[0].reshape(n_dp, 2, pairs, 2, group_len)
    tot_sib = exchange(lax.dynamic_index_in_dim(totals, 1 - core, 1, keepdims=False), "ctx", 1)
    totals = (
        totals.reshape(n_dp * 2 * pairs, 2, group_len),
        tot_sib.reshape(n_dp * pairs, 2, group_len),
    )

    offer_plan = offered[0]
    span = group_len + 16
    blocks, starts, usables = [], [], []
    for side in range(2):
        group = ctx ^ side
        offsets = [0] * per_block + list(partner_offsets)
        blocks += [(offset + side) % 2 for offset in offsets]
        source = jnp.stack([group - offset for offset in offsets])
        sender = jnp.maximum(source, 0)
        inner = jnp.concatenate(
            [
                jnp.arange(per_block, dtype=jnp.int32),
                offer_plan[sender[per_block:], jnp.arange(len(partner_offsets))],
            ]
        )
        usable = source >= 0
        behind = ctx // 2 - sender // 2
        starts.append(jnp.where(usable, behind * span + inner * BLOCK, 0))
        usables.append(usable)
        if side == 0:
            ids = jnp.where(usable, sender * per_block + inner, -1)
            query_ids = group * per_block + jnp.arange(per_block, dtype=jnp.int32)
            picked = jnp.any(selected[0][None, :, :] == ids[:, None, None], axis=2)
            picked = picked & (ids >= 0)[:, None]
            same = ids[:, None] == query_ids[None, :]
            kinds = jnp.where(picked, 2.0, jnp.where(same, 1.0, 0.0)).reshape(1, -1)
    plan = jnp.concatenate([ctx[None], *starts, *usables]).astype(jnp.int32)
    kinds = jnp.pad(kinds.astype(jnp.bfloat16), ((0, 15), (0, LAT + ROPE - kinds.shape[1])))
    bundle = jnp.concatenate([kv_latent[0], kinds], axis=0)
    bundles = [bundle, from_behind(bundle, "ctx", 2), from_behind(bundle, "ctx", 4)]
    own_bundles = stack(bundles, (((0, 0), (1, 0), (2, 0)),), LAT + ROPE)[0]
    sib_bundles = exchange(own_bundles, "ctx", 1)
    shared = collect(plan, own_bundles, sib_bundles, tuple(blocks), lat_block)

    earlier = None
    weight_grads, latents, ropes, far_arrived = {}, [], [], []
    bits = [1 << b for b in range(n_dp.bit_length() - 1)]
    orders = (bits, bits[::-1])
    order = [0, far] + list(range(1, far))
    for t in order:
        weight_grads[t] = ([], [])
        half_pairs = pairs // 2
        units = [(0, pairs)] if t != order[-1] else [(0, half_pairs), (half_pairs, half_pairs)]
        for unit in units:
            weight = weights[t]
            if unit[0]:
                weight = after(weight, *[arrived for arrived, in far_arrived])
            rest = chunk_backward(
                place,
                t,
                unit,
                (queries, rope_queries, out_grads),
                packed,
                totals,
                weight,
                shared,
                earlier,
                (n_dp, pairs),
            )
            earlier = rest[:3]
            for side in range(2):
                weight_grads[t][side].append(rest[3 + side])
            latents.append(rest[5])
            ropes.append(rest[6])
        if t == far:
            far_arrived = [
                [exchange(weight_grads[t][side][0], "dp", orders[side][0])] for side in range(2)
            ]

    q_full, rope_full, sib_grads = earlier
    received = exchange(sib_grads, "ctx", 1)
    grad_nope, grad_rope = place_columns(place, received, q_full, rope_full, n_dp)

    own_grads, sib_grads = spread(plan, latents, ropes, 3 * span, tuple(blocks), lat_block)
    grad_rows = own_grads + exchange(sib_grads, "ctx", 1)
    by_chip = [grad_rows[at * span : at * span + group_len] for at in range(3)]
    grad_rows = by_chip[0]
    for chips in (1, 2):
        grad_rows = grad_rows + from_behind(by_chip[chips], "ctx", -2 * chips)

    half_cols = part_cols // 2

    def columns(pieces, half):
        if len(pieces) == 2:
            return pieces[half]
        return pieces[0][:, half * half_cols : (half + 1) * half_cols]

    def total(addends, half):
        return functools.reduce(
            lambda left, right: left + right, [columns(pieces, half) for pieces in addends]
        )

    sums = []
    for side, order in enumerate(orders):
        addends = {t: [weight_grads[t][side]] for t in weight_grads}
        for bit in order:
            arrived = {}
            for t in sorted((t for t in addends if t & bit), reverse=True):
                if t == far and bit == order[0]:
                    arrived[t ^ bit] = far_arrived[side]
                    continue
                pieces = addends[t][0]
                if len(addends[t]) > 1:
                    pieces = [total(addends[t], half) for half in range(2)]
                if bit == order[-1]:
                    pieces = [after(piece, *addends[0][-1]) for piece in pieces]
                arrived[t ^ bit] = [exchange(piece, "dp", bit) for piece in pieces]
            addends = {t: addends[t] + [more] for t, more in arrived.items()}
        sums.append([total(addends[0], half) for half in range(2)])

    ctx_bits = [1 << b for b in range(1, n_ctx.bit_length() - 1)]
    finished = []
    for half in range(2):
        leaving = after(sums[1][half], (grad_rows, grad_nope)[half])
        rows = sums[0][half] + exchange(leaving, "ctx", ctx_bits[0])
        for bit in ctx_bits[1:]:
            rows = halve(rows, "ctx", bit)
        piece = join_cores(place, rows[:lat_block], exchange(rows[lat_block:], "ctx", 1))
        finished.append([piece] + [exchange(piece, "dp", t) for t in range(1, n_dp)])
    grad_weight = lay_out(place, [piece for both in zip(*finished) for piece in both])
    return (grad_nope[None], grad_rope[None], grad_rows[None], grad_weight)


def solution(mesh):
    in_specs = (
        P("dp", "ctx", None),
        P("dp", "ctx", None),
        P("dp", "ctx", None),
        P("dp", None, "ctx"),
        P("dp", "ctx", None),
        P("ctx", None),
        P("dp", "ctx", None),
        P("dp", None, None),
    )
    out_specs = (P("dp", "ctx", None), P("dp", "ctx", None), P("dp", "ctx", None), P("ctx", None))
    return jax.shard_map(shards, mesh=mesh, in_specs=in_specs, out_specs=out_specs, check_vma=False)
```

```python
import functools

import jax
import jax.numpy as jnp
from jax import lax
from jax.experimental import pallas as pl
from jax.experimental.pallas import tpu as pltpu
from jax.sharding import PartitionSpec as P

LAT = 256
ROPE = 64
NOPE = 128
VDIM = 128
BLOCK = 64

partner_offsets = (1, 2, 3, 4)
HIDDEN = -1e30
KERNEL_BYTES = 12 * 1024 * 1024
INPUT_BYTES = 56 * 1024 * 1024


def from_behind(value, axis, steps):
    count = lax.axis_size(axis)
    initial, last = (max(0, -steps), min(count, count - steps))
    return lax.ppermute(value, axis, [(source, source + steps) for source in range(initial, last)])


def exchange(value, axis, bits):
    count = lax.axis_size(axis)
    return lax.ppermute(value, axis, [(source, source ^ bits) for source in range(count)])


def after(value, *earlier):
    return lax.optimization_barrier((value, *earlier))[0]


def dot(left, right, left_dim, right_dim):
    return lax.dot_general(
        left,
        right,
        (((left_dim,), (right_dim,)), ((), ())),
        preferred_element_type=jnp.float32,
    )


def heads_kernel(
    place,
    q_own, rope_own, out_own, tot_own,
    q_sib, rope_sib, out_sib, tot_sib,
    weight, cand, cand_t, rope_keys, bias,
    *rest,
    earlier,
):
    gq_own, gr_own, sib_grads, *weight_grads, lat_sum, rope_sum = rest[earlier:]
    scale = 1.0 / jnp.sqrt(jnp.float32(NOPE + ROPE))
    rows = cand.shape[0] // 2
    half = weight_grads[0].shape[0]
    sib_q, sib_rope = sib_grads.at[:, : 2 * NOPE], sib_grads.at[:, 2 * NOPE :]
    lane_half = lax.broadcasted_iota(jnp.int32, (rows, 2 * ROPE), 1) // ROPE

    @pl.when(pl.program_id(0) == 0)
    def _():
        lat_sum[...] = jnp.zeros_like(lat_sum)
        rope_sum[...] = jnp.zeros_like(rope_sum)

    groups = (
        (q_own, rope_own, out_own, tot_own, gq_own, gr_own),
        (q_sib, rope_sib, out_sib, tot_sib, sib_q, sib_rope),
    )
    rope_grads = [None, None]
    for head in range(2):
        columns = pl.ds(head * (NOPE + VDIM), NOPE + VDIM)
        head_weight = weight[:, columns]
        expanded = dot(cand[...], head_weight, 1, 0).astype(jnp.bfloat16)
        both_grads = []
        for side, (q_ref, rope_ref, out_ref, tot_ref, gq_ref, gr_ref) in enumerate(groups):
            own_rows = slice(side * rows, (side + 1) * rows)
            here = pl.ds(head * NOPE, NOPE)
            rope_part = jnp.where(
                lane_half == head, rope_keys[own_rows, :], jnp.zeros((), jnp.bfloat16)
            )
            keys = jnp.concatenate([expanded[own_rows, :NOPE], rope_part], axis=1)
            values = expanded[own_rows, NOPE:]
            queries = jnp.concatenate([q_ref[:, here], rope_ref[...]], axis=1)
            out_grads = out_ref[:, here]
            scores = dot(keys, queries, 1, 1) * scale
            probs = jnp.exp(scores - tot_ref[0, head : head + 1, :] + bias[own_rows, :])
            prob_grads = dot(values, out_grads, 1, 1)
            row_dot = jnp.sum(probs * prob_grads, axis=0, keepdims=True)
            score_grads = (probs * (prob_grads - row_dot)).astype(jnp.bfloat16)
            query_grad = dot(score_grads, keys, 0, 0) * scale
            gq_ref[:, here] = query_grad[:, :NOPE].astype(jnp.bfloat16)
            if head == 0:
                rope_grads[side] = query_grad[:, NOPE:]
            else:
                gr_ref[...] = (rope_grads[side] + query_grad[:, NOPE:]).astype(jnp.bfloat16)
            key_grad = dot(score_grads, queries, 1, 0) * scale
            value_grad = dot(probs.astype(jnp.bfloat16), out_grads, 1, 0)
            rope_sum[own_rows, :] += jnp.where(lane_half == head, key_grad[:, NOPE:], 0.0)
            both_grads.append(
                jnp.concatenate([key_grad[:, :NOPE], value_grad], axis=1).astype(jnp.bfloat16)
            )
        key_grads = jnp.concatenate(both_grads, axis=0)
        lat_sum[...] += dot(key_grads, head_weight, 1, 1)
        weight_grad = dot(cand_t[...], key_grads, 1, 0)
        weight_grads[0][:, columns] = weight_grad[:half]
        weight_grads[1][:, columns] = weight_grad[half:]


def chunk_backward(place, t, unit, own, sibling, weight, shared, earlier, sizes):
    q_own, rope_own, out_own, tot_own = own
    cand, cand_t, rope_keys, bias = shared
    tokens = q_own.shape[0]
    chunks, pairs = sizes
    wide, narrow = 2 * NOPE, 2 * ROPE
    first, count = unit
    mine = lambda p, place: (place[1 + t] * 2 + place[0]) * pairs + first + p
    theirs = lambda p, place: place[1 + t] * pairs + first + p
    whole = lambda array: pl.BlockSpec(array.shape, lambda p, place: (0, 0))
    in_specs = [
        pl.BlockSpec((tokens, wide), lambda p, place: (0, mine(p, place))),
        pl.BlockSpec((tokens, narrow), lambda p, place: (0, mine(p, place))),
        pl.BlockSpec((tokens, wide), lambda p, place: (0, mine(p, place))),
        pl.BlockSpec((1, 2, tokens), lambda p, place: (mine(p, place), 0, 0)),
    ] * 2 + [
        pl.BlockSpec((LAT, 2 * (NOPE + VDIM)), lambda p, place: (0, first + p)),
        whole(cand),
        whole(cand_t),
        whole(rope_keys),
        whole(bias),
    ]
    operands = [*own, *sibling, weight, cand, cand_t, rope_keys, bias]
    aliases = {}
    if earlier is not None:
        for index, array in enumerate(earlier):
            aliases[1 + len(operands)] = index
            in_specs.append(pl.BlockSpec(memory_space=pl.ANY))
            operands.append(array)
    columns = 2 * (NOPE + VDIM) * count
    bf16, f32 = jnp.bfloat16, jnp.float32
    out_shape = [
        jax.ShapeDtypeStruct(q_own.shape, bf16),
        jax.ShapeDtypeStruct(rope_own.shape, bf16),
        jax.ShapeDtypeStruct((tokens, chunks * pairs * (wide + narrow)), bf16),
        *[jax.ShapeDtypeStruct((LAT // 2, columns), f32)] * 2,
        jax.ShapeDtypeStruct((cand.shape[0], LAT), f32),
        jax.ShapeDtypeStruct((cand.shape[0], narrow), f32),
    ]
    out_specs = [
        pl.BlockSpec((tokens, wide), lambda p, place: (0, mine(p, place))),
        pl.BlockSpec((tokens, narrow), lambda p, place: (0, mine(p, place))),
        pl.BlockSpec((tokens, wide + narrow), lambda p, place: (0, theirs(p, place))),
        *[pl.BlockSpec((LAT // 2, 2 * (NOPE + VDIM)), lambda p, place: (0, p))] * 2,
        pl.BlockSpec((cand.shape[0], LAT), lambda p, place: (0, 0)),
        pl.BlockSpec((cand.shape[0], narrow), lambda p, place: (0, 0)),
    ]
    return pl.pallas_call(
        functools.partial(heads_kernel, earlier=len(aliases)),
        grid_spec=pltpu.PrefetchScalarGridSpec(
            num_scalar_prefetch=1, grid=(count,), in_specs=in_specs, out_specs=out_specs
        ),
        out_shape=out_shape,
        input_output_aliases=aliases,
        compiler_params=pltpu.CompilerParams(vmem_limit_bytes=KERNEL_BYTES),
        cost_estimate=pl.CostEstimate(
            flops=count * 100_000_000, bytes_accessed=count * 300_000, transcendentals=0
        ),
        name="heads_backward",
    )(place, *operands)


def place_kernel(place, received, q_in, rope_in, q_out, rope_out):
    wide, narrow = 2 * NOPE, 2 * ROPE
    for pair in range(q_out.shape[1] // wide):
        start = pair * (wide + narrow)
        q_out[:, pair * wide : (pair + 1) * wide] = received[:, start : start + wide]
        rope_out[:, pair * narrow : (pair + 1) * narrow] = received[
            :, start + wide : start + wide + narrow
        ]


def place_columns(place, received, q_full, rope_full, chunks):
    tokens = q_full.shape[0]
    q_cols, rope_cols = q_full.shape[1] // chunks // 2, rope_full.shape[1] // chunks // 2
    put = lambda c, place: (0, c * 2 + 1 - place[0])
    return pl.pallas_call(
        place_kernel,
        grid_spec=pltpu.PrefetchScalarGridSpec(
            num_scalar_prefetch=1,
            grid=(chunks,),
            in_specs=[
                pl.BlockSpec((tokens, q_cols + rope_cols), lambda c, place: (0, c)),
                pl.BlockSpec(memory_space=pl.ANY),
                pl.BlockSpec(memory_space=pl.ANY),
            ],
            out_specs=[
                pl.BlockSpec((tokens, q_cols), put),
                pl.BlockSpec((tokens, rope_cols), put),
            ],
        ),
        out_shape=[
            jax.ShapeDtypeStruct(q_full.shape, q_full.dtype),
            jax.ShapeDtypeStruct(rope_full.shape, rope_full.dtype),
        ],
        input_output_aliases={2: 0, 3: 1},
        compiler_params=pltpu.CompilerParams(vmem_limit_bytes=KERNEL_BYTES),
        cost_estimate=pl.CostEstimate(flops=0, bytes_accessed=4_000_000, transcendentals=0),
        name="place_columns",
    )(place, received, q_full, rope_full)


def stack_kernel(*refs, arrangement):
    outs = refs[len(refs) - len(arrangement) :]
    for out, sources in zip(outs, arrangement):
        row = 0
        for index, block in sources:
            piece = refs[index]
            columns = slice(block * out.shape[1], (block + 1) * out.shape[1])
            out[row : row + piece.shape[0], :] = piece[:, columns]
            row += piece.shape[0]


def stack(inputs, arrangement, columns):
    whole = lambda shape: pl.BlockSpec(shape, lambda: (0, 0))
    shapes = [(sum(inputs[i].shape[0] for i, _ in sources), columns) for sources in arrangement]
    return pl.pallas_call(
        functools.partial(stack_kernel, arrangement=arrangement),
        in_specs=[whole(array.shape) for array in inputs],
        out_specs=[whole(shape) for shape in shapes],
        out_shape=[jax.ShapeDtypeStruct(shape, inputs[0].dtype) for shape in shapes],
        compiler_params=pltpu.CompilerParams(vmem_limit_bytes=KERNEL_BYTES),
        cost_estimate=pl.CostEstimate(flops=0, bytes_accessed=2_000_000, transcendentals=0),
        name="stack",
    )(*inputs)


def leave_kernel(place, near, distant, leaving):
    width = near.shape[1]
    leaving[:, :width] = near[...]
    leaving[:, width:] = distant[...]


def join_rows_kernel(place, near, distant, crossed, near_rows, distant_rows):
    rows, width = near.shape
    for at, (own, out) in enumerate(((near, near_rows), (distant, distant_rows))):
        out[:rows, :] = own[...]
        out[rows:, :] = crossed[:, at * width : (at + 1) * width]


def weight_parts(place, up_weight, chunks, far, crossed=None):
    rows = up_weight.shape[0]
    width = up_weight.shape[1] // chunks // 2
    joins = crossed is not None

    def column_block(t):
        def block(i, place):
            return (0, place[1 + t] * 2 + (place[0] if joins else 1 - place[0]))

        return pl.BlockSpec((rows, width), block)

    whole = lambda shape: pl.BlockSpec(shape, lambda i, place: (0, 0))
    shapes = [(2 * rows, width)] * 2 if joins else [(rows, 2 * width)]
    return pl.pallas_call(
        join_rows_kernel if joins else leave_kernel,
        grid_spec=pltpu.PrefetchScalarGridSpec(
            num_scalar_prefetch=1,
            grid=(1,),
            in_specs=[column_block(t) for t in (0, far)] + [whole((rows, 2 * width))] * joins,
            out_specs=[whole(shape) for shape in shapes],
        ),
        out_shape=[jax.ShapeDtypeStruct(shape, up_weight.dtype) for shape in shapes],
        compiler_params=pltpu.CompilerParams(vmem_limit_bytes=INPUT_BYTES),
        cost_estimate=pl.CostEstimate(flops=0, bytes_accessed=1_000_000, transcendentals=0),
        name="weight_parts",
    )(place, up_weight, up_weight, *([crossed] if joins else []))


def lay_kernel(place, *refs):
    *pieces, out = refs
    width = out.shape[1] // 4
    for step in range(len(pieces) // 2):
        early, late = pieces[2 * step], pieces[2 * step + 1]

        @pl.when(pl.program_id(0) == step)
        def _():
            for which in range(2):
                source = slice(which * width, (which + 1) * width)
                out[:, 2 * which * width : (2 * which + 1) * width] = early[:, source]
                out[:, (2 * which + 1) * width : (2 * which + 2) * width] = late[:, source]


def lay_out(place, pieces):
    rows, columns = pieces[0].shape
    count = len(pieces) // 2
    return pl.pallas_call(
        lay_kernel,
        grid_spec=pltpu.PrefetchScalarGridSpec(
            num_scalar_prefetch=1,
            grid=(count,),
            in_specs=[pl.BlockSpec((rows, columns), lambda t, place: (0, 0))] * len(pieces),
            out_specs=pl.BlockSpec((rows, 2 * columns), lambda t, place: (0, place[1 + t])),
        ),
        out_shape=jax.ShapeDtypeStruct((rows, count * 2 * columns), pieces[0].dtype),
        compiler_params=pltpu.CompilerParams(vmem_limit_bytes=KERNEL_BYTES),
        cost_estimate=pl.CostEstimate(flops=0, bytes_accessed=4_000_000, transcendentals=0),
        name="lay_out",
    )(place, *pieces)


def piece_kernel(place, kept, crossed, out):
    width = kept.shape[1]

    @pl.when(place[0] == 0)
    def _():
        out[:, :width] = kept[...]
        out[:, width:] = crossed[...]

    @pl.when(place[0] != 0)
    def _():
        out[:, :width] = crossed[...]
        out[:, width:] = kept[...]


def join_cores(place, kept, crossed):
    rows, columns = kept.shape
    return pl.pallas_call(
        piece_kernel,
        grid_spec=pltpu.PrefetchScalarGridSpec(
            num_scalar_prefetch=1,
            grid=(1,),
            in_specs=[pl.BlockSpec((rows, columns), lambda i, place: (0, 0))] * 2,
            out_specs=pl.BlockSpec((rows, 2 * columns), lambda i, place: (0, 0)),
        ),
        out_shape=jax.ShapeDtypeStruct((rows, 2 * columns), kept.dtype),
        compiler_params=pltpu.CompilerParams(vmem_limit_bytes=KERNEL_BYTES),
        cost_estimate=pl.CostEstimate(flops=0, bytes_accessed=500_000, transcendentals=0),
        name="join_cores",
    )(place, kept, crossed)


def halving_order(count):
    bits = count.bit_length() - 1
    partners = []
    for place in range(count):
        partner = place & 1
        for bit in range(1, bits):
            partner |= ((place >> (bits - bit)) & 1) << bit
        partners.append(partner)
    return partners


def channel_order(ctx, lat_block):
    channel = lax.broadcasted_iota(jnp.int32, (LAT, LAT), 0)
    place = lax.broadcasted_iota(jnp.int32, (LAT, LAT), 1)
    count = LAT // lat_block
    bits = count.bit_length() - 1
    block = place // lat_block
    partner = block & 1
    for bit in range(1, bits):
        partner |= ((block >> (bits - bit)) & 1) << bit
    return channel == (ctx ^ partner) * lat_block + place % lat_block


def collect_kernel(plan, own, sib, cand, cand_t, rope_keys, bias, *, blocks, lat_block):
    pieces = []
    key_at = lax.broadcasted_iota(jnp.int32, (BLOCK, 2 * BLOCK), 0)
    query = lax.broadcasted_iota(jnp.int32, (BLOCK, 2 * BLOCK), 1)
    per_side = len(blocks) // 2
    for block, other in enumerate(blocks):
        rows_ref = sib if other else own
        start = pl.multiple_of(plan[1 + block], 16)
        rows = rows_ref[pl.ds(start, BLOCK), :]
        usable = plan[1 + len(blocks) + block]
        pieces.append(jnp.where(usable > 0, rows, jnp.zeros_like(rows)))
        side, at = divmod(block, per_side)
        kinds = (sib if side else own)[2 * BLOCK : 2 * BLOCK + 16, :][:1].astype(jnp.float32)
        kind = jnp.where(
            query < BLOCK, kinds[:, 2 * at : 2 * at + 1], kinds[:, 2 * at + 1 : 2 * at + 2]
        )
        allowed = (kind > 1.5) | (kind > 0.5) & (key_at <= query % BLOCK)
        bias[block * BLOCK : (block + 1) * BLOCK, :] = jnp.where(allowed, 0.0, HIDDEN)
    both = jnp.concatenate(pieces, axis=0)
    order = channel_order(plan[0], lat_block).astype(jnp.bfloat16)
    latent = both[:, :LAT]
    cand[...] = dot(latent, order, 1, 0).astype(jnp.bfloat16)
    cand_t[...] = dot(order, latent, 0, 1).astype(jnp.bfloat16)
    twice = lax.broadcasted_iota(jnp.int32, (ROPE, 2 * ROPE), 0)
    twice = twice == lax.broadcasted_iota(jnp.int32, (ROPE, 2 * ROPE), 1) % ROPE
    rope_keys[...] = dot(both[:, LAT:], twice.astype(jnp.bfloat16), 1, 0).astype(jnp.bfloat16)


def collect(plan, own, sib, blocks, lat_block):
    rows = len(blocks) * BLOCK
    bf16 = jnp.bfloat16
    shapes = [((rows, LAT), bf16), ((LAT, rows), bf16), ((rows, 2 * ROPE), bf16)]
    shapes.append(((rows, 2 * BLOCK), jnp.float32))
    whole = lambda shape: pl.BlockSpec(shape, lambda i, plan: (0, 0))
    return pl.pallas_call(
        functools.partial(collect_kernel, blocks=blocks, lat_block=lat_block),
        grid_spec=pltpu.PrefetchScalarGridSpec(
            num_scalar_prefetch=1,
            grid=(1,),
            in_specs=[whole(own.shape), whole(sib.shape)],
            out_specs=[whole(shape) for shape, _ in shapes],
        ),
        out_shape=[jax.ShapeDtypeStruct(shape, dtype) for shape, dtype in shapes],
        compiler_params=pltpu.CompilerParams(vmem_limit_bytes=KERNEL_BYTES),
        cost_estimate=pl.CostEstimate(
            flops=250_000_000, bytes_accessed=3_000_000, transcendentals=0
        ),
        name="collect",
    )(plan, own, sib)


def spread_kernel(plan, *refs, blocks, lat_block):
    *sums, own, sib = refs
    count = len(sums) // 2
    latent, rope = sums[0][...], sums[count][...]
    for index in range(1, count):
        latent, rope = latent + sums[index][...], rope + sums[count + index][...]
    order = channel_order(plan[0], lat_block).astype(jnp.float32)
    latent = lax.dot_general(
        latent,
        order,
        (((1,), (1,)), ((), ())),
        precision=lax.Precision.HIGHEST,
        preferred_element_type=jnp.float32,
    )
    rows = jnp.concatenate([latent, rope[:, :ROPE] + rope[:, ROPE:]], axis=1)
    own[...] = jnp.zeros_like(own)
    sib[...] = jnp.zeros_like(sib)
    for block, other in enumerate(blocks):
        here = pl.ds(pl.multiple_of(plan[1 + block], 16), BLOCK)
        target = sib if other else own
        target[here, :] += rows[block * BLOCK : (block + 1) * BLOCK]


def spread(plan, latents, ropes, rows, blocks, lat_block):
    shape = (rows, LAT + ROPE)
    sums = [*latents, *ropes]
    return pl.pallas_call(
        functools.partial(spread_kernel, blocks=blocks, lat_block=lat_block),
        grid_spec=pltpu.PrefetchScalarGridSpec(
            num_scalar_prefetch=1,
            grid=(1,),
            in_specs=[pl.BlockSpec(array.shape, lambda i, plan: (0, 0)) for array in sums],
            out_specs=[pl.BlockSpec(shape, lambda i, plan: (0, 0))] * 2,
        ),
        out_shape=[jax.ShapeDtypeStruct(shape, jnp.float32)] * 2,
        compiler_params=pltpu.CompilerParams(vmem_limit_bytes=KERNEL_BYTES),
        cost_estimate=pl.CostEstimate(
            flops=700_000_000, bytes_accessed=6_000_000, transcendentals=0
        ),
        name="spread",
    )(plan, *sums)


def halve(value, axis, bit):
    half = value.shape[0] // 2
    return value[:half] + exchange(value[half:], axis, bit)


def shards(q_nope, q_rope, grad_out, log_total, kv_latent, up_weight, selected, offered):
    n_dp, n_ctx = lax.axis_size("dp"), lax.axis_size("ctx")
    dp, ctx = lax.axis_index("dp"), lax.axis_index("ctx")
    core = ctx % 2
    group_len = kv_latent.shape[1]
    per_block = group_len // BLOCK
    heads = log_total.shape[1]
    part_heads = heads // n_dp // 2
    pairs = part_heads // 2
    part_cols = part_heads * (NOPE + VDIM)
    far = n_dp - 1
    lat_block = up_weight.shape[0]

    place = jnp.stack([core] + [dp ^ t for t in range(n_dp)]).astype(jnp.int32)

    leaving, = weight_parts(place, up_weight, n_dp, far)
    crossed = exchange(leaving, "ctx", 1)
    crossed, place, selected, offered, q_nope, q_rope, grad_out, log_total, kv_latent = (
        lax.optimization_barrier(
            (crossed, place, selected, offered, q_nope, q_rope, grad_out, log_total, kv_latent)
        )
    )
    chip_rows = weight_parts(place, up_weight, n_dp, far, crossed)
    own = [q_nope[0], q_rope[0], grad_out[0]]
    sibling = [exchange(array, "ctx", 1) for array in own]

    partners = halving_order(n_ctx)[::2]

    def over_chips(start, onward, *earlier):
        at_step = {0: start}
        for step in range(4, n_ctx, 4):
            at_step[step] = exchange(start, "ctx", step)
        at_step[2] = exchange(start, "ctx", 2)
        for step in range(4, n_ctx, 4):
            if onward:
                forwarded = after(at_step[step], at_step[2], *earlier)
                at_step[step + 2] = exchange(forwarded, "ctx", 2)
            else:
                at_step[step + 2] = exchange(start, "ctx", step + 2)
        return [at_step[partner] for partner in partners], at_step[n_ctx - 4]

    def joined(pieces):
        return stack(pieces, (tuple((index, 0) for index in range(len(pieces))),), part_cols)[0]

    near_pieces, last = over_chips(chip_rows[0], True, *sibling)
    far_pieces, _ = over_chips(after(chip_rows[1], last), False)
    weights = {0: joined(near_pieces)}
    for t in range(1, far):
        weights[t] = exchange(weights[0], "dp", t)
    log_total = after(log_total, last)[0]
    sibling.append(exchange(log_total, "ctx", 1))
    own.append(log_total)
    for arrays in (own, sibling):
        arrays[3] = arrays[3].reshape(heads // 2, 2, group_len)

    offer_plan = offered[0]
    span = group_len + 16
    blocks, starts, usables = [], [], []
    for side in range(2):
        group = ctx ^ side
        offsets = [0] * per_block + list(partner_offsets)
        blocks += [(offset + side) % 2 for offset in offsets]
        source = jnp.stack([group - offset for offset in offsets])
        sender = jnp.maximum(source, 0)
        inner = jnp.concatenate(
            [
                jnp.arange(per_block, dtype=jnp.int32),
                offer_plan[sender[per_block:], jnp.arange(len(partner_offsets))],
            ]
        )
        usable = source >= 0
        behind = ctx // 2 - sender // 2
        starts.append(jnp.where(usable, behind * span + inner * BLOCK, 0))
        usables.append(usable)
        if side == 0:
            ids = jnp.where(usable, sender * per_block + inner, -1)
            query_ids = group * per_block + jnp.arange(per_block, dtype=jnp.int32)
            picked = jnp.any(selected[0][None, :, :] == ids[:, None, None], axis=2)
            picked = picked & (ids >= 0)[:, None]
            same = ids[:, None] == query_ids[None, :]
            kinds = jnp.where(picked, 2.0, jnp.where(same, 1.0, 0.0)).reshape(1, -1)
    plan = jnp.concatenate([ctx[None], *starts, *usables]).astype(jnp.int32)
    kinds = jnp.pad(kinds.astype(jnp.bfloat16), ((0, 15), (0, LAT + ROPE - kinds.shape[1])))
    bundle = after(jnp.concatenate([kv_latent[0], kinds], axis=0), *sibling[:3])
    bundles = [bundle, from_behind(bundle, "ctx", 2), from_behind(bundle, "ctx", 4)]
    own_bundles = stack(bundles, (((0, 0), (1, 0), (2, 0)),), LAT + ROPE)[0]
    sib_bundles = exchange(own_bundles, "ctx", 1)
    shared = collect(plan, own_bundles, sib_bundles, tuple(blocks), lat_block)

    earlier = None
    latents, ropes = [], []
    weight_grads = {t: ([], []) for t in range(n_dp)}
    bits = [1 << b for b in range(n_dp.bit_length() - 1)]
    orders = (bits, bits[::-1])
    first_sums = [{t: [] for t in range(n_dp) if t & order[0]} for order in orders]
    units = [(0, 0), (0, 1)]
    units += [(t, half) for half in range(2) for t in [far] + list(range(1, far))]
    for t, half in units:
        if (t, half) == (far, 0):
            weights[far] = joined([after(far_pieces[0], latents[-1])] + far_pieces[1:])
        weight = weights[t]
        if (t, half) == (far, 1):
            weight = after(weight, *[sent[far][0] for sent in first_sums])
        if (t, half) == (far - 1, 1):
            weight = after(weight, *[sent[u][0] for sent in first_sums for u in sent if u != far])
        rest = chunk_backward(
            place,
            t,
            (half * pairs // 2, pairs // 2),
            own,
            sibling,
            weight,
            shared,
            earlier,
            (n_dp, pairs),
        )
        earlier = rest[:3]
        for side, sent in enumerate(first_sums):
            grad = rest[3 + side]
            weight_grads[t][side].append(grad)
            if t in sent:
                leaving = after(grad, sent[t][0]) if half else grad
                sent[t].append(exchange(leaving, "dp", orders[side][0]))
        latents.append(rest[5])
        ropes.append(rest[6])

    def total(addends, half):
        return functools.reduce(
            lambda left, right: left + right, [pieces[half] for pieces in addends]
        )

    sums = []
    for side, order in enumerate(orders):
        addends = {t: [weight_grads[t][side]] for t in weight_grads}
        arrived = {t ^ order[0]: pieces for t, pieces in first_sums[side].items()}
        addends = {t: addends[t] + [more] for t, more in arrived.items()}
        for bit in order[1:]:
            arrived = {}
            for t in sorted((t for t in addends if t & bit), reverse=True):
                behind = first_sums[1 - side].get(bit, first_sums[side][order[0]])
                arrived[t ^ bit] = [
                    exchange(after(total(addends[t], half), behind[half]), "dp", bit)
                    for half in range(2)
                ]
            addends = {t: addends[t] + [more] for t, more in arrived.items()}
        sums.append(addends[0])

    q_full, rope_full, sib_grads = earlier
    received = exchange(sib_grads, "ctx", 1)
    grad_nope, grad_rope = place_columns(place, received, q_full, rope_full, n_dp)

    latents[-1] = after(latents[-1], *[sent[far][1] for sent in first_sums])
    own_grads, sib_grads = spread(plan, latents, ropes, 3 * span, tuple(blocks), lat_block)
    swapped = exchange(sib_grads, "ctx", 1)
    grad_rows = own_grads + swapped
    by_chip = [grad_rows[at * span : at * span + group_len] for at in range(3)]
    grad_rows = by_chip[0]
    for chips in (1, 2):
        grad_rows = grad_rows + from_behind(by_chip[chips], "ctx", -2 * chips)

    ctx_bits = [1 << b for b in range(1, n_ctx.bit_length() - 1)]
    finished, arrived = [], None
    for half in range(2):
        if half:
            sums = [[[after(piece, arrived) for piece in pieces] for pieces in side] for side in sums]
        first, second = [total(side, half) for side in sums]
        second = after(second, *((grad_rows, grad_nope) if half else (received, swapped)))
        arrived = exchange(second, "ctx", ctx_bits[0])
        rows = first + arrived
        for bit in ctx_bits[1:]:
            rows = halve(rows, "ctx", bit)
        piece = join_cores(place, rows[:lat_block], exchange(rows[lat_block:], "ctx", 1))
        finished.append([piece] + [exchange(piece, "dp", t) for t in range(1, n_dp)])
    grad_weight = lay_out(place, [piece for both in zip(*finished) for piece in both])
    return (grad_nope[None], grad_rope[None], grad_rows[None], grad_weight)


def solution(mesh):
    in_specs = (
        P("dp", "ctx", None),
        P("dp", "ctx", None),
        P("dp", "ctx", None),
        P("dp", None, "ctx"),
        P("dp", "ctx", None),
        P("ctx", None),
        P("dp", "ctx", None),
        P("dp", None, None),
    )
    out_specs = (P("dp", "ctx", None), P("dp", "ctx", None), P("dp", "ctx", None), P("ctx", None))
    return jax.shard_map(shards, mesh=mesh, in_specs=in_specs, out_specs=out_specs, check_vma=False)
```

```python
import functools

import jax
import jax.numpy as jnp
from jax import lax
from jax.experimental import pallas as pl
from jax.experimental.pallas import tpu as pltpu
from jax.sharding import PartitionSpec as P

LAT = 256
ROPE = 64
NOPE = 128
VDIM = 128
BLOCK = 64

partner_offsets = (1, 2, 3, 4)
HIDDEN = -1e30
KERNEL_BYTES = 12 * 1024 * 1024
INPUT_BYTES = 56 * 1024 * 1024


def from_behind(value, axis, steps):
    count = lax.axis_size(axis)
    initial, last = (max(0, -steps), min(count, count - steps))
    return lax.ppermute(value, axis, [(source, source + steps) for source in range(initial, last)])


def exchange(value, axis, bits):
    count = lax.axis_size(axis)
    return lax.ppermute(value, axis, [(source, source ^ bits) for source in range(count)])


def after(value, *earlier):
    return lax.optimization_barrier((value, *earlier))[0]


def dot(left, right, left_dim, right_dim):
    return lax.dot_general(
        left,
        right,
        (((left_dim,), (right_dim,)), ((), ())),
        preferred_element_type=jnp.float32,
    )


def heads_kernel(
    place,
    q_own, rope_own, out_own, tot_own,
    q_sib, rope_sib, out_sib, tot_sib,
    weight, cand, cand_t, rope_keys, bias,
    *rest,
    earlier,
):
    gq_own, gr_own, sib_grads, *weight_grads, lat_sum, rope_sum = rest[earlier:]
    scale = 1.0 / jnp.sqrt(jnp.float32(NOPE + ROPE))
    rows = cand.shape[0] // 2
    half = weight_grads[0].shape[0]
    sib_q, sib_rope = sib_grads.at[:, : 2 * NOPE], sib_grads.at[:, 2 * NOPE :]
    lane_half = lax.broadcasted_iota(jnp.int32, (rows, 2 * ROPE), 1) // ROPE

    @pl.when(pl.program_id(0) == 0)
    def _():
        lat_sum[...] = jnp.zeros_like(lat_sum)
        rope_sum[...] = jnp.zeros_like(rope_sum)

    groups = (
        (q_own, rope_own, out_own, tot_own, gq_own, gr_own),
        (q_sib, rope_sib, out_sib, tot_sib, sib_q, sib_rope),
    )
    rope_grads = [None, None]
    for head in range(2):
        columns = pl.ds(head * (NOPE + VDIM), NOPE + VDIM)
        head_weight = weight[:, columns]
        expanded = dot(cand[...], head_weight, 1, 0).astype(jnp.bfloat16)
        both_grads = []
        for side, (q_ref, rope_ref, out_ref, tot_ref, gq_ref, gr_ref) in enumerate(groups):
            own_rows = slice(side * rows, (side + 1) * rows)
            here = pl.ds(head * NOPE, NOPE)
            rope_part = jnp.where(
                lane_half == head, rope_keys[own_rows, :], jnp.zeros((), jnp.bfloat16)
            )
            keys = jnp.concatenate([expanded[own_rows, :NOPE], rope_part], axis=1)
            values = expanded[own_rows, NOPE:]
            queries = jnp.concatenate([q_ref[:, here], rope_ref[...]], axis=1)
            out_grads = out_ref[:, here]
            scores = dot(keys, queries, 1, 1) * scale
            probs = jnp.exp(scores - tot_ref[0, head : head + 1, :] + bias[own_rows, :])
            prob_grads = dot(values, out_grads, 1, 1)
            row_dot = jnp.sum(probs * prob_grads, axis=0, keepdims=True)
            score_grads = (probs * (prob_grads - row_dot)).astype(jnp.bfloat16)
            query_grad = dot(score_grads, keys, 0, 0) * scale
            gq_ref[:, here] = query_grad[:, :NOPE].astype(jnp.bfloat16)
            if head == 0:
                rope_grads[side] = query_grad[:, NOPE:]
            else:
                gr_ref[...] = (rope_grads[side] + query_grad[:, NOPE:]).astype(jnp.bfloat16)
            key_grad = dot(score_grads, queries, 1, 0) * scale
            value_grad = dot(probs.astype(jnp.bfloat16), out_grads, 1, 0)
            rope_sum[own_rows, :] += jnp.where(lane_half == head, key_grad[:, NOPE:], 0.0)
            both_grads.append(
                jnp.concatenate([key_grad[:, :NOPE], value_grad], axis=1).astype(jnp.bfloat16)
            )
        key_grads = jnp.concatenate(both_grads, axis=0)
        lat_sum[...] += dot(key_grads, head_weight, 1, 1)
        weight_grad = dot(cand_t[...], key_grads, 1, 0)
        weight_grads[0][:, columns] = weight_grad[:half]
        weight_grads[1][:, columns] = weight_grad[half:]


def chunk_backward(place, t, unit, own, sibling, weight, shared, earlier, sizes):
    q_own, rope_own, out_own, tot_own = own
    cand, cand_t, rope_keys, bias = shared
    tokens = q_own.shape[0]
    chunks, pairs = sizes
    wide, narrow = 2 * NOPE, 2 * ROPE
    first, count = unit
    mine = lambda p, place: (place[1 + t] * 2 + place[0]) * pairs + first + p
    theirs = lambda p, place: place[1 + t] * pairs + first + p
    whole = lambda array: pl.BlockSpec(array.shape, lambda p, place: (0, 0))
    in_specs = [
        pl.BlockSpec((tokens, wide), lambda p, place: (0, mine(p, place))),
        pl.BlockSpec((tokens, narrow), lambda p, place: (0, mine(p, place))),
        pl.BlockSpec((tokens, wide), lambda p, place: (0, mine(p, place))),
        pl.BlockSpec((1, 2, tokens), lambda p, place: (mine(p, place), 0, 0)),
    ] * 2 + [
        pl.BlockSpec((LAT, 2 * (NOPE + VDIM)), lambda p, place: (0, first + p)),
        whole(cand),
        whole(cand_t),
        whole(rope_keys),
        whole(bias),
    ]
    operands = [*own, *sibling, weight, cand, cand_t, rope_keys, bias]
    aliases = {}
    if earlier is not None:
        for index, array in enumerate(earlier):
            aliases[1 + len(operands)] = index
            in_specs.append(pl.BlockSpec(memory_space=pl.ANY))
            operands.append(array)
    columns = 2 * (NOPE + VDIM) * count
    bf16, f32 = jnp.bfloat16, jnp.float32
    out_shape = [
        jax.ShapeDtypeStruct(q_own.shape, bf16),
        jax.ShapeDtypeStruct(rope_own.shape, bf16),
        jax.ShapeDtypeStruct((tokens, chunks * pairs * (wide + narrow)), bf16),
        *[jax.ShapeDtypeStruct((LAT // 2, columns), f32)] * 2,
        jax.ShapeDtypeStruct((cand.shape[0], LAT), f32),
        jax.ShapeDtypeStruct((cand.shape[0], narrow), f32),
    ]
    out_specs = [
        pl.BlockSpec((tokens, wide), lambda p, place: (0, mine(p, place))),
        pl.BlockSpec((tokens, narrow), lambda p, place: (0, mine(p, place))),
        pl.BlockSpec((tokens, wide + narrow), lambda p, place: (0, theirs(p, place))),
        *[pl.BlockSpec((LAT // 2, 2 * (NOPE + VDIM)), lambda p, place: (0, p))] * 2,
        pl.BlockSpec((cand.shape[0], LAT), lambda p, place: (0, 0)),
        pl.BlockSpec((cand.shape[0], narrow), lambda p, place: (0, 0)),
    ]
    return pl.pallas_call(
        functools.partial(heads_kernel, earlier=len(aliases)),
        grid_spec=pltpu.PrefetchScalarGridSpec(
            num_scalar_prefetch=1, grid=(count,), in_specs=in_specs, out_specs=out_specs
        ),
        out_shape=out_shape,
        input_output_aliases=aliases,
        compiler_params=pltpu.CompilerParams(vmem_limit_bytes=KERNEL_BYTES),
        cost_estimate=pl.CostEstimate(
            flops=count * 100_000_000, bytes_accessed=count * 300_000, transcendentals=0
        ),
        name="heads_backward",
    )(place, *operands)


def place_kernel(place, received, q_in, rope_in, q_out, rope_out):
    wide, narrow = 2 * NOPE, 2 * ROPE
    for pair in range(q_out.shape[1] // wide):
        start = pair * (wide + narrow)
        q_out[:, pair * wide : (pair + 1) * wide] = received[:, start : start + wide]
        rope_out[:, pair * narrow : (pair + 1) * narrow] = received[
            :, start + wide : start + wide + narrow
        ]


def place_columns(place, received, q_full, rope_full, chunks):
    tokens = q_full.shape[0]
    q_cols, rope_cols = q_full.shape[1] // chunks // 2, rope_full.shape[1] // chunks // 2
    put = lambda c, place: (0, c * 2 + 1 - place[0])
    return pl.pallas_call(
        place_kernel,
        grid_spec=pltpu.PrefetchScalarGridSpec(
            num_scalar_prefetch=1,
            grid=(chunks,),
            in_specs=[
                pl.BlockSpec((tokens, q_cols + rope_cols), lambda c, place: (0, c)),
                pl.BlockSpec(memory_space=pl.ANY),
                pl.BlockSpec(memory_space=pl.ANY),
            ],
            out_specs=[
                pl.BlockSpec((tokens, q_cols), put),
                pl.BlockSpec((tokens, rope_cols), put),
            ],
        ),
        out_shape=[
            jax.ShapeDtypeStruct(q_full.shape, q_full.dtype),
            jax.ShapeDtypeStruct(rope_full.shape, rope_full.dtype),
        ],
        input_output_aliases={2: 0, 3: 1},
        compiler_params=pltpu.CompilerParams(vmem_limit_bytes=KERNEL_BYTES),
        cost_estimate=pl.CostEstimate(flops=0, bytes_accessed=4_000_000, transcendentals=0),
        name="place_columns",
    )(place, received, q_full, rope_full)


def stack_kernel(*refs, arrangement):
    outs = refs[len(refs) - len(arrangement) :]
    for out, sources in zip(outs, arrangement):
        row = 0
        for index, block in sources:
            piece = refs[index]
            columns = slice(block * out.shape[1], (block + 1) * out.shape[1])
            out[row : row + piece.shape[0], :] = piece[:, columns]
            row += piece.shape[0]


def stack(inputs, arrangement, columns):
    whole = lambda shape: pl.BlockSpec(shape, lambda: (0, 0))
    shapes = [(sum(inputs[i].shape[0] for i, _ in sources), columns) for sources in arrangement]
    return pl.pallas_call(
        functools.partial(stack_kernel, arrangement=arrangement),
        in_specs=[whole(array.shape) for array in inputs],
        out_specs=[whole(shape) for shape in shapes],
        out_shape=[jax.ShapeDtypeStruct(shape, inputs[0].dtype) for shape in shapes],
        compiler_params=pltpu.CompilerParams(vmem_limit_bytes=KERNEL_BYTES),
        cost_estimate=pl.CostEstimate(flops=0, bytes_accessed=2_000_000, transcendentals=0),
        name="stack",
    )(*inputs)


def leave_kernel(place, near, distant, leaving):
    width = near.shape[1]
    leaving[:, :width] = near[...]
    leaving[:, width:] = distant[...]


def join_rows_kernel(place, near, distant, crossed, near_rows, distant_rows):
    rows, width = near.shape
    for at, (own, out) in enumerate(((near, near_rows), (distant, distant_rows))):
        out[:rows, :] = own[...]
        out[rows:, :] = crossed[:, at * width : (at + 1) * width]


def weight_parts(place, up_weight, chunks, far, crossed=None):
    rows = up_weight.shape[0]
    width = up_weight.shape[1] // chunks // 2
    joins = crossed is not None

    def column_block(t):
        def block(i, place):
            return (0, place[1 + t] * 2 + (place[0] if joins else 1 - place[0]))

        return pl.BlockSpec((rows, width), block)

    whole = lambda shape: pl.BlockSpec(shape, lambda i, place: (0, 0))
    shapes = [(2 * rows, width)] * 2 if joins else [(rows, 2 * width)]
    return pl.pallas_call(
        join_rows_kernel if joins else leave_kernel,
        grid_spec=pltpu.PrefetchScalarGridSpec(
            num_scalar_prefetch=1,
            grid=(1,),
            in_specs=[column_block(t) for t in (0, far)] + [whole((rows, 2 * width))] * joins,
            out_specs=[whole(shape) for shape in shapes],
        ),
        out_shape=[jax.ShapeDtypeStruct(shape, up_weight.dtype) for shape in shapes],
        compiler_params=pltpu.CompilerParams(vmem_limit_bytes=INPUT_BYTES),
        cost_estimate=pl.CostEstimate(flops=0, bytes_accessed=1_000_000, transcendentals=0),
        name="weight_parts",
    )(place, up_weight, up_weight, *([crossed] if joins else []))


def lay_kernel(place, *refs):
    *pieces, out = refs
    width = out.shape[1] // 4
    for step in range(len(pieces) // 2):
        early, late = pieces[2 * step], pieces[2 * step + 1]

        @pl.when(pl.program_id(0) == step)
        def _():
            for which in range(2):
                source = slice(which * width, (which + 1) * width)
                out[:, 2 * which * width : (2 * which + 1) * width] = early[:, source]
                out[:, (2 * which + 1) * width : (2 * which + 2) * width] = late[:, source]


def lay_out(place, pieces):
    rows, columns = pieces[0].shape
    count = len(pieces) // 2
    return pl.pallas_call(
        lay_kernel,
        grid_spec=pltpu.PrefetchScalarGridSpec(
            num_scalar_prefetch=1,
            grid=(count,),
            in_specs=[pl.BlockSpec((rows, columns), lambda t, place: (0, 0))] * len(pieces),
            out_specs=pl.BlockSpec((rows, 2 * columns), lambda t, place: (0, place[1 + t])),
        ),
        out_shape=jax.ShapeDtypeStruct((rows, count * 2 * columns), pieces[0].dtype),
        compiler_params=pltpu.CompilerParams(vmem_limit_bytes=KERNEL_BYTES),
        cost_estimate=pl.CostEstimate(flops=0, bytes_accessed=4_000_000, transcendentals=0),
        name="lay_out",
    )(place, *pieces)


def piece_kernel(place, kept, crossed, out):
    width = kept.shape[1]

    @pl.when(place[0] == 0)
    def _():
        out[:, :width] = kept[...]
        out[:, width:] = crossed[...]

    @pl.when(place[0] != 0)
    def _():
        out[:, :width] = crossed[...]
        out[:, width:] = kept[...]


def join_cores(place, kept, crossed):
    rows, columns = kept.shape
    return pl.pallas_call(
        piece_kernel,
        grid_spec=pltpu.PrefetchScalarGridSpec(
            num_scalar_prefetch=1,
            grid=(1,),
            in_specs=[pl.BlockSpec((rows, columns), lambda i, place: (0, 0))] * 2,
            out_specs=pl.BlockSpec((rows, 2 * columns), lambda i, place: (0, 0)),
        ),
        out_shape=jax.ShapeDtypeStruct((rows, 2 * columns), kept.dtype),
        compiler_params=pltpu.CompilerParams(vmem_limit_bytes=KERNEL_BYTES),
        cost_estimate=pl.CostEstimate(flops=0, bytes_accessed=500_000, transcendentals=0),
        name="join_cores",
    )(place, kept, crossed)


def halving_order(count):
    bits = count.bit_length() - 1
    partners = []
    for place in range(count):
        partner = place & 1
        for bit in range(1, bits):
            partner |= ((place >> (bits - bit)) & 1) << bit
        partners.append(partner)
    return partners


def channel_order(ctx, lat_block):
    channel = lax.broadcasted_iota(jnp.int32, (LAT, LAT), 0)
    place = lax.broadcasted_iota(jnp.int32, (LAT, LAT), 1)
    count = LAT // lat_block
    bits = count.bit_length() - 1
    block = place // lat_block
    partner = block & 1
    for bit in range(1, bits):
        partner |= ((block >> (bits - bit)) & 1) << bit
    return channel == (ctx ^ partner) * lat_block + place % lat_block


def collect_kernel(plan, own, sib, cand, cand_t, rope_keys, bias, *, blocks, lat_block):
    pieces = []
    key_at = lax.broadcasted_iota(jnp.int32, (BLOCK, 2 * BLOCK), 0)
    query = lax.broadcasted_iota(jnp.int32, (BLOCK, 2 * BLOCK), 1)
    per_side = len(blocks) // 2
    for block, other in enumerate(blocks):
        rows_ref = sib if other else own
        start = pl.multiple_of(plan[1 + block], 16)
        rows = rows_ref[pl.ds(start, BLOCK), :]
        usable = plan[1 + len(blocks) + block]
        pieces.append(jnp.where(usable > 0, rows, jnp.zeros_like(rows)))
        side, at = divmod(block, per_side)
        kinds = (sib if side else own)[2 * BLOCK : 2 * BLOCK + 16, :][:1].astype(jnp.float32)
        kind = jnp.where(
            query < BLOCK, kinds[:, 2 * at : 2 * at + 1], kinds[:, 2 * at + 1 : 2 * at + 2]
        )
        allowed = (kind > 1.5) | (kind > 0.5) & (key_at <= query % BLOCK)
        bias[block * BLOCK : (block + 1) * BLOCK, :] = jnp.where(allowed, 0.0, HIDDEN)
    both = jnp.concatenate(pieces, axis=0)
    order = channel_order(plan[0], lat_block).astype(jnp.bfloat16)
    latent = both[:, :LAT]
    cand[...] = dot(latent, order, 1, 0).astype(jnp.bfloat16)
    cand_t[...] = dot(order, latent, 0, 1).astype(jnp.bfloat16)
    twice = lax.broadcasted_iota(jnp.int32, (ROPE, 2 * ROPE), 0)
    twice = twice == lax.broadcasted_iota(jnp.int32, (ROPE, 2 * ROPE), 1) % ROPE
    rope_keys[...] = dot(both[:, LAT:], twice.astype(jnp.bfloat16), 1, 0).astype(jnp.bfloat16)


def collect(plan, own, sib, blocks, lat_block):
    rows = len(blocks) * BLOCK
    bf16 = jnp.bfloat16
    shapes = [((rows, LAT), bf16), ((LAT, rows), bf16), ((rows, 2 * ROPE), bf16)]
    shapes.append(((rows, 2 * BLOCK), jnp.float32))
    whole = lambda shape: pl.BlockSpec(shape, lambda i, plan: (0, 0))
    return pl.pallas_call(
        functools.partial(collect_kernel, blocks=blocks, lat_block=lat_block),
        grid_spec=pltpu.PrefetchScalarGridSpec(
            num_scalar_prefetch=1,
            grid=(1,),
            in_specs=[whole(own.shape), whole(sib.shape)],
            out_specs=[whole(shape) for shape, _ in shapes],
        ),
        out_shape=[jax.ShapeDtypeStruct(shape, dtype) for shape, dtype in shapes],
        compiler_params=pltpu.CompilerParams(vmem_limit_bytes=KERNEL_BYTES),
        cost_estimate=pl.CostEstimate(
            flops=250_000_000, bytes_accessed=3_000_000, transcendentals=0
        ),
        name="collect",
    )(plan, own, sib)


def spread_kernel(plan, *refs, blocks, lat_block):
    *sums, own, sib = refs
    count = len(sums) // 2
    latent, rope = sums[0][...], sums[count][...]
    for index in range(1, count):
        latent, rope = latent + sums[index][...], rope + sums[count + index][...]
    order = channel_order(plan[0], lat_block).astype(jnp.float32)
    latent = lax.dot_general(
        latent,
        order,
        (((1,), (1,)), ((), ())),
        precision=lax.Precision.HIGHEST,
        preferred_element_type=jnp.float32,
    )
    rows = jnp.concatenate([latent, rope[:, :ROPE] + rope[:, ROPE:]], axis=1)
    own[...] = jnp.zeros_like(own)
    sib[...] = jnp.zeros_like(sib)
    for block, other in enumerate(blocks):
        here = pl.ds(pl.multiple_of(plan[1 + block], 16), BLOCK)
        target = sib if other else own
        target[here, :] += rows[block * BLOCK : (block + 1) * BLOCK]


def spread(plan, latents, ropes, rows, blocks, lat_block):
    shape = (rows, LAT + ROPE)
    sums = [*latents, *ropes]
    return pl.pallas_call(
        functools.partial(spread_kernel, blocks=blocks, lat_block=lat_block),
        grid_spec=pltpu.PrefetchScalarGridSpec(
            num_scalar_prefetch=1,
            grid=(1,),
            in_specs=[pl.BlockSpec(array.shape, lambda i, plan: (0, 0)) for array in sums],
            out_specs=[pl.BlockSpec(shape, lambda i, plan: (0, 0))] * 2,
        ),
        out_shape=[jax.ShapeDtypeStruct(shape, jnp.float32)] * 2,
        compiler_params=pltpu.CompilerParams(vmem_limit_bytes=KERNEL_BYTES),
        cost_estimate=pl.CostEstimate(
            flops=700_000_000, bytes_accessed=6_000_000, transcendentals=0
        ),
        name="spread",
    )(plan, *sums)


def halve(value, axis, bit):
    half = value.shape[0] // 2
    return value[:half] + exchange(value[half:], axis, bit)


def shards(q_nope, q_rope, grad_out, log_total, kv_latent, up_weight, selected, offered):
    n_dp, n_ctx = lax.axis_size("dp"), lax.axis_size("ctx")
    dp, ctx = lax.axis_index("dp"), lax.axis_index("ctx")
    core = ctx % 2
    group_len = kv_latent.shape[1]
    per_block = group_len // BLOCK
    heads = log_total.shape[1]
    part_heads = heads // n_dp // 2
    pairs = part_heads // 2
    part_cols = part_heads * (NOPE + VDIM)
    far = n_dp - 1
    lat_block = up_weight.shape[0]

    place = jnp.stack([core] + [dp ^ t for t in range(n_dp)]).astype(jnp.int32)

    leaving, = weight_parts(place, up_weight, n_dp, far)
    crossed = exchange(leaving, "ctx", 1)
    crossed, place, selected, offered, q_nope, q_rope, grad_out, log_total, kv_latent = (
        lax.optimization_barrier(
            (crossed, place, selected, offered, q_nope, q_rope, grad_out, log_total, kv_latent)
        )
    )
    chip_rows = weight_parts(place, up_weight, n_dp, far, crossed)
    own = [q_nope[0], q_rope[0], grad_out[0]]
    sibling = [exchange(array, "ctx", 1) for array in own]
    offer_plan = offered[0]
    span = group_len + 16
    blocks, starts, usables = [], [], []
    for side in range(2):
        group = ctx ^ side
        offsets = [0] * per_block + list(partner_offsets)
        blocks += [(offset + side) % 2 for offset in offsets]
        source = jnp.stack([group - offset for offset in offsets])
        sender = jnp.maximum(source, 0)
        inner = jnp.concatenate(
            [
                jnp.arange(per_block, dtype=jnp.int32),
                offer_plan[sender[per_block:], jnp.arange(len(partner_offsets))],
            ]
        )
        usable = source >= 0
        behind = ctx // 2 - sender // 2
        starts.append(jnp.where(usable, behind * span + inner * BLOCK, 0))
        usables.append(usable)
        if side == 0:
            ids = jnp.where(usable, sender * per_block + inner, -1)
            query_ids = group * per_block + jnp.arange(per_block, dtype=jnp.int32)
            picked = jnp.any(selected[0][None, :, :] == ids[:, None, None], axis=2)
            picked = picked & (ids >= 0)[:, None]
            same = ids[:, None] == query_ids[None, :]
            kinds = jnp.where(picked, 2.0, jnp.where(same, 1.0, 0.0)).reshape(1, -1)
    plan = jnp.concatenate([ctx[None], *starts, *usables]).astype(jnp.int32)
    kinds = jnp.pad(kinds.astype(jnp.bfloat16), ((0, 15), (0, LAT + ROPE - kinds.shape[1])))
    bundle = after(jnp.concatenate([kv_latent[0], kinds], axis=0), *sibling)
    bundles = [bundle, from_behind(bundle, "ctx", 2), from_behind(bundle, "ctx", 4)]
    own_bundles = stack(bundles, (((0, 0), (1, 0), (2, 0)),), LAT + ROPE)[0]
    sib_bundles = exchange(own_bundles, "ctx", 1)
    shared = collect(plan, own_bundles, sib_bundles, tuple(blocks), lat_block)

    partners = halving_order(n_ctx)[::2]

    def over_chips(start, onward, *earlier):
        at_step = {0: start}
        for step in range(4, n_ctx, 4):
            at_step[step] = exchange(start, "ctx", step)
        at_step[2] = exchange(start, "ctx", 2)
        for step in range(4, n_ctx, 4):
            if onward:
                forwarded = after(at_step[step], at_step[2], *earlier)
                at_step[step + 2] = exchange(forwarded, "ctx", 2)
            else:
                at_step[step + 2] = exchange(start, "ctx", step + 2)
        return [at_step[partner] for partner in partners], at_step[n_ctx - 4]

    def joined(pieces):
        return stack(pieces, (tuple((index, 0) for index in range(len(pieces))),), part_cols)[0]

    near_pieces, last = over_chips(chip_rows[0], True, *bundles[1:])
    far_pieces, _ = over_chips(after(chip_rows[1], last), False)
    weights = {0: joined(near_pieces), far: joined(far_pieces)}
    for t in range(1, far):
        weights[t] = exchange(weights[0], "dp", t)
    log_total = after(log_total, last)[0]
    sibling.append(exchange(log_total, "ctx", 1))
    own.append(log_total)
    for arrays in (own, sibling):
        arrays[3] = arrays[3].reshape(heads // 2, 2, group_len)

    earlier = None
    latents, ropes = [], []
    weight_grads = {t: ([], []) for t in range(n_dp)}
    bits = [1 << b for b in range(n_dp.bit_length() - 1)]
    orders = (bits, bits[::-1])
    first_sums = [{t: [] for t in range(n_dp) if t & order[0]} for order in orders]
    units = [(t, 0, pairs) for t in [far] + list(range(1, far - 1))]
    units += [(t, start, pairs // 2) for t in (far - 1, 0) for start in (0, pairs // 2)]
    for t, start, count in units:
        weight = weights[t]
        if t == 0:
            weight = after(weight, *[sent[u][-1 if start else 0] for sent in first_sums for u in sent])
        if t == far - 1 and start:
            weight = after(weight, *[sent[far][0] for sent in first_sums])
        rest = chunk_backward(
            place,
            t,
            (start, count),
            own,
            sibling,
            weight,
            shared,
            earlier,
            (n_dp, pairs),
        )
        earlier = rest[:3]
        for side, sent in enumerate(first_sums):
            weight_grads[t][side].append(rest[3 + side])
            if t in sent:
                sent[t].append(exchange(rest[3 + side], "dp", orders[side][0]))
        latents.append(rest[5])
        ropes.append(rest[6])

    half_cols = part_cols // 2

    def columns(pieces, half):
        if len(pieces) == 2:
            return pieces[half]
        return pieces[0][:, half * half_cols : (half + 1) * half_cols]

    def total(addends, half):
        return functools.reduce(
            lambda left, right: left + right, [columns(pieces, half) for pieces in addends]
        )

    sums = []
    last_sums = first_sums[1][far - 1]
    for side, order in enumerate(orders):
        addends = {t: [weight_grads[t][side]] for t in weight_grads}
        arrived = {t ^ order[0]: pieces for t, pieces in first_sums[side].items()}
        addends = {t: addends[t] + [more] for t, more in arrived.items()}
        for bit in order[1:]:
            arrived = {}
            for t in sorted((t for t in addends if t & bit), reverse=True):
                leaving = [total(addends[t], half) for half in range(2)]
                if side == 0:
                    behind = (first_sums[0][order[0]][0], last_sums[0])
                    leaving = [after(half, there) for half, there in zip(leaving, behind)]
                arrived[t ^ bit] = [exchange(half, "dp", bit) for half in leaving]
            addends = {t: addends[t] + [more] for t, more in arrived.items()}
        sums.append(addends[0])

    q_full, rope_full, sib_grads = earlier
    received = exchange(sib_grads, "ctx", 1)
    grad_nope, grad_rope = place_columns(place, received, q_full, rope_full, n_dp)

    own_grads, sib_grads = spread(plan, latents, ropes, 3 * span, tuple(blocks), lat_block)
    swapped = exchange(sib_grads, "ctx", 1)
    grad_rows = own_grads + swapped
    by_chip = [grad_rows[at * span : at * span + group_len] for at in range(3)]
    grad_rows = by_chip[0]
    for chips in (1, 2):
        grad_rows = grad_rows + from_behind(by_chip[chips], "ctx", -2 * chips)

    ctx_bits = [1 << b for b in range(1, n_ctx.bit_length() - 1)]
    finished, arrived = [], None
    for half in range(2):
        if half:
            sums = [[[after(piece, arrived) for piece in pieces] for pieces in side] for side in sums]
        first, second = [total(side, half) for side in sums]
        arrived = exchange(second, "ctx", ctx_bits[0])
        rows = first + arrived
        for bit in ctx_bits[1:]:
            rows = halve(rows, "ctx", bit)
        crossing = rows[lat_block:]
        if half:
            crossing = after(crossing, grad_rows, grad_nope)
        piece = join_cores(place, rows[:lat_block], exchange(crossing, "ctx", 1))
        finished.append([piece] + [exchange(piece, "dp", t) for t in range(1, n_dp)])
    grad_weight = lay_out(place, [piece for both in zip(*finished) for piece in both])
    return (grad_nope[None], grad_rope[None], grad_rows[None], grad_weight)


def solution(mesh):
    in_specs = (
        P("dp", "ctx", None),
        P("dp", "ctx", None),
        P("dp", "ctx", None),
        P("dp", None, "ctx"),
        P("dp", "ctx", None),
        P("ctx", None),
        P("dp", "ctx", None),
        P("dp", None, None),
    )
    out_specs = (P("dp", "ctx", None), P("dp", "ctx", None), P("dp", "ctx", None), P("ctx", None))
    return jax.shard_map(shards, mesh=mesh, in_specs=in_specs, out_specs=out_specs, check_vma=False)
```

```python
import functools

import jax
import jax.numpy as jnp
from jax import lax
from jax.experimental import pallas as pl
from jax.experimental.pallas import tpu as pltpu
from jax.sharding import PartitionSpec as P

LAT = 256
ROPE = 64
NOPE = 128
VDIM = 128
BLOCK = 64

partner_offsets = (1, 2, 3, 4)
HIDDEN = -1e30
KERNEL_BYTES = 12 * 1024 * 1024
INPUT_BYTES = 56 * 1024 * 1024


def from_behind(value, axis, steps):
    count = lax.axis_size(axis)
    initial, last = (max(0, -steps), min(count, count - steps))
    return lax.ppermute(value, axis, [(source, source + steps) for source in range(initial, last)])


def exchange(value, axis, bits):
    count = lax.axis_size(axis)
    return lax.ppermute(value, axis, [(source, source ^ bits) for source in range(count)])


def after(value, *earlier):
    return lax.optimization_barrier((value, *earlier))[0]


def dot(left, right, left_dim, right_dim):
    return lax.dot_general(
        left,
        right,
        (((left_dim,), (right_dim,)), ((), ())),
        preferred_element_type=jnp.float32,
    )


def heads_kernel(
    place,
    q_own, rope_own, out_own, tot_own,
    q_sib, rope_sib, out_sib, tot_sib,
    weight, cand, cand_t, rope_keys, bias,
    *rest,
    earlier,
):
    gq_own, gr_own, sib_grads, *weight_grads, lat_sum, rope_sum = rest[earlier:]
    scale = 1.0 / jnp.sqrt(jnp.float32(NOPE + ROPE))
    rows = cand.shape[0] // 2
    half = weight_grads[0].shape[0]
    sib_q, sib_rope = sib_grads.at[:, : 2 * NOPE], sib_grads.at[:, 2 * NOPE :]
    lane_half = lax.broadcasted_iota(jnp.int32, (rows, 2 * ROPE), 1) // ROPE

    @pl.when(pl.program_id(0) == 0)
    def _():
        lat_sum[...] = jnp.zeros_like(lat_sum)
        rope_sum[...] = jnp.zeros_like(rope_sum)

    groups = (
        (q_own, rope_own, out_own, tot_own, gq_own, gr_own),
        (q_sib, rope_sib, out_sib, tot_sib, sib_q, sib_rope),
    )
    rope_grads = [None, None]
    for head in range(2):
        columns = pl.ds(head * (NOPE + VDIM), NOPE + VDIM)
        head_weight = weight[:, columns]
        expanded = dot(cand[...], head_weight, 1, 0).astype(jnp.bfloat16)
        both_grads = []
        for side, (q_ref, rope_ref, out_ref, tot_ref, gq_ref, gr_ref) in enumerate(groups):
            own_rows = slice(side * rows, (side + 1) * rows)
            here = pl.ds(head * NOPE, NOPE)
            rope_part = jnp.where(
                lane_half == head, rope_keys[own_rows, :], jnp.zeros((), jnp.bfloat16)
            )
            keys = jnp.concatenate([expanded[own_rows, :NOPE], rope_part], axis=1)
            values = expanded[own_rows, NOPE:]
            queries = jnp.concatenate([q_ref[:, here], rope_ref[...]], axis=1)
            out_grads = out_ref[:, here]
            scores = dot(keys, queries, 1, 1) * scale
            probs = jnp.exp(scores - tot_ref[0, head : head + 1, :] + bias[own_rows, :])
            prob_grads = dot(values, out_grads, 1, 1)
            row_dot = jnp.sum(probs * prob_grads, axis=0, keepdims=True)
            score_grads = (probs * (prob_grads - row_dot)).astype(jnp.bfloat16)
            query_grad = dot(score_grads, keys, 0, 0) * scale
            gq_ref[:, here] = query_grad[:, :NOPE].astype(jnp.bfloat16)
            if head == 0:
                rope_grads[side] = query_grad[:, NOPE:]
            else:
                gr_ref[...] = (rope_grads[side] + query_grad[:, NOPE:]).astype(jnp.bfloat16)
            key_grad = dot(score_grads, queries, 1, 0) * scale
            value_grad = dot(probs.astype(jnp.bfloat16), out_grads, 1, 0)
            rope_sum[own_rows, :] += jnp.where(lane_half == head, key_grad[:, NOPE:], 0.0)
            both_grads.append(
                jnp.concatenate([key_grad[:, :NOPE], value_grad], axis=1).astype(jnp.bfloat16)
            )
        key_grads = jnp.concatenate(both_grads, axis=0)
        lat_sum[...] += dot(key_grads, head_weight, 1, 1)
        weight_grad = dot(cand_t[...], key_grads, 1, 0)
        weight_grads[0][:, columns] = weight_grad[:half]
        weight_grads[1][:, columns] = weight_grad[half:]


def chunk_backward(place, t, unit, own, sibling, weight, shared, earlier, sizes):
    q_own, rope_own, out_own, tot_own = own
    cand, cand_t, rope_keys, bias = shared
    tokens = q_own.shape[0]
    chunks, pairs = sizes
    wide, narrow = 2 * NOPE, 2 * ROPE
    first, count = unit
    mine = lambda p, place: (place[1 + t] * 2 + place[0]) * pairs + first + p
    theirs = lambda p, place: place[1 + t] * pairs + first + p
    whole = lambda array: pl.BlockSpec(array.shape, lambda p, place: (0, 0))
    in_specs = [
        pl.BlockSpec((tokens, wide), lambda p, place: (0, mine(p, place))),
        pl.BlockSpec((tokens, narrow), lambda p, place: (0, mine(p, place))),
        pl.BlockSpec((tokens, wide), lambda p, place: (0, mine(p, place))),
        pl.BlockSpec((1, 2, tokens), lambda p, place: (mine(p, place), 0, 0)),
    ] * 2 + [
        pl.BlockSpec((LAT, 2 * (NOPE + VDIM)), lambda p, place: (0, first + p)),
        whole(cand),
        whole(cand_t),
        whole(rope_keys),
        whole(bias),
    ]
    operands = [*own, *sibling, weight, cand, cand_t, rope_keys, bias]
    aliases = {}
    if earlier is not None:
        for index, array in enumerate(earlier):
            aliases[1 + len(operands)] = index
            in_specs.append(pl.BlockSpec(memory_space=pl.ANY))
            operands.append(array)
    columns = 2 * (NOPE + VDIM) * count
    bf16, f32 = jnp.bfloat16, jnp.float32
    out_shape = [
        jax.ShapeDtypeStruct(q_own.shape, bf16),
        jax.ShapeDtypeStruct(rope_own.shape, bf16),
        jax.ShapeDtypeStruct((tokens, chunks * pairs * (wide + narrow)), bf16),
        *[jax.ShapeDtypeStruct((LAT // 2, columns), f32)] * 2,
        jax.ShapeDtypeStruct((cand.shape[0], LAT), f32),
        jax.ShapeDtypeStruct((cand.shape[0], narrow), f32),
    ]
    out_specs = [
        pl.BlockSpec((tokens, wide), lambda p, place: (0, mine(p, place))),
        pl.BlockSpec((tokens, narrow), lambda p, place: (0, mine(p, place))),
        pl.BlockSpec((tokens, wide + narrow), lambda p, place: (0, theirs(p, place))),
        *[pl.BlockSpec((LAT // 2, 2 * (NOPE + VDIM)), lambda p, place: (0, p))] * 2,
        pl.BlockSpec((cand.shape[0], LAT), lambda p, place: (0, 0)),
        pl.BlockSpec((cand.shape[0], narrow), lambda p, place: (0, 0)),
    ]
    return pl.pallas_call(
        functools.partial(heads_kernel, earlier=len(aliases)),
        grid_spec=pltpu.PrefetchScalarGridSpec(
            num_scalar_prefetch=1, grid=(count,), in_specs=in_specs, out_specs=out_specs
        ),
        out_shape=out_shape,
        input_output_aliases=aliases,
        compiler_params=pltpu.CompilerParams(vmem_limit_bytes=KERNEL_BYTES),
        cost_estimate=pl.CostEstimate(
            flops=count * 100_000_000, bytes_accessed=count * 300_000, transcendentals=0
        ),
        name="heads_backward",
    )(place, *operands)


def place_kernel(place, received, q_in, rope_in, q_out, rope_out):
    wide, narrow = 2 * NOPE, 2 * ROPE
    for pair in range(q_out.shape[1] // wide):
        start = pair * (wide + narrow)
        q_out[:, pair * wide : (pair + 1) * wide] = received[:, start : start + wide]
        rope_out[:, pair * narrow : (pair + 1) * narrow] = received[
            :, start + wide : start + wide + narrow
        ]


def place_columns(place, received, q_full, rope_full, chunks):
    tokens = q_full.shape[0]
    q_cols, rope_cols = q_full.shape[1] // chunks // 2, rope_full.shape[1] // chunks // 2
    put = lambda c, place: (0, c * 2 + 1 - place[0])
    return pl.pallas_call(
        place_kernel,
        grid_spec=pltpu.PrefetchScalarGridSpec(
            num_scalar_prefetch=1,
            grid=(chunks,),
            in_specs=[
                pl.BlockSpec((tokens, q_cols + rope_cols), lambda c, place: (0, c)),
                pl.BlockSpec(memory_space=pl.ANY),
                pl.BlockSpec(memory_space=pl.ANY),
            ],
            out_specs=[
                pl.BlockSpec((tokens, q_cols), put),
                pl.BlockSpec((tokens, rope_cols), put),
            ],
        ),
        out_shape=[
            jax.ShapeDtypeStruct(q_full.shape, q_full.dtype),
            jax.ShapeDtypeStruct(rope_full.shape, rope_full.dtype),
        ],
        input_output_aliases={2: 0, 3: 1},
        compiler_params=pltpu.CompilerParams(vmem_limit_bytes=KERNEL_BYTES),
        cost_estimate=pl.CostEstimate(flops=0, bytes_accessed=4_000_000, transcendentals=0),
        name="place_columns",
    )(place, received, q_full, rope_full)


def stack_kernel(*refs, arrangement):
    outs = refs[len(refs) - len(arrangement) :]
    for out, sources in zip(outs, arrangement):
        row = 0
        for index, block in sources:
            piece = refs[index]
            columns = slice(block * out.shape[1], (block + 1) * out.shape[1])
            out[row : row + piece.shape[0], :] = piece[:, columns]
            row += piece.shape[0]


def stack(inputs, arrangement, columns):
    whole = lambda shape: pl.BlockSpec(shape, lambda: (0, 0))
    shapes = [(sum(inputs[i].shape[0] for i, _ in sources), columns) for sources in arrangement]
    return pl.pallas_call(
        functools.partial(stack_kernel, arrangement=arrangement),
        in_specs=[whole(array.shape) for array in inputs],
        out_specs=[whole(shape) for shape in shapes],
        out_shape=[jax.ShapeDtypeStruct(shape, inputs[0].dtype) for shape in shapes],
        compiler_params=pltpu.CompilerParams(vmem_limit_bytes=KERNEL_BYTES),
        cost_estimate=pl.CostEstimate(flops=0, bytes_accessed=2_000_000, transcendentals=0),
        name="stack",
    )(*inputs)


def leave_kernel(place, near, distant, leaving):
    width = near.shape[1]
    leaving[:, :width] = near[...]
    leaving[:, width:] = distant[...]


def join_rows_kernel(place, near, distant, crossed, near_rows, distant_rows):
    rows, width = near.shape
    for at, (own, out) in enumerate(((near, near_rows), (distant, distant_rows))):
        out[:rows, :] = own[...]
        out[rows:, :] = crossed[:, at * width : (at + 1) * width]


def weight_parts(place, up_weight, chunks, far, crossed=None):
    rows = up_weight.shape[0]
    width = up_weight.shape[1] // chunks // 2
    joins = crossed is not None

    def column_block(t):
        def block(i, place):
            return (0, place[1 + t] * 2 + (place[0] if joins else 1 - place[0]))

        return pl.BlockSpec((rows, width), block)

    whole = lambda shape: pl.BlockSpec(shape, lambda i, place: (0, 0))
    shapes = [(2 * rows, width)] * 2 if joins else [(rows, 2 * width)]
    return pl.pallas_call(
        join_rows_kernel if joins else leave_kernel,
        grid_spec=pltpu.PrefetchScalarGridSpec(
            num_scalar_prefetch=1,
            grid=(1,),
            in_specs=[column_block(t) for t in (0, far)] + [whole((rows, 2 * width))] * joins,
            out_specs=[whole(shape) for shape in shapes],
        ),
        out_shape=[jax.ShapeDtypeStruct(shape, up_weight.dtype) for shape in shapes],
        compiler_params=pltpu.CompilerParams(vmem_limit_bytes=INPUT_BYTES),
        cost_estimate=pl.CostEstimate(flops=0, bytes_accessed=1_000_000, transcendentals=0),
        name="weight_parts",
    )(place, up_weight, up_weight, *([crossed] if joins else []))


def lay_kernel(place, *refs):
    *pieces, out = refs
    width = out.shape[1] // 4
    for step in range(len(pieces) // 2):
        early, late = pieces[2 * step], pieces[2 * step + 1]

        @pl.when(pl.program_id(0) == step)
        def _():
            for which in range(2):
                source = slice(which * width, (which + 1) * width)
                out[:, 2 * which * width : (2 * which + 1) * width] = early[:, source]
                out[:, (2 * which + 1) * width : (2 * which + 2) * width] = late[:, source]


def lay_out(place, pieces):
    rows, columns = pieces[0].shape
    count = len(pieces) // 2
    return pl.pallas_call(
        lay_kernel,
        grid_spec=pltpu.PrefetchScalarGridSpec(
            num_scalar_prefetch=1,
            grid=(count,),
            in_specs=[pl.BlockSpec((rows, columns), lambda t, place: (0, 0))] * len(pieces),
            out_specs=pl.BlockSpec((rows, 2 * columns), lambda t, place: (0, place[1 + t])),
        ),
        out_shape=jax.ShapeDtypeStruct((rows, count * 2 * columns), pieces[0].dtype),
        compiler_params=pltpu.CompilerParams(vmem_limit_bytes=KERNEL_BYTES),
        cost_estimate=pl.CostEstimate(flops=0, bytes_accessed=4_000_000, transcendentals=0),
        name="lay_out",
    )(place, *pieces)


def piece_kernel(place, kept, crossed, out):
    width = kept.shape[1]

    @pl.when(place[0] == 0)
    def _():
        out[:, :width] = kept[...]
        out[:, width:] = crossed[...]

    @pl.when(place[0] != 0)
    def _():
        out[:, :width] = crossed[...]
        out[:, width:] = kept[...]


def join_cores(place, kept, crossed):
    rows, columns = kept.shape
    return pl.pallas_call(
        piece_kernel,
        grid_spec=pltpu.PrefetchScalarGridSpec(
            num_scalar_prefetch=1,
            grid=(1,),
            in_specs=[pl.BlockSpec((rows, columns), lambda i, place: (0, 0))] * 2,
            out_specs=pl.BlockSpec((rows, 2 * columns), lambda i, place: (0, 0)),
        ),
        out_shape=jax.ShapeDtypeStruct((rows, 2 * columns), kept.dtype),
        compiler_params=pltpu.CompilerParams(vmem_limit_bytes=KERNEL_BYTES),
        cost_estimate=pl.CostEstimate(flops=0, bytes_accessed=500_000, transcendentals=0),
        name="join_cores",
    )(place, kept, crossed)


def halving_order(count):
    bits = count.bit_length() - 1
    partners = []
    for place in range(count):
        partner = place & 1
        for bit in range(1, bits):
            partner |= ((place >> (bits - bit)) & 1) << bit
        partners.append(partner)
    return partners


def channel_order(ctx, lat_block):
    channel = lax.broadcasted_iota(jnp.int32, (LAT, LAT), 0)
    place = lax.broadcasted_iota(jnp.int32, (LAT, LAT), 1)
    count = LAT // lat_block
    bits = count.bit_length() - 1
    block = place // lat_block
    partner = block & 1
    for bit in range(1, bits):
        partner |= ((block >> (bits - bit)) & 1) << bit
    return channel == (ctx ^ partner) * lat_block + place % lat_block


def collect_kernel(plan, own, sib, cand, cand_t, rope_keys, bias, *, blocks, lat_block):
    pieces = []
    key_at = lax.broadcasted_iota(jnp.int32, (BLOCK, 2 * BLOCK), 0)
    query = lax.broadcasted_iota(jnp.int32, (BLOCK, 2 * BLOCK), 1)
    per_side = len(blocks) // 2
    for block, other in enumerate(blocks):
        rows_ref = sib if other else own
        start = pl.multiple_of(plan[1 + block], 16)
        rows = rows_ref[pl.ds(start, BLOCK), :]
        usable = plan[1 + len(blocks) + block]
        pieces.append(jnp.where(usable > 0, rows, jnp.zeros_like(rows)))
        side, at = divmod(block, per_side)
        kinds = (sib if side else own)[2 * BLOCK : 2 * BLOCK + 16, :][:1].astype(jnp.float32)
        kind = jnp.where(
            query < BLOCK, kinds[:, 2 * at : 2 * at + 1], kinds[:, 2 * at + 1 : 2 * at + 2]
        )
        allowed = (kind > 1.5) | (kind > 0.5) & (key_at <= query % BLOCK)
        bias[block * BLOCK : (block + 1) * BLOCK, :] = jnp.where(allowed, 0.0, HIDDEN)
    both = jnp.concatenate(pieces, axis=0)
    order = channel_order(plan[0], lat_block).astype(jnp.bfloat16)
    latent = both[:, :LAT]
    cand[...] = dot(latent, order, 1, 0).astype(jnp.bfloat16)
    cand_t[...] = dot(order, latent, 0, 1).astype(jnp.bfloat16)
    twice = lax.broadcasted_iota(jnp.int32, (ROPE, 2 * ROPE), 0)
    twice = twice == lax.broadcasted_iota(jnp.int32, (ROPE, 2 * ROPE), 1) % ROPE
    rope_keys[...] = dot(both[:, LAT:], twice.astype(jnp.bfloat16), 1, 0).astype(jnp.bfloat16)


def collect(plan, own, sib, blocks, lat_block):
    rows = len(blocks) * BLOCK
    bf16 = jnp.bfloat16
    shapes = [((rows, LAT), bf16), ((LAT, rows), bf16), ((rows, 2 * ROPE), bf16)]
    shapes.append(((rows, 2 * BLOCK), jnp.float32))
    whole = lambda shape: pl.BlockSpec(shape, lambda i, plan: (0, 0))
    return pl.pallas_call(
        functools.partial(collect_kernel, blocks=blocks, lat_block=lat_block),
        grid_spec=pltpu.PrefetchScalarGridSpec(
            num_scalar_prefetch=1,
            grid=(1,),
            in_specs=[whole(own.shape), whole(sib.shape)],
            out_specs=[whole(shape) for shape, _ in shapes],
        ),
        out_shape=[jax.ShapeDtypeStruct(shape, dtype) for shape, dtype in shapes],
        compiler_params=pltpu.CompilerParams(vmem_limit_bytes=KERNEL_BYTES),
        cost_estimate=pl.CostEstimate(
            flops=250_000_000, bytes_accessed=3_000_000, transcendentals=0
        ),
        name="collect",
    )(plan, own, sib)


def spread_kernel(plan, *refs, blocks, lat_block):
    *sums, own, sib = refs
    count = len(sums) // 2
    latent, rope = sums[0][...], sums[count][...]
    for index in range(1, count):
        latent, rope = latent + sums[index][...], rope + sums[count + index][...]
    order = channel_order(plan[0], lat_block).astype(jnp.float32)
    latent = lax.dot_general(
        latent,
        order,
        (((1,), (1,)), ((), ())),
        precision=lax.Precision.HIGHEST,
        preferred_element_type=jnp.float32,
    )
    rows = jnp.concatenate([latent, rope[:, :ROPE] + rope[:, ROPE:]], axis=1)
    own[...] = jnp.zeros_like(own)
    sib[...] = jnp.zeros_like(sib)
    for block, other in enumerate(blocks):
        here = pl.ds(pl.multiple_of(plan[1 + block], 16), BLOCK)
        target = sib if other else own
        target[here, :] += rows[block * BLOCK : (block + 1) * BLOCK]


def spread(plan, latents, ropes, rows, blocks, lat_block):
    shape = (rows, LAT + ROPE)
    sums = [*latents, *ropes]
    return pl.pallas_call(
        functools.partial(spread_kernel, blocks=blocks, lat_block=lat_block),
        grid_spec=pltpu.PrefetchScalarGridSpec(
            num_scalar_prefetch=1,
            grid=(1,),
            in_specs=[pl.BlockSpec(array.shape, lambda i, plan: (0, 0)) for array in sums],
            out_specs=[pl.BlockSpec(shape, lambda i, plan: (0, 0))] * 2,
        ),
        out_shape=[jax.ShapeDtypeStruct(shape, jnp.float32)] * 2,
        compiler_params=pltpu.CompilerParams(vmem_limit_bytes=KERNEL_BYTES),
        cost_estimate=pl.CostEstimate(
            flops=700_000_000, bytes_accessed=6_000_000, transcendentals=0
        ),
        name="spread",
    )(plan, *sums)


def halve(value, axis, bit):
    half = value.shape[0] // 2
    return value[:half] + exchange(value[half:], axis, bit)


def shards(q_nope, q_rope, grad_out, log_total, kv_latent, up_weight, selected, offered):
    n_dp, n_ctx = lax.axis_size("dp"), lax.axis_size("ctx")
    dp, ctx = lax.axis_index("dp"), lax.axis_index("ctx")
    core = ctx % 2
    group_len = kv_latent.shape[1]
    per_block = group_len // BLOCK
    heads = log_total.shape[1]
    part_heads = heads // n_dp // 2
    pairs = part_heads // 2
    part_cols = part_heads * (NOPE + VDIM)
    far = n_dp - 1
    lat_block = up_weight.shape[0]

    place = jnp.stack([core] + [dp ^ t for t in range(n_dp)]).astype(jnp.int32)

    leaving, = weight_parts(place, up_weight, n_dp, far)
    crossed = exchange(leaving, "ctx", 1)
    crossed, place, selected, offered, q_nope, q_rope, grad_out, log_total, kv_latent = (
        lax.optimization_barrier(
            (crossed, place, selected, offered, q_nope, q_rope, grad_out, log_total, kv_latent)
        )
    )
    chip_rows = weight_parts(place, up_weight, n_dp, far, crossed)
    own = [q_nope[0], q_rope[0], grad_out[0]]
    sibling = [exchange(array, "ctx", 1) for array in own]
    offer_plan = offered[0]
    span = group_len + 16
    blocks, starts, usables = [], [], []
    for side in range(2):
        group = ctx ^ side
        offsets = [0] * per_block + list(partner_offsets)
        blocks += [(offset + side) % 2 for offset in offsets]
        source = jnp.stack([group - offset for offset in offsets])
        sender = jnp.maximum(source, 0)
        inner = jnp.concatenate(
            [
                jnp.arange(per_block, dtype=jnp.int32),
                offer_plan[sender[per_block:], jnp.arange(len(partner_offsets))],
            ]
        )
        usable = source >= 0
        behind = ctx // 2 - sender // 2
        starts.append(jnp.where(usable, behind * span + inner * BLOCK, 0))
        usables.append(usable)
        if side == 0:
            ids = jnp.where(usable, sender * per_block + inner, -1)
            query_ids = group * per_block + jnp.arange(per_block, dtype=jnp.int32)
            picked = jnp.any(selected[0][None, :, :] == ids[:, None, None], axis=2)
            picked = picked & (ids >= 0)[:, None]
            same = ids[:, None] == query_ids[None, :]
            kinds = jnp.where(picked, 2.0, jnp.where(same, 1.0, 0.0)).reshape(1, -1)
    plan = jnp.concatenate([ctx[None], *starts, *usables]).astype(jnp.int32)
    kinds = jnp.pad(kinds.astype(jnp.bfloat16), ((0, 15), (0, LAT + ROPE - kinds.shape[1])))
    bundle = after(jnp.concatenate([kv_latent[0], kinds], axis=0), *sibling)
    bundles = [bundle, from_behind(bundle, "ctx", 2), from_behind(bundle, "ctx", 4)]
    own_bundles = stack(bundles, (((0, 0), (1, 0), (2, 0)),), LAT + ROPE)[0]
    sib_bundles = exchange(own_bundles, "ctx", 1)
    shared = collect(plan, own_bundles, sib_bundles, tuple(blocks), lat_block)

    partners = halving_order(n_ctx)[::2]

    def over_chips(start):
        at_step = {0: start}
        for step in range(4, n_ctx, 4):
            at_step[step] = exchange(start, "ctx", step)
        at_step[2] = exchange(start, "ctx", 2)
        for step in range(4, n_ctx, 4):
            at_step[step + 2] = exchange(after(at_step[step], at_step[2]), "ctx", 2)
        return [at_step[partner] for partner in partners], at_step[n_ctx - 4]

    def joined(pieces):
        return stack(pieces, (tuple((index, 0) for index in range(len(pieces))),), part_cols)[0]

    near_pieces, last = over_chips(chip_rows[0])
    far_pieces, _ = over_chips(after(chip_rows[1], last))
    log_total = after(log_total, last)[0]
    sibling.append(exchange(log_total, "ctx", 1))
    own.append(log_total)
    for arrays in (own, sibling):
        arrays[3] = arrays[3].reshape(heads // 2, 2, group_len)

    weights = {0: joined([after(near_pieces[0], sib_bundles, sibling[3])] + near_pieces[1:])}
    for t in range(1, far):
        weights[t] = exchange(weights[0], "dp", t)
    earlier = None
    latents, ropes = [], []
    weight_grads = {t: ([], []) for t in range(n_dp)}
    bits = [1 << b for b in range(n_dp.bit_length() - 1)]
    orders = (bits, bits[::-1])
    first_sums = [{t: [] for t in range(n_dp) if t & order[0]} for order in orders]
    half_pairs = pairs // 2
    units = [(0, 0, half_pairs)] + [(t, 0, pairs) for t in [far] + list(range(1, far - 1))]
    units += [(far - 1, 0, half_pairs), (far - 1, half_pairs, half_pairs)]
    units.append((0, half_pairs, half_pairs))
    for t, start, count in units:
        if t == far:
            weights[far] = joined([after(far_pieces[0], latents[-1])] + far_pieces[1:])
        weight = weights[t]
        if t == 0 and start:
            weight = after(weight, *[piece for sent in first_sums for u in sent for piece in sent[u]])
        if t == 1 and not start:
            weight = after(weight, *[weights[near] for near in range(2, far)])
        if t == far - 1 and start:
            weight = after(weight, *[sent[far][0] for sent in first_sums])
        rest = chunk_backward(
            place,
            t,
            (start, count),
            own,
            sibling,
            weight,
            shared,
            earlier,
            (n_dp, pairs),
        )
        earlier = rest[:3]
        for side, sent in enumerate(first_sums):
            weight_grads[t][side].append(rest[3 + side])
            if t in sent:
                sent[t].append(exchange(rest[3 + side], "dp", orders[side][0]))
        latents.append(rest[5])
        ropes.append(rest[6])

    half_cols = part_cols // 2

    def columns(pieces, half):
        if len(pieces) == 2:
            return pieces[half]
        return pieces[0][:, half * half_cols : (half + 1) * half_cols]

    def total(addends, half):
        return functools.reduce(
            lambda left, right: left + right, [columns(pieces, half) for pieces in addends]
        )

    sums = []
    last_sums = first_sums[1][far - 1]
    for side, order in enumerate(orders):
        addends = {t: [weight_grads[t][side]] for t in weight_grads}
        arrived = {t ^ order[0]: pieces for t, pieces in first_sums[side].items()}
        addends = {t: addends[t] + [more] for t, more in arrived.items()}
        for bit in order[1:]:
            arrived = {}
            for t in sorted((t for t in addends if t & bit), reverse=True):
                leaving = [total(addends[t], half) for half in range(2)]
                if side == 0:
                    behind = (first_sums[0][order[0]][0], last_sums[0])
                else:
                    behind = [weight_grads[far - 1][side][0]] * 2
                leaving = [after(half, there) for half, there in zip(leaving, behind)]
                arrived[t ^ bit] = [exchange(half, "dp", bit) for half in leaving]
            addends = {t: addends[t] + [more] for t, more in arrived.items()}
        sums.append(addends[0])

    q_full, rope_full, sib_grads = earlier
    received = exchange(sib_grads, "ctx", 1)
    grad_nope, grad_rope = place_columns(place, received, q_full, rope_full, n_dp)

    own_grads, sib_grads = spread(plan, latents, ropes, 3 * span, tuple(blocks), lat_block)
    swapped = exchange(sib_grads, "ctx", 1)
    grad_rows = own_grads + swapped
    by_chip = [grad_rows[at * span : at * span + group_len] for at in range(3)]
    grad_rows = by_chip[0]
    for chips in (1, 2):
        grad_rows = grad_rows + from_behind(by_chip[chips], "ctx", -2 * chips)

    ctx_bits = [1 << b for b in range(1, n_ctx.bit_length() - 1)]
    finished, arrived = [], None
    for half in range(2):
        if half:
            sums = [[[after(piece, arrived) for piece in pieces] for pieces in side] for side in sums]
        first, second = [total(side, half) for side in sums]
        there = (sums[0][-1][half], latents[-1]) if half == 0 else (sums[0][-1][half],)
        arrived = exchange(after(second, *there), "ctx", ctx_bits[0])
        rows = first + arrived
        for bit in ctx_bits[1:]:
            rows = halve(rows, "ctx", bit)
        piece = join_cores(place, rows[:lat_block], exchange(rows[lat_block:], "ctx", 1))
        finished.append([piece] + [exchange(piece, "dp", t) for t in range(1, n_dp)])
    finished[0][0] = after(finished[0][0], grad_rows, grad_nope)
    grad_weight = lay_out(place, [piece for both in zip(*finished) for piece in both])
    return (grad_nope[None], grad_rope[None], grad_rows[None], grad_weight)


def solution(mesh):
    in_specs = (
        P("dp", "ctx", None),
        P("dp", "ctx", None),
        P("dp", "ctx", None),
        P("dp", None, "ctx"),
        P("dp", "ctx", None),
        P("ctx", None),
        P("dp", "ctx", None),
        P("dp", None, None),
    )
    out_specs = (P("dp", "ctx", None), P("dp", "ctx", None), P("dp", "ctx", None), P("ctx", None))
    return jax.shard_map(shards, mesh=mesh, in_specs=in_specs, out_specs=out_specs, check_vma=False)
```

```python
import functools

import jax
import jax.numpy as jnp
from jax import lax
from jax.experimental import pallas as pl
from jax.experimental.pallas import tpu as pltpu
from jax.sharding import PartitionSpec as P

LAT = 256
ROPE = 64
NOPE = 128
VDIM = 128
BLOCK = 64
TOPK = 3

partner_offsets = (1, 2, 3, 4)
HIDDEN = -1e30
KERNEL_BYTES = 12 * 1024 * 1024
INPUT_BYTES = 56 * 1024 * 1024


def from_behind(value, axis, steps):
    count = lax.axis_size(axis)
    initial, last = (max(0, -steps), min(count, count - steps))
    return lax.ppermute(value, axis, [(source, source + steps) for source in range(initial, last)])


def exchange(value, axis, bits):
    count = lax.axis_size(axis)
    return lax.ppermute(value, axis, [(source, source ^ bits) for source in range(count)])


def after(value, *earlier):
    return lax.optimization_barrier((value, *earlier))[0]


def dot(left, right, left_dim, right_dim):
    return lax.dot_general(
        left,
        right,
        (((left_dim,), (right_dim,)), ((), ())),
        preferred_element_type=jnp.float32,
    )


def heads_kernel(
    place,
    q_own, rope_own, out_own, tot_own,
    q_sib, rope_sib, out_sib, tot_sib,
    weight, cand, cand_t, rope_keys, bias,
    *rest,
    earlier,
):
    gq_own, gr_own, sib_grads, *weight_grads, lat_sum, rope_sum = rest[earlier:]
    scale = 1.0 / jnp.sqrt(jnp.float32(NOPE + ROPE))
    rows = cand.shape[0] // 2
    half = weight_grads[0].shape[0]
    sib_q, sib_rope = sib_grads.at[:, : 2 * NOPE], sib_grads.at[:, 2 * NOPE :]
    lane_half = lax.broadcasted_iota(jnp.int32, (rows, 2 * ROPE), 1) // ROPE

    @pl.when(pl.program_id(0) == 0)
    def _():
        lat_sum[...] = jnp.zeros_like(lat_sum)
        rope_sum[...] = jnp.zeros_like(rope_sum)

    groups = (
        (q_own, rope_own, out_own, tot_own, gq_own, gr_own),
        (q_sib, rope_sib, out_sib, tot_sib, sib_q, sib_rope),
    )
    rope_grads = [None, None]
    for head in range(2):
        columns = pl.ds(head * (NOPE + VDIM), NOPE + VDIM)
        head_weight = weight[:, columns]
        expanded = dot(cand[...], head_weight, 1, 0).astype(jnp.bfloat16)
        both_grads = []
        for side, (q_ref, rope_ref, out_ref, tot_ref, gq_ref, gr_ref) in enumerate(groups):
            own_rows = slice(side * rows, (side + 1) * rows)
            here = pl.ds(head * NOPE, NOPE)
            rope_part = jnp.where(
                lane_half == head, rope_keys[own_rows, :], jnp.zeros((), jnp.bfloat16)
            )
            keys = jnp.concatenate([expanded[own_rows, :NOPE], rope_part], axis=1)
            values = expanded[own_rows, NOPE:]
            queries = jnp.concatenate([q_ref[:, here], rope_ref[...]], axis=1)
            out_grads = out_ref[:, here]
            scores = dot(keys, queries, 1, 1) * scale
            probs = jnp.exp(scores - tot_ref[0, head : head + 1, :] + bias[own_rows, :])
            prob_grads = dot(values, out_grads, 1, 1)
            row_dot = jnp.sum(probs * prob_grads, axis=0, keepdims=True)
            score_grads = (probs * (prob_grads - row_dot)).astype(jnp.bfloat16)
            query_grad = dot(score_grads, keys, 0, 0) * scale
            gq_ref[:, here] = query_grad[:, :NOPE].astype(jnp.bfloat16)
            if head == 0:
                rope_grads[side] = query_grad[:, NOPE:]
            else:
                gr_ref[...] = (rope_grads[side] + query_grad[:, NOPE:]).astype(jnp.bfloat16)
            key_grad = dot(score_grads, queries, 1, 0) * scale
            value_grad = dot(probs.astype(jnp.bfloat16), out_grads, 1, 0)
            rope_sum[own_rows, :] += jnp.where(lane_half == head, key_grad[:, NOPE:], 0.0)
            both_grads.append(
                jnp.concatenate([key_grad[:, :NOPE], value_grad], axis=1).astype(jnp.bfloat16)
            )
        key_grads = jnp.concatenate(both_grads, axis=0)
        lat_sum[...] += dot(key_grads, head_weight, 1, 1)
        weight_grad = dot(cand_t[...], key_grads, 1, 0)
        weight_grads[0][:, columns] = weight_grad[:half]
        weight_grads[1][:, columns] = weight_grad[half:]


def chunk_backward(place, t, unit, own, sibling, weight, shared, earlier, sizes):
    q_own, rope_own, out_own, tot_own = own
    cand, cand_t, rope_keys, bias = shared
    tokens = q_own.shape[0]
    chunks, pairs = sizes
    wide, narrow = 2 * NOPE, 2 * ROPE
    first, count = unit
    mine = lambda p, place: (place[1 + t] * 2 + place[0]) * pairs + first + p
    theirs = lambda p, place: place[1 + t] * pairs + first + p
    whole = lambda array: pl.BlockSpec(array.shape, lambda p, place: (0, 0))
    in_specs = [
        pl.BlockSpec((tokens, wide), lambda p, place: (0, mine(p, place))),
        pl.BlockSpec((tokens, narrow), lambda p, place: (0, mine(p, place))),
        pl.BlockSpec((tokens, wide), lambda p, place: (0, mine(p, place))),
        pl.BlockSpec((1, 2, tokens), lambda p, place: (mine(p, place), 0, 0)),
    ] * 2 + [
        pl.BlockSpec((LAT, 2 * (NOPE + VDIM)), lambda p, place: (0, first + p)),
        whole(cand),
        whole(cand_t),
        whole(rope_keys),
        whole(bias),
    ]
    operands = [*own, *sibling, weight, cand, cand_t, rope_keys, bias]
    aliases = {}
    if earlier is not None:
        for index, array in enumerate(earlier):
            aliases[1 + len(operands)] = index
            in_specs.append(pl.BlockSpec(memory_space=pl.ANY))
            operands.append(array)
    columns = 2 * (NOPE + VDIM) * count
    bf16, f32 = jnp.bfloat16, jnp.float32
    out_shape = [
        jax.ShapeDtypeStruct(q_own.shape, bf16),
        jax.ShapeDtypeStruct(rope_own.shape, bf16),
        jax.ShapeDtypeStruct((tokens, chunks * pairs * (wide + narrow)), bf16),
        *[jax.ShapeDtypeStruct((LAT // 2, columns), f32)] * 2,
        jax.ShapeDtypeStruct((cand.shape[0], LAT), f32),
        jax.ShapeDtypeStruct((cand.shape[0], narrow), f32),
    ]
    out_specs = [
        pl.BlockSpec((tokens, wide), lambda p, place: (0, mine(p, place))),
        pl.BlockSpec((tokens, narrow), lambda p, place: (0, mine(p, place))),
        pl.BlockSpec((tokens, wide + narrow), lambda p, place: (0, theirs(p, place))),
        *[pl.BlockSpec((LAT // 2, 2 * (NOPE + VDIM)), lambda p, place: (0, p))] * 2,
        pl.BlockSpec((cand.shape[0], LAT), lambda p, place: (0, 0)),
        pl.BlockSpec((cand.shape[0], narrow), lambda p, place: (0, 0)),
    ]
    return pl.pallas_call(
        functools.partial(heads_kernel, earlier=len(aliases)),
        grid_spec=pltpu.PrefetchScalarGridSpec(
            num_scalar_prefetch=1, grid=(count,), in_specs=in_specs, out_specs=out_specs
        ),
        out_shape=out_shape,
        input_output_aliases=aliases,
        compiler_params=pltpu.CompilerParams(vmem_limit_bytes=KERNEL_BYTES),
        cost_estimate=pl.CostEstimate(
            flops=count * 100_000_000, bytes_accessed=count * 300_000, transcendentals=0
        ),
        name="heads_backward",
    )(place, *operands)


def place_kernel(place, received, q_in, rope_in, q_out, rope_out):
    wide, narrow = 2 * NOPE, 2 * ROPE
    for pair in range(q_out.shape[1] // wide):
        start = pair * (wide + narrow)
        q_out[:, pair * wide : (pair + 1) * wide] = received[:, start : start + wide]
        rope_out[:, pair * narrow : (pair + 1) * narrow] = received[
            :, start + wide : start + wide + narrow
        ]


def place_columns(place, received, q_full, rope_full, chunks):
    tokens = q_full.shape[0]
    q_cols, rope_cols = q_full.shape[1] // chunks // 2, rope_full.shape[1] // chunks // 2
    put = lambda c, place: (0, c * 2 + 1 - place[0])
    return pl.pallas_call(
        place_kernel,
        grid_spec=pltpu.PrefetchScalarGridSpec(
            num_scalar_prefetch=1,
            grid=(chunks,),
            in_specs=[
                pl.BlockSpec((tokens, q_cols + rope_cols), lambda c, place: (0, c)),
                pl.BlockSpec(memory_space=pl.ANY),
                pl.BlockSpec(memory_space=pl.ANY),
            ],
            out_specs=[
                pl.BlockSpec((tokens, q_cols), put),
                pl.BlockSpec((tokens, rope_cols), put),
            ],
        ),
        out_shape=[
            jax.ShapeDtypeStruct(q_full.shape, q_full.dtype),
            jax.ShapeDtypeStruct(rope_full.shape, rope_full.dtype),
        ],
        input_output_aliases={2: 0, 3: 1},
        compiler_params=pltpu.CompilerParams(vmem_limit_bytes=KERNEL_BYTES),
        cost_estimate=pl.CostEstimate(flops=0, bytes_accessed=4_000_000, transcendentals=0),
        name="place_columns",
    )(place, received, q_full, rope_full)


def stack_kernel(*refs, arrangement):
    outs = refs[len(refs) - len(arrangement) :]
    for out, sources in zip(outs, arrangement):
        row = 0
        for index, block in sources:
            piece = refs[index]
            columns = slice(block * out.shape[1], (block + 1) * out.shape[1])
            out[row : row + piece.shape[0], :] = piece[:, columns]
            row += piece.shape[0]


def stack(inputs, arrangement, columns):
    whole = lambda shape: pl.BlockSpec(shape, lambda: (0, 0))
    shapes = [(sum(inputs[i].shape[0] for i, _ in sources), columns) for sources in arrangement]
    return pl.pallas_call(
        functools.partial(stack_kernel, arrangement=arrangement),
        in_specs=[whole(array.shape) for array in inputs],
        out_specs=[whole(shape) for shape in shapes],
        out_shape=[jax.ShapeDtypeStruct(shape, inputs[0].dtype) for shape in shapes],
        compiler_params=pltpu.CompilerParams(vmem_limit_bytes=KERNEL_BYTES),
        cost_estimate=pl.CostEstimate(flops=0, bytes_accessed=2_000_000, transcendentals=0),
        name="stack",
    )(*inputs)


def leave_kernel(place, near, distant, leaving):
    width = near.shape[1]
    leaving[:, :width] = near[...]
    leaving[:, width:] = distant[...]


def join_rows_kernel(place, near, distant, crossed, near_rows, distant_rows):
    rows, width = near.shape
    for at, (own, out) in enumerate(((near, near_rows), (distant, distant_rows))):
        out[:rows, :] = own[...]
        out[rows:, :] = crossed[:, at * width : (at + 1) * width]


def weight_parts(place, up_weight, chunks, far, crossed=None):
    rows = up_weight.shape[0]
    width = up_weight.shape[1] // chunks // 2
    joins = crossed is not None

    def column_block(t):
        def block(i, place):
            return (0, place[1 + t] * 2 + (place[0] if joins else 1 - place[0]))

        return pl.BlockSpec((rows, width), block)

    whole = lambda shape: pl.BlockSpec(shape, lambda i, place: (0, 0))
    shapes = [(2 * rows, width)] * 2 if joins else [(rows, 2 * width)]
    return pl.pallas_call(
        join_rows_kernel if joins else leave_kernel,
        grid_spec=pltpu.PrefetchScalarGridSpec(
            num_scalar_prefetch=1,
            grid=(1,),
            in_specs=[column_block(t) for t in (0, far)] + [whole((rows, 2 * width))] * joins,
            out_specs=[whole(shape) for shape in shapes],
        ),
        out_shape=[jax.ShapeDtypeStruct(shape, up_weight.dtype) for shape in shapes],
        compiler_params=pltpu.CompilerParams(vmem_limit_bytes=INPUT_BYTES),
        cost_estimate=pl.CostEstimate(flops=0, bytes_accessed=1_000_000, transcendentals=0),
        name="weight_parts",
    )(place, up_weight, up_weight, *([crossed] if joins else []))


def lay_kernel(place, *refs):
    *pieces, out = refs
    width = out.shape[1] // 4
    for step in range(len(pieces) // 2):
        early, late = pieces[2 * step], pieces[2 * step + 1]

        @pl.when(pl.program_id(0) == step)
        def _():
            for which in range(2):
                source = slice(which * width, (which + 1) * width)
                out[:, 2 * which * width : (2 * which + 1) * width] = early[:, source]
                out[:, (2 * which + 1) * width : (2 * which + 2) * width] = late[:, source]


def lay_out(place, pieces):
    rows, columns = pieces[0].shape
    count = len(pieces) // 2
    return pl.pallas_call(
        lay_kernel,
        grid_spec=pltpu.PrefetchScalarGridSpec(
            num_scalar_prefetch=1,
            grid=(count,),
            in_specs=[pl.BlockSpec((rows, columns), lambda t, place: (0, 0))] * len(pieces),
            out_specs=pl.BlockSpec((rows, 2 * columns), lambda t, place: (0, place[1 + t])),
        ),
        out_shape=jax.ShapeDtypeStruct((rows, count * 2 * columns), pieces[0].dtype),
        compiler_params=pltpu.CompilerParams(vmem_limit_bytes=KERNEL_BYTES),
        cost_estimate=pl.CostEstimate(flops=0, bytes_accessed=4_000_000, transcendentals=0),
        name="lay_out",
    )(place, *pieces)


def piece_kernel(place, kept, crossed, out):
    width = kept.shape[1]

    @pl.when(place[0] == 0)
    def _():
        out[:, :width] = kept[...]
        out[:, width:] = crossed[...]

    @pl.when(place[0] != 0)
    def _():
        out[:, :width] = crossed[...]
        out[:, width:] = kept[...]


def join_cores(place, kept, crossed):
    rows, columns = kept.shape
    return pl.pallas_call(
        piece_kernel,
        grid_spec=pltpu.PrefetchScalarGridSpec(
            num_scalar_prefetch=1,
            grid=(1,),
            in_specs=[pl.BlockSpec((rows, columns), lambda i, place: (0, 0))] * 2,
            out_specs=pl.BlockSpec((rows, 2 * columns), lambda i, place: (0, 0)),
        ),
        out_shape=jax.ShapeDtypeStruct((rows, 2 * columns), kept.dtype),
        compiler_params=pltpu.CompilerParams(vmem_limit_bytes=KERNEL_BYTES),
        cost_estimate=pl.CostEstimate(flops=0, bytes_accessed=500_000, transcendentals=0),
        name="join_cores",
    )(place, kept, crossed)


def halving_order(count):
    bits = count.bit_length() - 1
    partners = []
    for place in range(count):
        partner = place & 1
        for bit in range(1, bits):
            partner |= ((place >> (bits - bit)) & 1) << bit
        partners.append(partner)
    return partners


def channel_order(ctx, lat_block):
    channel = lax.broadcasted_iota(jnp.int32, (LAT, LAT), 0)
    place = lax.broadcasted_iota(jnp.int32, (LAT, LAT), 1)
    count = LAT // lat_block
    bits = count.bit_length() - 1
    block = place // lat_block
    partner = block & 1
    for bit in range(1, bits):
        partner |= ((block >> (bits - bit)) & 1) << bit
    return channel == (ctx ^ partner) * lat_block + place % lat_block


def block_sources(place, offered, per_block, span):
    ctx = place[place.shape[0] - 1]
    sources = []
    for side in range(2):
        group = ctx ^ side
        for at in range(per_block + len(partner_offsets)):
            matching = at - per_block
            offset = partner_offsets[matching] if matching >= 0 else 0
            source = group - offset
            usable = source >= 0
            sender = jnp.maximum(source, 0)
            inner = offered[sender, matching] if matching >= 0 else at
            start = jnp.where(usable, ((ctx >> 1) - (sender >> 1)) * span + inner * BLOCK, 0)
            block_id = jnp.where(usable, sender * per_block + inner, -2)
            sources.append(((offset + side) % 2, start, usable, block_id))
    return sources


def collect_kernel(place, offered, own, sib, cand, cand_t, rope_keys, bias, *, lat_block):
    ctx = place[place.shape[0] - 1]
    span = own.shape[0] // 3
    per_block = (span - 16) // BLOCK
    pieces = []
    key_at = lax.broadcasted_iota(jnp.int32, (BLOCK, 2 * BLOCK), 0)
    query = lax.broadcasted_iota(jnp.int32, (BLOCK, 2 * BLOCK), 1)
    causal = jnp.where(key_at <= query % BLOCK, 1.0, 0.0)
    sources = block_sources(place, offered, per_block, span)
    for block, (other, start, usable, block_id) in enumerate(sources):
        rows_ref = sib if other else own
        rows = rows_ref[pl.ds(pl.multiple_of(start, 16), BLOCK), :]
        pieces.append(jnp.where(usable, rows, jnp.zeros_like(rows)))
        side = block // (len(sources) // 2)
        lists = (sib if side else own)[span - 16 : span, :][:1].astype(jnp.int32)
        open_for = []
        for at in range(per_block):
            picks = [lists[:, at * TOPK + k : at * TOPK + k + 1] for k in range(TOPK)]
            picked = functools.reduce(
                jnp.maximum, [jnp.where(pick == block_id, 1.0, 0.0) for pick in picks]
            )
            same = jnp.where(block_id == (ctx ^ side) * per_block + at, 1.0, 0.0)
            open_for.append(jnp.maximum(picked, same * causal))
        allowed = jnp.where(query < BLOCK, open_for[0], open_for[1])
        bias[block * BLOCK : (block + 1) * BLOCK, :] = jnp.where(allowed > 0.5, 0.0, HIDDEN)
    both = jnp.concatenate(pieces, axis=0)
    order = channel_order(ctx, lat_block).astype(jnp.bfloat16)
    latent = both[:, :LAT]
    cand[...] = dot(latent, order, 1, 0).astype(jnp.bfloat16)
    cand_t[...] = dot(order, latent, 0, 1).astype(jnp.bfloat16)
    twice = lax.broadcasted_iota(jnp.int32, (ROPE, 2 * ROPE), 0)
    twice = twice == lax.broadcasted_iota(jnp.int32, (ROPE, 2 * ROPE), 1) % ROPE
    rope_keys[...] = dot(both[:, LAT:], twice.astype(jnp.bfloat16), 1, 0).astype(jnp.bfloat16)


def collect(place, offered, own, sib, rows, lat_block):
    bf16 = jnp.bfloat16
    shapes = [((rows, LAT), bf16), ((LAT, rows), bf16), ((rows, 2 * ROPE), bf16)]
    shapes.append(((rows, 2 * BLOCK), jnp.float32))
    whole = lambda shape: pl.BlockSpec(shape, lambda i, place, offered: (0, 0))
    return pl.pallas_call(
        functools.partial(collect_kernel, lat_block=lat_block),
        grid_spec=pltpu.PrefetchScalarGridSpec(
            num_scalar_prefetch=2,
            grid=(1,),
            in_specs=[whole(own.shape), whole(sib.shape)],
            out_specs=[whole(shape) for shape, _ in shapes],
        ),
        out_shape=[jax.ShapeDtypeStruct(shape, dtype) for shape, dtype in shapes],
        compiler_params=pltpu.CompilerParams(vmem_limit_bytes=KERNEL_BYTES),
        cost_estimate=pl.CostEstimate(
            flops=250_000_000, bytes_accessed=3_000_000, transcendentals=0
        ),
        name="collect",
    )(place, offered, own, sib)


def spread_kernel(place, offered, *refs, lat_block):
    *sums, own, sib = refs
    count = len(sums) // 2
    latent, rope = sums[0][...], sums[count][...]
    for index in range(1, count):
        latent, rope = latent + sums[index][...], rope + sums[count + index][...]
    order = channel_order(place[place.shape[0] - 1], lat_block).astype(jnp.float32)
    latent = lax.dot_general(
        latent,
        order,
        (((1,), (1,)), ((), ())),
        precision=lax.Precision.HIGHEST,
        preferred_element_type=jnp.float32,
    )
    rows = jnp.concatenate([latent, rope[:, :ROPE] + rope[:, ROPE:]], axis=1)
    own[...] = jnp.zeros_like(own)
    sib[...] = jnp.zeros_like(sib)
    span = own.shape[0] // 3
    sources = block_sources(place, offered, (span - 16) // BLOCK, span)
    for block, (other, start, _, _) in enumerate(sources):
        here = pl.ds(pl.multiple_of(start, 16), BLOCK)
        target = sib if other else own
        target[here, :] += rows[block * BLOCK : (block + 1) * BLOCK]


def spread(place, offered, latents, ropes, rows, lat_block):
    shape = (rows, LAT + ROPE)
    sums = [*latents, *ropes]
    whole = lambda shape: pl.BlockSpec(shape, lambda i, place, offered: (0, 0))
    return pl.pallas_call(
        functools.partial(spread_kernel, lat_block=lat_block),
        grid_spec=pltpu.PrefetchScalarGridSpec(
            num_scalar_prefetch=2,
            grid=(1,),
            in_specs=[whole(array.shape) for array in sums],
            out_specs=[whole(shape)] * 2,
        ),
        out_shape=[jax.ShapeDtypeStruct(shape, jnp.float32)] * 2,
        compiler_params=pltpu.CompilerParams(vmem_limit_bytes=KERNEL_BYTES),
        cost_estimate=pl.CostEstimate(
            flops=700_000_000, bytes_accessed=6_000_000, transcendentals=0
        ),
        name="spread",
    )(place, offered, *sums)


def halve(value, axis, bit):
    half = value.shape[0] // 2
    return value[:half] + exchange(value[half:], axis, bit)


def shards(q_nope, q_rope, grad_out, log_total, kv_latent, up_weight, selected, offered):
    n_dp, n_ctx = lax.axis_size("dp"), lax.axis_size("ctx")
    dp, ctx = lax.axis_index("dp"), lax.axis_index("ctx")
    core = ctx % 2
    group_len = kv_latent.shape[1]
    per_block = group_len // BLOCK
    heads = log_total.shape[1]
    part_heads = heads // n_dp // 2
    pairs = part_heads // 2
    part_cols = part_heads * (NOPE + VDIM)
    far = n_dp - 1
    lat_block = up_weight.shape[0]

    place = jnp.stack([core] + [dp ^ t for t in range(n_dp)] + [ctx]).astype(jnp.int32)

    leaving, = weight_parts(place, up_weight, n_dp, far)
    crossed = exchange(leaving, "ctx", 1)
    crossed, place, selected, offered, q_nope, q_rope, grad_out, log_total, kv_latent = (
        lax.optimization_barrier(
            (crossed, place, selected, offered, q_nope, q_rope, grad_out, log_total, kv_latent)
        )
    )
    chip_rows = weight_parts(place, up_weight, n_dp, far, crossed)
    own = [q_nope[0], q_rope[0], grad_out[0]]
    sibling = [exchange(array, "ctx", 1) for array in own]
    offered = offered[0]
    span = group_len + 16
    lists = selected[0].reshape(1, -1).astype(jnp.bfloat16)
    lists = jnp.pad(lists, ((0, 15), (0, LAT + ROPE - lists.shape[1])))
    bundle = after(jnp.concatenate([kv_latent[0], lists], axis=0), *sibling)
    bundles = [bundle, from_behind(bundle, "ctx", 2), from_behind(bundle, "ctx", 4)]
    own_bundles = stack(bundles, (((0, 0), (1, 0), (2, 0)),), LAT + ROPE)[0]
    sib_bundles = exchange(own_bundles, "ctx", 1)
    key_len = 2 * (group_len + len(partner_offsets) * BLOCK)
    shared = collect(place, offered, own_bundles, sib_bundles, key_len, lat_block)

    partners = halving_order(n_ctx)[::2]

    def over_chips(start):
        at_step = {0: start}
        for step in range(4, n_ctx, 4):
            at_step[step] = exchange(start, "ctx", step)
        at_step[2] = exchange(start, "ctx", 2)
        for step in range(4, n_ctx, 4):
            at_step[step + 2] = exchange(after(at_step[step], at_step[2]), "ctx", 2)
        return [at_step[partner] for partner in partners], at_step[n_ctx - 4]

    def joined(pieces):
        return stack(pieces, (tuple((index, 0) for index in range(len(pieces))),), part_cols)[0]

    near_pieces, last = over_chips(chip_rows[0])
    far_pieces, _ = over_chips(after(chip_rows[1], last))
    log_total = after(log_total, last)[0]
    sibling.append(exchange(log_total, "ctx", 1))
    own.append(log_total)
    for arrays in (own, sibling):
        arrays[3] = arrays[3].reshape(heads // 2, 2, group_len)

    weights = {0: joined([after(near_pieces[0], sib_bundles, sibling[3])] + near_pieces[1:])}
    for t in range(1, far):
        weights[t] = exchange(weights[0], "dp", t)
    earlier = None
    latents, ropes = [], []
    weight_grads = {t: ([], []) for t in range(n_dp)}
    bits = [1 << b for b in range(n_dp.bit_length() - 1)]
    orders = (bits, bits[::-1])
    first_sums = [{t: [] for t in range(n_dp) if t & order[0]} for order in orders]
    half_pairs = pairs // 2
    units = [(0, 0, half_pairs)] + [(t, 0, pairs) for t in [far] + list(range(1, far - 1))]
    units += [(far - 1, 0, half_pairs), (far - 1, half_pairs, half_pairs)]
    units.append((0, half_pairs, half_pairs))
    for t, start, count in units:
        if t == far:
            weights[far] = joined([after(far_pieces[0], latents[-1])] + far_pieces[1:])
        weight = weights[t]
        if t == 0 and start:
            there = [piece for sent in first_sums for u in sent for piece in sent[u]]
            weight = after(weight, latents[-1], *there)
        if t == 1 and not start:
            weight = after(weight, *[weights[near] for near in range(2, far)])
        if t == far - 1 and start:
            weight = after(weight, latents[-1], *[sent[far][0] for sent in first_sums])
        rest = chunk_backward(
            place,
            t,
            (start, count),
            own,
            sibling,
            weight,
            shared,
            earlier,
            (n_dp, pairs),
        )
        earlier = rest[:3]
        for side, sent in enumerate(first_sums):
            weight_grads[t][side].append(rest[3 + side])
            if t in sent:
                sent[t].append(exchange(rest[3 + side], "dp", orders[side][0]))
        latents.append(rest[5])
        ropes.append(rest[6])

    half_cols = part_cols // 2

    def columns(pieces, half):
        if len(pieces) == 2:
            return pieces[half]
        return pieces[0][:, half * half_cols : (half + 1) * half_cols]

    def total(addends, half):
        return functools.reduce(
            lambda left, right: left + right, [columns(pieces, half) for pieces in addends]
        )

    sums = []
    last_sums = first_sums[1][far - 1]
    for side, order in enumerate(orders):
        addends = {t: [weight_grads[t][side]] for t in weight_grads}
        arrived = {t ^ order[0]: pieces for t, pieces in first_sums[side].items()}
        addends = {t: addends[t] + [more] for t, more in arrived.items()}
        for bit in order[1:]:
            arrived = {}
            for t in sorted((t for t in addends if t & bit), reverse=True):
                leaving = [total(addends[t], half) for half in range(2)]
                if side == 0:
                    behind = (first_sums[0][order[0]][0], last_sums[0])
                else:
                    behind = [weight_grads[far - 1][side][0]] * 2
                leaving = [after(half, there) for half, there in zip(leaving, behind)]
                arrived[t ^ bit] = [exchange(half, "dp", bit) for half in leaving]
            addends = {t: addends[t] + [more] for t, more in arrived.items()}
        sums.append(addends[0])

    q_full, rope_full, sib_grads = earlier
    received = exchange(sib_grads, "ctx", 1)
    grad_nope, grad_rope = place_columns(place, received, q_full, rope_full, n_dp)

    own_grads, sib_grads = spread(place, offered, latents, ropes, 3 * span, lat_block)
    swapped = exchange(sib_grads, "ctx", 1)
    grad_rows = own_grads + swapped
    by_chip = [grad_rows[at * span : at * span + group_len] for at in range(3)]
    grad_rows = by_chip[0]
    for chips in (1, 2):
        grad_rows = grad_rows + from_behind(by_chip[chips], "ctx", -2 * chips)

    ctx_bits = [1 << b for b in range(1, n_ctx.bit_length() - 1)]
    finished, arrived = [], None
    for half in range(2):
        if half:
            sums = [[[after(piece, arrived) for piece in pieces] for pieces in side] for side in sums]
        first, second = [total(side, half) for side in sums]
        there = (sums[0][-1][half], latents[-1]) if half == 0 else (sums[0][-1][half],)
        arrived = exchange(after(second, *there), "ctx", ctx_bits[0])
        rows = first + arrived
        if half:
            rows = after(rows, received, grad_rows)
        for bit in ctx_bits[1:]:
            rows = halve(rows, "ctx", bit)
        piece = join_cores(place, rows[:lat_block], exchange(rows[lat_block:], "ctx", 1))
        finished.append([piece] + [exchange(piece, "dp", t) for t in range(1, n_dp)])
    finished[0][0] = after(finished[0][0], grad_rows, grad_nope)
    grad_weight = lay_out(place, [piece for both in zip(*finished) for piece in both])
    return (grad_nope[None], grad_rope[None], grad_rows[None], grad_weight)


def solution(mesh):
    in_specs = (
        P("dp", "ctx", None),
        P("dp", "ctx", None),
        P("dp", "ctx", None),
        P("dp", None, "ctx"),
        P("dp", "ctx", None),
        P("ctx", None),
        P("dp", "ctx", None),
        P("dp", None, None),
    )
    out_specs = (P("dp", "ctx", None), P("dp", "ctx", None), P("dp", "ctx", None), P("ctx", None))
    return jax.shard_map(shards, mesh=mesh, in_specs=in_specs, out_specs=out_specs, check_vma=False)
```

```python
import functools

import jax
import jax.numpy as jnp
from jax import lax
from jax.experimental import pallas as pl
from jax.experimental.pallas import tpu as pltpu
from jax.sharding import PartitionSpec as P

LAT = 256
ROPE = 64
NOPE = 128
VDIM = 128
BLOCK = 64
TOPK = 3

partner_offsets = (1, 2, 3, 4)
HIDDEN = -1e30
KERNEL_BYTES = 12 * 1024 * 1024
INPUT_BYTES = 56 * 1024 * 1024


def from_behind(value, axis, steps):
    count = lax.axis_size(axis)
    initial, last = (max(0, -steps), min(count, count - steps))
    return lax.ppermute(value, axis, [(source, source + steps) for source in range(initial, last)])


def exchange(value, axis, bits):
    count = lax.axis_size(axis)
    return lax.ppermute(value, axis, [(source, source ^ bits) for source in range(count)])


def after(value, *earlier):
    return lax.optimization_barrier((value, *earlier))[0]


def dot(left, right, left_dim, right_dim):
    return lax.dot_general(
        left,
        right,
        (((left_dim,), (right_dim,)), ((), ())),
        preferred_element_type=jnp.float32,
    )


def heads_kernel(
    place,
    q_own, rope_own, out_own, tot_own,
    q_sib, rope_sib, out_sib, tot_sib,
    weight, cand, cand_t, rope_keys, bias,
    *rest,
    earlier,
):
    gq_own, gr_own, sib_grads, *weight_grads, lat_sum, rope_sum = rest[earlier:]
    scale = 1.0 / jnp.sqrt(jnp.float32(NOPE + ROPE))
    rows = cand.shape[0] // 2
    half = weight_grads[0].shape[0]
    sib_q, sib_rope = sib_grads.at[:, : 2 * NOPE], sib_grads.at[:, 2 * NOPE :]
    lane_half = lax.broadcasted_iota(jnp.int32, (rows, 2 * ROPE), 1) // ROPE

    @pl.when(pl.program_id(0) == 0)
    def _():
        lat_sum[...] = jnp.zeros_like(lat_sum)
        rope_sum[...] = jnp.zeros_like(rope_sum)

    groups = (
        (q_own, rope_own, out_own, tot_own, gq_own, gr_own),
        (q_sib, rope_sib, out_sib, tot_sib, sib_q, sib_rope),
    )
    rope_grads = [None, None]
    for head in range(2):
        columns = pl.ds(head * (NOPE + VDIM), NOPE + VDIM)
        head_weight = weight[:, columns]
        expanded = dot(cand[...], head_weight, 1, 0).astype(jnp.bfloat16)
        both_grads = []
        for side, (q_ref, rope_ref, out_ref, tot_ref, gq_ref, gr_ref) in enumerate(groups):
            own_rows = slice(side * rows, (side + 1) * rows)
            here = pl.ds(head * NOPE, NOPE)
            rope_part = jnp.where(
                lane_half == head, rope_keys[own_rows, :], jnp.zeros((), jnp.bfloat16)
            )
            keys = jnp.concatenate([expanded[own_rows, :NOPE], rope_part], axis=1)
            values = expanded[own_rows, NOPE:]
            queries = jnp.concatenate([q_ref[:, here], rope_ref[...]], axis=1)
            out_grads = out_ref[:, here]
            scores = dot(keys, queries, 1, 1) * scale
            probs = jnp.exp(scores - tot_ref[0, head : head + 1, :] + bias[own_rows, :])
            prob_grads = dot(values, out_grads, 1, 1)
            row_dot = jnp.sum(probs * prob_grads, axis=0, keepdims=True)
            score_grads = (probs * (prob_grads - row_dot)).astype(jnp.bfloat16)
            query_grad = dot(score_grads, keys, 0, 0) * scale
            gq_ref[:, here] = query_grad[:, :NOPE].astype(jnp.bfloat16)
            if head == 0:
                rope_grads[side] = query_grad[:, NOPE:]
            else:
                gr_ref[...] = (rope_grads[side] + query_grad[:, NOPE:]).astype(jnp.bfloat16)
            key_grad = dot(score_grads, queries, 1, 0) * scale
            value_grad = dot(probs.astype(jnp.bfloat16), out_grads, 1, 0)
            rope_sum[own_rows, :] += jnp.where(lane_half == head, key_grad[:, NOPE:], 0.0)
            both_grads.append(
                jnp.concatenate([key_grad[:, :NOPE], value_grad], axis=1).astype(jnp.bfloat16)
            )
        key_grads = jnp.concatenate(both_grads, axis=0)
        lat_sum[...] += dot(key_grads, head_weight, 1, 1)
        weight_grad = dot(cand_t[...], key_grads, 1, 0)
        weight_grads[0][:, columns] = weight_grad[:half]
        weight_grads[1][:, columns] = weight_grad[half:]


def chunk_backward(place, t, unit, own, sibling, weight, shared, earlier, sizes):
    q_own, rope_own, out_own, tot_own = own
    cand, cand_t, rope_keys, bias = shared
    tokens = q_own.shape[0]
    chunks, pairs = sizes
    wide, narrow = 2 * NOPE, 2 * ROPE
    first, count = unit
    mine = lambda p, place: (place[1 + t] * 2 + place[0]) * pairs + first + p
    theirs = lambda p, place: place[1 + t] * pairs + first + p
    whole = lambda array: pl.BlockSpec(array.shape, lambda p, place: (0, 0))
    in_specs = [
        pl.BlockSpec((tokens, wide), lambda p, place: (0, mine(p, place))),
        pl.BlockSpec((tokens, narrow), lambda p, place: (0, mine(p, place))),
        pl.BlockSpec((tokens, wide), lambda p, place: (0, mine(p, place))),
        pl.BlockSpec((1, 2, tokens), lambda p, place: (mine(p, place), 0, 0)),
    ] * 2 + [
        pl.BlockSpec((LAT, 2 * (NOPE + VDIM)), lambda p, place: (0, first + p)),
        whole(cand),
        whole(cand_t),
        whole(rope_keys),
        whole(bias),
    ]
    operands = [*own, *sibling, weight, cand, cand_t, rope_keys, bias]
    aliases = {}
    if earlier is not None:
        for index, array in enumerate(earlier):
            aliases[1 + len(operands)] = index
            in_specs.append(pl.BlockSpec(memory_space=pl.ANY))
            operands.append(array)
    columns = 2 * (NOPE + VDIM) * count
    bf16, f32 = jnp.bfloat16, jnp.float32
    out_shape = [
        jax.ShapeDtypeStruct(q_own.shape, bf16),
        jax.ShapeDtypeStruct(rope_own.shape, bf16),
        jax.ShapeDtypeStruct((tokens, chunks * pairs * (wide + narrow)), bf16),
        *[jax.ShapeDtypeStruct((LAT // 2, columns), f32)] * 2,
        jax.ShapeDtypeStruct((cand.shape[0], LAT), f32),
        jax.ShapeDtypeStruct((cand.shape[0], narrow), f32),
    ]
    out_specs = [
        pl.BlockSpec((tokens, wide), lambda p, place: (0, mine(p, place))),
        pl.BlockSpec((tokens, narrow), lambda p, place: (0, mine(p, place))),
        pl.BlockSpec((tokens, wide + narrow), lambda p, place: (0, theirs(p, place))),
        *[pl.BlockSpec((LAT // 2, 2 * (NOPE + VDIM)), lambda p, place: (0, p))] * 2,
        pl.BlockSpec((cand.shape[0], LAT), lambda p, place: (0, 0)),
        pl.BlockSpec((cand.shape[0], narrow), lambda p, place: (0, 0)),
    ]
    return pl.pallas_call(
        functools.partial(heads_kernel, earlier=len(aliases)),
        grid_spec=pltpu.PrefetchScalarGridSpec(
            num_scalar_prefetch=1, grid=(count,), in_specs=in_specs, out_specs=out_specs
        ),
        out_shape=out_shape,
        input_output_aliases=aliases,
        compiler_params=pltpu.CompilerParams(vmem_limit_bytes=KERNEL_BYTES),
        cost_estimate=pl.CostEstimate(
            flops=count * 100_000_000, bytes_accessed=count * 300_000, transcendentals=0
        ),
        name="heads_backward",
    )(place, *operands)


def place_kernel(place, received, q_in, rope_in, q_out, rope_out):
    wide, narrow = 2 * NOPE, 2 * ROPE
    for pair in range(q_out.shape[1] // wide):
        start = pair * (wide + narrow)
        q_out[:, pair * wide : (pair + 1) * wide] = received[:, start : start + wide]
        rope_out[:, pair * narrow : (pair + 1) * narrow] = received[
            :, start + wide : start + wide + narrow
        ]


def place_columns(place, received, q_full, rope_full, chunks):
    tokens = q_full.shape[0]
    q_cols, rope_cols = q_full.shape[1] // chunks // 2, rope_full.shape[1] // chunks // 2
    put = lambda c, place: (0, c * 2 + 1 - place[0])
    return pl.pallas_call(
        place_kernel,
        grid_spec=pltpu.PrefetchScalarGridSpec(
            num_scalar_prefetch=1,
            grid=(chunks,),
            in_specs=[
                pl.BlockSpec((tokens, q_cols + rope_cols), lambda c, place: (0, c)),
                pl.BlockSpec(memory_space=pl.ANY),
                pl.BlockSpec(memory_space=pl.ANY),
            ],
            out_specs=[
                pl.BlockSpec((tokens, q_cols), put),
                pl.BlockSpec((tokens, rope_cols), put),
            ],
        ),
        out_shape=[
            jax.ShapeDtypeStruct(q_full.shape, q_full.dtype),
            jax.ShapeDtypeStruct(rope_full.shape, rope_full.dtype),
        ],
        input_output_aliases={2: 0, 3: 1},
        compiler_params=pltpu.CompilerParams(vmem_limit_bytes=KERNEL_BYTES),
        cost_estimate=pl.CostEstimate(flops=0, bytes_accessed=4_000_000, transcendentals=0),
        name="place_columns",
    )(place, received, q_full, rope_full)


def stack_kernel(*refs, arrangement):
    outs = refs[len(refs) - len(arrangement) :]
    for out, sources in zip(outs, arrangement):
        row = 0
        for index, block in sources:
            piece = refs[index]
            columns = slice(block * out.shape[1], (block + 1) * out.shape[1])
            out[row : row + piece.shape[0], :] = piece[:, columns]
            row += piece.shape[0]


def stack(inputs, arrangement, columns):
    whole = lambda shape: pl.BlockSpec(shape, lambda: (0, 0))
    shapes = [(sum(inputs[i].shape[0] for i, _ in sources), columns) for sources in arrangement]
    return pl.pallas_call(
        functools.partial(stack_kernel, arrangement=arrangement),
        in_specs=[whole(array.shape) for array in inputs],
        out_specs=[whole(shape) for shape in shapes],
        out_shape=[jax.ShapeDtypeStruct(shape, inputs[0].dtype) for shape in shapes],
        compiler_params=pltpu.CompilerParams(vmem_limit_bytes=KERNEL_BYTES),
        cost_estimate=pl.CostEstimate(flops=0, bytes_accessed=2_000_000, transcendentals=0),
        name="stack",
    )(*inputs)


def leave_kernel(place, near, distant, leaving):
    width = near.shape[1]
    leaving[:, :width] = near[...]
    leaving[:, width:] = distant[...]


def join_rows_kernel(place, near, distant, crossed, near_rows, distant_rows):
    rows, width = near.shape
    for at, (own, out) in enumerate(((near, near_rows), (distant, distant_rows))):
        out[:rows, :] = own[...]
        out[rows:, :] = crossed[:, at * width : (at + 1) * width]


def weight_parts(place, up_weight, chunks, far, crossed=None):
    rows = up_weight.shape[0]
    width = up_weight.shape[1] // chunks // 2
    joins = crossed is not None

    def column_block(t):
        def block(i, place):
            return (0, place[1 + t] * 2 + (place[0] if joins else 1 - place[0]))

        return pl.BlockSpec((rows, width), block)

    whole = lambda shape: pl.BlockSpec(shape, lambda i, place: (0, 0))
    shapes = [(2 * rows, width)] * 2 if joins else [(rows, 2 * width)]
    return pl.pallas_call(
        join_rows_kernel if joins else leave_kernel,
        grid_spec=pltpu.PrefetchScalarGridSpec(
            num_scalar_prefetch=1,
            grid=(1,),
            in_specs=[column_block(t) for t in (0, far)] + [whole((rows, 2 * width))] * joins,
            out_specs=[whole(shape) for shape in shapes],
        ),
        out_shape=[jax.ShapeDtypeStruct(shape, up_weight.dtype) for shape in shapes],
        compiler_params=pltpu.CompilerParams(vmem_limit_bytes=INPUT_BYTES),
        cost_estimate=pl.CostEstimate(flops=0, bytes_accessed=1_000_000, transcendentals=0),
        name="weight_parts",
    )(place, up_weight, up_weight, *([crossed] if joins else []))


def lay_kernel(place, *refs):
    *pieces, out = refs
    width = out.shape[1] // 4
    for step in range(len(pieces) // 2):
        early, late = pieces[2 * step], pieces[2 * step + 1]

        @pl.when(pl.program_id(0) == step)
        def _():
            for which in range(2):
                source = slice(which * width, (which + 1) * width)
                out[:, 2 * which * width : (2 * which + 1) * width] = early[:, source]
                out[:, (2 * which + 1) * width : (2 * which + 2) * width] = late[:, source]


def lay_out(place, pieces):
    rows, columns = pieces[0].shape
    count = len(pieces) // 2
    return pl.pallas_call(
        lay_kernel,
        grid_spec=pltpu.PrefetchScalarGridSpec(
            num_scalar_prefetch=1,
            grid=(count,),
            in_specs=[pl.BlockSpec((rows, columns), lambda t, place: (0, 0))] * len(pieces),
            out_specs=pl.BlockSpec((rows, 2 * columns), lambda t, place: (0, place[1 + t])),
        ),
        out_shape=jax.ShapeDtypeStruct((rows, count * 2 * columns), pieces[0].dtype),
        compiler_params=pltpu.CompilerParams(vmem_limit_bytes=KERNEL_BYTES),
        cost_estimate=pl.CostEstimate(flops=0, bytes_accessed=4_000_000, transcendentals=0),
        name="lay_out",
    )(place, *pieces)


def piece_kernel(place, kept, crossed, out):
    width = kept.shape[1]

    @pl.when(place[0] == 0)
    def _():
        out[:, :width] = kept[...]
        out[:, width:] = crossed[...]

    @pl.when(place[0] != 0)
    def _():
        out[:, :width] = crossed[...]
        out[:, width:] = kept[...]


def join_cores(place, kept, crossed):
    rows, columns = kept.shape
    return pl.pallas_call(
        piece_kernel,
        grid_spec=pltpu.PrefetchScalarGridSpec(
            num_scalar_prefetch=1,
            grid=(1,),
            in_specs=[pl.BlockSpec((rows, columns), lambda i, place: (0, 0))] * 2,
            out_specs=pl.BlockSpec((rows, 2 * columns), lambda i, place: (0, 0)),
        ),
        out_shape=jax.ShapeDtypeStruct((rows, 2 * columns), kept.dtype),
        compiler_params=pltpu.CompilerParams(vmem_limit_bytes=KERNEL_BYTES),
        cost_estimate=pl.CostEstimate(flops=0, bytes_accessed=500_000, transcendentals=0),
        name="join_cores",
    )(place, kept, crossed)


def halving_order(count):
    bits = count.bit_length() - 1
    partners = []
    for place in range(count):
        partner = place & 1
        for bit in range(1, bits):
            partner |= ((place >> (bits - bit)) & 1) << bit
        partners.append(partner)
    return partners


def channel_order(ctx, lat_block):
    channel = lax.broadcasted_iota(jnp.int32, (LAT, LAT), 0)
    place = lax.broadcasted_iota(jnp.int32, (LAT, LAT), 1)
    count = LAT // lat_block
    bits = count.bit_length() - 1
    block = place // lat_block
    partner = block & 1
    for bit in range(1, bits):
        partner |= ((block >> (bits - bit)) & 1) << bit
    return channel == (ctx ^ partner) * lat_block + place % lat_block


def block_sources(place, offered, per_block, span):
    ctx = place[place.shape[0] - 1]
    sources = []
    for side in range(2):
        group = ctx ^ side
        for at in range(per_block + len(partner_offsets)):
            matching = at - per_block
            offset = partner_offsets[matching] if matching >= 0 else 0
            source = group - offset
            usable = source >= 0
            sender = jnp.maximum(source, 0)
            inner = offered[sender, matching] if matching >= 0 else at
            start = jnp.where(usable, ((ctx >> 1) - (sender >> 1)) * span + inner * BLOCK, 0)
            block_id = jnp.where(usable, sender * per_block + inner, -2)
            sources.append(((offset + side) % 2, start, usable, block_id))
    return sources


def collect_kernel(place, offered, own, sib, cand, cand_t, rope_keys, bias, *, lat_block):
    ctx = place[place.shape[0] - 1]
    span = own.shape[0] // 3
    per_block = (span - 16) // BLOCK
    pieces = []
    key_at = lax.broadcasted_iota(jnp.int32, (BLOCK, 2 * BLOCK), 0)
    query = lax.broadcasted_iota(jnp.int32, (BLOCK, 2 * BLOCK), 1)
    causal = jnp.where(key_at <= query % BLOCK, 1.0, 0.0)
    sources = block_sources(place, offered, per_block, span)
    for block, (other, start, usable, block_id) in enumerate(sources):
        rows_ref = sib if other else own
        rows = rows_ref[pl.ds(pl.multiple_of(start, 16), BLOCK), :]
        pieces.append(jnp.where(usable, rows, jnp.zeros_like(rows)))
        side = block // (len(sources) // 2)
        lists = (sib if side else own)[span - 16 : span, :][:1].astype(jnp.int32)
        open_for = []
        for at in range(per_block):
            picks = [lists[:, at * TOPK + k : at * TOPK + k + 1] for k in range(TOPK)]
            picked = functools.reduce(
                jnp.maximum, [jnp.where(pick == block_id, 1.0, 0.0) for pick in picks]
            )
            same = jnp.where(block_id == (ctx ^ side) * per_block + at, 1.0, 0.0)
            open_for.append(jnp.maximum(picked, same * causal))
        allowed = jnp.where(query < BLOCK, open_for[0], open_for[1])
        bias[block * BLOCK : (block + 1) * BLOCK, :] = jnp.where(allowed > 0.5, 0.0, HIDDEN)
    both = jnp.concatenate(pieces, axis=0)
    order = channel_order(ctx, lat_block).astype(jnp.bfloat16)
    latent = both[:, :LAT]
    cand[...] = dot(latent, order, 1, 0).astype(jnp.bfloat16)
    cand_t[...] = dot(order, latent, 0, 1).astype(jnp.bfloat16)
    twice = lax.broadcasted_iota(jnp.int32, (ROPE, 2 * ROPE), 0)
    twice = twice == lax.broadcasted_iota(jnp.int32, (ROPE, 2 * ROPE), 1) % ROPE
    rope_keys[...] = dot(both[:, LAT:], twice.astype(jnp.bfloat16), 1, 0).astype(jnp.bfloat16)


def collect(place, offered, own, sib, rows, lat_block):
    bf16 = jnp.bfloat16
    shapes = [((rows, LAT), bf16), ((LAT, rows), bf16), ((rows, 2 * ROPE), bf16)]
    shapes.append(((rows, 2 * BLOCK), jnp.float32))
    whole = lambda shape: pl.BlockSpec(shape, lambda i, place, offered: (0, 0))
    return pl.pallas_call(
        functools.partial(collect_kernel, lat_block=lat_block),
        grid_spec=pltpu.PrefetchScalarGridSpec(
            num_scalar_prefetch=2,
            grid=(1,),
            in_specs=[whole(own.shape), whole(sib.shape)],
            out_specs=[whole(shape) for shape, _ in shapes],
        ),
        out_shape=[jax.ShapeDtypeStruct(shape, dtype) for shape, dtype in shapes],
        compiler_params=pltpu.CompilerParams(vmem_limit_bytes=KERNEL_BYTES),
        cost_estimate=pl.CostEstimate(
            flops=250_000_000, bytes_accessed=3_000_000, transcendentals=0
        ),
        name="collect",
    )(place, offered, own, sib)


def spread_kernel(place, offered, *refs, lat_block):
    *sums, own, sib = refs
    count = len(sums) // 2
    latent, rope = sums[0][...], sums[count][...]
    for index in range(1, count):
        latent, rope = latent + sums[index][...], rope + sums[count + index][...]
    order = channel_order(place[place.shape[0] - 1], lat_block).astype(jnp.float32)
    latent = lax.dot_general(
        latent,
        order,
        (((1,), (1,)), ((), ())),
        precision=lax.Precision.HIGHEST,
        preferred_element_type=jnp.float32,
    )
    rows = jnp.concatenate([latent, rope[:, :ROPE] + rope[:, ROPE:]], axis=1)
    own[...] = jnp.zeros_like(own)
    sib[...] = jnp.zeros_like(sib)
    span = own.shape[0] // 3
    sources = block_sources(place, offered, (span - 16) // BLOCK, span)
    for block, (other, start, _, _) in enumerate(sources):
        here = pl.ds(pl.multiple_of(start, 16), BLOCK)
        target = sib if other else own
        target[here, :] += rows[block * BLOCK : (block + 1) * BLOCK]


def spread(place, offered, latents, ropes, rows, lat_block):
    shape = (rows, LAT + ROPE)
    sums = [*latents, *ropes]
    whole = lambda shape: pl.BlockSpec(shape, lambda i, place, offered: (0, 0))
    return pl.pallas_call(
        functools.partial(spread_kernel, lat_block=lat_block),
        grid_spec=pltpu.PrefetchScalarGridSpec(
            num_scalar_prefetch=2,
            grid=(1,),
            in_specs=[whole(array.shape) for array in sums],
            out_specs=[whole(shape)] * 2,
        ),
        out_shape=[jax.ShapeDtypeStruct(shape, jnp.float32)] * 2,
        compiler_params=pltpu.CompilerParams(vmem_limit_bytes=KERNEL_BYTES),
        cost_estimate=pl.CostEstimate(
            flops=700_000_000, bytes_accessed=6_000_000, transcendentals=0
        ),
        name="spread",
    )(place, offered, *sums)


def halve(value, axis, bit):
    half = value.shape[0] // 2
    return value[:half] + exchange(value[half:], axis, bit)


def shards(q_nope, q_rope, grad_out, log_total, kv_latent, up_weight, selected, offered):
    n_dp, n_ctx = lax.axis_size("dp"), lax.axis_size("ctx")
    dp, ctx = lax.axis_index("dp"), lax.axis_index("ctx")
    core = ctx % 2
    group_len = kv_latent.shape[1]
    per_block = group_len // BLOCK
    heads = log_total.shape[1]
    part_heads = heads // n_dp // 2
    pairs = part_heads // 2
    part_cols = part_heads * (NOPE + VDIM)
    far = n_dp - 1
    lat_block = up_weight.shape[0]

    place = jnp.stack([core] + [dp ^ t for t in range(n_dp)] + [ctx]).astype(jnp.int32)

    leaving, = weight_parts(place, up_weight, n_dp, far)
    crossed = exchange(leaving, "ctx", 1)
    crossed, place, selected, offered, q_nope, q_rope, grad_out, log_total, kv_latent = (
        lax.optimization_barrier(
            (crossed, place, selected, offered, q_nope, q_rope, grad_out, log_total, kv_latent)
        )
    )
    chip_rows = weight_parts(place, up_weight, n_dp, far, crossed)
    own = [q_nope[0], q_rope[0], grad_out[0]]
    sibling = [exchange(array, "ctx", 1) for array in own]
    offered = offered[0]
    span = group_len + 16
    lists = selected[0].reshape(1, -1).astype(jnp.bfloat16)
    lists = jnp.pad(lists, ((0, 15), (0, LAT + ROPE - lists.shape[1])))
    bundle = after(jnp.concatenate([kv_latent[0], lists], axis=0), *sibling)
    bundles = [bundle, from_behind(bundle, "ctx", 2), from_behind(bundle, "ctx", 4)]
    own_bundles = stack(bundles, (((0, 0), (1, 0), (2, 0)),), LAT + ROPE)[0]
    sib_bundles = exchange(own_bundles, "ctx", 1)
    key_len = 2 * (group_len + len(partner_offsets) * BLOCK)
    shared = collect(place, offered, own_bundles, sib_bundles, key_len, lat_block)

    partners = halving_order(n_ctx)[::2]

    def over_chips(start):
        at_step = {0: start}
        for step in range(4, n_ctx, 4):
            at_step[step] = exchange(start, "ctx", step)
        at_step[2] = exchange(start, "ctx", 2)
        for step in range(4, n_ctx, 4):
            at_step[step + 2] = exchange(after(at_step[step], at_step[2]), "ctx", 2)
        return [at_step[partner] for partner in partners], at_step[n_ctx - 2]

    def joined(pieces):
        return stack(pieces, (tuple((index, 0) for index in range(len(pieces))),), part_cols)[0]

    near_pieces, last = over_chips(chip_rows[0])
    far_pieces, _ = over_chips(after(chip_rows[1], last))
    log_total = after(log_total, last)[0]
    sibling.append(exchange(log_total, "ctx", 1))
    own.append(log_total)
    for arrays in (own, sibling):
        arrays[3] = arrays[3].reshape(heads // 2, 2, group_len)

    weights = {0: joined([after(near_pieces[0], shared[0], sibling[3])] + near_pieces[1:])}
    for t in range(1, far):
        weights[t] = exchange(weights[0], "dp", t)
    earlier = None
    latents, ropes = [], []
    weight_grads = {t: ([], []) for t in range(n_dp)}
    bits = [1 << b for b in range(n_dp.bit_length() - 1)]
    orders = (bits, bits[::-1])
    first_sums = [{t: [] for t in range(n_dp) if t & order[0]} for order in orders]
    half_pairs = pairs // 2
    units = [(t, 0, pairs) for t in [0, far] + list(range(1, far - 1))]
    units += [(far - 1, 0, half_pairs), (far - 1, half_pairs, half_pairs)]
    for t, start, count in units:
        if t == far:
            weights[far] = joined([after(far_pieces[0], latents[-1])] + far_pieces[1:])
        weight = weights[t]
        if t == 1 and not start:
            weight = after(weight, *[weights[near] for near in range(2, far)])
        if t == far - 1 and start:
            weight = after(weight, latents[-1], *[sent[far][0] for sent in first_sums])
        rest = chunk_backward(
            place,
            t,
            (start, count),
            own,
            sibling,
            weight,
            shared,
            earlier,
            (n_dp, pairs),
        )
        earlier = rest[:3]
        for side, sent in enumerate(first_sums):
            weight_grads[t][side].append(rest[3 + side])
            if t in sent:
                sent[t].append(exchange(rest[3 + side], "dp", orders[side][0]))
        latents.append(rest[5])
        ropes.append(rest[6])

    half_cols = part_cols // 2

    def columns(pieces, half):
        if len(pieces) == 2:
            return pieces[half]
        return pieces[0][:, half * half_cols : (half + 1) * half_cols]

    def total(addends, half):
        return functools.reduce(
            lambda left, right: left + right, [columns(pieces, half) for pieces in addends]
        )

    sums = []
    last_sums = first_sums[1][far - 1]
    for side, order in enumerate(orders):
        addends = {t: [weight_grads[t][side]] for t in weight_grads}
        arrived = {t ^ order[0]: pieces for t, pieces in first_sums[side].items()}
        addends = {t: addends[t] + [more] for t, more in arrived.items()}
        for bit in order[1:]:
            arrived = {}
            for t in sorted((t for t in addends if t & bit), reverse=True):
                leaving = [total(addends[t], half) for half in range(2)]
                if side == 0:
                    behind = [(first_sums[0][order[0]][0], last_sums[-1])] * 2
                else:
                    behind = [(weight_grads[far - 1][side][0],)] * 2
                leaving = [after(half, *there) for half, there in zip(leaving, behind)]
                arrived[t ^ bit] = [exchange(half, "dp", bit) for half in leaving]
            addends = {t: addends[t] + [more] for t, more in arrived.items()}
        sums.append(addends[0])

    q_full, rope_full, sib_grads = earlier
    received = exchange(sib_grads, "ctx", 1)
    grad_nope, grad_rope = place_columns(place, received, q_full, rope_full, n_dp)

    first_come = [sent[u][0] for sent in first_sums for u in sent if u != far]
    latents[-1] = after(latents[-1], *first_come)
    own_grads, sib_grads = spread(place, offered, latents, ropes, 3 * span, lat_block)
    swapped = exchange(sib_grads, "ctx", 1)
    grad_rows = own_grads + swapped
    by_chip = [grad_rows[at * span : at * span + group_len] for at in range(3)]
    grad_rows = by_chip[0]
    for chips in (1, 2):
        grad_rows = grad_rows + from_behind(by_chip[chips], "ctx", -2 * chips)

    ctx_bits = [1 << b for b in range(1, n_ctx.bit_length() - 1)]
    finished, arrived = [], None
    for half in range(2):
        if half:
            sums = [[[after(piece, arrived) for piece in pieces] for pieces in side] for side in sums]
        first, second = [total(side, half) for side in sums]
        there = (sums[0][-1][half], received if half else grad_rows)
        arrived = exchange(after(second, *there), "ctx", ctx_bits[0])
        rows = first + arrived
        for bit in ctx_bits[1:]:
            rows = halve(rows, "ctx", bit)
        kept, crossed = rows[:lat_block], exchange(rows[lat_block:], "ctx", 1)
        if half:
            kept = after(kept, *finished[0][1:])
        piece = join_cores(place, kept, crossed)
        finished.append([piece] + [exchange(piece, "dp", t) for t in range(1, n_dp)])
    finished[0][0] = after(finished[0][0], grad_rows, grad_nope)
    grad_weight = lay_out(place, [piece for both in zip(*finished) for piece in both])
    return (grad_nope[None], grad_rope[None], grad_rows[None], grad_weight)


def solution(mesh):
    in_specs = (
        P("dp", "ctx", None),
        P("dp", "ctx", None),
        P("dp", "ctx", None),
        P("dp", None, "ctx"),
        P("dp", "ctx", None),
        P("ctx", None),
        P("dp", "ctx", None),
        P("dp", None, None),
    )
    out_specs = (P("dp", "ctx", None), P("dp", "ctx", None), P("dp", "ctx", None), P("ctx", None))
    return jax.shard_map(shards, mesh=mesh, in_specs=in_specs, out_specs=out_specs, check_vma=False)
```

```python
import functools

import jax
import jax.numpy as jnp
from jax import lax
from jax.experimental import pallas as pl
from jax.experimental.pallas import tpu as pltpu
from jax.sharding import PartitionSpec as P

LAT = 256
ROPE = 64
NOPE = 128
VDIM = 128
BLOCK = 64
TOPK = 3

partner_offsets = (1, 2, 3, 4)
HIDDEN = -1e30
KERNEL_BYTES = 12 * 1024 * 1024
INPUT_BYTES = 56 * 1024 * 1024


def from_behind(value, axis, steps):
    count = lax.axis_size(axis)
    initial, last = (max(0, -steps), min(count, count - steps))
    return lax.ppermute(value, axis, [(source, source + steps) for source in range(initial, last)])


def exchange(value, axis, bits):
    count = lax.axis_size(axis)
    return lax.ppermute(value, axis, [(source, source ^ bits) for source in range(count)])


def after(value, *earlier):
    return lax.optimization_barrier((value, *earlier))[0]


def dot(left, right, left_dim, right_dim):
    return lax.dot_general(
        left,
        right,
        (((left_dim,), (right_dim,)), ((), ())),
        preferred_element_type=jnp.float32,
    )


def heads_kernel(
    place,
    q_own, rope_own, out_own, tot_own,
    q_sib, rope_sib, out_sib, tot_sib,
    weight, cand, cand_t, rope_keys, bias,
    *rest,
    earlier,
):
    gq_own, gr_own, sib_grads, *weight_grads, lat_sum, rope_sum = rest[earlier:]
    scale = 1.0 / jnp.sqrt(jnp.float32(NOPE + ROPE))
    rows = cand.shape[0] // 2
    half = weight_grads[0].shape[0]
    sib_q, sib_rope = sib_grads.at[:, : 2 * NOPE], sib_grads.at[:, 2 * NOPE :]
    lane_half = lax.broadcasted_iota(jnp.int32, (rows, 2 * ROPE), 1) // ROPE

    @pl.when(pl.program_id(0) == 0)
    def _():
        lat_sum[...] = jnp.zeros_like(lat_sum)
        rope_sum[...] = jnp.zeros_like(rope_sum)

    groups = (
        (q_own, rope_own, out_own, tot_own, gq_own, gr_own),
        (q_sib, rope_sib, out_sib, tot_sib, sib_q, sib_rope),
    )
    rope_grads = [None, None]
    for head in range(2):
        columns = pl.ds(head * (NOPE + VDIM), NOPE + VDIM)
        head_weight = weight[:, columns]
        expanded = dot(cand[...], head_weight, 1, 0).astype(jnp.bfloat16)
        both_grads = []
        for side, (q_ref, rope_ref, out_ref, tot_ref, gq_ref, gr_ref) in enumerate(groups):
            own_rows = slice(side * rows, (side + 1) * rows)
            here = pl.ds(head * NOPE, NOPE)
            rope_part = jnp.where(
                lane_half == head, rope_keys[own_rows, :], jnp.zeros((), jnp.bfloat16)
            )
            keys = jnp.concatenate([expanded[own_rows, :NOPE], rope_part], axis=1)
            values = expanded[own_rows, NOPE:]
            queries = jnp.concatenate([q_ref[:, here], rope_ref[...]], axis=1)
            out_grads = out_ref[:, here]
            scores = dot(keys, queries, 1, 1) * scale
            probs = jnp.exp(scores - tot_ref[0, head : head + 1, :] + bias[own_rows, :])
            prob_grads = dot(values, out_grads, 1, 1)
            row_dot = jnp.sum(probs * prob_grads, axis=0, keepdims=True)
            score_grads = (probs * (prob_grads - row_dot)).astype(jnp.bfloat16)
            query_grad = dot(score_grads, keys, 0, 0) * scale
            gq_ref[:, here] = query_grad[:, :NOPE].astype(jnp.bfloat16)
            if head == 0:
                rope_grads[side] = query_grad[:, NOPE:]
            else:
                gr_ref[...] = (rope_grads[side] + query_grad[:, NOPE:]).astype(jnp.bfloat16)
            key_grad = dot(score_grads, queries, 1, 0) * scale
            value_grad = dot(probs.astype(jnp.bfloat16), out_grads, 1, 0)
            rope_sum[own_rows, :] += jnp.where(lane_half == head, key_grad[:, NOPE:], 0.0)
            both_grads.append(
                jnp.concatenate([key_grad[:, :NOPE], value_grad], axis=1).astype(jnp.bfloat16)
            )
        key_grads = jnp.concatenate(both_grads, axis=0)
        lat_sum[...] += dot(key_grads, head_weight, 1, 1)
        weight_grad = dot(cand_t[...], key_grads, 1, 0)
        weight_grads[0][:, columns] = weight_grad[:half]
        weight_grads[1][:, columns] = weight_grad[half:]


def chunk_backward(place, t, unit, own, sibling, weight, shared, earlier, sizes):
    q_own, rope_own, out_own, tot_own = own
    cand, cand_t, rope_keys, bias = shared
    tokens = q_own.shape[0]
    chunks, pairs = sizes
    wide, narrow = 2 * NOPE, 2 * ROPE
    first, count = unit
    mine = lambda p, place: (place[1 + t] * 2 + place[0]) * pairs + first + p
    theirs = lambda p, place: place[1 + t] * pairs + first + p
    whole = lambda array: pl.BlockSpec(array.shape, lambda p, place: (0, 0))
    in_specs = [
        pl.BlockSpec((tokens, wide), lambda p, place: (0, mine(p, place))),
        pl.BlockSpec((tokens, narrow), lambda p, place: (0, mine(p, place))),
        pl.BlockSpec((tokens, wide), lambda p, place: (0, mine(p, place))),
        pl.BlockSpec((1, 2, tokens), lambda p, place: (mine(p, place), 0, 0)),
    ] * 2 + [
        pl.BlockSpec((LAT, 2 * (NOPE + VDIM)), lambda p, place: (0, first + p)),
        whole(cand),
        whole(cand_t),
        whole(rope_keys),
        whole(bias),
    ]
    operands = [*own, *sibling, weight, cand, cand_t, rope_keys, bias]
    aliases = {}
    if earlier is not None:
        for index, array in enumerate(earlier):
            aliases[1 + len(operands)] = index
            in_specs.append(pl.BlockSpec(memory_space=pl.ANY))
            operands.append(array)
    columns = 2 * (NOPE + VDIM) * count
    bf16, f32 = jnp.bfloat16, jnp.float32
    out_shape = [
        jax.ShapeDtypeStruct(q_own.shape, bf16),
        jax.ShapeDtypeStruct(rope_own.shape, bf16),
        jax.ShapeDtypeStruct((tokens, chunks * pairs * (wide + narrow)), bf16),
        *[jax.ShapeDtypeStruct((LAT // 2, columns), f32)] * 2,
        jax.ShapeDtypeStruct((cand.shape[0], LAT), f32),
        jax.ShapeDtypeStruct((cand.shape[0], narrow), f32),
    ]
    out_specs = [
        pl.BlockSpec((tokens, wide), lambda p, place: (0, mine(p, place))),
        pl.BlockSpec((tokens, narrow), lambda p, place: (0, mine(p, place))),
        pl.BlockSpec((tokens, wide + narrow), lambda p, place: (0, theirs(p, place))),
        *[pl.BlockSpec((LAT // 2, 2 * (NOPE + VDIM)), lambda p, place: (0, p))] * 2,
        pl.BlockSpec((cand.shape[0], LAT), lambda p, place: (0, 0)),
        pl.BlockSpec((cand.shape[0], narrow), lambda p, place: (0, 0)),
    ]
    return pl.pallas_call(
        functools.partial(heads_kernel, earlier=len(aliases)),
        grid_spec=pltpu.PrefetchScalarGridSpec(
            num_scalar_prefetch=1, grid=(count,), in_specs=in_specs, out_specs=out_specs
        ),
        out_shape=out_shape,
        input_output_aliases=aliases,
        compiler_params=pltpu.CompilerParams(vmem_limit_bytes=KERNEL_BYTES),
        cost_estimate=pl.CostEstimate(
            flops=count * 100_000_000, bytes_accessed=count * 300_000, transcendentals=0
        ),
        name="heads_backward",
    )(place, *operands)


def place_kernel(place, received, q_in, rope_in, q_out, rope_out):
    wide, narrow = 2 * NOPE, 2 * ROPE
    for pair in range(q_out.shape[1] // wide):
        start = pair * (wide + narrow)
        q_out[:, pair * wide : (pair + 1) * wide] = received[:, start : start + wide]
        rope_out[:, pair * narrow : (pair + 1) * narrow] = received[
            :, start + wide : start + wide + narrow
        ]


def place_columns(place, received, q_full, rope_full, chunks):
    tokens = q_full.shape[0]
    q_cols, rope_cols = q_full.shape[1] // chunks // 2, rope_full.shape[1] // chunks // 2
    put = lambda c, place: (0, c * 2 + 1 - place[0])
    return pl.pallas_call(
        place_kernel,
        grid_spec=pltpu.PrefetchScalarGridSpec(
            num_scalar_prefetch=1,
            grid=(chunks,),
            in_specs=[
                pl.BlockSpec((tokens, q_cols + rope_cols), lambda c, place: (0, c)),
                pl.BlockSpec(memory_space=pl.ANY),
                pl.BlockSpec(memory_space=pl.ANY),
            ],
            out_specs=[
                pl.BlockSpec((tokens, q_cols), put),
                pl.BlockSpec((tokens, rope_cols), put),
            ],
        ),
        out_shape=[
            jax.ShapeDtypeStruct(q_full.shape, q_full.dtype),
            jax.ShapeDtypeStruct(rope_full.shape, rope_full.dtype),
        ],
        input_output_aliases={2: 0, 3: 1},
        compiler_params=pltpu.CompilerParams(vmem_limit_bytes=KERNEL_BYTES),
        cost_estimate=pl.CostEstimate(flops=0, bytes_accessed=4_000_000, transcendentals=0),
        name="place_columns",
    )(place, received, q_full, rope_full)


def stack_kernel(*refs, arrangement):
    outs = refs[len(refs) - len(arrangement) :]
    for out, sources in zip(outs, arrangement):
        row = 0
        for index, block in sources:
            piece = refs[index]
            columns = slice(block * out.shape[1], (block + 1) * out.shape[1])
            out[row : row + piece.shape[0], :] = piece[:, columns]
            row += piece.shape[0]


def stack(inputs, arrangement, columns):
    whole = lambda shape: pl.BlockSpec(shape, lambda: (0, 0))
    shapes = [(sum(inputs[i].shape[0] for i, _ in sources), columns) for sources in arrangement]
    return pl.pallas_call(
        functools.partial(stack_kernel, arrangement=arrangement),
        in_specs=[whole(array.shape) for array in inputs],
        out_specs=[whole(shape) for shape in shapes],
        out_shape=[jax.ShapeDtypeStruct(shape, inputs[0].dtype) for shape in shapes],
        compiler_params=pltpu.CompilerParams(vmem_limit_bytes=KERNEL_BYTES),
        cost_estimate=pl.CostEstimate(flops=0, bytes_accessed=2_000_000, transcendentals=0),
        name="stack",
    )(*inputs)


def leave_kernel(place, near, distant, leaving):
    width = near.shape[1]
    leaving[:, :width] = near[...]
    leaving[:, width:] = distant[...]


def join_rows_kernel(place, near, distant, crossed, near_rows, distant_rows):
    rows, width = near.shape
    for at, (own, out) in enumerate(((near, near_rows), (distant, distant_rows))):
        out[:rows, :] = own[...]
        out[rows:, :] = crossed[:, at * width : (at + 1) * width]


def weight_parts(place, up_weight, chunks, far, crossed=None):
    rows = up_weight.shape[0]
    width = up_weight.shape[1] // chunks // 2
    joins = crossed is not None

    def column_block(t):
        def block(i, place):
            return (0, place[1 + t] * 2 + (place[0] if joins else 1 - place[0]))

        return pl.BlockSpec((rows, width), block)

    whole = lambda shape: pl.BlockSpec(shape, lambda i, place: (0, 0))
    shapes = [(2 * rows, width)] * 2 if joins else [(rows, 2 * width)]
    return pl.pallas_call(
        join_rows_kernel if joins else leave_kernel,
        grid_spec=pltpu.PrefetchScalarGridSpec(
            num_scalar_prefetch=1,
            grid=(1,),
            in_specs=[column_block(t) for t in (0, far)] + [whole((rows, 2 * width))] * joins,
            out_specs=[whole(shape) for shape in shapes],
        ),
        out_shape=[jax.ShapeDtypeStruct(shape, up_weight.dtype) for shape in shapes],
        compiler_params=pltpu.CompilerParams(vmem_limit_bytes=INPUT_BYTES),
        cost_estimate=pl.CostEstimate(flops=0, bytes_accessed=1_000_000, transcendentals=0),
        name="weight_parts",
    )(place, up_weight, up_weight, *([crossed] if joins else []))


def lay_kernel(place, *refs):
    *pieces, out = refs
    width = out.shape[1] // 4
    for step in range(len(pieces) // 2):
        early, late = pieces[2 * step], pieces[2 * step + 1]

        @pl.when(pl.program_id(0) == step)
        def _():
            for which in range(2):
                source = slice(which * width, (which + 1) * width)
                out[:, 2 * which * width : (2 * which + 1) * width] = early[:, source]
                out[:, (2 * which + 1) * width : (2 * which + 2) * width] = late[:, source]


def lay_out(place, pieces):
    rows, columns = pieces[0].shape
    count = len(pieces) // 2
    return pl.pallas_call(
        lay_kernel,
        grid_spec=pltpu.PrefetchScalarGridSpec(
            num_scalar_prefetch=1,
            grid=(count,),
            in_specs=[pl.BlockSpec((rows, columns), lambda t, place: (0, 0))] * len(pieces),
            out_specs=pl.BlockSpec((rows, 2 * columns), lambda t, place: (0, place[1 + t])),
        ),
        out_shape=jax.ShapeDtypeStruct((rows, count * 2 * columns), pieces[0].dtype),
        compiler_params=pltpu.CompilerParams(vmem_limit_bytes=KERNEL_BYTES),
        cost_estimate=pl.CostEstimate(flops=0, bytes_accessed=4_000_000, transcendentals=0),
        name="lay_out",
    )(place, *pieces)


def piece_kernel(place, kept, crossed, out):
    width = kept.shape[1]

    @pl.when(place[0] == 0)
    def _():
        out[:, :width] = kept[...]
        out[:, width:] = crossed[...]

    @pl.when(place[0] != 0)
    def _():
        out[:, :width] = crossed[...]
        out[:, width:] = kept[...]


def join_cores(place, kept, crossed):
    rows, columns = kept.shape
    return pl.pallas_call(
        piece_kernel,
        grid_spec=pltpu.PrefetchScalarGridSpec(
            num_scalar_prefetch=1,
            grid=(1,),
            in_specs=[pl.BlockSpec((rows, columns), lambda i, place: (0, 0))] * 2,
            out_specs=pl.BlockSpec((rows, 2 * columns), lambda i, place: (0, 0)),
        ),
        out_shape=jax.ShapeDtypeStruct((rows, 2 * columns), kept.dtype),
        compiler_params=pltpu.CompilerParams(vmem_limit_bytes=KERNEL_BYTES),
        cost_estimate=pl.CostEstimate(flops=0, bytes_accessed=500_000, transcendentals=0),
        name="join_cores",
    )(place, kept, crossed)


def halving_order(count):
    bits = count.bit_length() - 1
    partners = []
    for place in range(count):
        partner = place & 1
        for bit in range(1, bits):
            partner |= ((place >> (bits - bit)) & 1) << bit
        partners.append(partner)
    return partners


def channel_order(ctx, lat_block):
    channel = lax.broadcasted_iota(jnp.int32, (LAT, LAT), 0)
    place = lax.broadcasted_iota(jnp.int32, (LAT, LAT), 1)
    count = LAT // lat_block
    bits = count.bit_length() - 1
    block = place // lat_block
    partner = block & 1
    for bit in range(1, bits):
        partner |= ((block >> (bits - bit)) & 1) << bit
    return channel == (ctx ^ partner) * lat_block + place % lat_block


def block_sources(place, offered, per_block, span):
    ctx = place[place.shape[0] - 1]
    sources = []
    for side in range(2):
        group = ctx ^ side
        for at in range(per_block + len(partner_offsets)):
            matching = at - per_block
            offset = partner_offsets[matching] if matching >= 0 else 0
            source = group - offset
            usable = source >= 0
            sender = jnp.maximum(source, 0)
            inner = offered[sender, matching] if matching >= 0 else at
            start = jnp.where(usable, ((ctx >> 1) - (sender >> 1)) * span + inner * BLOCK, 0)
            block_id = jnp.where(usable, sender * per_block + inner, -2)
            sources.append(((offset + side) % 2, start, usable, block_id))
    return sources


def collect_kernel(place, offered, own, sib, cand, cand_t, rope_keys, bias, *, lat_block):
    ctx = place[place.shape[0] - 1]
    span = own.shape[0] // 3
    per_block = (span - 16) // BLOCK
    pieces = []
    key_at = lax.broadcasted_iota(jnp.int32, (BLOCK, 2 * BLOCK), 0)
    query = lax.broadcasted_iota(jnp.int32, (BLOCK, 2 * BLOCK), 1)
    causal = jnp.where(key_at <= query % BLOCK, 1.0, 0.0)
    sources = block_sources(place, offered, per_block, span)
    for block, (other, start, usable, block_id) in enumerate(sources):
        rows_ref = sib if other else own
        rows = rows_ref[pl.ds(pl.multiple_of(start, 16), BLOCK), :]
        pieces.append(jnp.where(usable, rows, jnp.zeros_like(rows)))
        side = block // (len(sources) // 2)
        lists = (sib if side else own)[span - 16 : span, :][:1].astype(jnp.int32)
        open_for = []
        for at in range(per_block):
            picks = [lists[:, at * TOPK + k : at * TOPK + k + 1] for k in range(TOPK)]
            picked = functools.reduce(
                jnp.maximum, [jnp.where(pick == block_id, 1.0, 0.0) for pick in picks]
            )
            same = jnp.where(block_id == (ctx ^ side) * per_block + at, 1.0, 0.0)
            open_for.append(jnp.maximum(picked, same * causal))
        allowed = jnp.where(query < BLOCK, open_for[0], open_for[1])
        bias[block * BLOCK : (block + 1) * BLOCK, :] = jnp.where(allowed > 0.5, 0.0, HIDDEN)
    both = jnp.concatenate(pieces, axis=0)
    order = channel_order(ctx, lat_block).astype(jnp.bfloat16)
    latent = both[:, :LAT]
    cand[...] = dot(latent, order, 1, 0).astype(jnp.bfloat16)
    cand_t[...] = dot(order, latent, 0, 1).astype(jnp.bfloat16)
    twice = lax.broadcasted_iota(jnp.int32, (ROPE, 2 * ROPE), 0)
    twice = twice == lax.broadcasted_iota(jnp.int32, (ROPE, 2 * ROPE), 1) % ROPE
    rope_keys[...] = dot(both[:, LAT:], twice.astype(jnp.bfloat16), 1, 0).astype(jnp.bfloat16)


def collect(place, offered, own, sib, rows, lat_block):
    bf16 = jnp.bfloat16
    shapes = [((rows, LAT), bf16), ((LAT, rows), bf16), ((rows, 2 * ROPE), bf16)]
    shapes.append(((rows, 2 * BLOCK), jnp.float32))
    whole = lambda shape: pl.BlockSpec(shape, lambda i, place, offered: (0, 0))
    return pl.pallas_call(
        functools.partial(collect_kernel, lat_block=lat_block),
        grid_spec=pltpu.PrefetchScalarGridSpec(
            num_scalar_prefetch=2,
            grid=(1,),
            in_specs=[whole(own.shape), whole(sib.shape)],
            out_specs=[whole(shape) for shape, _ in shapes],
        ),
        out_shape=[jax.ShapeDtypeStruct(shape, dtype) for shape, dtype in shapes],
        compiler_params=pltpu.CompilerParams(vmem_limit_bytes=KERNEL_BYTES),
        cost_estimate=pl.CostEstimate(
            flops=250_000_000, bytes_accessed=3_000_000, transcendentals=0
        ),
        name="collect",
    )(place, offered, own, sib)


def spread_kernel(place, offered, *refs, lat_block):
    *sums, own, sib = refs
    count = len(sums) // 2
    latent, rope = sums[0][...], sums[count][...]
    for index in range(1, count):
        latent, rope = latent + sums[index][...], rope + sums[count + index][...]
    order = channel_order(place[place.shape[0] - 1], lat_block).astype(jnp.float32)
    latent = lax.dot_general(
        latent,
        order,
        (((1,), (1,)), ((), ())),
        precision=lax.Precision.HIGHEST,
        preferred_element_type=jnp.float32,
    )
    rows = jnp.concatenate([latent, rope[:, :ROPE] + rope[:, ROPE:]], axis=1)
    own[...] = jnp.zeros_like(own)
    sib[...] = jnp.zeros_like(sib)
    span = own.shape[0] // 3
    sources = block_sources(place, offered, (span - 16) // BLOCK, span)
    for block, (other, start, _, _) in enumerate(sources):
        here = pl.ds(pl.multiple_of(start, 16), BLOCK)
        target = sib if other else own
        target[here, :] += rows[block * BLOCK : (block + 1) * BLOCK]


def spread(place, offered, latents, ropes, rows, lat_block):
    shape = (rows, LAT + ROPE)
    sums = [*latents, *ropes]
    whole = lambda shape: pl.BlockSpec(shape, lambda i, place, offered: (0, 0))
    return pl.pallas_call(
        functools.partial(spread_kernel, lat_block=lat_block),
        grid_spec=pltpu.PrefetchScalarGridSpec(
            num_scalar_prefetch=2,
            grid=(1,),
            in_specs=[whole(array.shape) for array in sums],
            out_specs=[whole(shape)] * 2,
        ),
        out_shape=[jax.ShapeDtypeStruct(shape, jnp.float32)] * 2,
        compiler_params=pltpu.CompilerParams(vmem_limit_bytes=KERNEL_BYTES),
        cost_estimate=pl.CostEstimate(
            flops=700_000_000, bytes_accessed=6_000_000, transcendentals=0
        ),
        name="spread",
    )(place, offered, *sums)


def halve(value, axis, bit):
    half = value.shape[0] // 2
    return value[:half] + exchange(value[half:], axis, bit)


def shards(q_nope, q_rope, grad_out, log_total, kv_latent, up_weight, selected, offered):
    n_dp, n_ctx = lax.axis_size("dp"), lax.axis_size("ctx")
    dp, ctx = lax.axis_index("dp"), lax.axis_index("ctx")
    core = ctx % 2
    group_len = kv_latent.shape[1]
    per_block = group_len // BLOCK
    heads = log_total.shape[1]
    part_heads = heads // n_dp // 2
    pairs = part_heads // 2
    part_cols = part_heads * (NOPE + VDIM)
    far = n_dp - 1
    lat_block = up_weight.shape[0]

    place = jnp.stack([core] + [dp ^ t for t in range(n_dp)] + [ctx]).astype(jnp.int32)

    leaving, = weight_parts(place, up_weight, n_dp, far)
    crossed = exchange(leaving, "ctx", 1)
    crossed, place, selected, offered, q_nope, q_rope, grad_out, log_total, kv_latent = (
        lax.optimization_barrier(
            (crossed, place, selected, offered, q_nope, q_rope, grad_out, log_total, kv_latent)
        )
    )
    chip_rows = weight_parts(place, up_weight, n_dp, far, crossed)
    own = [q_nope[0], q_rope[0], grad_out[0]]
    sibling = [exchange(array, "ctx", 1) for array in own]
    offered = offered[0]
    span = group_len + 16
    lists = selected[0].reshape(1, -1).astype(jnp.bfloat16)
    lists = jnp.pad(lists, ((0, 15), (0, LAT + ROPE - lists.shape[1])))
    bundle = after(jnp.concatenate([kv_latent[0], lists], axis=0), *sibling)
    bundles = [bundle, from_behind(bundle, "ctx", 2), from_behind(bundle, "ctx", 4)]
    own_bundles = stack(bundles, (((0, 0), (1, 0), (2, 0)),), LAT + ROPE)[0]
    sib_bundles = exchange(own_bundles, "ctx", 1)
    key_len = 2 * (group_len + len(partner_offsets) * BLOCK)
    shared = collect(place, offered, own_bundles, sib_bundles, key_len, lat_block)

    partners = halving_order(n_ctx)[::2]

    def over_chips(start):
        at_step = {0: start}
        for step in range(4, n_ctx, 4):
            at_step[step] = exchange(start, "ctx", step)
        at_step[2] = exchange(start, "ctx", 2)
        for step in range(4, n_ctx, 4):
            at_step[step + 2] = exchange(after(at_step[step], at_step[2]), "ctx", 2)
        return [at_step[partner] for partner in partners], at_step[n_ctx - 4]

    def joined(pieces):
        return stack(pieces, (tuple((index, 0) for index in range(len(pieces))),), part_cols)[0]

    near_pieces, last = over_chips(chip_rows[0])
    far_pieces, _ = over_chips(after(chip_rows[1], last))
    log_total = after(log_total, last)[0]
    sibling.append(exchange(log_total, "ctx", 1))
    own.append(log_total)
    for arrays in (own, sibling):
        arrays[3] = arrays[3].reshape(heads // 2, 2, group_len)

    weights = {0: joined([after(near_pieces[0], shared[0], sibling[3])] + near_pieces[1:])}
    for t in range(1, far):
        weights[t] = exchange(weights[0], "dp", t)
    earlier = None
    latents, ropes = [], []
    weight_grads = {t: ([], []) for t in range(n_dp)}
    bits = [1 << b for b in range(n_dp.bit_length() - 1)]
    orders = (bits, bits[::-1])
    first_sums = [{t: [] for t in range(n_dp) if t & order[0]} for order in orders]
    half_pairs = pairs // 2
    units = [(0, 0, half_pairs)] + [(t, 0, pairs) for t in [far] + list(range(1, far - 1))]
    units += [(far - 1, 0, half_pairs), (far - 1, half_pairs, half_pairs)]
    units.append((0, half_pairs, half_pairs))
    for t, start, count in units:
        if t == far:
            weights[far] = joined([after(far_pieces[0], latents[-1])] + far_pieces[1:])
        weight = weights[t]
        if t == 0 and start:
            there = [piece for sent in first_sums for u in sent for piece in sent[u]]
            weight = after(weight, latents[-1], *there)
        if t == 1 and not start:
            weight = after(weight, *[weights[near] for near in range(2, far)])
        if t == far - 1 and start:
            weight = after(weight, latents[-1], *[sent[far][0] for sent in first_sums])
        rest = chunk_backward(
            place,
            t,
            (start, count),
            own,
            sibling,
            weight,
            shared,
            earlier,
            (n_dp, pairs),
        )
        earlier = rest[:3]
        for side, sent in enumerate(first_sums):
            weight_grads[t][side].append(rest[3 + side])
            if t in sent:
                sent[t].append(exchange(rest[3 + side], "dp", orders[side][0]))
        latents.append(rest[5])
        ropes.append(rest[6])

    half_cols = part_cols // 2

    def columns(pieces, half):
        if len(pieces) == 2:
            return pieces[half]
        return pieces[0][:, half * half_cols : (half + 1) * half_cols]

    def total(addends, half):
        return functools.reduce(
            lambda left, right: left + right, [columns(pieces, half) for pieces in addends]
        )

    sums = []
    last_sums = first_sums[1][far - 1]
    for side, order in enumerate(orders):
        addends = {t: [weight_grads[t][side]] for t in weight_grads}
        arrived = {t ^ order[0]: pieces for t, pieces in first_sums[side].items()}
        addends = {t: addends[t] + [more] for t, more in arrived.items()}
        for bit in order[1:]:
            arrived = {}
            for t in sorted((t for t in addends if t & bit), reverse=True):
                leaving = [total(addends[t], half) for half in range(2)]
                if side == 0:
                    behind = [(first_sums[0][order[0]][0], last_sums[-1])] * 2
                else:
                    behind = [(weight_grads[far - 1][side][0],)] * 2
                leaving = [after(half, *there) for half, there in zip(leaving, behind)]
                arrived[t ^ bit] = [exchange(half, "dp", bit) for half in leaving]
            addends = {t: addends[t] + [more] for t, more in arrived.items()}
        sums.append(addends[0])

    q_full, rope_full, sib_grads = earlier
    received = exchange(sib_grads, "ctx", 1)
    grad_nope, grad_rope = place_columns(place, received, q_full, rope_full, n_dp)

    own_grads, sib_grads = spread(place, offered, latents, ropes, 3 * span, lat_block)
    swapped = exchange(sib_grads, "ctx", 1)
    grad_rows = own_grads + swapped
    ctx_bits = [1 << b for b in range(1, n_ctx.bit_length() - 1)]
    finished, arrived = [], None
    for half in range(2):
        if half:
            sums = [[[after(piece, arrived) for piece in pieces] for pieces in side] for side in sums]
        first, second = [total(side, half) for side in sums]
        arrived = exchange(after(second, sums[0][-1][half]), "ctx", ctx_bits[0])
        rows = first + arrived
        if half:
            rows = after(rows, received, swapped)
        for bit in ctx_bits[1:]:
            rows = halve(rows, "ctx", bit)
        kept, crossed = rows[:lat_block], exchange(rows[lat_block:], "ctx", 1)
        if half:
            kept = after(kept, *finished[0][1:])
        piece = join_cores(place, kept, crossed)
        finished.append([piece] + [exchange(piece, "dp", t) for t in range(1, n_dp)])

    grad_rows = after(grad_rows, rows)
    by_chip = [grad_rows[at * span : at * span + group_len] for at in range(3)]
    grad_rows = by_chip[0]
    for chips in (1, 2):
        grad_rows = grad_rows + from_behind(by_chip[chips], "ctx", -2 * chips)
    finished[0][0] = after(finished[0][0], grad_rows, grad_nope)
    grad_weight = lay_out(place, [piece for both in zip(*finished) for piece in both])
    return (grad_nope[None], grad_rope[None], grad_rows[None], grad_weight)


def solution(mesh):
    in_specs = (
        P("dp", "ctx", None),
        P("dp", "ctx", None),
        P("dp", "ctx", None),
        P("dp", None, "ctx"),
        P("dp", "ctx", None),
        P("ctx", None),
        P("dp", "ctx", None),
        P("dp", None, None),
    )
    out_specs = (P("dp", "ctx", None), P("dp", "ctx", None), P("dp", "ctx", None), P("ctx", None))
    return jax.shard_map(shards, mesh=mesh, in_specs=in_specs, out_specs=out_specs, check_vma=False)
```

```python
import functools

import jax
import jax.numpy as jnp
from jax import lax
from jax.experimental import pallas as pl
from jax.experimental.pallas import tpu as pltpu
from jax.sharding import PartitionSpec as P

LAT = 256
ROPE = 64
NOPE = 128
VDIM = 128
BLOCK = 64
TOPK = 3

partner_offsets = (1, 2, 3, 4)
HIDDEN = -1e30
KERNEL_BYTES = 12 * 1024 * 1024
INPUT_BYTES = 56 * 1024 * 1024


def from_behind(value, axis, steps):
    count = lax.axis_size(axis)
    initial, last = (max(0, -steps), min(count, count - steps))
    return lax.ppermute(value, axis, [(source, source + steps) for source in range(initial, last)])


def exchange(value, axis, bits):
    count = lax.axis_size(axis)
    return lax.ppermute(value, axis, [(source, source ^ bits) for source in range(count)])


def after(value, *earlier):
    return lax.optimization_barrier((value, *earlier))[0]


def dot(left, right, left_dim, right_dim):
    return lax.dot_general(
        left,
        right,
        (((left_dim,), (right_dim,)), ((), ())),
        preferred_element_type=jnp.float32,
    )


def heads_kernel(
    place,
    q_own, rope_own, out_own, tot_own,
    q_sib, rope_sib, out_sib, tot_sib,
    weight, cand, cand_t, rope_keys, bias,
    *rest,
    earlier,
):
    gq_own, gr_own, sib_grads, *weight_grads, lat_sum, rope_sum = rest[earlier:]
    scale = 1.0 / jnp.sqrt(jnp.float32(NOPE + ROPE))
    rows = cand.shape[0] // 2
    half = weight_grads[0].shape[0]
    sib_q, sib_rope = sib_grads.at[:, : 2 * NOPE], sib_grads.at[:, 2 * NOPE :]
    lane_half = lax.broadcasted_iota(jnp.int32, (rows, 2 * ROPE), 1) // ROPE

    @pl.when(pl.program_id(0) == 0)
    def _():
        lat_sum[...] = jnp.zeros_like(lat_sum)
        rope_sum[...] = jnp.zeros_like(rope_sum)

    groups = (
        (q_own, rope_own, out_own, tot_own, gq_own, gr_own),
        (q_sib, rope_sib, out_sib, tot_sib, sib_q, sib_rope),
    )
    rope_grads = [None, None]
    for head in range(2):
        columns = pl.ds(head * (NOPE + VDIM), NOPE + VDIM)
        head_weight = weight[:, columns]
        expanded = dot(cand[...], head_weight, 1, 0).astype(jnp.bfloat16)
        both_grads = []
        for side, (q_ref, rope_ref, out_ref, tot_ref, gq_ref, gr_ref) in enumerate(groups):
            own_rows = slice(side * rows, (side + 1) * rows)
            here = pl.ds(head * NOPE, NOPE)
            rope_part = jnp.where(
                lane_half == head, rope_keys[own_rows, :], jnp.zeros((), jnp.bfloat16)
            )
            keys = jnp.concatenate([expanded[own_rows, :NOPE], rope_part], axis=1)
            values = expanded[own_rows, NOPE:]
            queries = jnp.concatenate([q_ref[:, here], rope_ref[...]], axis=1)
            out_grads = out_ref[:, here]
            scores = dot(keys, queries, 1, 1) * scale
            probs = jnp.exp(scores - tot_ref[0, head : head + 1, :] + bias[own_rows, :])
            prob_grads = dot(values, out_grads, 1, 1)
            row_dot = jnp.sum(probs * prob_grads, axis=0, keepdims=True)
            score_grads = (probs * (prob_grads - row_dot)).astype(jnp.bfloat16)
            query_grad = dot(score_grads, keys, 0, 0) * scale
            gq_ref[:, here] = query_grad[:, :NOPE].astype(jnp.bfloat16)
            if head == 0:
                rope_grads[side] = query_grad[:, NOPE:]
            else:
                gr_ref[...] = (rope_grads[side] + query_grad[:, NOPE:]).astype(jnp.bfloat16)
            key_grad = dot(score_grads, queries, 1, 0) * scale
            value_grad = dot(probs.astype(jnp.bfloat16), out_grads, 1, 0)
            rope_sum[own_rows, :] += jnp.where(lane_half == head, key_grad[:, NOPE:], 0.0)
            both_grads.append(
                jnp.concatenate([key_grad[:, :NOPE], value_grad], axis=1).astype(jnp.bfloat16)
            )
        key_grads = jnp.concatenate(both_grads, axis=0)
        lat_sum[...] += dot(key_grads, head_weight, 1, 1)
        weight_grad = dot(cand_t[...], key_grads, 1, 0)
        weight_grads[0][:, columns] = weight_grad[:half]
        weight_grads[1][:, columns] = weight_grad[half:]


def chunk_backward(place, t, unit, own, sibling, weight, shared, earlier, sizes):
    q_own, rope_own, out_own, tot_own = own
    cand, cand_t, rope_keys, bias = shared
    tokens = q_own.shape[0]
    chunks, pairs = sizes
    wide, narrow = 2 * NOPE, 2 * ROPE
    first, count = unit
    mine = lambda p, place: (place[1 + t] * 2 + place[0]) * pairs + first + p
    theirs = lambda p, place: place[1 + t] * pairs + first + p
    whole = lambda array: pl.BlockSpec(array.shape, lambda p, place: (0, 0))
    in_specs = [
        pl.BlockSpec((tokens, wide), lambda p, place: (0, mine(p, place))),
        pl.BlockSpec((tokens, narrow), lambda p, place: (0, mine(p, place))),
        pl.BlockSpec((tokens, wide), lambda p, place: (0, mine(p, place))),
        pl.BlockSpec((1, 2, tokens), lambda p, place: (mine(p, place), 0, 0)),
    ] * 2 + [
        pl.BlockSpec((LAT, 2 * (NOPE + VDIM)), lambda p, place: (0, first + p)),
        whole(cand),
        whole(cand_t),
        whole(rope_keys),
        whole(bias),
    ]
    operands = [*own, *sibling, weight, cand, cand_t, rope_keys, bias]
    aliases = {}
    if earlier is not None:
        for index, array in enumerate(earlier):
            aliases[1 + len(operands)] = index
            in_specs.append(pl.BlockSpec(memory_space=pl.ANY))
            operands.append(array)
    columns = 2 * (NOPE + VDIM) * count
    bf16, f32 = jnp.bfloat16, jnp.float32
    out_shape = [
        jax.ShapeDtypeStruct(q_own.shape, bf16),
        jax.ShapeDtypeStruct(rope_own.shape, bf16),
        jax.ShapeDtypeStruct((tokens, chunks * pairs * (wide + narrow)), bf16),
        *[jax.ShapeDtypeStruct((LAT // 2, columns), f32)] * 2,
        jax.ShapeDtypeStruct((cand.shape[0], LAT), f32),
        jax.ShapeDtypeStruct((cand.shape[0], narrow), f32),
    ]
    out_specs = [
        pl.BlockSpec((tokens, wide), lambda p, place: (0, mine(p, place))),
        pl.BlockSpec((tokens, narrow), lambda p, place: (0, mine(p, place))),
        pl.BlockSpec((tokens, wide + narrow), lambda p, place: (0, theirs(p, place))),
        *[pl.BlockSpec((LAT // 2, 2 * (NOPE + VDIM)), lambda p, place: (0, p))] * 2,
        pl.BlockSpec((cand.shape[0], LAT), lambda p, place: (0, 0)),
        pl.BlockSpec((cand.shape[0], narrow), lambda p, place: (0, 0)),
    ]
    return pl.pallas_call(
        functools.partial(heads_kernel, earlier=len(aliases)),
        grid_spec=pltpu.PrefetchScalarGridSpec(
            num_scalar_prefetch=1, grid=(count,), in_specs=in_specs, out_specs=out_specs
        ),
        out_shape=out_shape,
        input_output_aliases=aliases,
        compiler_params=pltpu.CompilerParams(vmem_limit_bytes=KERNEL_BYTES),
        cost_estimate=pl.CostEstimate(
            flops=count * 1_500_000_000, bytes_accessed=count * 300_000, transcendentals=0
        ),
        name="heads_backward",
    )(place, *operands)


def place_kernel(place, received, q_in, rope_in, q_out, rope_out):
    wide, narrow = 2 * NOPE, 2 * ROPE
    for pair in range(q_out.shape[1] // wide):
        start = pair * (wide + narrow)
        q_out[:, pair * wide : (pair + 1) * wide] = received[:, start : start + wide]
        rope_out[:, pair * narrow : (pair + 1) * narrow] = received[
            :, start + wide : start + wide + narrow
        ]


def place_columns(place, received, q_full, rope_full, chunks):
    tokens = q_full.shape[0]
    q_cols, rope_cols = q_full.shape[1] // chunks // 2, rope_full.shape[1] // chunks // 2
    put = lambda c, place: (0, c * 2 + 1 - place[0])
    return pl.pallas_call(
        place_kernel,
        grid_spec=pltpu.PrefetchScalarGridSpec(
            num_scalar_prefetch=1,
            grid=(chunks,),
            in_specs=[
                pl.BlockSpec((tokens, q_cols + rope_cols), lambda c, place: (0, c)),
                pl.BlockSpec(memory_space=pl.ANY),
                pl.BlockSpec(memory_space=pl.ANY),
            ],
            out_specs=[
                pl.BlockSpec((tokens, q_cols), put),
                pl.BlockSpec((tokens, rope_cols), put),
            ],
        ),
        out_shape=[
            jax.ShapeDtypeStruct(q_full.shape, q_full.dtype),
            jax.ShapeDtypeStruct(rope_full.shape, rope_full.dtype),
        ],
        input_output_aliases={2: 0, 3: 1},
        compiler_params=pltpu.CompilerParams(vmem_limit_bytes=KERNEL_BYTES),
        cost_estimate=pl.CostEstimate(flops=0, bytes_accessed=4_000_000, transcendentals=0),
        name="place_columns",
    )(place, received, q_full, rope_full)


def stack_kernel(*refs, arrangement):
    outs = refs[len(refs) - len(arrangement) :]
    for out, sources in zip(outs, arrangement):
        row = 0
        for index, block in sources:
            piece = refs[index]
            columns = slice(block * out.shape[1], (block + 1) * out.shape[1])
            out[row : row + piece.shape[0], :] = piece[:, columns]
            row += piece.shape[0]


def stack(inputs, arrangement, columns):
    whole = lambda shape: pl.BlockSpec(shape, lambda: (0, 0))
    shapes = [(sum(inputs[i].shape[0] for i, _ in sources), columns) for sources in arrangement]
    return pl.pallas_call(
        functools.partial(stack_kernel, arrangement=arrangement),
        in_specs=[whole(array.shape) for array in inputs],
        out_specs=[whole(shape) for shape in shapes],
        out_shape=[jax.ShapeDtypeStruct(shape, inputs[0].dtype) for shape in shapes],
        compiler_params=pltpu.CompilerParams(vmem_limit_bytes=KERNEL_BYTES),
        cost_estimate=pl.CostEstimate(flops=0, bytes_accessed=2_000_000, transcendentals=0),
        name="stack",
    )(*inputs)


def join_rows_kernel(place, near, distant, near_crossed, distant_crossed, near_rows, distant_rows):
    rows = near.shape[0]
    for own, crossed, out in (
        (near, near_crossed, near_rows),
        (distant, distant_crossed, distant_rows),
    ):
        out[:rows, :] = own[...]
        out[rows:, :] = crossed[...]


def weight_parts(place, up_weight, crossed, chunks, far):
    rows = up_weight.shape[0]
    width = up_weight.shape[1] // chunks // 2

    def column_block(t):
        return pl.BlockSpec((rows, width), lambda i, place: (0, place[1 + t] * 2 + place[0]))

    shape = (2 * rows, width)
    return pl.pallas_call(
        join_rows_kernel,
        grid_spec=pltpu.PrefetchScalarGridSpec(
            num_scalar_prefetch=1,
            grid=(1,),
            in_specs=[column_block(t) for t in (0, far)] * 2,
            out_specs=[pl.BlockSpec(shape, lambda i, place: (0, 0))] * 2,
        ),
        out_shape=[jax.ShapeDtypeStruct(shape, up_weight.dtype)] * 2,
        compiler_params=pltpu.CompilerParams(vmem_limit_bytes=INPUT_BYTES),
        cost_estimate=pl.CostEstimate(flops=0, bytes_accessed=1_000_000, transcendentals=0),
        name="weight_parts",
    )(place, up_weight, up_weight, crossed, crossed)


def lay_kernel(place, *refs, count):
    pieces, out = refs[:count], refs[-1]
    width = out.shape[1]
    for step, piece in enumerate(pieces):
        for which in range(2):

            @pl.when(pl.program_id(0) == 2 * step + which)
            def _():
                out[...] = piece[:, which * width : (which + 1) * width]


def lay_out(place, pieces, half, earlier=None):
    rows, columns = pieces[0].shape
    count, width = len(pieces), columns // 2
    total = 2 * count * columns

    def target(step, place):
        chunk = place[1]
        for t in range(1, count):
            chunk = jnp.where((step >> 1) == t, place[1 + t], chunk)
        return (0, chunk * 4 + (step & 1) * 2 + half)

    in_specs = [pl.BlockSpec((rows, columns), lambda step, place: (0, 0))] * count
    operands, aliases = list(pieces), {}
    if earlier is not None:
        in_specs.append(pl.BlockSpec(memory_space=pl.ANY))
        operands.append(earlier)
        aliases = {count + 1: 0}
    return pl.pallas_call(
        functools.partial(lay_kernel, count=count),
        grid_spec=pltpu.PrefetchScalarGridSpec(
            num_scalar_prefetch=1,
            grid=(2 * count,),
            in_specs=in_specs,
            out_specs=pl.BlockSpec((rows, width), target),
        ),
        out_shape=jax.ShapeDtypeStruct((rows, total), pieces[0].dtype),
        input_output_aliases=aliases,
        compiler_params=pltpu.CompilerParams(vmem_limit_bytes=KERNEL_BYTES),
        cost_estimate=pl.CostEstimate(flops=0, bytes_accessed=2_000_000, transcendentals=0),
        name="lay_out",
    )(place, *operands)


def piece_kernel(place, kept, crossed, out):
    width = kept.shape[1]

    @pl.when(place[0] == 0)
    def _():
        out[:, :width] = kept[...]
        out[:, width:] = crossed[...]

    @pl.when(place[0] != 0)
    def _():
        out[:, :width] = crossed[...]
        out[:, width:] = kept[...]


def join_cores(place, kept, crossed):
    rows, columns = kept.shape
    return pl.pallas_call(
        piece_kernel,
        grid_spec=pltpu.PrefetchScalarGridSpec(
            num_scalar_prefetch=1,
            grid=(1,),
            in_specs=[pl.BlockSpec((rows, columns), lambda i, place: (0, 0))] * 2,
            out_specs=pl.BlockSpec((rows, 2 * columns), lambda i, place: (0, 0)),
        ),
        out_shape=jax.ShapeDtypeStruct((rows, 2 * columns), kept.dtype),
        compiler_params=pltpu.CompilerParams(vmem_limit_bytes=KERNEL_BYTES),
        cost_estimate=pl.CostEstimate(flops=0, bytes_accessed=500_000, transcendentals=0),
        name="join_cores",
    )(place, kept, crossed)


def halving_order(count):
    bits = count.bit_length() - 1
    partners = []
    for place in range(count):
        partner = place & 1
        for bit in range(1, bits):
            partner |= ((place >> (bits - bit)) & 1) << bit
        partners.append(partner)
    return partners


def channel_order(ctx, lat_block):
    channel = lax.broadcasted_iota(jnp.int32, (LAT, LAT), 0)
    place = lax.broadcasted_iota(jnp.int32, (LAT, LAT), 1)
    count = LAT // lat_block
    bits = count.bit_length() - 1
    block = place // lat_block
    partner = block & 1
    for bit in range(1, bits):
        partner |= ((block >> (bits - bit)) & 1) << bit
    return channel == (ctx ^ partner) * lat_block + place % lat_block


def block_sources(place, offered, per_block, span):
    ctx = place[place.shape[0] - 1]
    sources = []
    for side in range(2):
        group = ctx ^ side
        for at in range(per_block + len(partner_offsets)):
            matching = at - per_block
            offset = partner_offsets[matching] if matching >= 0 else 0
            source = group - offset
            usable = source >= 0
            sender = jnp.maximum(source, 0)
            inner = offered[sender, matching] if matching >= 0 else at
            start = jnp.where(usable, ((ctx >> 1) - (sender >> 1)) * span + inner * BLOCK, 0)
            block_id = jnp.where(usable, sender * per_block + inner, -2)
            sources.append(((offset + side) % 2, start, usable, block_id))
    return sources


def collect_kernel(place, offered, own, sib, cand, cand_t, rope_keys, bias, *, lat_block):
    ctx = place[place.shape[0] - 1]
    span = own.shape[0] // 3
    per_block = (span - 16) // BLOCK
    pieces = []
    key_at = lax.broadcasted_iota(jnp.int32, (BLOCK, 2 * BLOCK), 0)
    query = lax.broadcasted_iota(jnp.int32, (BLOCK, 2 * BLOCK), 1)
    causal = jnp.where(key_at <= query % BLOCK, 1.0, 0.0)
    sources = block_sources(place, offered, per_block, span)
    for block, (other, start, usable, block_id) in enumerate(sources):
        rows_ref = sib if other else own
        rows = rows_ref[pl.ds(pl.multiple_of(start, 16), BLOCK), :]
        pieces.append(jnp.where(usable, rows, jnp.zeros_like(rows)))
        side = block // (len(sources) // 2)
        lists = (sib if side else own)[span - 16 : span, :][:1].astype(jnp.int32)
        open_for = []
        for at in range(per_block):
            picks = [lists[:, at * TOPK + k : at * TOPK + k + 1] for k in range(TOPK)]
            picked = functools.reduce(
                jnp.maximum, [jnp.where(pick == block_id, 1.0, 0.0) for pick in picks]
            )
            same = jnp.where(block_id == (ctx ^ side) * per_block + at, 1.0, 0.0)
            open_for.append(jnp.maximum(picked, same * causal))
        allowed = jnp.where(query < BLOCK, open_for[0], open_for[1])
        bias[block * BLOCK : (block + 1) * BLOCK, :] = jnp.where(allowed > 0.5, 0.0, HIDDEN)
    both = jnp.concatenate(pieces, axis=0)
    order = channel_order(ctx, lat_block).astype(jnp.bfloat16)
    latent = both[:, :LAT]
    cand[...] = dot(latent, order, 1, 0).astype(jnp.bfloat16)
    cand_t[...] = dot(order, latent, 0, 1).astype(jnp.bfloat16)
    twice = lax.broadcasted_iota(jnp.int32, (ROPE, 2 * ROPE), 0)
    twice = twice == lax.broadcasted_iota(jnp.int32, (ROPE, 2 * ROPE), 1) % ROPE
    rope_keys[...] = dot(both[:, LAT:], twice.astype(jnp.bfloat16), 1, 0).astype(jnp.bfloat16)


def collect(place, offered, own, sib, rows, lat_block):
    bf16 = jnp.bfloat16
    shapes = [((rows, LAT), bf16), ((LAT, rows), bf16), ((rows, 2 * ROPE), bf16)]
    shapes.append(((rows, 2 * BLOCK), jnp.float32))
    whole = lambda shape: pl.BlockSpec(shape, lambda i, place, offered: (0, 0))
    return pl.pallas_call(
        functools.partial(collect_kernel, lat_block=lat_block),
        grid_spec=pltpu.PrefetchScalarGridSpec(
            num_scalar_prefetch=2,
            grid=(1,),
            in_specs=[whole(own.shape), whole(sib.shape)],
            out_specs=[whole(shape) for shape, _ in shapes],
        ),
        out_shape=[jax.ShapeDtypeStruct(shape, dtype) for shape, dtype in shapes],
        compiler_params=pltpu.CompilerParams(vmem_limit_bytes=KERNEL_BYTES),
        cost_estimate=pl.CostEstimate(
            flops=250_000_000, bytes_accessed=3_000_000, transcendentals=0
        ),
        name="collect",
    )(place, offered, own, sib)


def spread_kernel(place, offered, *refs, lat_block):
    *sums, own, sib = refs
    count = len(sums) // 2
    latent, rope = sums[0][...], sums[count][...]
    for index in range(1, count):
        latent, rope = latent + sums[index][...], rope + sums[count + index][...]
    order = channel_order(place[place.shape[0] - 1], lat_block).astype(jnp.float32)
    latent = lax.dot_general(
        latent,
        order,
        (((1,), (1,)), ((), ())),
        precision=lax.Precision.HIGHEST,
        preferred_element_type=jnp.float32,
    )
    rows = jnp.concatenate([latent, rope[:, :ROPE] + rope[:, ROPE:]], axis=1)
    own[...] = jnp.zeros_like(own)
    sib[...] = jnp.zeros_like(sib)
    span = own.shape[0] // 3
    sources = block_sources(place, offered, (span - 16) // BLOCK, span)
    for block, (other, start, _, _) in enumerate(sources):
        here = pl.ds(pl.multiple_of(start, 16), BLOCK)
        target = sib if other else own
        target[here, :] += rows[block * BLOCK : (block + 1) * BLOCK]


def spread(place, offered, latents, ropes, rows, lat_block):
    shape = (rows, LAT + ROPE)
    sums = [*latents, *ropes]
    whole = lambda shape: pl.BlockSpec(shape, lambda i, place, offered: (0, 0))
    return pl.pallas_call(
        functools.partial(spread_kernel, lat_block=lat_block),
        grid_spec=pltpu.PrefetchScalarGridSpec(
            num_scalar_prefetch=2,
            grid=(1,),
            in_specs=[whole(array.shape) for array in sums],
            out_specs=[whole(shape)] * 2,
        ),
        out_shape=[jax.ShapeDtypeStruct(shape, jnp.float32)] * 2,
        compiler_params=pltpu.CompilerParams(vmem_limit_bytes=KERNEL_BYTES),
        cost_estimate=pl.CostEstimate(
            flops=700_000_000, bytes_accessed=6_000_000, transcendentals=0
        ),
        name="spread",
    )(place, offered, *sums)


def halve(value, axis, bit):
    half = value.shape[0] // 2
    return value[:half] + exchange(value[half:], axis, bit)


def shards(q_nope, q_rope, grad_out, log_total, kv_latent, up_weight, selected, offered):
    n_dp, n_ctx = lax.axis_size("dp"), lax.axis_size("ctx")
    dp, ctx = lax.axis_index("dp"), lax.axis_index("ctx")
    core = ctx % 2
    group_len = kv_latent.shape[1]
    per_block = group_len // BLOCK
    heads = log_total.shape[1]
    part_heads = heads // n_dp // 2
    pairs = part_heads // 2
    part_cols = part_heads * (NOPE + VDIM)
    far = n_dp - 1
    lat_block = up_weight.shape[0]

    place = jnp.stack([core] + [dp ^ t for t in range(n_dp)] + [ctx]).astype(jnp.int32)

    crossed = exchange(up_weight, "ctx", 1)
    crossed, place, selected, offered, q_nope, q_rope, grad_out, log_total, kv_latent = (
        lax.optimization_barrier(
            (crossed, place, selected, offered, q_nope, q_rope, grad_out, log_total, kv_latent)
        )
    )
    chip_rows = weight_parts(place, up_weight, crossed, n_dp, far)
    own = [q_nope[0], q_rope[0], grad_out[0]]
    sibling = [exchange(array, "ctx", 1) for array in own]
    offered = offered[0]
    span = group_len + 16
    lists = selected[0].reshape(1, -1).astype(jnp.bfloat16)
    lists = jnp.pad(lists, ((0, 15), (0, LAT + ROPE - lists.shape[1])))
    bundle = after(jnp.concatenate([kv_latent[0], lists], axis=0), *sibling)
    bundles = [bundle, from_behind(bundle, "ctx", 2), from_behind(bundle, "ctx", 4)]
    own_bundles = stack(bundles, (((0, 0), (1, 0), (2, 0)),), LAT + ROPE)[0]
    sib_bundles = exchange(own_bundles, "ctx", 1)
    key_len = 2 * (group_len + len(partner_offsets) * BLOCK)
    shared = collect(place, offered, own_bundles, sib_bundles, key_len, lat_block)

    partners = halving_order(n_ctx)[::2]

    def over_chips(start):
        at_step = {0: start}
        for step in range(4, n_ctx, 4):
            at_step[step] = exchange(start, "ctx", step)
        at_step[2] = exchange(start, "ctx", 2)
        for step in range(4, n_ctx, 4):
            at_step[step + 2] = exchange(after(at_step[step], at_step[2]), "ctx", 2)
        return [at_step[partner] for partner in partners], at_step[n_ctx - 4]

    def joined(pieces):
        return stack(pieces, (tuple((index, 0) for index in range(len(pieces))),), part_cols)[0]

    near_pieces, last = over_chips(chip_rows[0])
    far_pieces, _ = over_chips(after(chip_rows[1], last))
    log_total = after(log_total, last)[0]
    sibling.append(exchange(log_total, "ctx", 1))
    own.append(log_total)
    for arrays in (own, sibling):
        arrays[3] = arrays[3].reshape(heads // 2, 2, group_len)

    weights = {0: joined([after(near_pieces[0], shared[0], sibling[3])] + near_pieces[1:])}
    for t in range(1, far):
        weights[t] = exchange(weights[0], "dp", t)
    earlier = None
    latents, ropes = [], []
    weight_grads = {t: ([], []) for t in range(n_dp)}
    bits = [1 << b for b in range(n_dp.bit_length() - 1)]
    orders = (bits, bits[::-1])
    first_sums = [{t: [] for t in range(n_dp) if t & order[0]} for order in orders]
    half_pairs = pairs // 2
    halved = lambda t: [(t, 0, half_pairs), (t, half_pairs, half_pairs)]
    units = [(0, 0, half_pairs), *halved(far)] + [(t, 0, pairs) for t in range(1, far - 1)]
    units += [*halved(far - 1), (0, half_pairs, half_pairs)]
    for t, start, count in units:
        if t == far and not start:
            weights[far] = joined([after(far_pieces[0], latents[-1])] + far_pieces[1:])
        weight = weights[t]
        if t == 0 and start:
            there = [piece for sent in first_sums for u in sent for piece in sent[u]]
            weight = after(weight, latents[-1], *there)
        if t == 1 and not start:
            weight = after(weight, *[weights[near] for near in range(2, far)])
        if t == far - 1:
            far_sums = [sent[far][1 if start else 0] for sent in first_sums]
            weight = after(weight, latents[-1], *far_sums)
        rest = chunk_backward(
            place,
            t,
            (start, count),
            own,
            sibling,
            weight,
            shared,
            earlier,
            (n_dp, pairs),
        )
        earlier = rest[:3]
        for side, sent in enumerate(first_sums):
            weight_grads[t][side].append(rest[3 + side])
            if t in sent:
                leaving = rest[3 + side]
                if t == far - 1 and start:
                    leaving = after(leaving, sent[t][0])
                sent[t].append(exchange(leaving, "dp", orders[side][0]))
        latents.append(rest[5])
        ropes.append(rest[6])

    half_cols = part_cols // 2

    def columns(pieces, half):
        if len(pieces) == 2:
            return pieces[half]
        return pieces[0][:, half * half_cols : (half + 1) * half_cols]

    def total(addends, half):
        return functools.reduce(
            lambda left, right: left + right, [columns(pieces, half) for pieces in addends]
        )

    sums = []
    last_sums = first_sums[1][far - 1]
    for side, order in enumerate(orders):
        addends = {t: [weight_grads[t][side]] for t in weight_grads}
        arrived = {t ^ order[0]: pieces for t, pieces in first_sums[side].items()}
        addends = {t: addends[t] + [more] for t, more in arrived.items()}
        for bit in order[1:]:
            arrived = {}
            for t in sorted((t for t in addends if t & bit), reverse=True):
                leaving = [total(addends[t], half) for half in range(2)]
                if side == 0:
                    behind = [(first_sums[0][order[0]][0], last_sums[-1])] * 2
                else:
                    behind = [(weight_grads[far - 1][side][0],)] * 2
                leaving = [after(half, *there) for half, there in zip(leaving, behind)]
                arrived[t ^ bit] = [exchange(half, "dp", bit) for half in leaving]
            addends = {t: addends[t] + [more] for t, more in arrived.items()}
        sums.append(addends[0])

    q_full, rope_full, sib_grads = earlier
    received = exchange(sib_grads, "ctx", 1)
    grad_nope, grad_rope = place_columns(place, received, q_full, rope_full, n_dp)

    own_grads, sib_grads = spread(place, offered, latents, ropes, 3 * span, lat_block)
    swapped = exchange(sib_grads, "ctx", 1)
    grad_rows = own_grads + swapped
    ctx_bits = [1 << b for b in range(1, n_ctx.bit_length() - 1)]
    finished, arrived = [], None
    for half in range(2):
        if half:
            sums = [[[after(piece, arrived) for piece in pieces] for pieces in side] for side in sums]
        first, second = [total(side, half) for side in sums]
        arrived = exchange(after(second, sums[0][-1][half]), "ctx", ctx_bits[0])
        rows = first + arrived
        if half:
            rows = after(rows, received, swapped)
        for bit in ctx_bits[1:]:
            rows = halve(rows, "ctx", bit)
        kept, crossed = rows[:lat_block], exchange(rows[lat_block:], "ctx", 1)
        if half:
            kept = after(kept, *finished[0][1:])
        piece = join_cores(place, kept, crossed)
        finished.append([piece] + [exchange(piece, "dp", t) for t in range(1, n_dp)])

    grad_rows = after(grad_rows, rows)
    by_chip = [grad_rows[at * span : at * span + group_len] for at in range(3)]
    grad_rows = by_chip[0]
    for chips in (1, 2):
        grad_rows = grad_rows + from_behind(by_chip[chips], "ctx", -2 * chips)
    grad_weight = lay_out(place, finished[0], 0)
    finished[1][0] = after(finished[1][0], grad_rows, grad_nope)
    grad_weight = lay_out(place, finished[1], 1, grad_weight)
    return (grad_nope[None], grad_rope[None], grad_rows[None], grad_weight)


def solution(mesh):
    in_specs = (
        P("dp", "ctx", None),
        P("dp", "ctx", None),
        P("dp", "ctx", None),
        P("dp", None, "ctx"),
        P("dp", "ctx", None),
        P("ctx", None),
        P("dp", "ctx", None),
        P("dp", None, None),
    )
    out_specs = (P("dp", "ctx", None), P("dp", "ctx", None), P("dp", "ctx", None), P("ctx", None))
    return jax.shard_map(shards, mesh=mesh, in_specs=in_specs, out_specs=out_specs, check_vma=False)
```

```python
import functools

import jax
import jax.numpy as jnp
from jax import lax
from jax.experimental import pallas as pl
from jax.experimental.pallas import tpu as pltpu
from jax.sharding import PartitionSpec as P

LAT = 256
ROPE = 64
NOPE = 128
VDIM = 128
BLOCK = 64
TOPK = 3

partner_offsets = (1, 2, 3, 4)
HIDDEN = -1e30
KERNEL_BYTES = 12 * 1024 * 1024
INPUT_BYTES = 56 * 1024 * 1024


def from_behind(value, axis, steps):
    count = lax.axis_size(axis)
    initial, last = (max(0, -steps), min(count, count - steps))
    return lax.ppermute(value, axis, [(source, source + steps) for source in range(initial, last)])


def exchange(value, axis, bits):
    count = lax.axis_size(axis)
    return lax.ppermute(value, axis, [(source, source ^ bits) for source in range(count)])


def after(value, *earlier):
    return lax.optimization_barrier((value, *earlier))[0]


def dot(left, right, left_dim, right_dim):
    return lax.dot_general(
        left,
        right,
        (((left_dim,), (right_dim,)), ((), ())),
        preferred_element_type=jnp.float32,
    )


def heads_kernel(
    place,
    q_own, rope_own, out_own, tot_own,
    q_sib, rope_sib, out_sib, tot_sib,
    weight, cand, cand_t, rope_keys, bias,
    *rest,
    earlier,
):
    gq_own, gr_own, sib_grads, *weight_grads, lat_sum, rope_sum = rest[earlier:]
    scale = 1.0 / jnp.sqrt(jnp.float32(NOPE + ROPE))
    rows = cand.shape[0] // 2
    half = weight_grads[0].shape[0]
    sib_q, sib_rope = sib_grads.at[:, : 2 * NOPE], sib_grads.at[:, 2 * NOPE :]
    lane_half = lax.broadcasted_iota(jnp.int32, (rows, 2 * ROPE), 1) // ROPE

    @pl.when(pl.program_id(0) == 0)
    def _():
        lat_sum[...] = jnp.zeros_like(lat_sum)
        rope_sum[...] = jnp.zeros_like(rope_sum)

    groups = (
        (q_own, rope_own, out_own, tot_own, gq_own, gr_own),
        (q_sib, rope_sib, out_sib, tot_sib, sib_q, sib_rope),
    )
    rope_grads = [None, None]
    for head in range(2):
        columns = pl.ds(head * (NOPE + VDIM), NOPE + VDIM)
        head_weight = weight[:, columns]
        expanded = dot(cand[...], head_weight, 1, 0).astype(jnp.bfloat16)
        both_grads = []
        for side, (q_ref, rope_ref, out_ref, tot_ref, gq_ref, gr_ref) in enumerate(groups):
            own_rows = slice(side * rows, (side + 1) * rows)
            here = pl.ds(head * NOPE, NOPE)
            rope_part = jnp.where(
                lane_half == head, rope_keys[own_rows, :], jnp.zeros((), jnp.bfloat16)
            )
            keys = jnp.concatenate([expanded[own_rows, :NOPE], rope_part], axis=1)
            values = expanded[own_rows, NOPE:]
            queries = jnp.concatenate([q_ref[:, here], rope_ref[...]], axis=1)
            out_grads = out_ref[:, here]
            scores = dot(keys, queries, 1, 1) * scale
            probs = jnp.exp(scores - tot_ref[0, head : head + 1, :] + bias[own_rows, :])
            prob_grads = dot(values, out_grads, 1, 1)
            row_dot = jnp.sum(probs * prob_grads, axis=0, keepdims=True)
            score_grads = (probs * (prob_grads - row_dot)).astype(jnp.bfloat16)
            query_grad = dot(score_grads, keys, 0, 0) * scale
            gq_ref[:, here] = query_grad[:, :NOPE].astype(jnp.bfloat16)
            if head == 0:
                rope_grads[side] = query_grad[:, NOPE:]
            else:
                gr_ref[...] = (rope_grads[side] + query_grad[:, NOPE:]).astype(jnp.bfloat16)
            key_grad = dot(score_grads, queries, 1, 0) * scale
            value_grad = dot(probs.astype(jnp.bfloat16), out_grads, 1, 0)
            rope_sum[own_rows, :] += jnp.where(lane_half == head, key_grad[:, NOPE:], 0.0)
            both_grads.append(
                jnp.concatenate([key_grad[:, :NOPE], value_grad], axis=1).astype(jnp.bfloat16)
            )
        key_grads = jnp.concatenate(both_grads, axis=0)
        lat_sum[...] += dot(key_grads, head_weight, 1, 1)
        weight_grad = dot(cand_t[...], key_grads, 1, 0)
        weight_grads[0][:, columns] = weight_grad[:half]
        weight_grads[1][:, columns] = weight_grad[half:]


def chunk_backward(place, t, unit, own, sibling, weight, shared, earlier, sizes):
    q_own, rope_own, out_own, tot_own = own
    cand, cand_t, rope_keys, bias = shared
    tokens = q_own.shape[0]
    chunks, pairs = sizes
    wide, narrow = 2 * NOPE, 2 * ROPE
    first, count = unit
    mine = lambda p, place: (place[1 + t] * 2 + place[0]) * pairs + first + p
    theirs = lambda p, place: place[1 + t] * pairs + first + p
    whole = lambda array: pl.BlockSpec(array.shape, lambda p, place: (0, 0))
    in_specs = [
        pl.BlockSpec((tokens, wide), lambda p, place: (0, mine(p, place))),
        pl.BlockSpec((tokens, narrow), lambda p, place: (0, mine(p, place))),
        pl.BlockSpec((tokens, wide), lambda p, place: (0, mine(p, place))),
        pl.BlockSpec((1, 2, tokens), lambda p, place: (mine(p, place), 0, 0)),
    ] * 2 + [
        pl.BlockSpec((LAT, 2 * (NOPE + VDIM)), lambda p, place: (0, first + p)),
        whole(cand),
        whole(cand_t),
        whole(rope_keys),
        whole(bias),
    ]
    operands = [*own, *sibling, weight, cand, cand_t, rope_keys, bias]
    aliases = {}
    if earlier is not None:
        for index, array in enumerate(earlier):
            aliases[1 + len(operands)] = index
            in_specs.append(pl.BlockSpec(memory_space=pl.ANY))
            operands.append(array)
    columns = 2 * (NOPE + VDIM) * count
    bf16, f32 = jnp.bfloat16, jnp.float32
    out_shape = [
        jax.ShapeDtypeStruct(q_own.shape, bf16),
        jax.ShapeDtypeStruct(rope_own.shape, bf16),
        jax.ShapeDtypeStruct((tokens, chunks * pairs * (wide + narrow)), bf16),
        *[jax.ShapeDtypeStruct((LAT // 2, columns), f32)] * 2,
        jax.ShapeDtypeStruct((cand.shape[0], LAT), f32),
        jax.ShapeDtypeStruct((cand.shape[0], narrow), f32),
    ]
    out_specs = [
        pl.BlockSpec((tokens, wide), lambda p, place: (0, mine(p, place))),
        pl.BlockSpec((tokens, narrow), lambda p, place: (0, mine(p, place))),
        pl.BlockSpec((tokens, wide + narrow), lambda p, place: (0, theirs(p, place))),
        *[pl.BlockSpec((LAT // 2, 2 * (NOPE + VDIM)), lambda p, place: (0, p))] * 2,
        pl.BlockSpec((cand.shape[0], LAT), lambda p, place: (0, 0)),
        pl.BlockSpec((cand.shape[0], narrow), lambda p, place: (0, 0)),
    ]
    return pl.pallas_call(
        functools.partial(heads_kernel, earlier=len(aliases)),
        grid_spec=pltpu.PrefetchScalarGridSpec(
            num_scalar_prefetch=1, grid=(count,), in_specs=in_specs, out_specs=out_specs
        ),
        out_shape=out_shape,
        input_output_aliases=aliases,
        compiler_params=pltpu.CompilerParams(vmem_limit_bytes=KERNEL_BYTES),
        cost_estimate=pl.CostEstimate(
            flops=count * 100_000_000, bytes_accessed=count * 300_000, transcendentals=0
        ),
        name="heads_backward",
    )(place, *operands)


def place_kernel(place, received, q_in, rope_in, q_out, rope_out):
    wide, narrow = 2 * NOPE, 2 * ROPE
    for pair in range(q_out.shape[1] // wide):
        start = pair * (wide + narrow)
        q_out[:, pair * wide : (pair + 1) * wide] = received[:, start : start + wide]
        rope_out[:, pair * narrow : (pair + 1) * narrow] = received[
            :, start + wide : start + wide + narrow
        ]


def place_columns(place, received, q_full, rope_full, chunks):
    tokens = q_full.shape[0]
    q_cols, rope_cols = q_full.shape[1] // chunks // 2, rope_full.shape[1] // chunks // 2
    put = lambda c, place: (0, c * 2 + 1 - place[0])
    return pl.pallas_call(
        place_kernel,
        grid_spec=pltpu.PrefetchScalarGridSpec(
            num_scalar_prefetch=1,
            grid=(chunks,),
            in_specs=[
                pl.BlockSpec((tokens, q_cols + rope_cols), lambda c, place: (0, c)),
                pl.BlockSpec(memory_space=pl.ANY),
                pl.BlockSpec(memory_space=pl.ANY),
            ],
            out_specs=[
                pl.BlockSpec((tokens, q_cols), put),
                pl.BlockSpec((tokens, rope_cols), put),
            ],
        ),
        out_shape=[
            jax.ShapeDtypeStruct(q_full.shape, q_full.dtype),
            jax.ShapeDtypeStruct(rope_full.shape, rope_full.dtype),
        ],
        input_output_aliases={2: 0, 3: 1},
        compiler_params=pltpu.CompilerParams(vmem_limit_bytes=KERNEL_BYTES),
        cost_estimate=pl.CostEstimate(flops=0, bytes_accessed=4_000_000, transcendentals=0),
        name="place_columns",
    )(place, received, q_full, rope_full)


def stack_kernel(*refs, arrangement):
    outs = refs[len(refs) - len(arrangement) :]
    for out, sources in zip(outs, arrangement):
        row = 0
        for index, block in sources:
            piece = refs[index]
            columns = slice(block * out.shape[1], (block + 1) * out.shape[1])
            out[row : row + piece.shape[0], :] = piece[:, columns]
            row += piece.shape[0]


def stack(inputs, arrangement, columns):
    whole = lambda shape: pl.BlockSpec(shape, lambda: (0, 0))
    shapes = [(sum(inputs[i].shape[0] for i, _ in sources), columns) for sources in arrangement]
    return pl.pallas_call(
        functools.partial(stack_kernel, arrangement=arrangement),
        in_specs=[whole(array.shape) for array in inputs],
        out_specs=[whole(shape) for shape in shapes],
        out_shape=[jax.ShapeDtypeStruct(shape, inputs[0].dtype) for shape in shapes],
        compiler_params=pltpu.CompilerParams(vmem_limit_bytes=KERNEL_BYTES),
        cost_estimate=pl.CostEstimate(flops=0, bytes_accessed=2_000_000, transcendentals=0),
        name="stack",
    )(*inputs)


def join_rows_kernel(place, near, distant, near_crossed, distant_crossed, near_rows, distant_rows):
    rows = near.shape[0]
    for own, crossed, out in (
        (near, near_crossed, near_rows),
        (distant, distant_crossed, distant_rows),
    ):
        out[:rows, :] = own[...]
        out[rows:, :] = crossed[...]


def weight_parts(place, up_weight, crossed, chunks, far):
    rows = up_weight.shape[0]
    width = up_weight.shape[1] // chunks // 2

    def column_block(t):
        return pl.BlockSpec((rows, width), lambda i, place: (0, place[1 + t] * 2 + place[0]))

    shape = (2 * rows, width)
    return pl.pallas_call(
        join_rows_kernel,
        grid_spec=pltpu.PrefetchScalarGridSpec(
            num_scalar_prefetch=1,
            grid=(1,),
            in_specs=[column_block(t) for t in (0, far)] * 2,
            out_specs=[pl.BlockSpec(shape, lambda i, place: (0, 0))] * 2,
        ),
        out_shape=[jax.ShapeDtypeStruct(shape, up_weight.dtype)] * 2,
        compiler_params=pltpu.CompilerParams(vmem_limit_bytes=INPUT_BYTES),
        cost_estimate=pl.CostEstimate(flops=0, bytes_accessed=1_000_000, transcendentals=0),
        name="weight_parts",
    )(place, up_weight, up_weight, crossed, crossed)


def lay_kernel(place, *refs, count):
    pieces, out, sems = refs[:count], refs[count], refs[count + 1]
    width = pieces[0].shape[1] // 2
    copies = []
    for index, piece in enumerate(pieces):
        t, half = divmod(index, 2)
        for which in range(2):
            start = (place[1 + t] * 4 + which * 2 + half) * width
            copies.append(
                pltpu.make_async_copy(
                    piece.at[:, pl.ds(which * width, width)],
                    out.at[:, pl.ds(pl.multiple_of(start, width), width)],
                    sems.at[2 * index + which],
                )
            )
    for copy in copies:
        copy.start()
    for copy in copies:
        copy.wait()


def lay_out(place, pieces):
    rows, columns = pieces[0].shape
    count = len(pieces)
    return pl.pallas_call(
        functools.partial(lay_kernel, count=count),
        grid_spec=pltpu.PrefetchScalarGridSpec(
            num_scalar_prefetch=1,
            grid=(1,),
            in_specs=[pl.BlockSpec(memory_space=pl.ANY)] * count,
            out_specs=pl.BlockSpec(memory_space=pl.ANY),
            scratch_shapes=[pltpu.SemaphoreType.DMA((2 * count,))],
        ),
        out_shape=jax.ShapeDtypeStruct((rows, count * columns), pieces[0].dtype),
        compiler_params=pltpu.CompilerParams(vmem_limit_bytes=KERNEL_BYTES),
        cost_estimate=pl.CostEstimate(flops=0, bytes_accessed=4_000_000, transcendentals=0),
        name="lay_out",
    )(place, *pieces)


def piece_kernel(place, kept, crossed, out):
    width = kept.shape[1]

    @pl.when(place[0] == 0)
    def _():
        out[:, :width] = kept[...]
        out[:, width:] = crossed[...]

    @pl.when(place[0] != 0)
    def _():
        out[:, :width] = crossed[...]
        out[:, width:] = kept[...]


def join_cores(place, kept, crossed):
    rows, columns = kept.shape
    return pl.pallas_call(
        piece_kernel,
        grid_spec=pltpu.PrefetchScalarGridSpec(
            num_scalar_prefetch=1,
            grid=(1,),
            in_specs=[pl.BlockSpec((rows, columns), lambda i, place: (0, 0))] * 2,
            out_specs=pl.BlockSpec((rows, 2 * columns), lambda i, place: (0, 0)),
        ),
        out_shape=jax.ShapeDtypeStruct((rows, 2 * columns), kept.dtype),
        compiler_params=pltpu.CompilerParams(vmem_limit_bytes=KERNEL_BYTES),
        cost_estimate=pl.CostEstimate(flops=0, bytes_accessed=500_000, transcendentals=0),
        name="join_cores",
    )(place, kept, crossed)


def halving_order(count):
    bits = count.bit_length() - 1
    partners = []
    for place in range(count):
        partner = place & 1
        for bit in range(1, bits):
            partner |= ((place >> (bits - bit)) & 1) << bit
        partners.append(partner)
    return partners


def channel_order(ctx, lat_block):
    channel = lax.broadcasted_iota(jnp.int32, (LAT, LAT), 0)
    place = lax.broadcasted_iota(jnp.int32, (LAT, LAT), 1)
    count = LAT // lat_block
    bits = count.bit_length() - 1
    block = place // lat_block
    partner = block & 1
    for bit in range(1, bits):
        partner |= ((block >> (bits - bit)) & 1) << bit
    return channel == (ctx ^ partner) * lat_block + place % lat_block


def block_sources(place, offered, per_block, span):
    ctx = place[place.shape[0] - 1]
    sources = []
    for side in range(2):
        group = ctx ^ side
        for at in range(per_block + len(partner_offsets)):
            matching = at - per_block
            offset = partner_offsets[matching] if matching >= 0 else 0
            source = group - offset
            usable = source >= 0
            sender = jnp.maximum(source, 0)
            inner = offered[sender, matching] if matching >= 0 else at
            start = jnp.where(usable, ((ctx >> 1) - (sender >> 1)) * span + inner * BLOCK, 0)
            block_id = jnp.where(usable, sender * per_block + inner, -2)
            sources.append(((offset + side) % 2, start, usable, block_id))
    return sources


def collect_kernel(place, offered, own, sib, cand, cand_t, rope_keys, bias, *, lat_block):
    ctx = place[place.shape[0] - 1]
    span = own.shape[0] // 3
    per_block = (span - 16) // BLOCK
    pieces = []
    key_at = lax.broadcasted_iota(jnp.int32, (BLOCK, 2 * BLOCK), 0)
    query = lax.broadcasted_iota(jnp.int32, (BLOCK, 2 * BLOCK), 1)
    causal = jnp.where(key_at <= query % BLOCK, 1.0, 0.0)
    sources = block_sources(place, offered, per_block, span)
    for block, (other, start, usable, block_id) in enumerate(sources):
        rows_ref = sib if other else own
        rows = rows_ref[pl.ds(pl.multiple_of(start, 16), BLOCK), :]
        pieces.append(jnp.where(usable, rows, jnp.zeros_like(rows)))
        side = block // (len(sources) // 2)
        lists = (sib if side else own)[span - 16 : span, :][:1].astype(jnp.int32)
        open_for = []
        for at in range(per_block):
            picks = [lists[:, at * TOPK + k : at * TOPK + k + 1] for k in range(TOPK)]
            picked = functools.reduce(
                jnp.maximum, [jnp.where(pick == block_id, 1.0, 0.0) for pick in picks]
            )
            same = jnp.where(block_id == (ctx ^ side) * per_block + at, 1.0, 0.0)
            open_for.append(jnp.maximum(picked, same * causal))
        allowed = jnp.where(query < BLOCK, open_for[0], open_for[1])
        bias[block * BLOCK : (block + 1) * BLOCK, :] = jnp.where(allowed > 0.5, 0.0, HIDDEN)
    both = jnp.concatenate(pieces, axis=0)
    order = channel_order(ctx, lat_block).astype(jnp.bfloat16)
    latent = both[:, :LAT]
    cand[...] = dot(latent, order, 1, 0).astype(jnp.bfloat16)
    cand_t[...] = dot(order, latent, 0, 1).astype(jnp.bfloat16)
    twice = lax.broadcasted_iota(jnp.int32, (ROPE, 2 * ROPE), 0)
    twice = twice == lax.broadcasted_iota(jnp.int32, (ROPE, 2 * ROPE), 1) % ROPE
    rope_keys[...] = dot(both[:, LAT:], twice.astype(jnp.bfloat16), 1, 0).astype(jnp.bfloat16)


def collect(place, offered, own, sib, rows, lat_block):
    bf16 = jnp.bfloat16
    shapes = [((rows, LAT), bf16), ((LAT, rows), bf16), ((rows, 2 * ROPE), bf16)]
    shapes.append(((rows, 2 * BLOCK), jnp.float32))
    whole = lambda shape: pl.BlockSpec(shape, lambda i, place, offered: (0, 0))
    return pl.pallas_call(
        functools.partial(collect_kernel, lat_block=lat_block),
        grid_spec=pltpu.PrefetchScalarGridSpec(
            num_scalar_prefetch=2,
            grid=(1,),
            in_specs=[whole(own.shape), whole(sib.shape)],
            out_specs=[whole(shape) for shape, _ in shapes],
        ),
        out_shape=[jax.ShapeDtypeStruct(shape, dtype) for shape, dtype in shapes],
        compiler_params=pltpu.CompilerParams(vmem_limit_bytes=KERNEL_BYTES),
        cost_estimate=pl.CostEstimate(
            flops=250_000_000, bytes_accessed=3_000_000, transcendentals=0
        ),
        name="collect",
    )(place, offered, own, sib)


def spread_kernel(place, offered, *refs, lat_block):
    *sums, own, sib = refs
    count = len(sums) // 2
    latent, rope = sums[0][...], sums[count][...]
    for index in range(1, count):
        latent, rope = latent + sums[index][...], rope + sums[count + index][...]
    order = channel_order(place[place.shape[0] - 1], lat_block).astype(jnp.float32)
    latent = lax.dot_general(
        latent,
        order,
        (((1,), (1,)), ((), ())),
        precision=lax.Precision.HIGHEST,
        preferred_element_type=jnp.float32,
    )
    rows = jnp.concatenate([latent, rope[:, :ROPE] + rope[:, ROPE:]], axis=1)
    own[...] = jnp.zeros_like(own)
    sib[...] = jnp.zeros_like(sib)
    span = own.shape[0] // 3
    sources = block_sources(place, offered, (span - 16) // BLOCK, span)
    for block, (other, start, _, _) in enumerate(sources):
        here = pl.ds(pl.multiple_of(start, 16), BLOCK)
        target = sib if other else own
        target[here, :] += rows[block * BLOCK : (block + 1) * BLOCK]


def spread(place, offered, latents, ropes, rows, lat_block):
    shape = (rows, LAT + ROPE)
    sums = [*latents, *ropes]
    whole = lambda shape: pl.BlockSpec(shape, lambda i, place, offered: (0, 0))
    return pl.pallas_call(
        functools.partial(spread_kernel, lat_block=lat_block),
        grid_spec=pltpu.PrefetchScalarGridSpec(
            num_scalar_prefetch=2,
            grid=(1,),
            in_specs=[whole(array.shape) for array in sums],
            out_specs=[whole(shape)] * 2,
        ),
        out_shape=[jax.ShapeDtypeStruct(shape, jnp.float32)] * 2,
        compiler_params=pltpu.CompilerParams(vmem_limit_bytes=KERNEL_BYTES),
        cost_estimate=pl.CostEstimate(
            flops=700_000_000, bytes_accessed=6_000_000, transcendentals=0
        ),
        name="spread",
    )(place, offered, *sums)


def halve(value, axis, bit):
    half = value.shape[0] // 2
    return value[:half] + exchange(value[half:], axis, bit)


def shards(q_nope, q_rope, grad_out, log_total, kv_latent, up_weight, selected, offered):
    n_dp, n_ctx = lax.axis_size("dp"), lax.axis_size("ctx")
    dp, ctx = lax.axis_index("dp"), lax.axis_index("ctx")
    core = ctx % 2
    group_len = kv_latent.shape[1]
    per_block = group_len // BLOCK
    heads = log_total.shape[1]
    part_heads = heads // n_dp // 2
    pairs = part_heads // 2
    part_cols = part_heads * (NOPE + VDIM)
    far = n_dp - 1
    lat_block = up_weight.shape[0]

    place = jnp.stack([core] + [dp ^ t for t in range(n_dp)] + [ctx]).astype(jnp.int32)

    crossed = exchange(up_weight, "ctx", 1)
    crossed, place, selected, offered, q_nope, q_rope, grad_out, log_total, kv_latent = (
        lax.optimization_barrier(
            (crossed, place, selected, offered, q_nope, q_rope, grad_out, log_total, kv_latent)
        )
    )
    chip_rows = weight_parts(place, up_weight, crossed, n_dp, far)
    own = [q_nope[0], q_rope[0], grad_out[0]]
    sibling = [exchange(array, "ctx", 1) for array in own]
    offered = offered[0]
    span = group_len + 16
    lists = selected[0].reshape(1, -1).astype(jnp.bfloat16)
    lists = jnp.pad(lists, ((0, 15), (0, LAT + ROPE - lists.shape[1])))
    bundle = after(jnp.concatenate([kv_latent[0], lists], axis=0), *sibling)
    bundles = [bundle, from_behind(bundle, "ctx", 2), from_behind(bundle, "ctx", 4)]
    own_bundles = stack(bundles, (((0, 0), (1, 0), (2, 0)),), LAT + ROPE)[0]
    sib_bundles = exchange(own_bundles, "ctx", 1)
    key_len = 2 * (group_len + len(partner_offsets) * BLOCK)
    shared = collect(place, offered, own_bundles, sib_bundles, key_len, lat_block)

    partners = halving_order(n_ctx)[::2]

    def over_chips(start):
        at_step = {0: start}
        for step in range(4, n_ctx, 4):
            at_step[step] = exchange(start, "ctx", step)
        at_step[2] = exchange(start, "ctx", 2)
        for step in range(4, n_ctx, 4):
            at_step[step + 2] = exchange(after(at_step[step], at_step[2]), "ctx", 2)
        return [at_step[partner] for partner in partners], at_step[n_ctx - 4]

    def joined(pieces):
        return stack(pieces, (tuple((index, 0) for index in range(len(pieces))),), part_cols)[0]

    near_pieces, last = over_chips(chip_rows[0])
    far_pieces, _ = over_chips(after(chip_rows[1], last))
    log_total = after(log_total, last)[0]
    sibling.append(exchange(log_total, "ctx", 1))
    own.append(log_total)
    for arrays in (own, sibling):
        arrays[3] = arrays[3].reshape(heads // 2, 2, group_len)

    weights = {0: joined([after(near_pieces[0], shared[0], sibling[3])] + near_pieces[1:])}
    for t in range(1, far):
        weights[t] = exchange(weights[0], "dp", t)
    earlier = None
    latents, ropes = [], []
    weight_grads = {t: ([], []) for t in range(n_dp)}
    bits = [1 << b for b in range(n_dp.bit_length() - 1)]
    orders = (bits, bits[::-1])
    first_sums = [{t: [] for t in range(n_dp) if t & order[0]} for order in orders]
    half_pairs = pairs // 2
    units = [(t, 0, pairs) for t in [far] + list(range(1, far - 1))]
    units += [(t, start, half_pairs) for t in (far - 1, 0) for start in (0, half_pairs)]
    for t, start, count in units:
        if t == far:
            weights[far] = joined(far_pieces)
        weight = weights[t]
        if t == 0 and start:
            there = [piece for sent in first_sums for u in sent for piece in sent[u]]
            weight = after(weight, latents[-1], *there)
        if t == 1 and not start:
            weight = after(weight, *[weights[near] for near in range(2, far)])
        if t == far - 1 and start:
            weight = after(weight, latents[-1], *[sent[far][0] for sent in first_sums])
        rest = chunk_backward(
            place,
            t,
            (start, count),
            own,
            sibling,
            weight,
            shared,
            earlier,
            (n_dp, pairs),
        )
        earlier = rest[:3]
        for side, sent in enumerate(first_sums):
            weight_grads[t][side].append(rest[3 + side])
            if t in sent:
                sent[t].append(exchange(rest[3 + side], "dp", orders[side][0]))
        latents.append(rest[5])
        ropes.append(rest[6])

    half_cols = part_cols // 2

    def columns(pieces, half):
        if len(pieces) == 2:
            return pieces[half]
        return pieces[0][:, half * half_cols : (half + 1) * half_cols]

    def total(addends, half):
        return functools.reduce(
            lambda left, right: left + right, [columns(pieces, half) for pieces in addends]
        )

    sums = []
    last_sums = first_sums[1][far - 1]
    for side, order in enumerate(orders):
        addends = {t: [weight_grads[t][side]] for t in weight_grads}
        arrived = {t ^ order[0]: pieces for t, pieces in first_sums[side].items()}
        addends = {t: addends[t] + [more] for t, more in arrived.items()}
        for bit in order[1:]:
            arrived = {}
            for t in sorted((t for t in addends if t & bit), reverse=True):
                leaving = [total(addends[t], half) for half in range(2)]
                if side == 0:
                    behind = [(first_sums[0][order[0]][0], last_sums[-1], latents[-2])] * 2
                else:
                    behind = [(weight_grads[far - 1][side][0],)] * 2
                leaving = [after(half, *there) for half, there in zip(leaving, behind)]
                arrived[t ^ bit] = [exchange(half, "dp", bit) for half in leaving]
            addends = {t: addends[t] + [more] for t, more in arrived.items()}
        sums.append(addends[0])

    q_full, rope_full, sib_grads = earlier
    received = exchange(sib_grads, "ctx", 1)
    grad_nope, grad_rope = place_columns(place, received, q_full, rope_full, n_dp)

    own_grads, sib_grads = spread(place, offered, latents, ropes, 3 * span, lat_block)
    swapped = exchange(sib_grads, "ctx", 1)
    grad_rows = own_grads + swapped
    ctx_bits = [1 << b for b in range(1, n_ctx.bit_length() - 1)]
    finished, arrived = [], None
    for half in range(2):
        if half:
            sums = [[[after(piece, arrived) for piece in pieces] for pieces in side] for side in sums]
        first, second = [total(side, half) for side in sums]
        arrived = exchange(after(second, sums[0][-1][half]), "ctx", ctx_bits[0])
        rows = first + arrived
        if half:
            rows = after(rows, received, swapped)
        for bit in ctx_bits[1:]:
            rows = halve(rows, "ctx", bit)
        kept, crossed = rows[:lat_block], exchange(rows[lat_block:], "ctx", 1)
        if half:
            kept = after(kept, *finished[0][1:])
        piece = join_cores(place, kept, crossed)
        finished.append([piece] + [exchange(piece, "dp", t) for t in range(1, n_dp)])

    grad_rows = after(grad_rows, rows)
    by_chip = [grad_rows[at * span : at * span + group_len] for at in range(3)]
    grad_rows = by_chip[0]
    for chips in (1, 2):
        grad_rows = grad_rows + from_behind(by_chip[chips], "ctx", -2 * chips)
    finished[0][0] = after(finished[0][0], grad_rows, grad_nope)
    grad_weight = lay_out(place, [piece for both in zip(*finished) for piece in both])
    return (grad_nope[None], grad_rope[None], grad_rows[None], grad_weight)


def solution(mesh):
    in_specs = (
        P("dp", "ctx", None),
        P("dp", "ctx", None),
        P("dp", "ctx", None),
        P("dp", None, "ctx"),
        P("dp", "ctx", None),
        P("ctx", None),
        P("dp", "ctx", None),
        P("dp", None, None),
    )
    out_specs = (P("dp", "ctx", None), P("dp", "ctx", None), P("dp", "ctx", None), P("ctx", None))
    return jax.shard_map(shards, mesh=mesh, in_specs=in_specs, out_specs=out_specs, check_vma=False)
```

```python
import functools

import jax
import jax.numpy as jnp
from jax import lax
from jax.experimental import pallas as pl
from jax.experimental.pallas import tpu as pltpu
from jax.sharding import PartitionSpec as P

LAT = 256
ROPE = 64
NOPE = 128
VDIM = 128
BLOCK = 64
TOPK = 3

partner_offsets = (1, 2, 3, 4)
HIDDEN = -1e30
KERNEL_BYTES = 12 * 1024 * 1024
INPUT_BYTES = 56 * 1024 * 1024


def from_behind(value, axis, steps):
    count = lax.axis_size(axis)
    initial, last = (max(0, -steps), min(count, count - steps))
    return lax.ppermute(value, axis, [(source, source + steps) for source in range(initial, last)])


def exchange(value, axis, bits):
    count = lax.axis_size(axis)
    return lax.ppermute(value, axis, [(source, source ^ bits) for source in range(count)])


def after(value, *earlier):
    return lax.optimization_barrier((value, *earlier))[0]


def dot(left, right, left_dim, right_dim):
    return lax.dot_general(
        left,
        right,
        (((left_dim,), (right_dim,)), ((), ())),
        preferred_element_type=jnp.float32,
    )


def heads_kernel(
    place,
    q_own, rope_own, out_own, tot_own,
    q_sib, rope_sib, out_sib, tot_sib,
    weight, cand, cand_t, rope_keys, bias,
    *rest,
    earlier,
):
    gq_own, gr_own, sib_grads, *weight_grads, lat_sum, rope_sum = rest[earlier:]
    scale = 1.0 / jnp.sqrt(jnp.float32(NOPE + ROPE))
    rows = cand.shape[0] // 2
    half = weight_grads[0].shape[0]
    sib_q, sib_rope = sib_grads.at[:, : 2 * NOPE], sib_grads.at[:, 2 * NOPE :]
    lane_half = lax.broadcasted_iota(jnp.int32, (rows, 2 * ROPE), 1) // ROPE

    @pl.when(pl.program_id(0) == 0)
    def _():
        lat_sum[...] = jnp.zeros_like(lat_sum)
        rope_sum[...] = jnp.zeros_like(rope_sum)

    groups = (
        (q_own, rope_own, out_own, tot_own, gq_own, gr_own),
        (q_sib, rope_sib, out_sib, tot_sib, sib_q, sib_rope),
    )
    rope_grads = [None, None]
    for head in range(2):
        columns = pl.ds(head * (NOPE + VDIM), NOPE + VDIM)
        head_weight = weight[:, columns]
        expanded = dot(cand[...], head_weight, 1, 0).astype(jnp.bfloat16)
        both_grads = []
        for side, (q_ref, rope_ref, out_ref, tot_ref, gq_ref, gr_ref) in enumerate(groups):
            own_rows = slice(side * rows, (side + 1) * rows)
            here = pl.ds(head * NOPE, NOPE)
            rope_part = jnp.where(
                lane_half == head, rope_keys[own_rows, :], jnp.zeros((), jnp.bfloat16)
            )
            keys = jnp.concatenate([expanded[own_rows, :NOPE], rope_part], axis=1)
            values = expanded[own_rows, NOPE:]
            queries = jnp.concatenate([q_ref[:, here], rope_ref[...]], axis=1)
            out_grads = out_ref[:, here]
            scores = dot(keys, queries, 1, 1) * scale
            probs = jnp.exp(scores - tot_ref[0, head : head + 1, :] + bias[own_rows, :])
            prob_grads = dot(values, out_grads, 1, 1)
            row_dot = jnp.sum(probs * prob_grads, axis=0, keepdims=True)
            score_grads = (probs * (prob_grads - row_dot)).astype(jnp.bfloat16)
            query_grad = dot(score_grads, keys, 0, 0) * scale
            gq_ref[:, here] = query_grad[:, :NOPE].astype(jnp.bfloat16)
            if head == 0:
                rope_grads[side] = query_grad[:, NOPE:]
            else:
                gr_ref[...] = (rope_grads[side] + query_grad[:, NOPE:]).astype(jnp.bfloat16)
            key_grad = dot(score_grads, queries, 1, 0) * scale
            value_grad = dot(probs.astype(jnp.bfloat16), out_grads, 1, 0)
            rope_sum[own_rows, :] += jnp.where(lane_half == head, key_grad[:, NOPE:], 0.0)
            both_grads.append(
                jnp.concatenate([key_grad[:, :NOPE], value_grad], axis=1).astype(jnp.bfloat16)
            )
        key_grads = jnp.concatenate(both_grads, axis=0)
        lat_sum[...] += dot(key_grads, head_weight, 1, 1)
        weight_grad = dot(cand_t[...], key_grads, 1, 0)
        weight_grads[0][:, columns] = weight_grad[:half]
        weight_grads[1][:, columns] = weight_grad[half:]


def chunk_backward(place, t, unit, own, sibling, weight, shared, earlier, sizes):
    q_own, rope_own, out_own, tot_own = own
    cand, cand_t, rope_keys, bias = shared
    tokens = q_own.shape[0]
    chunks, pairs = sizes
    wide, narrow = 2 * NOPE, 2 * ROPE
    first, count = unit
    mine = lambda p, place: (place[1 + t] * 2 + place[0]) * pairs + first + p
    theirs = lambda p, place: place[1 + t] * pairs + first + p
    whole = lambda array: pl.BlockSpec(array.shape, lambda p, place: (0, 0))
    in_specs = [
        pl.BlockSpec((tokens, wide), lambda p, place: (0, mine(p, place))),
        pl.BlockSpec((tokens, narrow), lambda p, place: (0, mine(p, place))),
        pl.BlockSpec((tokens, wide), lambda p, place: (0, mine(p, place))),
        pl.BlockSpec((1, 2, tokens), lambda p, place: (mine(p, place), 0, 0)),
    ] * 2 + [
        pl.BlockSpec((LAT, 2 * (NOPE + VDIM)), lambda p, place: (0, first + p)),
        whole(cand),
        whole(cand_t),
        whole(rope_keys),
        whole(bias),
    ]
    operands = [*own, *sibling, weight, cand, cand_t, rope_keys, bias]
    aliases = {}
    if earlier is not None:
        for index, array in enumerate(earlier):
            aliases[1 + len(operands)] = index
            in_specs.append(pl.BlockSpec(memory_space=pl.ANY))
            operands.append(array)
    columns = 2 * (NOPE + VDIM) * count
    bf16, f32 = jnp.bfloat16, jnp.float32
    out_shape = [
        jax.ShapeDtypeStruct(q_own.shape, bf16),
        jax.ShapeDtypeStruct(rope_own.shape, bf16),
        jax.ShapeDtypeStruct((tokens, chunks * pairs * (wide + narrow)), bf16),
        *[jax.ShapeDtypeStruct((LAT // 2, columns), f32)] * 2,
        jax.ShapeDtypeStruct((cand.shape[0], LAT), f32),
        jax.ShapeDtypeStruct((cand.shape[0], narrow), f32),
    ]
    out_specs = [
        pl.BlockSpec((tokens, wide), lambda p, place: (0, mine(p, place))),
        pl.BlockSpec((tokens, narrow), lambda p, place: (0, mine(p, place))),
        pl.BlockSpec((tokens, wide + narrow), lambda p, place: (0, theirs(p, place))),
        *[pl.BlockSpec((LAT // 2, 2 * (NOPE + VDIM)), lambda p, place: (0, p))] * 2,
        pl.BlockSpec((cand.shape[0], LAT), lambda p, place: (0, 0)),
        pl.BlockSpec((cand.shape[0], narrow), lambda p, place: (0, 0)),
    ]
    return pl.pallas_call(
        functools.partial(heads_kernel, earlier=len(aliases)),
        grid_spec=pltpu.PrefetchScalarGridSpec(
            num_scalar_prefetch=1, grid=(count,), in_specs=in_specs, out_specs=out_specs
        ),
        out_shape=out_shape,
        input_output_aliases=aliases,
        compiler_params=pltpu.CompilerParams(vmem_limit_bytes=KERNEL_BYTES),
        cost_estimate=pl.CostEstimate(
            flops=count * 100_000_000, bytes_accessed=count * 300_000, transcendentals=0
        ),
        name="heads_backward",
    )(place, *operands)


def place_kernel(place, received, q_in, rope_in, q_out, rope_out):
    wide, narrow = 2 * NOPE, 2 * ROPE
    for pair in range(q_out.shape[1] // wide):
        start = pair * (wide + narrow)
        q_out[:, pair * wide : (pair + 1) * wide] = received[:, start : start + wide]
        rope_out[:, pair * narrow : (pair + 1) * narrow] = received[
            :, start + wide : start + wide + narrow
        ]


def place_columns(place, received, q_full, rope_full, chunks):
    tokens = q_full.shape[0]
    q_cols, rope_cols = q_full.shape[1] // chunks // 2, rope_full.shape[1] // chunks // 2
    put = lambda c, place: (0, c * 2 + 1 - place[0])
    return pl.pallas_call(
        place_kernel,
        grid_spec=pltpu.PrefetchScalarGridSpec(
            num_scalar_prefetch=1,
            grid=(chunks,),
            in_specs=[
                pl.BlockSpec((tokens, q_cols + rope_cols), lambda c, place: (0, c)),
                pl.BlockSpec(memory_space=pl.ANY),
                pl.BlockSpec(memory_space=pl.ANY),
            ],
            out_specs=[
                pl.BlockSpec((tokens, q_cols), put),
                pl.BlockSpec((tokens, rope_cols), put),
            ],
        ),
        out_shape=[
            jax.ShapeDtypeStruct(q_full.shape, q_full.dtype),
            jax.ShapeDtypeStruct(rope_full.shape, rope_full.dtype),
        ],
        input_output_aliases={2: 0, 3: 1},
        compiler_params=pltpu.CompilerParams(vmem_limit_bytes=KERNEL_BYTES),
        cost_estimate=pl.CostEstimate(flops=0, bytes_accessed=4_000_000, transcendentals=0),
        name="place_columns",
    )(place, received, q_full, rope_full)


def stack_kernel(*refs, arrangement):
    outs = refs[len(refs) - len(arrangement) :]
    for out, sources in zip(outs, arrangement):
        row = 0
        for index, block in sources:
            piece = refs[index]
            columns = slice(block * out.shape[1], (block + 1) * out.shape[1])
            out[row : row + piece.shape[0], :] = piece[:, columns]
            row += piece.shape[0]


def stack(inputs, arrangement, columns):
    whole = lambda shape: pl.BlockSpec(shape, lambda: (0, 0))
    shapes = [(sum(inputs[i].shape[0] for i, _ in sources), columns) for sources in arrangement]
    return pl.pallas_call(
        functools.partial(stack_kernel, arrangement=arrangement),
        in_specs=[whole(array.shape) for array in inputs],
        out_specs=[whole(shape) for shape in shapes],
        out_shape=[jax.ShapeDtypeStruct(shape, inputs[0].dtype) for shape in shapes],
        compiler_params=pltpu.CompilerParams(vmem_limit_bytes=KERNEL_BYTES),
        cost_estimate=pl.CostEstimate(flops=0, bytes_accessed=2_000_000, transcendentals=0),
        name="stack",
    )(*inputs)


def join_rows_kernel(place, near, distant, near_crossed, distant_crossed, near_rows, distant_rows):
    rows = near.shape[0]
    for own, crossed, out in (
        (near, near_crossed, near_rows),
        (distant, distant_crossed, distant_rows),
    ):
        out[:rows, :] = own[...]
        out[rows:, :] = crossed[...]


def weight_parts(place, up_weight, crossed, chunks, far):
    rows = up_weight.shape[0]
    width = up_weight.shape[1] // chunks // 2

    def column_block(t):
        return pl.BlockSpec((rows, width), lambda i, place: (0, place[1 + t] * 2 + place[0]))

    shape = (2 * rows, width)
    return pl.pallas_call(
        join_rows_kernel,
        grid_spec=pltpu.PrefetchScalarGridSpec(
            num_scalar_prefetch=1,
            grid=(1,),
            in_specs=[column_block(t) for t in (0, far)] * 2,
            out_specs=[pl.BlockSpec(shape, lambda i, place: (0, 0))] * 2,
        ),
        out_shape=[jax.ShapeDtypeStruct(shape, up_weight.dtype)] * 2,
        compiler_params=pltpu.CompilerParams(vmem_limit_bytes=INPUT_BYTES),
        cost_estimate=pl.CostEstimate(flops=0, bytes_accessed=1_000_000, transcendentals=0),
        name="weight_parts",
    )(place, up_weight, up_weight, crossed, crossed)


def lay_kernel(place, *refs):
    *pieces, out = refs
    width = out.shape[1] // 4
    for step in range(len(pieces) // 2):
        early, late = pieces[2 * step], pieces[2 * step + 1]

        @pl.when(pl.program_id(0) == step)
        def _():
            for which in range(2):
                source = slice(which * width, (which + 1) * width)
                out[:, 2 * which * width : (2 * which + 1) * width] = early[:, source]
                out[:, (2 * which + 1) * width : (2 * which + 2) * width] = late[:, source]


def lay_out(place, pieces):
    rows, columns = pieces[0].shape
    count = len(pieces) // 2
    return pl.pallas_call(
        lay_kernel,
        grid_spec=pltpu.PrefetchScalarGridSpec(
            num_scalar_prefetch=1,
            grid=(count,),
            in_specs=[pl.BlockSpec(memory_space=pltpu.VMEM)] * len(pieces),
            out_specs=pl.BlockSpec((rows, 2 * columns), lambda t, place: (0, place[1 + t])),
        ),
        out_shape=jax.ShapeDtypeStruct((rows, count * 2 * columns), pieces[0].dtype),
        compiler_params=pltpu.CompilerParams(vmem_limit_bytes=KERNEL_BYTES),
        cost_estimate=pl.CostEstimate(flops=0, bytes_accessed=4_000_000, transcendentals=0),
        name="lay_out",
    )(place, *pieces)


def piece_kernel(place, kept, crossed, out):
    width = kept.shape[1]

    @pl.when(place[0] == 0)
    def _():
        out[:, :width] = kept[...]
        out[:, width:] = crossed[...]

    @pl.when(place[0] != 0)
    def _():
        out[:, :width] = crossed[...]
        out[:, width:] = kept[...]


def join_cores(place, kept, crossed):
    rows, columns = kept.shape
    return pl.pallas_call(
        piece_kernel,
        grid_spec=pltpu.PrefetchScalarGridSpec(
            num_scalar_prefetch=1,
            grid=(1,),
            in_specs=[pl.BlockSpec((rows, columns), lambda i, place: (0, 0))] * 2,
            out_specs=pl.BlockSpec((rows, 2 * columns), lambda i, place: (0, 0)),
        ),
        out_shape=jax.ShapeDtypeStruct((rows, 2 * columns), kept.dtype),
        compiler_params=pltpu.CompilerParams(vmem_limit_bytes=KERNEL_BYTES),
        cost_estimate=pl.CostEstimate(flops=0, bytes_accessed=500_000, transcendentals=0),
        name="join_cores",
    )(place, kept, crossed)


def halving_order(count):
    bits = count.bit_length() - 1
    partners = []
    for place in range(count):
        partner = place & 1
        for bit in range(1, bits):
            partner |= ((place >> (bits - bit)) & 1) << bit
        partners.append(partner)
    return partners


def channel_order(ctx, lat_block):
    channel = lax.broadcasted_iota(jnp.int32, (LAT, LAT), 0)
    place = lax.broadcasted_iota(jnp.int32, (LAT, LAT), 1)
    count = LAT // lat_block
    bits = count.bit_length() - 1
    block = place // lat_block
    partner = block & 1
    for bit in range(1, bits):
        partner |= ((block >> (bits - bit)) & 1) << bit
    return channel == (ctx ^ partner) * lat_block + place % lat_block


def block_sources(place, offered, per_block, span):
    ctx = place[place.shape[0] - 1]
    sources = []
    for side in range(2):
        group = ctx ^ side
        for at in range(per_block + len(partner_offsets)):
            matching = at - per_block
            offset = partner_offsets[matching] if matching >= 0 else 0
            source = group - offset
            usable = source >= 0
            sender = jnp.maximum(source, 0)
            inner = offered[sender, matching] if matching >= 0 else at
            start = jnp.where(usable, ((ctx >> 1) - (sender >> 1)) * span + inner * BLOCK, 0)
            block_id = jnp.where(usable, sender * per_block + inner, -2)
            sources.append(((offset + side) % 2, start, usable, block_id))
    return sources


def collect_kernel(place, offered, own, sib, cand, cand_t, rope_keys, bias, *, lat_block):
    ctx = place[place.shape[0] - 1]
    span = own.shape[0] // 3
    per_block = (span - 16) // BLOCK
    pieces = []
    key_at = lax.broadcasted_iota(jnp.int32, (BLOCK, 2 * BLOCK), 0)
    query = lax.broadcasted_iota(jnp.int32, (BLOCK, 2 * BLOCK), 1)
    causal = jnp.where(key_at <= query % BLOCK, 1.0, 0.0)
    sources = block_sources(place, offered, per_block, span)
    for block, (other, start, usable, block_id) in enumerate(sources):
        rows_ref = sib if other else own
        rows = rows_ref[pl.ds(pl.multiple_of(start, 16), BLOCK), :]
        pieces.append(jnp.where(usable, rows, jnp.zeros_like(rows)))
        side = block // (len(sources) // 2)
        lists = (sib if side else own)[span - 16 : span, :][:1].astype(jnp.int32)
        open_for = []
        for at in range(per_block):
            picks = [lists[:, at * TOPK + k : at * TOPK + k + 1] for k in range(TOPK)]
            picked = functools.reduce(
                jnp.maximum, [jnp.where(pick == block_id, 1.0, 0.0) for pick in picks]
            )
            same = jnp.where(block_id == (ctx ^ side) * per_block + at, 1.0, 0.0)
            open_for.append(jnp.maximum(picked, same * causal))
        allowed = jnp.where(query < BLOCK, open_for[0], open_for[1])
        bias[block * BLOCK : (block + 1) * BLOCK, :] = jnp.where(allowed > 0.5, 0.0, HIDDEN)
    both = jnp.concatenate(pieces, axis=0)
    order = channel_order(ctx, lat_block).astype(jnp.bfloat16)
    latent = both[:, :LAT]
    cand[...] = dot(latent, order, 1, 0).astype(jnp.bfloat16)
    cand_t[...] = dot(order, latent, 0, 1).astype(jnp.bfloat16)
    twice = lax.broadcasted_iota(jnp.int32, (ROPE, 2 * ROPE), 0)
    twice = twice == lax.broadcasted_iota(jnp.int32, (ROPE, 2 * ROPE), 1) % ROPE
    rope_keys[...] = dot(both[:, LAT:], twice.astype(jnp.bfloat16), 1, 0).astype(jnp.bfloat16)


def collect(place, offered, own, sib, rows, lat_block):
    bf16 = jnp.bfloat16
    shapes = [((rows, LAT), bf16), ((LAT, rows), bf16), ((rows, 2 * ROPE), bf16)]
    shapes.append(((rows, 2 * BLOCK), jnp.float32))
    whole = lambda shape: pl.BlockSpec(shape, lambda i, place, offered: (0, 0))
    return pl.pallas_call(
        functools.partial(collect_kernel, lat_block=lat_block),
        grid_spec=pltpu.PrefetchScalarGridSpec(
            num_scalar_prefetch=2,
            grid=(1,),
            in_specs=[whole(own.shape), whole(sib.shape)],
            out_specs=[whole(shape) for shape, _ in shapes],
        ),
        out_shape=[jax.ShapeDtypeStruct(shape, dtype) for shape, dtype in shapes],
        compiler_params=pltpu.CompilerParams(vmem_limit_bytes=KERNEL_BYTES),
        cost_estimate=pl.CostEstimate(
            flops=250_000_000, bytes_accessed=3_000_000, transcendentals=0
        ),
        name="collect",
    )(place, offered, own, sib)


def spread_kernel(place, offered, *refs, lat_block):
    *sums, own, sib = refs
    count = len(sums) // 2
    latent, rope = sums[0][...], sums[count][...]
    for index in range(1, count):
        latent, rope = latent + sums[index][...], rope + sums[count + index][...]
    order = channel_order(place[place.shape[0] - 1], lat_block).astype(jnp.float32)
    latent = lax.dot_general(
        latent,
        order,
        (((1,), (1,)), ((), ())),
        precision=lax.Precision.HIGHEST,
        preferred_element_type=jnp.float32,
    )
    rows = jnp.concatenate([latent, rope[:, :ROPE] + rope[:, ROPE:]], axis=1)
    own[...] = jnp.zeros_like(own)
    sib[...] = jnp.zeros_like(sib)
    span = own.shape[0] // 3
    sources = block_sources(place, offered, (span - 16) // BLOCK, span)
    for block, (other, start, _, _) in enumerate(sources):
        here = pl.ds(pl.multiple_of(start, 16), BLOCK)
        target = sib if other else own
        target[here, :] += rows[block * BLOCK : (block + 1) * BLOCK]


def spread(place, offered, latents, ropes, rows, lat_block):
    shape = (rows, LAT + ROPE)
    sums = [*latents, *ropes]
    whole = lambda shape: pl.BlockSpec(shape, lambda i, place, offered: (0, 0))
    return pl.pallas_call(
        functools.partial(spread_kernel, lat_block=lat_block),
        grid_spec=pltpu.PrefetchScalarGridSpec(
            num_scalar_prefetch=2,
            grid=(1,),
            in_specs=[whole(array.shape) for array in sums],
            out_specs=[whole(shape)] * 2,
        ),
        out_shape=[jax.ShapeDtypeStruct(shape, jnp.float32)] * 2,
        compiler_params=pltpu.CompilerParams(vmem_limit_bytes=KERNEL_BYTES),
        cost_estimate=pl.CostEstimate(
            flops=700_000_000, bytes_accessed=6_000_000, transcendentals=0
        ),
        name="spread",
    )(place, offered, *sums)


def halve(value, axis, bit):
    half = value.shape[0] // 2
    return value[:half] + exchange(value[half:], axis, bit)


def shards(q_nope, q_rope, grad_out, log_total, kv_latent, up_weight, selected, offered):
    n_dp, n_ctx = lax.axis_size("dp"), lax.axis_size("ctx")
    dp, ctx = lax.axis_index("dp"), lax.axis_index("ctx")
    core = ctx % 2
    group_len = kv_latent.shape[1]
    per_block = group_len // BLOCK
    heads = log_total.shape[1]
    part_heads = heads // n_dp // 2
    pairs = part_heads // 2
    part_cols = part_heads * (NOPE + VDIM)
    far = n_dp - 1
    lat_block = up_weight.shape[0]

    place = jnp.stack([core] + [dp ^ t for t in range(n_dp)] + [ctx]).astype(jnp.int32)

    crossed = exchange(up_weight, "ctx", 1)
    crossed, place, selected, offered, q_nope, q_rope, grad_out, log_total, kv_latent = (
        lax.optimization_barrier(
            (crossed, place, selected, offered, q_nope, q_rope, grad_out, log_total, kv_latent)
        )
    )
    chip_rows = weight_parts(place, up_weight, crossed, n_dp, far)
    own = [q_nope[0], q_rope[0], grad_out[0]]
    sibling = [exchange(array, "ctx", 1) for array in own]
    offered = offered[0]
    span = group_len + 16
    lists = selected[0].reshape(1, -1).astype(jnp.bfloat16)
    lists = jnp.pad(lists, ((0, 15), (0, LAT + ROPE - lists.shape[1])))
    bundle = after(jnp.concatenate([kv_latent[0], lists], axis=0), *sibling)
    bundles = [bundle, from_behind(bundle, "ctx", 2), from_behind(bundle, "ctx", 4)]
    own_bundles = stack(bundles, (((0, 0), (1, 0), (2, 0)),), LAT + ROPE)[0]
    sib_bundles = exchange(own_bundles, "ctx", 1)
    key_len = 2 * (group_len + len(partner_offsets) * BLOCK)
    shared = collect(place, offered, own_bundles, sib_bundles, key_len, lat_block)

    partners = halving_order(n_ctx)[::2]

    def over_chips(start):
        at_step = {0: start}
        for step in range(4, n_ctx, 4):
            at_step[step] = exchange(start, "ctx", step)
        at_step[2] = exchange(start, "ctx", 2)
        for step in range(4, n_ctx, 4):
            at_step[step + 2] = exchange(after(at_step[step], at_step[2]), "ctx", 2)
        return [at_step[partner] for partner in partners], at_step[n_ctx - 4]

    def joined(pieces):
        return stack(pieces, (tuple((index, 0) for index in range(len(pieces))),), part_cols)[0]

    near_pieces, last = over_chips(chip_rows[0])
    far_pieces, _ = over_chips(after(chip_rows[1], last))
    log_total = after(log_total, last)[0]
    sibling.append(exchange(log_total, "ctx", 1))
    own.append(log_total)
    for arrays in (own, sibling):
        arrays[3] = arrays[3].reshape(heads // 2, 2, group_len)

    weights = {0: joined([after(near_pieces[0], shared[0], sibling[3])] + near_pieces[1:])}
    for t in range(1, far):
        weights[t] = exchange(weights[0], "dp", t)
    earlier = None
    latents, ropes = [], []
    weight_grads = {t: ([], []) for t in range(n_dp)}
    bits = [1 << b for b in range(n_dp.bit_length() - 1)]
    orders = (bits, bits[::-1])
    first_sums = [{t: [] for t in range(n_dp) if t & order[0]} for order in orders]
    half_pairs = pairs // 2
    units = [(t, 0, pairs) for t in [far] + list(range(1, far - 1))]
    units += [(t, start, half_pairs) for t in (far - 1, 0) for start in (0, half_pairs)]
    for t, start, count in units:
        if t == far:
            weights[far] = joined(far_pieces)
        weight = weights[t]
        if t == 0 and start:
            there = [piece for sent in first_sums for u in sent for piece in sent[u]]
            weight = after(weight, latents[-1], *there)
        if t == 1 and not start:
            weight = after(weight, *[weights[near] for near in range(2, far)])
        if t == far - 1 and start:
            weight = after(weight, latents[-1], *[sent[far][0] for sent in first_sums])
        rest = chunk_backward(
            place,
            t,
            (start, count),
            own,
            sibling,
            weight,
            shared,
            earlier,
            (n_dp, pairs),
        )
        earlier = rest[:3]
        for side, sent in enumerate(first_sums):
            weight_grads[t][side].append(rest[3 + side])
            if t in sent:
                sent[t].append(exchange(rest[3 + side], "dp", orders[side][0]))
        latents.append(rest[5])
        ropes.append(rest[6])

    half_cols = part_cols // 2

    def columns(pieces, half):
        if len(pieces) == 2:
            return pieces[half]
        return pieces[0][:, half * half_cols : (half + 1) * half_cols]

    def total(addends, half):
        return functools.reduce(
            lambda left, right: left + right, [columns(pieces, half) for pieces in addends]
        )

    sums = []
    last_sums = first_sums[1][far - 1]
    for side, order in enumerate(orders):
        addends = {t: [weight_grads[t][side]] for t in weight_grads}
        arrived = {t ^ order[0]: pieces for t, pieces in first_sums[side].items()}
        addends = {t: addends[t] + [more] for t, more in arrived.items()}
        for bit in order[1:]:
            arrived = {}
            for t in sorted((t for t in addends if t & bit), reverse=True):
                leaving = [total(addends[t], half) for half in range(2)]
                if side == 0:
                    behind = [(first_sums[0][order[0]][0], last_sums[-1], latents[-2])] * 2
                else:
                    behind = [(weight_grads[far - 1][side][0],)] * 2
                leaving = [after(half, *there) for half, there in zip(leaving, behind)]
                arrived[t ^ bit] = [exchange(half, "dp", bit) for half in leaving]
            addends = {t: addends[t] + [more] for t, more in arrived.items()}
        sums.append(addends[0])

    q_full, rope_full, sib_grads = earlier
    received = exchange(sib_grads, "ctx", 1)
    grad_nope, grad_rope = place_columns(place, received, q_full, rope_full, n_dp)

    own_grads, sib_grads = spread(place, offered, latents, ropes, 3 * span, lat_block)
    swapped = exchange(sib_grads, "ctx", 1)
    grad_rows = own_grads + swapped
    ctx_bits = [1 << b for b in range(1, n_ctx.bit_length() - 1)]
    finished, arrived = [], None
    for half in range(2):
        if half:
            sums = [[[after(piece, arrived) for piece in pieces] for pieces in side] for side in sums]
        first, second = [total(side, half) for side in sums]
        arrived = exchange(after(second, sums[0][-1][half]), "ctx", ctx_bits[0])
        rows = first + arrived
        if half:
            rows = after(rows, received, swapped)
        for bit in ctx_bits[1:]:
            rows = halve(rows, "ctx", bit)
        kept, crossed = rows[:lat_block], exchange(rows[lat_block:], "ctx", 1)
        if half:
            kept = after(kept, *finished[0][1:])
        piece = join_cores(place, kept, crossed)
        finished.append([piece] + [exchange(piece, "dp", t) for t in range(1, n_dp)])

    grad_rows = after(grad_rows, rows)
    by_chip = [grad_rows[at * span : at * span + group_len] for at in range(3)]
    grad_rows = by_chip[0]
    for chips in (1, 2):
        grad_rows = grad_rows + from_behind(by_chip[chips], "ctx", -2 * chips)
    finished[0][0] = after(finished[0][0], grad_rows, grad_nope)
    grad_weight = lay_out(place, [piece for both in zip(*finished) for piece in both])
    return (grad_nope[None], grad_rope[None], grad_rows[None], grad_weight)


def solution(mesh):
    in_specs = (
        P("dp", "ctx", None),
        P("dp", "ctx", None),
        P("dp", "ctx", None),
        P("dp", None, "ctx"),
        P("dp", "ctx", None),
        P("ctx", None),
        P("dp", "ctx", None),
        P("dp", None, None),
    )
    out_specs = (P("dp", "ctx", None), P("dp", "ctx", None), P("dp", "ctx", None), P("ctx", None))
    return jax.shard_map(shards, mesh=mesh, in_specs=in_specs, out_specs=out_specs, check_vma=False)
```

```python
import functools

import jax
import jax.numpy as jnp
from jax import lax
from jax.experimental import pallas as pl
from jax.experimental.pallas import tpu as pltpu
from jax.sharding import PartitionSpec as P

LAT = 256
ROPE = 64
NOPE = 128
VDIM = 128
BLOCK = 64
TOPK = 3

partner_offsets = (1, 2, 3, 4)
HIDDEN = -1e30
KERNEL_BYTES = 12 * 1024 * 1024
INPUT_BYTES = 56 * 1024 * 1024


def from_behind(value, axis, steps):
    count = lax.axis_size(axis)
    initial, last = (max(0, -steps), min(count, count - steps))
    return lax.ppermute(value, axis, [(source, source + steps) for source in range(initial, last)])


def exchange(value, axis, bits):
    count = lax.axis_size(axis)
    return lax.ppermute(value, axis, [(source, source ^ bits) for source in range(count)])


def after(value, *earlier):
    return lax.optimization_barrier((value, *earlier))[0]


def dot(left, right, left_dim, right_dim):
    return lax.dot_general(
        left,
        right,
        (((left_dim,), (right_dim,)), ((), ())),
        preferred_element_type=jnp.float32,
    )


def heads_kernel(
    place,
    q_own, rope_own, out_own, tot_own,
    q_sib, rope_sib, out_sib, tot_sib,
    weight, cand, cand_t, rope_keys, bias,
    *rest,
    earlier,
):
    gq_own, gr_own, sib_grads, *weight_grads, lat_sum, rope_sum = rest[earlier:]
    scale = 1.0 / jnp.sqrt(jnp.float32(NOPE + ROPE))
    rows = cand.shape[0] // 2
    half = weight_grads[0].shape[0]
    sib_q, sib_rope = sib_grads.at[:, : 2 * NOPE], sib_grads.at[:, 2 * NOPE :]
    lane_half = lax.broadcasted_iota(jnp.int32, (rows, 2 * ROPE), 1) // ROPE

    @pl.when(pl.program_id(0) == 0)
    def _():
        lat_sum[...] = jnp.zeros_like(lat_sum)
        rope_sum[...] = jnp.zeros_like(rope_sum)

    groups = (
        (q_own, rope_own, out_own, tot_own, gq_own, gr_own),
        (q_sib, rope_sib, out_sib, tot_sib, sib_q, sib_rope),
    )
    rope_grads = [None, None]
    for head in range(2):
        columns = pl.ds(head * (NOPE + VDIM), NOPE + VDIM)
        head_weight = weight[:, columns]
        expanded = dot(cand[...], head_weight, 1, 0).astype(jnp.bfloat16)
        both_grads = []
        for side, (q_ref, rope_ref, out_ref, tot_ref, gq_ref, gr_ref) in enumerate(groups):
            own_rows = slice(side * rows, (side + 1) * rows)
            here = pl.ds(head * NOPE, NOPE)
            rope_part = jnp.where(
                lane_half == head, rope_keys[own_rows, :], jnp.zeros((), jnp.bfloat16)
            )
            keys = jnp.concatenate([expanded[own_rows, :NOPE], rope_part], axis=1)
            values = expanded[own_rows, NOPE:]
            queries = jnp.concatenate([q_ref[:, here], rope_ref[...]], axis=1)
            out_grads = out_ref[:, here]
            scores = dot(keys, queries, 1, 1) * scale
            probs = jnp.exp(scores - tot_ref[0, head : head + 1, :] + bias[own_rows, :])
            prob_grads = dot(values, out_grads, 1, 1)
            row_dot = jnp.sum(probs * prob_grads, axis=0, keepdims=True)
            score_grads = (probs * (prob_grads - row_dot)).astype(jnp.bfloat16)
            query_grad = dot(score_grads, keys, 0, 0) * scale
            gq_ref[:, here] = query_grad[:, :NOPE].astype(jnp.bfloat16)
            if head == 0:
                rope_grads[side] = query_grad[:, NOPE:]
            else:
                gr_ref[...] = (rope_grads[side] + query_grad[:, NOPE:]).astype(jnp.bfloat16)
            key_grad = dot(score_grads, queries, 1, 0) * scale
            value_grad = dot(probs.astype(jnp.bfloat16), out_grads, 1, 0)
            rope_sum[own_rows, :] += jnp.where(lane_half == head, key_grad[:, NOPE:], 0.0)
            both_grads.append(
                jnp.concatenate([key_grad[:, :NOPE], value_grad], axis=1).astype(jnp.bfloat16)
            )
        key_grads = jnp.concatenate(both_grads, axis=0)
        lat_sum[...] += dot(key_grads, head_weight, 1, 1)
        weight_grad = dot(cand_t[...], key_grads, 1, 0)
        weight_grads[0][:, columns] = weight_grad[:half]
        weight_grads[1][:, columns] = weight_grad[half:]


def chunk_backward(place, t, unit, own, sibling, weight, shared, earlier, sizes):
    q_own, rope_own, out_own, tot_own = own
    cand, cand_t, rope_keys, bias = shared
    tokens = q_own.shape[0]
    chunks, pairs = sizes
    wide, narrow = 2 * NOPE, 2 * ROPE
    first, count = unit
    mine = lambda p, place: (place[1 + t] * 2 + place[0]) * pairs + first + p
    theirs = lambda p, place: place[1 + t] * pairs + first + p
    whole = lambda array: pl.BlockSpec(array.shape, lambda p, place: (0, 0))
    in_specs = [
        pl.BlockSpec((tokens, wide), lambda p, place: (0, mine(p, place))),
        pl.BlockSpec((tokens, narrow), lambda p, place: (0, mine(p, place))),
        pl.BlockSpec((tokens, wide), lambda p, place: (0, mine(p, place))),
        pl.BlockSpec((1, 2, tokens), lambda p, place: (mine(p, place), 0, 0)),
    ] * 2 + [
        pl.BlockSpec((LAT, 2 * (NOPE + VDIM)), lambda p, place: (0, first + p)),
        whole(cand),
        whole(cand_t),
        whole(rope_keys),
        whole(bias),
    ]
    operands = [*own, *sibling, weight, cand, cand_t, rope_keys, bias]
    aliases = {}
    if earlier is not None:
        for index, array in enumerate(earlier):
            aliases[1 + len(operands)] = index
            in_specs.append(pl.BlockSpec(memory_space=pl.ANY))
            operands.append(array)
    columns = 2 * (NOPE + VDIM) * count
    bf16, f32 = jnp.bfloat16, jnp.float32
    out_shape = [
        jax.ShapeDtypeStruct(q_own.shape, bf16),
        jax.ShapeDtypeStruct(rope_own.shape, bf16),
        jax.ShapeDtypeStruct((tokens, chunks * pairs * (wide + narrow)), bf16),
        *[jax.ShapeDtypeStruct((LAT // 2, columns), f32)] * 2,
        jax.ShapeDtypeStruct((cand.shape[0], LAT), f32),
        jax.ShapeDtypeStruct((cand.shape[0], narrow), f32),
    ]
    out_specs = [
        pl.BlockSpec((tokens, wide), lambda p, place: (0, mine(p, place))),
        pl.BlockSpec((tokens, narrow), lambda p, place: (0, mine(p, place))),
        pl.BlockSpec((tokens, wide + narrow), lambda p, place: (0, theirs(p, place))),
        *[pl.BlockSpec((LAT // 2, 2 * (NOPE + VDIM)), lambda p, place: (0, p))] * 2,
        pl.BlockSpec((cand.shape[0], LAT), lambda p, place: (0, 0)),
        pl.BlockSpec((cand.shape[0], narrow), lambda p, place: (0, 0)),
    ]
    return pl.pallas_call(
        functools.partial(heads_kernel, earlier=len(aliases)),
        grid_spec=pltpu.PrefetchScalarGridSpec(
            num_scalar_prefetch=1, grid=(count,), in_specs=in_specs, out_specs=out_specs
        ),
        out_shape=out_shape,
        input_output_aliases=aliases,
        compiler_params=pltpu.CompilerParams(vmem_limit_bytes=KERNEL_BYTES),
        cost_estimate=pl.CostEstimate(
            flops=count * 1_500_000_000, bytes_accessed=count * 300_000, transcendentals=0
        ),
        name="heads_backward",
    )(place, *operands)


def place_kernel(place, received, q_in, rope_in, q_out, rope_out):
    wide, narrow = 2 * NOPE, 2 * ROPE
    for pair in range(q_out.shape[1] // wide):
        start = pair * (wide + narrow)
        q_out[:, pair * wide : (pair + 1) * wide] = received[:, start : start + wide]
        rope_out[:, pair * narrow : (pair + 1) * narrow] = received[
            :, start + wide : start + wide + narrow
        ]


def place_columns(place, received, q_full, rope_full, chunks):
    tokens = q_full.shape[0]
    q_cols, rope_cols = q_full.shape[1] // chunks // 2, rope_full.shape[1] // chunks // 2
    put = lambda c, place: (0, c * 2 + 1 - place[0])
    return pl.pallas_call(
        place_kernel,
        grid_spec=pltpu.PrefetchScalarGridSpec(
            num_scalar_prefetch=1,
            grid=(chunks,),
            in_specs=[
                pl.BlockSpec((tokens, q_cols + rope_cols), lambda c, place: (0, c)),
                pl.BlockSpec(memory_space=pl.ANY),
                pl.BlockSpec(memory_space=pl.ANY),
            ],
            out_specs=[
                pl.BlockSpec((tokens, q_cols), put),
                pl.BlockSpec((tokens, rope_cols), put),
            ],
        ),
        out_shape=[
            jax.ShapeDtypeStruct(q_full.shape, q_full.dtype),
            jax.ShapeDtypeStruct(rope_full.shape, rope_full.dtype),
        ],
        input_output_aliases={2: 0, 3: 1},
        compiler_params=pltpu.CompilerParams(vmem_limit_bytes=KERNEL_BYTES),
        cost_estimate=pl.CostEstimate(flops=0, bytes_accessed=4_000_000, transcendentals=0),
        name="place_columns",
    )(place, received, q_full, rope_full)


def stack_kernel(*refs, arrangement):
    outs = refs[len(refs) - len(arrangement) :]
    for out, sources in zip(outs, arrangement):
        row = 0
        for index, block in sources:
            piece = refs[index]
            columns = slice(block * out.shape[1], (block + 1) * out.shape[1])
            out[row : row + piece.shape[0], :] = piece[:, columns]
            row += piece.shape[0]


def stack(inputs, arrangement, columns):
    whole = lambda shape: pl.BlockSpec(shape, lambda: (0, 0))
    shapes = [(sum(inputs[i].shape[0] for i, _ in sources), columns) for sources in arrangement]
    return pl.pallas_call(
        functools.partial(stack_kernel, arrangement=arrangement),
        in_specs=[whole(array.shape) for array in inputs],
        out_specs=[whole(shape) for shape in shapes],
        out_shape=[jax.ShapeDtypeStruct(shape, inputs[0].dtype) for shape in shapes],
        compiler_params=pltpu.CompilerParams(vmem_limit_bytes=KERNEL_BYTES),
        cost_estimate=pl.CostEstimate(flops=0, bytes_accessed=2_000_000, transcendentals=0),
        name="stack",
    )(*inputs)


def join_rows_kernel(place, near, distant, near_crossed, distant_crossed, near_rows, distant_rows):
    rows = near.shape[0]
    for own, crossed, out in (
        (near, near_crossed, near_rows),
        (distant, distant_crossed, distant_rows),
    ):
        out[:rows, :] = own[...]
        out[rows:, :] = crossed[...]


def weight_parts(place, up_weight, crossed, chunks, far):
    rows = up_weight.shape[0]
    width = up_weight.shape[1] // chunks // 2

    def column_block(t):
        return pl.BlockSpec((rows, width), lambda i, place: (0, place[1 + t] * 2 + place[0]))

    shape = (2 * rows, width)
    return pl.pallas_call(
        join_rows_kernel,
        grid_spec=pltpu.PrefetchScalarGridSpec(
            num_scalar_prefetch=1,
            grid=(1,),
            in_specs=[column_block(t) for t in (0, far)] * 2,
            out_specs=[pl.BlockSpec(shape, lambda i, place: (0, 0))] * 2,
        ),
        out_shape=[jax.ShapeDtypeStruct(shape, up_weight.dtype)] * 2,
        compiler_params=pltpu.CompilerParams(vmem_limit_bytes=INPUT_BYTES),
        cost_estimate=pl.CostEstimate(flops=0, bytes_accessed=1_000_000, transcendentals=0),
        name="weight_parts",
    )(place, up_weight, up_weight, crossed, crossed)


def lay_kernel(place, *refs):
    *pieces, out = refs
    width = out.shape[1] // 4
    for step in range(len(pieces) // 2):
        early, late = pieces[2 * step], pieces[2 * step + 1]

        @pl.when(pl.program_id(0) == step)
        def _():
            for which in range(2):
                source = slice(which * width, (which + 1) * width)
                out[:, 2 * which * width : (2 * which + 1) * width] = early[:, source]
                out[:, (2 * which + 1) * width : (2 * which + 2) * width] = late[:, source]


def lay_out(place, pieces):
    rows, columns = pieces[0].shape
    count = len(pieces) // 2
    return pl.pallas_call(
        lay_kernel,
        grid_spec=pltpu.PrefetchScalarGridSpec(
            num_scalar_prefetch=1,
            grid=(count,),
            in_specs=[pl.BlockSpec(memory_space=pltpu.VMEM)] * len(pieces),
            out_specs=pl.BlockSpec((rows, 2 * columns), lambda t, place: (0, place[1 + t])),
        ),
        out_shape=jax.ShapeDtypeStruct((rows, count * 2 * columns), pieces[0].dtype),
        compiler_params=pltpu.CompilerParams(vmem_limit_bytes=KERNEL_BYTES),
        cost_estimate=pl.CostEstimate(flops=0, bytes_accessed=4_000_000, transcendentals=0),
        name="lay_out",
    )(place, *pieces)


def piece_kernel(place, kept, crossed, out):
    width = kept.shape[1]

    @pl.when(place[0] == 0)
    def _():
        out[:, :width] = kept[...]
        out[:, width:] = crossed[...]

    @pl.when(place[0] != 0)
    def _():
        out[:, :width] = crossed[...]
        out[:, width:] = kept[...]


def join_cores(place, kept, crossed):
    rows, columns = kept.shape
    return pl.pallas_call(
        piece_kernel,
        grid_spec=pltpu.PrefetchScalarGridSpec(
            num_scalar_prefetch=1,
            grid=(1,),
            in_specs=[pl.BlockSpec((rows, columns), lambda i, place: (0, 0))] * 2,
            out_specs=pl.BlockSpec((rows, 2 * columns), lambda i, place: (0, 0)),
        ),
        out_shape=jax.ShapeDtypeStruct((rows, 2 * columns), kept.dtype),
        compiler_params=pltpu.CompilerParams(vmem_limit_bytes=KERNEL_BYTES),
        cost_estimate=pl.CostEstimate(flops=0, bytes_accessed=500_000, transcendentals=0),
        name="join_cores",
    )(place, kept, crossed)


def halving_order(count):
    bits = count.bit_length() - 1
    partners = []
    for place in range(count):
        partner = place & 1
        for bit in range(1, bits):
            partner |= ((place >> (bits - bit)) & 1) << bit
        partners.append(partner)
    return partners


def channel_order(ctx, lat_block):
    channel = lax.broadcasted_iota(jnp.int32, (LAT, LAT), 0)
    place = lax.broadcasted_iota(jnp.int32, (LAT, LAT), 1)
    count = LAT // lat_block
    bits = count.bit_length() - 1
    block = place // lat_block
    partner = block & 1
    for bit in range(1, bits):
        partner |= ((block >> (bits - bit)) & 1) << bit
    return channel == (ctx ^ partner) * lat_block + place % lat_block


def block_sources(place, offered, per_block, span):
    ctx = place[place.shape[0] - 1]
    sources = []
    for side in range(2):
        group = ctx ^ side
        for at in range(per_block + len(partner_offsets)):
            matching = at - per_block
            offset = partner_offsets[matching] if matching >= 0 else 0
            source = group - offset
            usable = source >= 0
            sender = jnp.maximum(source, 0)
            inner = offered[sender, matching] if matching >= 0 else at
            start = jnp.where(usable, ((ctx >> 1) - (sender >> 1)) * span + inner * BLOCK, 0)
            block_id = jnp.where(usable, sender * per_block + inner, -2)
            sources.append(((offset + side) % 2, start, usable, block_id))
    return sources


def collect_kernel(place, offered, own, sib, cand, cand_t, rope_keys, bias, *, lat_block):
    ctx = place[place.shape[0] - 1]
    span = own.shape[0] // 3
    per_block = (span - 16) // BLOCK
    pieces = []
    key_at = lax.broadcasted_iota(jnp.int32, (BLOCK, 2 * BLOCK), 0)
    query = lax.broadcasted_iota(jnp.int32, (BLOCK, 2 * BLOCK), 1)
    causal = jnp.where(key_at <= query % BLOCK, 1.0, 0.0)
    sources = block_sources(place, offered, per_block, span)
    for block, (other, start, usable, block_id) in enumerate(sources):
        rows_ref = sib if other else own
        rows = rows_ref[pl.ds(pl.multiple_of(start, 16), BLOCK), :]
        pieces.append(jnp.where(usable, rows, jnp.zeros_like(rows)))
        side = block // (len(sources) // 2)
        lists = (sib if side else own)[span - 16 : span, :][:1].astype(jnp.int32)
        open_for = []
        for at in range(per_block):
            picks = [lists[:, at * TOPK + k : at * TOPK + k + 1] for k in range(TOPK)]
            picked = functools.reduce(
                jnp.maximum, [jnp.where(pick == block_id, 1.0, 0.0) for pick in picks]
            )
            same = jnp.where(block_id == (ctx ^ side) * per_block + at, 1.0, 0.0)
            open_for.append(jnp.maximum(picked, same * causal))
        allowed = jnp.where(query < BLOCK, open_for[0], open_for[1])
        bias[block * BLOCK : (block + 1) * BLOCK, :] = jnp.where(allowed > 0.5, 0.0, HIDDEN)
    both = jnp.concatenate(pieces, axis=0)
    order = channel_order(ctx, lat_block).astype(jnp.bfloat16)
    latent = both[:, :LAT]
    cand[...] = dot(latent, order, 1, 0).astype(jnp.bfloat16)
    cand_t[...] = dot(order, latent, 0, 1).astype(jnp.bfloat16)
    twice = lax.broadcasted_iota(jnp.int32, (ROPE, 2 * ROPE), 0)
    twice = twice == lax.broadcasted_iota(jnp.int32, (ROPE, 2 * ROPE), 1) % ROPE
    rope_keys[...] = dot(both[:, LAT:], twice.astype(jnp.bfloat16), 1, 0).astype(jnp.bfloat16)


def collect(place, offered, own, sib, rows, lat_block):
    bf16 = jnp.bfloat16
    shapes = [((rows, LAT), bf16), ((LAT, rows), bf16), ((rows, 2 * ROPE), bf16)]
    shapes.append(((rows, 2 * BLOCK), jnp.float32))
    whole = lambda shape: pl.BlockSpec(shape, lambda i, place, offered: (0, 0))
    return pl.pallas_call(
        functools.partial(collect_kernel, lat_block=lat_block),
        grid_spec=pltpu.PrefetchScalarGridSpec(
            num_scalar_prefetch=2,
            grid=(1,),
            in_specs=[whole(own.shape), whole(sib.shape)],
            out_specs=[whole(shape) for shape, _ in shapes],
        ),
        out_shape=[jax.ShapeDtypeStruct(shape, dtype) for shape, dtype in shapes],
        compiler_params=pltpu.CompilerParams(vmem_limit_bytes=KERNEL_BYTES),
        cost_estimate=pl.CostEstimate(
            flops=250_000_000, bytes_accessed=3_000_000, transcendentals=0
        ),
        name="collect",
    )(place, offered, own, sib)


def spread_kernel(place, offered, *refs, lat_block):
    *sums, own, sib = refs
    count = len(sums) // 2
    latent, rope = sums[0][...], sums[count][...]
    for index in range(1, count):
        latent, rope = latent + sums[index][...], rope + sums[count + index][...]
    order = channel_order(place[place.shape[0] - 1], lat_block).astype(jnp.float32)
    latent = lax.dot_general(
        latent,
        order,
        (((1,), (1,)), ((), ())),
        precision=lax.Precision.HIGHEST,
        preferred_element_type=jnp.float32,
    )
    rows = jnp.concatenate([latent, rope[:, :ROPE] + rope[:, ROPE:]], axis=1)
    own[...] = jnp.zeros_like(own)
    sib[...] = jnp.zeros_like(sib)
    span = own.shape[0] // 3
    sources = block_sources(place, offered, (span - 16) // BLOCK, span)
    for block, (other, start, _, _) in enumerate(sources):
        here = pl.ds(pl.multiple_of(start, 16), BLOCK)
        target = sib if other else own
        target[here, :] += rows[block * BLOCK : (block + 1) * BLOCK]


def spread(place, offered, latents, ropes, rows, lat_block):
    shape = (rows, LAT + ROPE)
    sums = [*latents, *ropes]
    whole = lambda shape: pl.BlockSpec(shape, lambda i, place, offered: (0, 0))
    return pl.pallas_call(
        functools.partial(spread_kernel, lat_block=lat_block),
        grid_spec=pltpu.PrefetchScalarGridSpec(
            num_scalar_prefetch=2,
            grid=(1,),
            in_specs=[whole(array.shape) for array in sums],
            out_specs=[whole(shape)] * 2,
        ),
        out_shape=[jax.ShapeDtypeStruct(shape, jnp.float32)] * 2,
        compiler_params=pltpu.CompilerParams(vmem_limit_bytes=KERNEL_BYTES),
        cost_estimate=pl.CostEstimate(
            flops=700_000_000, bytes_accessed=6_000_000, transcendentals=0
        ),
        name="spread",
    )(place, offered, *sums)


def halve(value, axis, bit):
    half = value.shape[0] // 2
    return value[:half] + exchange(value[half:], axis, bit)


def shards(q_nope, q_rope, grad_out, log_total, kv_latent, up_weight, selected, offered):
    n_dp, n_ctx = lax.axis_size("dp"), lax.axis_size("ctx")
    dp, ctx = lax.axis_index("dp"), lax.axis_index("ctx")
    core = ctx % 2
    group_len = kv_latent.shape[1]
    per_block = group_len // BLOCK
    heads = log_total.shape[1]
    part_heads = heads // n_dp // 2
    pairs = part_heads // 2
    part_cols = part_heads * (NOPE + VDIM)
    far = n_dp - 1
    lat_block = up_weight.shape[0]

    place = jnp.stack([core] + [dp ^ t for t in range(n_dp)] + [ctx]).astype(jnp.int32)

    crossed = exchange(up_weight, "ctx", 1)
    crossed, place, selected, offered, q_nope, q_rope, grad_out, log_total, kv_latent = (
        lax.optimization_barrier(
            (crossed, place, selected, offered, q_nope, q_rope, grad_out, log_total, kv_latent)
        )
    )
    chip_rows = weight_parts(place, up_weight, crossed, n_dp, far)
    own = [q_nope[0], q_rope[0], grad_out[0]]
    sibling = [exchange(array, "ctx", 1) for array in own]
    offered = offered[0]
    span = group_len + 16
    lists = selected[0].reshape(1, -1).astype(jnp.bfloat16)
    lists = jnp.pad(lists, ((0, 15), (0, LAT + ROPE - lists.shape[1])))
    bundle = after(jnp.concatenate([kv_latent[0], lists], axis=0), *sibling)
    bundles = [bundle, from_behind(bundle, "ctx", 2), from_behind(bundle, "ctx", 4)]
    own_bundles = stack(bundles, (((0, 0), (1, 0), (2, 0)),), LAT + ROPE)[0]
    sib_bundles = exchange(own_bundles, "ctx", 1)
    key_len = 2 * (group_len + len(partner_offsets) * BLOCK)
    shared = collect(place, offered, own_bundles, sib_bundles, key_len, lat_block)

    partners = halving_order(n_ctx)[::2]

    def over_chips(start):
        at_step = {0: start}
        for step in range(4, n_ctx, 4):
            at_step[step] = exchange(start, "ctx", step)
        at_step[2] = exchange(start, "ctx", 2)
        for step in range(4, n_ctx, 4):
            at_step[step + 2] = exchange(after(at_step[step], at_step[2]), "ctx", 2)
        return [at_step[partner] for partner in partners], at_step[n_ctx - 4]

    def joined(pieces):
        return stack(pieces, (tuple((index, 0) for index in range(len(pieces))),), part_cols)[0]

    near_pieces, last = over_chips(chip_rows[0])
    far_pieces, _ = over_chips(after(chip_rows[1], last))
    log_total = after(log_total, last)[0]
    sibling.append(exchange(log_total, "ctx", 1))
    own.append(log_total)
    for arrays in (own, sibling):
        arrays[3] = arrays[3].reshape(heads // 2, 2, group_len)

    weights = {0: joined([after(near_pieces[0], shared[0], sibling[3])] + near_pieces[1:])}
    for t in range(1, far):
        weights[t] = exchange(weights[0], "dp", t)
    earlier = None
    latents, ropes = [], []
    weight_grads = {t: ([], []) for t in range(n_dp)}
    bits = [1 << b for b in range(n_dp.bit_length() - 1)]
    orders = (bits, bits[::-1])
    first_sums = [{t: [] for t in range(n_dp) if t & order[0]} for order in orders]
    half_pairs = pairs // 2
    halved = lambda t: [(t, 0, half_pairs), (t, half_pairs, half_pairs)]
    units = [*halved(far)]
    units += [halved(t)[half] for half in range(2) for t in range(1, far)] + halved(0)
    for t, start, count in units:
        if t == far and not start:
            weights[far] = joined(far_pieces)
        weight = weights[t]
        if t == 0 and start:
            there = [piece for sent in first_sums for u in sent for piece in sent[u]]
            weight = after(weight, latents[-1], *there)
        if t == 1 and not start:
            weight = after(weight, *[weights[near] for near in range(2, far)])
        if t == far - 1:
            far_sums = [sent[far][1 if start else 0] for sent in first_sums]
            weight = after(weight, latents[-1], *far_sums)
        rest = chunk_backward(
            place,
            t,
            (start, count),
            own,
            sibling,
            weight,
            shared,
            earlier,
            (n_dp, pairs),
        )
        earlier = rest[:3]
        for side, sent in enumerate(first_sums):
            weight_grads[t][side].append(rest[3 + side])
            if t in sent:
                leaving = rest[3 + side]
                if t != far and start:
                    leaving = after(leaving, sent[t][0])
                sent[t].append(exchange(leaving, "dp", orders[side][0]))
        latents.append(rest[5])
        ropes.append(rest[6])

    half_cols = part_cols // 2

    def columns(pieces, half):
        if len(pieces) == 2:
            return pieces[half]
        return pieces[0][:, half * half_cols : (half + 1) * half_cols]

    def total(addends, half):
        return functools.reduce(
            lambda left, right: left + right, [columns(pieces, half) for pieces in addends]
        )

    sums = []
    last_sums = first_sums[1][far - 1]
    for side, order in enumerate(orders):
        addends = {t: [weight_grads[t][side]] for t in weight_grads}
        arrived = {t ^ order[0]: pieces for t, pieces in first_sums[side].items()}
        addends = {t: addends[t] + [more] for t, more in arrived.items()}
        for bit in order[1:]:
            arrived = {}
            for t in sorted((t for t in addends if t & bit), reverse=True):
                leaving = [total(addends[t], half) for half in range(2)]
                if side == 0:
                    behind = [(*first_sums[0][order[0]], last_sums[-1], latents[-2])] * 2
                else:
                    behind = [(weight_grads[far - 1][side][0],)] * 2
                leaving = [after(half, *there) for half, there in zip(leaving, behind)]
                arrived[t ^ bit] = [exchange(half, "dp", bit) for half in leaving]
            addends = {t: addends[t] + [more] for t, more in arrived.items()}
        sums.append(addends[0])

    q_full, rope_full, sib_grads = earlier
    received = exchange(sib_grads, "ctx", 1)
    grad_nope, grad_rope = place_columns(place, received, q_full, rope_full, n_dp)

    own_grads, sib_grads = spread(place, offered, latents, ropes, 3 * span, lat_block)
    swapped = exchange(sib_grads, "ctx", 1)
    grad_rows = own_grads + swapped
    ctx_bits = [1 << b for b in range(1, n_ctx.bit_length() - 1)]
    finished, arrived = [], None
    for half in range(2):
        if half:
            sums = [[[after(piece, arrived) for piece in pieces] for pieces in side] for side in sums]
        first, second = [total(side, half) for side in sums]
        arrived = exchange(after(second, sums[0][-1][half]), "ctx", ctx_bits[0])
        rows = first + arrived
        if half:
            rows = after(rows, received, swapped)
        for bit in ctx_bits[1:]:
            rows = halve(rows, "ctx", bit)
        kept, crossed = rows[:lat_block], exchange(rows[lat_block:], "ctx", 1)
        if half:
            kept = after(kept, *finished[0][1:])
        piece = join_cores(place, kept, crossed)
        finished.append([piece] + [exchange(piece, "dp", t) for t in range(1, n_dp)])

    grad_rows = after(grad_rows, rows)
    by_chip = [grad_rows[at * span : at * span + group_len] for at in range(3)]
    grad_rows = by_chip[0]
    for chips in (1, 2):
        grad_rows = grad_rows + from_behind(by_chip[chips], "ctx", -2 * chips)
    finished[0][0] = after(finished[0][0], grad_rows, grad_nope)
    grad_weight = lay_out(place, [piece for both in zip(*finished) for piece in both])
    return (grad_nope[None], grad_rope[None], grad_rows[None], grad_weight)


def solution(mesh):
    in_specs = (
        P("dp", "ctx", None),
        P("dp", "ctx", None),
        P("dp", "ctx", None),
        P("dp", None, "ctx"),
        P("dp", "ctx", None),
        P("ctx", None),
        P("dp", "ctx", None),
        P("dp", None, None),
    )
    out_specs = (P("dp", "ctx", None), P("dp", "ctx", None), P("dp", "ctx", None), P("ctx", None))
    return jax.shard_map(shards, mesh=mesh, in_specs=in_specs, out_specs=out_specs, check_vma=False)
```

```python
import functools

import jax
import jax.numpy as jnp
from jax import lax
from jax.experimental import pallas as pl
from jax.experimental.pallas import tpu as pltpu
from jax.sharding import PartitionSpec as P

LAT = 256
ROPE = 64
NOPE = 128
VDIM = 128
BLOCK = 64
TOPK = 3

partner_offsets = (1, 2, 3, 4)
HIDDEN = -1e30
KERNEL_BYTES = 12 * 1024 * 1024
INPUT_BYTES = 56 * 1024 * 1024


def from_behind(value, axis, steps):
    count = lax.axis_size(axis)
    initial, last = (max(0, -steps), min(count, count - steps))
    return lax.ppermute(value, axis, [(source, source + steps) for source in range(initial, last)])


def exchange(value, axis, bits):
    count = lax.axis_size(axis)
    return lax.ppermute(value, axis, [(source, source ^ bits) for source in range(count)])


def after(value, *earlier):
    return lax.optimization_barrier((value, *earlier))[0]


def dot(left, right, left_dim, right_dim):
    return lax.dot_general(
        left,
        right,
        (((left_dim,), (right_dim,)), ((), ())),
        preferred_element_type=jnp.float32,
    )


def heads_kernel(
    place,
    q_own, rope_own, out_own, tot_own,
    q_sib, rope_sib, out_sib, tot_sib,
    weight, cand, cand_t, rope_keys, bias,
    *rest,
    earlier,
):
    gq_own, gr_own, sib_grads, *weight_grads, lat_sum, rope_sum = rest[earlier:]
    scale = 1.0 / jnp.sqrt(jnp.float32(NOPE + ROPE))
    rows = cand.shape[0] // 2
    half = weight_grads[0].shape[0]
    sib_q, sib_rope = sib_grads.at[:, : 2 * NOPE], sib_grads.at[:, 2 * NOPE :]
    lane_half = lax.broadcasted_iota(jnp.int32, (rows, 2 * ROPE), 1) // ROPE

    @pl.when(pl.program_id(0) == 0)
    def _():
        lat_sum[...] = jnp.zeros_like(lat_sum)
        rope_sum[...] = jnp.zeros_like(rope_sum)

    groups = (
        (q_own, rope_own, out_own, tot_own, gq_own, gr_own),
        (q_sib, rope_sib, out_sib, tot_sib, sib_q, sib_rope),
    )
    rope_grads = [None, None]
    for head in range(2):
        columns = pl.ds(head * (NOPE + VDIM), NOPE + VDIM)
        head_weight = weight[:, columns]
        expanded = dot(cand[...], head_weight, 1, 0).astype(jnp.bfloat16)
        both_grads = []
        for side, (q_ref, rope_ref, out_ref, tot_ref, gq_ref, gr_ref) in enumerate(groups):
            own_rows = slice(side * rows, (side + 1) * rows)
            here = pl.ds(head * NOPE, NOPE)
            rope_part = jnp.where(
                lane_half == head, rope_keys[own_rows, :], jnp.zeros((), jnp.bfloat16)
            )
            keys = jnp.concatenate([expanded[own_rows, :NOPE], rope_part], axis=1)
            values = expanded[own_rows, NOPE:]
            queries = jnp.concatenate([q_ref[:, here], rope_ref[...]], axis=1)
            out_grads = out_ref[:, here]
            scores = dot(keys, queries, 1, 1) * scale
            probs = jnp.exp(scores - tot_ref[0, head : head + 1, :] + bias[own_rows, :])
            prob_grads = dot(values, out_grads, 1, 1)
            row_dot = jnp.sum(probs * prob_grads, axis=0, keepdims=True)
            score_grads = (probs * (prob_grads - row_dot)).astype(jnp.bfloat16)
            query_grad = dot(score_grads, keys, 0, 0) * scale
            gq_ref[:, here] = query_grad[:, :NOPE].astype(jnp.bfloat16)
            if head == 0:
                rope_grads[side] = query_grad[:, NOPE:]
            else:
                gr_ref[...] = (rope_grads[side] + query_grad[:, NOPE:]).astype(jnp.bfloat16)
            key_grad = dot(score_grads, queries, 1, 0) * scale
            value_grad = dot(probs.astype(jnp.bfloat16), out_grads, 1, 0)
            rope_sum[own_rows, :] += jnp.where(lane_half == head, key_grad[:, NOPE:], 0.0)
            both_grads.append(
                jnp.concatenate([key_grad[:, :NOPE], value_grad], axis=1).astype(jnp.bfloat16)
            )
        key_grads = jnp.concatenate(both_grads, axis=0)
        lat_sum[...] += dot(key_grads, head_weight, 1, 1)
        weight_grad = dot(cand_t[...], key_grads, 1, 0)
        weight_grads[0][:, columns] = weight_grad[:half]
        weight_grads[1][:, columns] = weight_grad[half:]


def chunk_backward(place, t, unit, own, sibling, weight, shared, earlier, sizes):
    q_own, rope_own, out_own, tot_own = own
    cand, cand_t, rope_keys, bias = shared
    tokens = q_own.shape[0]
    chunks, pairs = sizes
    wide, narrow = 2 * NOPE, 2 * ROPE
    first, count = unit
    mine = lambda p, place: (place[1 + t] * 2 + place[0]) * pairs + first + p
    theirs = lambda p, place: place[1 + t] * pairs + first + p
    whole = lambda array: pl.BlockSpec(array.shape, lambda p, place: (0, 0))
    in_specs = [
        pl.BlockSpec((tokens, wide), lambda p, place: (0, mine(p, place))),
        pl.BlockSpec((tokens, narrow), lambda p, place: (0, mine(p, place))),
        pl.BlockSpec((tokens, wide), lambda p, place: (0, mine(p, place))),
        pl.BlockSpec((1, 2, tokens), lambda p, place: (mine(p, place), 0, 0)),
    ] * 2 + [
        pl.BlockSpec((LAT, 2 * (NOPE + VDIM)), lambda p, place: (0, first + p)),
        whole(cand),
        whole(cand_t),
        whole(rope_keys),
        whole(bias),
    ]
    operands = [*own, *sibling, weight, cand, cand_t, rope_keys, bias]
    aliases = {}
    if earlier is not None:
        for index, array in enumerate(earlier):
            aliases[1 + len(operands)] = index
            in_specs.append(pl.BlockSpec(memory_space=pl.ANY))
            operands.append(array)
    columns = 2 * (NOPE + VDIM) * count
    bf16, f32 = jnp.bfloat16, jnp.float32
    out_shape = [
        jax.ShapeDtypeStruct(q_own.shape, bf16),
        jax.ShapeDtypeStruct(rope_own.shape, bf16),
        jax.ShapeDtypeStruct((tokens, chunks * pairs * (wide + narrow)), bf16),
        *[jax.ShapeDtypeStruct((LAT // 2, columns), f32)] * 2,
        jax.ShapeDtypeStruct((cand.shape[0], LAT), f32),
        jax.ShapeDtypeStruct((cand.shape[0], narrow), f32),
    ]
    out_specs = [
        pl.BlockSpec((tokens, wide), lambda p, place: (0, mine(p, place))),
        pl.BlockSpec((tokens, narrow), lambda p, place: (0, mine(p, place))),
        pl.BlockSpec((tokens, wide + narrow), lambda p, place: (0, theirs(p, place))),
        *[pl.BlockSpec((LAT // 2, 2 * (NOPE + VDIM)), lambda p, place: (0, p))] * 2,
        pl.BlockSpec((cand.shape[0], LAT), lambda p, place: (0, 0)),
        pl.BlockSpec((cand.shape[0], narrow), lambda p, place: (0, 0)),
    ]
    return pl.pallas_call(
        functools.partial(heads_kernel, earlier=len(aliases)),
        grid_spec=pltpu.PrefetchScalarGridSpec(
            num_scalar_prefetch=1, grid=(count,), in_specs=in_specs, out_specs=out_specs
        ),
        out_shape=out_shape,
        input_output_aliases=aliases,
        compiler_params=pltpu.CompilerParams(vmem_limit_bytes=KERNEL_BYTES),
        cost_estimate=pl.CostEstimate(
            flops=count * 1_000_000_000, bytes_accessed=count * 300_000, transcendentals=0
        ),
        name="heads_backward",
    )(place, *operands)


def place_kernel(place, received, q_in, rope_in, q_out, rope_out):
    wide, narrow = 2 * NOPE, 2 * ROPE
    for pair in range(q_out.shape[1] // wide):
        start = pair * (wide + narrow)
        q_out[:, pair * wide : (pair + 1) * wide] = received[:, start : start + wide]
        rope_out[:, pair * narrow : (pair + 1) * narrow] = received[
            :, start + wide : start + wide + narrow
        ]


def place_columns(place, received, q_full, rope_full, chunks):
    tokens = q_full.shape[0]
    q_cols, rope_cols = q_full.shape[1] // chunks // 2, rope_full.shape[1] // chunks // 2
    put = lambda c, place: (0, c * 2 + 1 - place[0])
    return pl.pallas_call(
        place_kernel,
        grid_spec=pltpu.PrefetchScalarGridSpec(
            num_scalar_prefetch=1,
            grid=(chunks,),
            in_specs=[
                pl.BlockSpec((tokens, q_cols + rope_cols), lambda c, place: (0, c)),
                pl.BlockSpec(memory_space=pl.ANY),
                pl.BlockSpec(memory_space=pl.ANY),
            ],
            out_specs=[
                pl.BlockSpec((tokens, q_cols), put),
                pl.BlockSpec((tokens, rope_cols), put),
            ],
        ),
        out_shape=[
            jax.ShapeDtypeStruct(q_full.shape, q_full.dtype),
            jax.ShapeDtypeStruct(rope_full.shape, rope_full.dtype),
        ],
        input_output_aliases={2: 0, 3: 1},
        compiler_params=pltpu.CompilerParams(vmem_limit_bytes=KERNEL_BYTES),
        cost_estimate=pl.CostEstimate(flops=0, bytes_accessed=4_000_000, transcendentals=0),
        name="place_columns",
    )(place, received, q_full, rope_full)


def stack_kernel(*refs, arrangement):
    outs = refs[len(refs) - len(arrangement) :]
    for out, sources in zip(outs, arrangement):
        row = 0
        for index, block in sources:
            piece = refs[index]
            columns = slice(block * out.shape[1], (block + 1) * out.shape[1])
            out[row : row + piece.shape[0], :] = piece[:, columns]
            row += piece.shape[0]


def stack(inputs, arrangement, columns):
    whole = lambda shape: pl.BlockSpec(shape, lambda: (0, 0))
    shapes = [(sum(inputs[i].shape[0] for i, _ in sources), columns) for sources in arrangement]
    return pl.pallas_call(
        functools.partial(stack_kernel, arrangement=arrangement),
        in_specs=[whole(array.shape) for array in inputs],
        out_specs=[whole(shape) for shape in shapes],
        out_shape=[jax.ShapeDtypeStruct(shape, inputs[0].dtype) for shape in shapes],
        compiler_params=pltpu.CompilerParams(vmem_limit_bytes=KERNEL_BYTES),
        cost_estimate=pl.CostEstimate(flops=0, bytes_accessed=2_000_000, transcendentals=0),
        name="stack",
    )(*inputs)


def join_rows_kernel(place, near, distant, near_crossed, distant_crossed, near_rows, distant_rows):
    rows = near.shape[0]
    for own, crossed, out in (
        (near, near_crossed, near_rows),
        (distant, distant_crossed, distant_rows),
    ):
        out[:rows, :] = own[...]
        out[rows:, :] = crossed[...]


def weight_parts(place, up_weight, crossed, chunks, far):
    rows = up_weight.shape[0]
    width = up_weight.shape[1] // chunks // 2

    def column_block(t):
        return pl.BlockSpec((rows, width), lambda i, place: (0, place[1 + t] * 2 + place[0]))

    shape = (2 * rows, width)
    return pl.pallas_call(
        join_rows_kernel,
        grid_spec=pltpu.PrefetchScalarGridSpec(
            num_scalar_prefetch=1,
            grid=(1,),
            in_specs=[column_block(t) for t in (0, far)] * 2,
            out_specs=[pl.BlockSpec(shape, lambda i, place: (0, 0))] * 2,
        ),
        out_shape=[jax.ShapeDtypeStruct(shape, up_weight.dtype)] * 2,
        compiler_params=pltpu.CompilerParams(vmem_limit_bytes=INPUT_BYTES),
        cost_estimate=pl.CostEstimate(flops=0, bytes_accessed=1_000_000, transcendentals=0),
        name="weight_parts",
    )(place, up_weight, up_weight, crossed, crossed)


def lay_kernel(place, *refs):
    *pieces, out = refs
    width = out.shape[1] // 4
    for step in range(len(pieces) // 2):
        early, late = pieces[2 * step], pieces[2 * step + 1]

        @pl.when(pl.program_id(0) == step)
        def _():
            for which in range(2):
                source = slice(which * width, (which + 1) * width)
                out[:, 2 * which * width : (2 * which + 1) * width] = early[:, source]
                out[:, (2 * which + 1) * width : (2 * which + 2) * width] = late[:, source]


def lay_out(place, pieces):
    rows, columns = pieces[0].shape
    count = len(pieces) // 2
    return pl.pallas_call(
        lay_kernel,
        grid_spec=pltpu.PrefetchScalarGridSpec(
            num_scalar_prefetch=1,
            grid=(count,),
            in_specs=[pl.BlockSpec(memory_space=pltpu.VMEM)] * len(pieces),
            out_specs=pl.BlockSpec((rows, 2 * columns), lambda t, place: (0, place[1 + t])),
        ),
        out_shape=jax.ShapeDtypeStruct((rows, count * 2 * columns), pieces[0].dtype),
        compiler_params=pltpu.CompilerParams(vmem_limit_bytes=KERNEL_BYTES),
        cost_estimate=pl.CostEstimate(flops=0, bytes_accessed=4_000_000, transcendentals=0),
        name="lay_out",
    )(place, *pieces)


def piece_kernel(place, kept, crossed, out):
    width = kept.shape[1]

    @pl.when(place[0] == 0)
    def _():
        out[:, :width] = kept[...]
        out[:, width:] = crossed[...]

    @pl.when(place[0] != 0)
    def _():
        out[:, :width] = crossed[...]
        out[:, width:] = kept[...]


def join_cores(place, kept, crossed):
    rows, columns = kept.shape
    return pl.pallas_call(
        piece_kernel,
        grid_spec=pltpu.PrefetchScalarGridSpec(
            num_scalar_prefetch=1,
            grid=(1,),
            in_specs=[pl.BlockSpec((rows, columns), lambda i, place: (0, 0))] * 2,
            out_specs=pl.BlockSpec((rows, 2 * columns), lambda i, place: (0, 0)),
        ),
        out_shape=jax.ShapeDtypeStruct((rows, 2 * columns), kept.dtype),
        compiler_params=pltpu.CompilerParams(vmem_limit_bytes=KERNEL_BYTES),
        cost_estimate=pl.CostEstimate(flops=0, bytes_accessed=500_000, transcendentals=0),
        name="join_cores",
    )(place, kept, crossed)


def halving_order(count):
    bits = count.bit_length() - 1
    partners = []
    for place in range(count):
        partner = place & 1
        for bit in range(1, bits):
            partner |= ((place >> (bits - bit)) & 1) << bit
        partners.append(partner)
    return partners


def channel_order(ctx, lat_block):
    channel = lax.broadcasted_iota(jnp.int32, (LAT, LAT), 0)
    place = lax.broadcasted_iota(jnp.int32, (LAT, LAT), 1)
    count = LAT // lat_block
    bits = count.bit_length() - 1
    block = place // lat_block
    partner = block & 1
    for bit in range(1, bits):
        partner |= ((block >> (bits - bit)) & 1) << bit
    return channel == (ctx ^ partner) * lat_block + place % lat_block


def block_sources(place, offered, per_block, span):
    ctx = place[place.shape[0] - 1]
    sources = []
    for side in range(2):
        group = ctx ^ side
        for at in range(per_block + len(partner_offsets)):
            matching = at - per_block
            offset = partner_offsets[matching] if matching >= 0 else 0
            source = group - offset
            usable = source >= 0
            sender = jnp.maximum(source, 0)
            inner = offered[sender, matching] if matching >= 0 else at
            start = jnp.where(usable, ((ctx >> 1) - (sender >> 1)) * span + inner * BLOCK, 0)
            block_id = jnp.where(usable, sender * per_block + inner, -2)
            sources.append(((offset + side) % 2, start, usable, block_id))
    return sources


def collect_kernel(place, offered, own, sib, cand, cand_t, rope_keys, bias, *, lat_block):
    ctx = place[place.shape[0] - 1]
    span = own.shape[0] // 3
    per_block = (span - 16) // BLOCK
    pieces = []
    key_at = lax.broadcasted_iota(jnp.int32, (BLOCK, 2 * BLOCK), 0)
    query = lax.broadcasted_iota(jnp.int32, (BLOCK, 2 * BLOCK), 1)
    causal = jnp.where(key_at <= query % BLOCK, 1.0, 0.0)
    sources = block_sources(place, offered, per_block, span)
    for block, (other, start, usable, block_id) in enumerate(sources):
        rows_ref = sib if other else own
        rows = rows_ref[pl.ds(pl.multiple_of(start, 16), BLOCK), :]
        pieces.append(jnp.where(usable, rows, jnp.zeros_like(rows)))
        side = block // (len(sources) // 2)
        lists = (sib if side else own)[span - 16 : span, :][:1].astype(jnp.int32)
        open_for = []
        for at in range(per_block):
            picks = [lists[:, at * TOPK + k : at * TOPK + k + 1] for k in range(TOPK)]
            picked = functools.reduce(
                jnp.maximum, [jnp.where(pick == block_id, 1.0, 0.0) for pick in picks]
            )
            same = jnp.where(block_id == (ctx ^ side) * per_block + at, 1.0, 0.0)
            open_for.append(jnp.maximum(picked, same * causal))
        allowed = jnp.where(query < BLOCK, open_for[0], open_for[1])
        bias[block * BLOCK : (block + 1) * BLOCK, :] = jnp.where(allowed > 0.5, 0.0, HIDDEN)
    both = jnp.concatenate(pieces, axis=0)
    order = channel_order(ctx, lat_block).astype(jnp.bfloat16)
    latent = both[:, :LAT]
    cand[...] = dot(latent, order, 1, 0).astype(jnp.bfloat16)
    cand_t[...] = dot(order, latent, 0, 1).astype(jnp.bfloat16)
    twice = lax.broadcasted_iota(jnp.int32, (ROPE, 2 * ROPE), 0)
    twice = twice == lax.broadcasted_iota(jnp.int32, (ROPE, 2 * ROPE), 1) % ROPE
    rope_keys[...] = dot(both[:, LAT:], twice.astype(jnp.bfloat16), 1, 0).astype(jnp.bfloat16)


def collect(place, offered, own, sib, rows, lat_block):
    bf16 = jnp.bfloat16
    shapes = [((rows, LAT), bf16), ((LAT, rows), bf16), ((rows, 2 * ROPE), bf16)]
    shapes.append(((rows, 2 * BLOCK), jnp.float32))
    whole = lambda shape: pl.BlockSpec(shape, lambda i, place, offered: (0, 0))
    return pl.pallas_call(
        functools.partial(collect_kernel, lat_block=lat_block),
        grid_spec=pltpu.PrefetchScalarGridSpec(
            num_scalar_prefetch=2,
            grid=(1,),
            in_specs=[whole(own.shape), whole(sib.shape)],
            out_specs=[whole(shape) for shape, _ in shapes],
        ),
        out_shape=[jax.ShapeDtypeStruct(shape, dtype) for shape, dtype in shapes],
        compiler_params=pltpu.CompilerParams(vmem_limit_bytes=KERNEL_BYTES),
        cost_estimate=pl.CostEstimate(
            flops=250_000_000, bytes_accessed=3_000_000, transcendentals=0
        ),
        name="collect",
    )(place, offered, own, sib)


def spread_kernel(place, offered, *refs, lat_block):
    *sums, own, sib = refs
    count = len(sums) // 2
    latent, rope = sums[0][...], sums[count][...]
    for index in range(1, count):
        latent, rope = latent + sums[index][...], rope + sums[count + index][...]
    order = channel_order(place[place.shape[0] - 1], lat_block).astype(jnp.float32)
    latent = lax.dot_general(
        latent,
        order,
        (((1,), (1,)), ((), ())),
        precision=lax.Precision.HIGHEST,
        preferred_element_type=jnp.float32,
    )
    rows = jnp.concatenate([latent, rope[:, :ROPE] + rope[:, ROPE:]], axis=1)
    own[...] = jnp.zeros_like(own)
    sib[...] = jnp.zeros_like(sib)
    span = own.shape[0] // 3
    sources = block_sources(place, offered, (span - 16) // BLOCK, span)
    for block, (other, start, _, _) in enumerate(sources):
        here = pl.ds(pl.multiple_of(start, 16), BLOCK)
        target = sib if other else own
        target[here, :] += rows[block * BLOCK : (block + 1) * BLOCK]


def spread(place, offered, latents, ropes, rows, lat_block):
    shape = (rows, LAT + ROPE)
    sums = [*latents, *ropes]
    whole = lambda shape: pl.BlockSpec(shape, lambda i, place, offered: (0, 0))
    return pl.pallas_call(
        functools.partial(spread_kernel, lat_block=lat_block),
        grid_spec=pltpu.PrefetchScalarGridSpec(
            num_scalar_prefetch=2,
            grid=(1,),
            in_specs=[whole(array.shape) for array in sums],
            out_specs=[whole(shape)] * 2,
        ),
        out_shape=[jax.ShapeDtypeStruct(shape, jnp.float32)] * 2,
        compiler_params=pltpu.CompilerParams(vmem_limit_bytes=KERNEL_BYTES),
        cost_estimate=pl.CostEstimate(
            flops=700_000_000, bytes_accessed=6_000_000, transcendentals=0
        ),
        name="spread",
    )(place, offered, *sums)


def halve(value, axis, bit):
    half = value.shape[0] // 2
    return value[:half] + exchange(value[half:], axis, bit)


def shards(q_nope, q_rope, grad_out, log_total, kv_latent, up_weight, selected, offered):
    n_dp, n_ctx = lax.axis_size("dp"), lax.axis_size("ctx")
    dp, ctx = lax.axis_index("dp"), lax.axis_index("ctx")
    core = ctx % 2
    group_len = kv_latent.shape[1]
    per_block = group_len // BLOCK
    heads = log_total.shape[1]
    part_heads = heads // n_dp // 2
    pairs = part_heads // 2
    part_cols = part_heads * (NOPE + VDIM)
    far = n_dp - 1
    lat_block = up_weight.shape[0]

    place = jnp.stack([core] + [dp ^ t for t in range(n_dp)] + [ctx]).astype(jnp.int32)

    crossed = exchange(up_weight, "ctx", 1)
    crossed, place, selected, offered, q_nope, q_rope, grad_out, log_total, kv_latent = (
        lax.optimization_barrier(
            (crossed, place, selected, offered, q_nope, q_rope, grad_out, log_total, kv_latent)
        )
    )
    chip_rows = weight_parts(place, up_weight, crossed, n_dp, far)
    own = [q_nope[0], q_rope[0], grad_out[0]]
    sibling = [exchange(array, "ctx", 1) for array in own]
    offered = offered[0]
    span = group_len + 16
    lists = selected[0].reshape(1, -1).astype(jnp.bfloat16)
    lists = jnp.pad(lists, ((0, 15), (0, LAT + ROPE - lists.shape[1])))
    bundle = after(jnp.concatenate([kv_latent[0], lists], axis=0), *sibling)
    bundles = [bundle, from_behind(bundle, "ctx", 2), from_behind(bundle, "ctx", 4)]
    own_bundles = stack(bundles, (((0, 0), (1, 0), (2, 0)),), LAT + ROPE)[0]
    sib_bundles = exchange(own_bundles, "ctx", 1)
    key_len = 2 * (group_len + len(partner_offsets) * BLOCK)
    shared = collect(place, offered, own_bundles, sib_bundles, key_len, lat_block)

    partners = halving_order(n_ctx)[::2]

    def over_chips(start):
        at_step = {0: start}
        for step in range(4, n_ctx, 4):
            at_step[step] = exchange(start, "ctx", step)
        at_step[2] = exchange(start, "ctx", 2)
        for step in range(4, n_ctx, 4):
            at_step[step + 2] = exchange(after(at_step[step], at_step[2]), "ctx", 2)
        return [at_step[partner] for partner in partners], at_step[n_ctx - 4]

    def joined(pieces):
        return stack(pieces, (tuple((index, 0) for index in range(len(pieces))),), part_cols)[0]

    near_pieces, last = over_chips(chip_rows[0])
    far_pieces, _ = over_chips(after(chip_rows[1], last))
    log_total = after(log_total, last)[0]
    sibling.append(exchange(log_total, "ctx", 1))
    own.append(log_total)
    for arrays in (own, sibling):
        arrays[3] = arrays[3].reshape(heads // 2, 2, group_len)

    weights = {0: joined([after(near_pieces[0], shared[0], sibling[3])] + near_pieces[1:])}
    for t in range(1, far):
        weights[t] = exchange(weights[0], "dp", t)
    earlier = None
    latents, ropes = [], []
    weight_grads = {t: ([], []) for t in range(n_dp)}
    bits = [1 << b for b in range(n_dp.bit_length() - 1)]
    orders = (bits, bits[::-1])
    first_sums = [{t: [] for t in range(n_dp) if t & order[0]} for order in orders]
    half_pairs = pairs // 2
    units = [(t, 0, pairs) for t in [far] + list(range(1, far - 1))]
    units += [(t, start, half_pairs) for t in (far - 1, 0) for start in (0, half_pairs)]
    for t, start, count in units:
        if t == far:
            weights[far] = joined(far_pieces)
        weight = weights[t]
        if t == 0 and start:
            there = [piece for sent in first_sums for u in sent for piece in sent[u]]
            weight = after(weight, latents[-1], *there)
        if t == 1 and not start:
            weight = after(weight, *[weights[near] for near in range(2, far)])
        if t == far - 1 and start:
            weight = after(weight, latents[-1], *[sent[far][0] for sent in first_sums])
        rest = chunk_backward(
            place,
            t,
            (start, count),
            own,
            sibling,
            weight,
            shared,
            earlier,
            (n_dp, pairs),
        )
        earlier = rest[:3]
        for side, sent in enumerate(first_sums):
            weight_grads[t][side].append(rest[3 + side])
            if t in sent:
                sent[t].append(exchange(rest[3 + side], "dp", orders[side][0]))
        latents.append(rest[5])
        ropes.append(rest[6])

    half_cols = part_cols // 2

    def columns(pieces, half):
        if len(pieces) == 2:
            return pieces[half]
        return pieces[0][:, half * half_cols : (half + 1) * half_cols]

    def total(addends, half):
        return functools.reduce(
            lambda left, right: left + right, [columns(pieces, half) for pieces in addends]
        )

    sums = []
    last_sums = first_sums[1][far - 1]
    for side, order in enumerate(orders):
        addends = {t: [weight_grads[t][side]] for t in weight_grads}
        arrived = {t ^ order[0]: pieces for t, pieces in first_sums[side].items()}
        addends = {t: addends[t] + [more] for t, more in arrived.items()}
        for bit in order[1:]:
            arrived = {}
            for t in sorted((t for t in addends if t & bit), reverse=True):
                leaving = [total(addends[t], half) for half in range(2)]
                if side == 0:
                    behind = [(first_sums[0][order[0]][0], last_sums[-1], latents[-2])] * 2
                else:
                    behind = [(weight_grads[far - 1][side][0],)] * 2
                leaving = [after(half, *there) for half, there in zip(leaving, behind)]
                arrived[t ^ bit] = [exchange(half, "dp", bit) for half in leaving]
            addends = {t: addends[t] + [more] for t, more in arrived.items()}
        sums.append(addends[0])

    q_full, rope_full, sib_grads = earlier
    received = exchange(sib_grads, "ctx", 1)
    grad_nope, grad_rope = place_columns(place, received, q_full, rope_full, n_dp)

    own_grads, sib_grads = spread(place, offered, latents, ropes, 3 * span, lat_block)
    swapped = exchange(sib_grads, "ctx", 1)
    grad_rows = own_grads + swapped
    ctx_bits = [1 << b for b in range(1, n_ctx.bit_length() - 1)]
    finished, arrived = [], None
    for half in range(2):
        if half:
            sums = [[[after(piece, arrived) for piece in pieces] for pieces in side] for side in sums]
        first, second = [total(side, half) for side in sums]
        arrived = exchange(after(second, sums[0][-1][half]), "ctx", ctx_bits[0])
        rows = first + arrived
        if half:
            rows = after(rows, received, swapped)
        for bit in ctx_bits[1:]:
            rows = halve(rows, "ctx", bit)
        kept, crossed = rows[:lat_block], exchange(rows[lat_block:], "ctx", 1)
        if half:
            kept = after(kept, *finished[0][1:])
        piece = join_cores(place, kept, crossed)
        finished.append([piece] + [exchange(piece, "dp", t) for t in range(1, n_dp)])

    grad_rows = after(grad_rows, rows)
    by_chip = [grad_rows[at * span : at * span + group_len] for at in range(3)]
    grad_rows = by_chip[0]
    for chips in (1, 2):
        grad_rows = grad_rows + from_behind(by_chip[chips], "ctx", -2 * chips)
    finished[0][0] = after(finished[0][0], grad_rows, grad_nope)
    grad_weight = lay_out(place, [piece for both in zip(*finished) for piece in both])
    return (grad_nope[None], grad_rope[None], grad_rows[None], grad_weight)


def solution(mesh):
    in_specs = (
        P("dp", "ctx", None),
        P("dp", "ctx", None),
        P("dp", "ctx", None),
        P("dp", None, "ctx"),
        P("dp", "ctx", None),
        P("ctx", None),
        P("dp", "ctx", None),
        P("dp", None, None),
    )
    out_specs = (P("dp", "ctx", None), P("dp", "ctx", None), P("dp", "ctx", None), P("ctx", None))
    return jax.shard_map(shards, mesh=mesh, in_specs=in_specs, out_specs=out_specs, check_vma=False)
```

```python
import functools

import jax
import jax.numpy as jnp
from jax import lax
from jax.experimental import pallas as pl
from jax.experimental.pallas import tpu as pltpu
from jax.sharding import PartitionSpec as P

LAT = 256
ROPE = 64
NOPE = 128
VDIM = 128
BLOCK = 64
TOPK = 3

partner_offsets = (1, 2, 3, 4)
HIDDEN = -1e30
KERNEL_BYTES = 12 * 1024 * 1024
INPUT_BYTES = 56 * 1024 * 1024


def from_behind(value, axis, steps):
    count = lax.axis_size(axis)
    initial, last = (max(0, -steps), min(count, count - steps))
    return lax.ppermute(value, axis, [(source, source + steps) for source in range(initial, last)])


def exchange(value, axis, bits):
    count = lax.axis_size(axis)
    return lax.ppermute(value, axis, [(source, source ^ bits) for source in range(count)])


def after(value, *earlier):
    return lax.optimization_barrier((value, *earlier))[0]


def dot(left, right, left_dim, right_dim):
    return lax.dot_general(
        left,
        right,
        (((left_dim,), (right_dim,)), ((), ())),
        preferred_element_type=jnp.float32,
    )


def heads_kernel(
    place,
    q_own, rope_own, out_own, tot_own,
    q_sib, rope_sib, out_sib, tot_sib,
    weight, cand, cand_t, rope_keys, bias,
    *rest,
    earlier,
):
    gq_own, gr_own, sib_grads, *weight_grads, lat_sum, rope_sum = rest[earlier:]
    scale = 1.0 / jnp.sqrt(jnp.float32(NOPE + ROPE))
    rows = cand.shape[0] // 2
    half = weight_grads[0].shape[0]
    sib_q, sib_rope = sib_grads.at[:, : 2 * NOPE], sib_grads.at[:, 2 * NOPE :]
    lane_half = lax.broadcasted_iota(jnp.int32, (rows, 2 * ROPE), 1) // ROPE

    @pl.when(pl.program_id(0) == 0)
    def _():
        lat_sum[...] = jnp.zeros_like(lat_sum)
        rope_sum[...] = jnp.zeros_like(rope_sum)

    groups = (
        (q_own, rope_own, out_own, tot_own, gq_own, gr_own),
        (q_sib, rope_sib, out_sib, tot_sib, sib_q, sib_rope),
    )
    rope_grads = [None, None]
    for head in range(2):
        columns = pl.ds(head * (NOPE + VDIM), NOPE + VDIM)
        head_weight = weight[:, columns]
        expanded = dot(cand[...], head_weight, 1, 0).astype(jnp.bfloat16)
        both_grads = []
        for side, (q_ref, rope_ref, out_ref, tot_ref, gq_ref, gr_ref) in enumerate(groups):
            own_rows = slice(side * rows, (side + 1) * rows)
            here = pl.ds(head * NOPE, NOPE)
            rope_part = jnp.where(
                lane_half == head, rope_keys[own_rows, :], jnp.zeros((), jnp.bfloat16)
            )
            keys = jnp.concatenate([expanded[own_rows, :NOPE], rope_part], axis=1)
            values = expanded[own_rows, NOPE:]
            queries = jnp.concatenate([q_ref[:, here], rope_ref[...]], axis=1)
            out_grads = out_ref[:, here]
            scores = dot(keys, queries, 1, 1) * scale
            probs = jnp.exp(scores - tot_ref[0, head : head + 1, :] + bias[own_rows, :])
            prob_grads = dot(values, out_grads, 1, 1)
            row_dot = jnp.sum(probs * prob_grads, axis=0, keepdims=True)
            score_grads = (probs * (prob_grads - row_dot)).astype(jnp.bfloat16)
            query_grad = dot(score_grads, keys, 0, 0) * scale
            gq_ref[:, here] = query_grad[:, :NOPE].astype(jnp.bfloat16)
            if head == 0:
                rope_grads[side] = query_grad[:, NOPE:]
            else:
                gr_ref[...] = (rope_grads[side] + query_grad[:, NOPE:]).astype(jnp.bfloat16)
            key_grad = dot(score_grads, queries, 1, 0) * scale
            value_grad = dot(probs.astype(jnp.bfloat16), out_grads, 1, 0)
            rope_sum[own_rows, :] += jnp.where(lane_half == head, key_grad[:, NOPE:], 0.0)
            both_grads.append(
                jnp.concatenate([key_grad[:, :NOPE], value_grad], axis=1).astype(jnp.bfloat16)
            )
        key_grads = jnp.concatenate(both_grads, axis=0)
        lat_sum[...] += dot(key_grads, head_weight, 1, 1)
        weight_grad = dot(cand_t[...], key_grads, 1, 0)
        weight_grads[0][:, columns] = weight_grad[:half]
        weight_grads[1][:, columns] = weight_grad[half:]


def chunk_backward(place, t, unit, own, sibling, weight, shared, earlier, sizes):
    q_own, rope_own, out_own, tot_own = own
    cand, cand_t, rope_keys, bias = shared
    tokens = q_own.shape[0]
    chunks, pairs = sizes
    wide, narrow = 2 * NOPE, 2 * ROPE
    first, count = unit
    mine = lambda p, place: (place[1 + t] * 2 + place[0]) * pairs + first + p
    theirs = lambda p, place: place[1 + t] * pairs + first + p
    whole = lambda array: pl.BlockSpec(array.shape, lambda p, place: (0, 0))
    in_specs = [
        pl.BlockSpec((tokens, wide), lambda p, place: (0, mine(p, place))),
        pl.BlockSpec((tokens, narrow), lambda p, place: (0, mine(p, place))),
        pl.BlockSpec((tokens, wide), lambda p, place: (0, mine(p, place))),
        pl.BlockSpec((1, 2, tokens), lambda p, place: (mine(p, place), 0, 0)),
    ] * 2 + [
        pl.BlockSpec((LAT, 2 * (NOPE + VDIM)), lambda p, place: (0, first + p)),
        whole(cand),
        whole(cand_t),
        whole(rope_keys),
        whole(bias),
    ]
    operands = [*own, *sibling, weight, cand, cand_t, rope_keys, bias]
    aliases = {}
    if earlier is not None:
        for index, array in enumerate(earlier):
            aliases[1 + len(operands)] = index
            in_specs.append(pl.BlockSpec(memory_space=pl.ANY))
            operands.append(array)
    columns = 2 * (NOPE + VDIM) * count
    bf16, f32 = jnp.bfloat16, jnp.float32
    out_shape = [
        jax.ShapeDtypeStruct(q_own.shape, bf16),
        jax.ShapeDtypeStruct(rope_own.shape, bf16),
        jax.ShapeDtypeStruct((tokens, chunks * pairs * (wide + narrow)), bf16),
        *[jax.ShapeDtypeStruct((LAT // 2, columns), f32)] * 2,
        jax.ShapeDtypeStruct((cand.shape[0], LAT), f32),
        jax.ShapeDtypeStruct((cand.shape[0], narrow), f32),
    ]
    out_specs = [
        pl.BlockSpec((tokens, wide), lambda p, place: (0, mine(p, place))),
        pl.BlockSpec((tokens, narrow), lambda p, place: (0, mine(p, place))),
        pl.BlockSpec((tokens, wide + narrow), lambda p, place: (0, theirs(p, place))),
        *[pl.BlockSpec((LAT // 2, 2 * (NOPE + VDIM)), lambda p, place: (0, p))] * 2,
        pl.BlockSpec((cand.shape[0], LAT), lambda p, place: (0, 0)),
        pl.BlockSpec((cand.shape[0], narrow), lambda p, place: (0, 0)),
    ]
    return pl.pallas_call(
        functools.partial(heads_kernel, earlier=len(aliases)),
        grid_spec=pltpu.PrefetchScalarGridSpec(
            num_scalar_prefetch=1, grid=(count,), in_specs=in_specs, out_specs=out_specs
        ),
        out_shape=out_shape,
        input_output_aliases=aliases,
        compiler_params=pltpu.CompilerParams(vmem_limit_bytes=KERNEL_BYTES),
        cost_estimate=pl.CostEstimate(
            flops=count * 1_000_000_000, bytes_accessed=count * 300_000, transcendentals=0
        ),
        name="heads_backward",
    )(place, *operands)


def place_kernel(place, received, q_in, rope_in, q_out, rope_out):
    wide, narrow = 2 * NOPE, 2 * ROPE
    for pair in range(q_out.shape[1] // wide):
        start = pair * (wide + narrow)
        q_out[:, pair * wide : (pair + 1) * wide] = received[:, start : start + wide]
        rope_out[:, pair * narrow : (pair + 1) * narrow] = received[
            :, start + wide : start + wide + narrow
        ]


def place_columns(place, received, q_full, rope_full, chunks):
    tokens = q_full.shape[0]
    q_cols, rope_cols = q_full.shape[1] // chunks // 2, rope_full.shape[1] // chunks // 2
    put = lambda c, place: (0, c * 2 + 1 - place[0])
    return pl.pallas_call(
        place_kernel,
        grid_spec=pltpu.PrefetchScalarGridSpec(
            num_scalar_prefetch=1,
            grid=(chunks,),
            in_specs=[
                pl.BlockSpec((tokens, q_cols + rope_cols), lambda c, place: (0, c)),
                pl.BlockSpec(memory_space=pl.ANY),
                pl.BlockSpec(memory_space=pl.ANY),
            ],
            out_specs=[
                pl.BlockSpec((tokens, q_cols), put),
                pl.BlockSpec((tokens, rope_cols), put),
            ],
        ),
        out_shape=[
            jax.ShapeDtypeStruct(q_full.shape, q_full.dtype),
            jax.ShapeDtypeStruct(rope_full.shape, rope_full.dtype),
        ],
        input_output_aliases={2: 0, 3: 1},
        compiler_params=pltpu.CompilerParams(vmem_limit_bytes=KERNEL_BYTES),
        cost_estimate=pl.CostEstimate(flops=0, bytes_accessed=4_000_000, transcendentals=0),
        name="place_columns",
    )(place, received, q_full, rope_full)


def stack_kernel(*refs, arrangement):
    outs = refs[len(refs) - len(arrangement) :]
    for out, sources in zip(outs, arrangement):
        row = 0
        for index, block in sources:
            piece = refs[index]
            columns = slice(block * out.shape[1], (block + 1) * out.shape[1])
            out[row : row + piece.shape[0], :] = piece[:, columns]
            row += piece.shape[0]


def stack(inputs, arrangement, columns):
    whole = lambda shape: pl.BlockSpec(shape, lambda: (0, 0))
    shapes = [(sum(inputs[i].shape[0] for i, _ in sources), columns) for sources in arrangement]
    return pl.pallas_call(
        functools.partial(stack_kernel, arrangement=arrangement),
        in_specs=[whole(array.shape) for array in inputs],
        out_specs=[whole(shape) for shape in shapes],
        out_shape=[jax.ShapeDtypeStruct(shape, inputs[0].dtype) for shape in shapes],
        compiler_params=pltpu.CompilerParams(vmem_limit_bytes=KERNEL_BYTES),
        cost_estimate=pl.CostEstimate(flops=0, bytes_accessed=2_000_000, transcendentals=0),
        name="stack",
    )(*inputs)


def join_rows_kernel(place, near, distant, near_crossed, distant_crossed, near_rows, distant_rows):
    rows = near.shape[0]
    for own, crossed, out in (
        (near, near_crossed, near_rows),
        (distant, distant_crossed, distant_rows),
    ):
        out[:rows, :] = own[...]
        out[rows:, :] = crossed[...]


def weight_parts(place, up_weight, crossed, chunks, far):
    rows = up_weight.shape[0]
    width = up_weight.shape[1] // chunks // 2

    def column_block(t):
        return pl.BlockSpec((rows, width), lambda i, place: (0, place[1 + t] * 2 + place[0]))

    shape = (2 * rows, width)
    return pl.pallas_call(
        join_rows_kernel,
        grid_spec=pltpu.PrefetchScalarGridSpec(
            num_scalar_prefetch=1,
            grid=(1,),
            in_specs=[column_block(t) for t in (0, far)] * 2,
            out_specs=[pl.BlockSpec(shape, lambda i, place: (0, 0))] * 2,
        ),
        out_shape=[jax.ShapeDtypeStruct(shape, up_weight.dtype)] * 2,
        compiler_params=pltpu.CompilerParams(vmem_limit_bytes=INPUT_BYTES),
        cost_estimate=pl.CostEstimate(flops=0, bytes_accessed=1_000_000, transcendentals=0),
        name="weight_parts",
    )(place, up_weight, up_weight, crossed, crossed)


def lay_kernel(place, *refs):
    *pieces, out = refs
    width = out.shape[1] // 4
    for step in range(len(pieces) // 2):
        early, late = pieces[2 * step], pieces[2 * step + 1]

        @pl.when(pl.program_id(0) == step)
        def _():
            for which in range(2):
                source = slice(which * width, (which + 1) * width)
                out[:, 2 * which * width : (2 * which + 1) * width] = early[:, source]
                out[:, (2 * which + 1) * width : (2 * which + 2) * width] = late[:, source]


def lay_out(place, pieces):
    rows, columns = pieces[0].shape
    count = len(pieces) // 2
    return pl.pallas_call(
        lay_kernel,
        grid_spec=pltpu.PrefetchScalarGridSpec(
            num_scalar_prefetch=1,
            grid=(count,),
            in_specs=[pl.BlockSpec(memory_space=pltpu.VMEM)] * len(pieces),
            out_specs=pl.BlockSpec((rows, 2 * columns), lambda t, place: (0, place[1 + t])),
        ),
        out_shape=jax.ShapeDtypeStruct((rows, count * 2 * columns), pieces[0].dtype),
        compiler_params=pltpu.CompilerParams(vmem_limit_bytes=KERNEL_BYTES),
        cost_estimate=pl.CostEstimate(flops=0, bytes_accessed=4_000_000, transcendentals=0),
        name="lay_out",
    )(place, *pieces)


def piece_kernel(place, kept, crossed, out):
    width = kept.shape[1]

    @pl.when(place[0] == 0)
    def _():
        out[:, :width] = kept[...]
        out[:, width:] = crossed[...]

    @pl.when(place[0] != 0)
    def _():
        out[:, :width] = crossed[...]
        out[:, width:] = kept[...]


def join_cores(place, kept, crossed):
    rows, columns = kept.shape
    return pl.pallas_call(
        piece_kernel,
        grid_spec=pltpu.PrefetchScalarGridSpec(
            num_scalar_prefetch=1,
            grid=(1,),
            in_specs=[pl.BlockSpec((rows, columns), lambda i, place: (0, 0))] * 2,
            out_specs=pl.BlockSpec((rows, 2 * columns), lambda i, place: (0, 0)),
        ),
        out_shape=jax.ShapeDtypeStruct((rows, 2 * columns), kept.dtype),
        compiler_params=pltpu.CompilerParams(vmem_limit_bytes=KERNEL_BYTES),
        cost_estimate=pl.CostEstimate(flops=0, bytes_accessed=500_000, transcendentals=0),
        name="join_cores",
    )(place, kept, crossed)


def halving_order(count):
    bits = count.bit_length() - 1
    partners = []
    for place in range(count):
        partner = place & 1
        for bit in range(1, bits):
            partner |= ((place >> (bits - bit)) & 1) << bit
        partners.append(partner)
    return partners


def channel_order(ctx, lat_block):
    channel = lax.broadcasted_iota(jnp.int32, (LAT, LAT), 0)
    place = lax.broadcasted_iota(jnp.int32, (LAT, LAT), 1)
    count = LAT // lat_block
    bits = count.bit_length() - 1
    block = place // lat_block
    partner = block & 1
    for bit in range(1, bits):
        partner |= ((block >> (bits - bit)) & 1) << bit
    return channel == (ctx ^ partner) * lat_block + place % lat_block


def block_sources(place, offered, per_block, span):
    ctx = place[place.shape[0] - 1]
    sources = []
    for side in range(2):
        group = ctx ^ side
        for at in range(per_block + len(partner_offsets)):
            matching = at - per_block
            offset = partner_offsets[matching] if matching >= 0 else 0
            source = group - offset
            usable = source >= 0
            sender = jnp.maximum(source, 0)
            inner = offered[sender, matching] if matching >= 0 else at
            start = jnp.where(usable, ((ctx >> 1) - (sender >> 1)) * span + inner * BLOCK, 0)
            block_id = jnp.where(usable, sender * per_block + inner, -2)
            sources.append(((offset + side) % 2, start, usable, block_id))
    return sources


def collect_kernel(place, offered, own, sib, cand, cand_t, rope_keys, bias, *, lat_block):
    ctx = place[place.shape[0] - 1]
    span = own.shape[0] // 3
    per_block = (span - 16) // BLOCK
    pieces = []
    key_at = lax.broadcasted_iota(jnp.int32, (BLOCK, 2 * BLOCK), 0)
    query = lax.broadcasted_iota(jnp.int32, (BLOCK, 2 * BLOCK), 1)
    causal = jnp.where(key_at <= query % BLOCK, 1.0, 0.0)
    sources = block_sources(place, offered, per_block, span)
    for block, (other, start, usable, block_id) in enumerate(sources):
        rows_ref = sib if other else own
        rows = rows_ref[pl.ds(pl.multiple_of(start, 16), BLOCK), :]
        pieces.append(jnp.where(usable, rows, jnp.zeros_like(rows)))
        side = block // (len(sources) // 2)
        lists = (sib if side else own)[span - 16 : span, :][:1].astype(jnp.int32)
        open_for = []
        for at in range(per_block):
            picks = [lists[:, at * TOPK + k : at * TOPK + k + 1] for k in range(TOPK)]
            picked = functools.reduce(
                jnp.maximum, [jnp.where(pick == block_id, 1.0, 0.0) for pick in picks]
            )
            same = jnp.where(block_id == (ctx ^ side) * per_block + at, 1.0, 0.0)
            open_for.append(jnp.maximum(picked, same * causal))
        allowed = jnp.where(query < BLOCK, open_for[0], open_for[1])
        bias[block * BLOCK : (block + 1) * BLOCK, :] = jnp.where(allowed > 0.5, 0.0, HIDDEN)
    both = jnp.concatenate(pieces, axis=0)
    order = channel_order(ctx, lat_block).astype(jnp.bfloat16)
    latent = both[:, :LAT]
    cand[...] = dot(latent, order, 1, 0).astype(jnp.bfloat16)
    cand_t[...] = dot(order, latent, 0, 1).astype(jnp.bfloat16)
    twice = lax.broadcasted_iota(jnp.int32, (ROPE, 2 * ROPE), 0)
    twice = twice == lax.broadcasted_iota(jnp.int32, (ROPE, 2 * ROPE), 1) % ROPE
    rope_keys[...] = dot(both[:, LAT:], twice.astype(jnp.bfloat16), 1, 0).astype(jnp.bfloat16)


def collect(place, offered, own, sib, rows, lat_block):
    bf16 = jnp.bfloat16
    shapes = [((rows, LAT), bf16), ((LAT, rows), bf16), ((rows, 2 * ROPE), bf16)]
    shapes.append(((rows, 2 * BLOCK), jnp.float32))
    whole = lambda shape: pl.BlockSpec(shape, lambda i, place, offered: (0, 0))
    return pl.pallas_call(
        functools.partial(collect_kernel, lat_block=lat_block),
        grid_spec=pltpu.PrefetchScalarGridSpec(
            num_scalar_prefetch=2,
            grid=(1,),
            in_specs=[whole(own.shape), whole(sib.shape)],
            out_specs=[whole(shape) for shape, _ in shapes],
        ),
        out_shape=[jax.ShapeDtypeStruct(shape, dtype) for shape, dtype in shapes],
        compiler_params=pltpu.CompilerParams(vmem_limit_bytes=KERNEL_BYTES),
        cost_estimate=pl.CostEstimate(
            flops=250_000_000, bytes_accessed=3_000_000, transcendentals=0
        ),
        name="collect",
    )(place, offered, own, sib)


def spread_kernel(place, offered, *refs, lat_block):
    *sums, own, sib = refs
    count = len(sums) // 2
    latent, rope = sums[0][...], sums[count][...]
    for index in range(1, count):
        latent, rope = latent + sums[index][...], rope + sums[count + index][...]
    order = channel_order(place[place.shape[0] - 1], lat_block).astype(jnp.float32)
    latent = lax.dot_general(
        latent,
        order,
        (((1,), (1,)), ((), ())),
        precision=lax.Precision.HIGHEST,
        preferred_element_type=jnp.float32,
    )
    rows = jnp.concatenate([latent, rope[:, :ROPE] + rope[:, ROPE:]], axis=1)
    own[...] = jnp.zeros_like(own)
    sib[...] = jnp.zeros_like(sib)
    span = own.shape[0] // 3
    sources = block_sources(place, offered, (span - 16) // BLOCK, span)
    for block, (other, start, _, _) in enumerate(sources):
        here = pl.ds(pl.multiple_of(start, 16), BLOCK)
        target = sib if other else own
        target[here, :] += rows[block * BLOCK : (block + 1) * BLOCK]


def spread(place, offered, latents, ropes, rows, lat_block):
    shape = (rows, LAT + ROPE)
    sums = [*latents, *ropes]
    whole = lambda shape: pl.BlockSpec(shape, lambda i, place, offered: (0, 0))
    return pl.pallas_call(
        functools.partial(spread_kernel, lat_block=lat_block),
        grid_spec=pltpu.PrefetchScalarGridSpec(
            num_scalar_prefetch=2,
            grid=(1,),
            in_specs=[whole(array.shape) for array in sums],
            out_specs=[whole(shape)] * 2,
        ),
        out_shape=[jax.ShapeDtypeStruct(shape, jnp.float32)] * 2,
        compiler_params=pltpu.CompilerParams(vmem_limit_bytes=KERNEL_BYTES),
        cost_estimate=pl.CostEstimate(
            flops=700_000_000, bytes_accessed=6_000_000, transcendentals=0
        ),
        name="spread",
    )(place, offered, *sums)


def halve(value, axis, bit):
    half = value.shape[0] // 2
    return value[:half] + exchange(value[half:], axis, bit)


def shards(q_nope, q_rope, grad_out, log_total, kv_latent, up_weight, selected, offered):
    n_dp, n_ctx = lax.axis_size("dp"), lax.axis_size("ctx")
    dp, ctx = lax.axis_index("dp"), lax.axis_index("ctx")
    core = ctx % 2
    group_len = kv_latent.shape[1]
    per_block = group_len // BLOCK
    heads = log_total.shape[1]
    part_heads = heads // n_dp // 2
    pairs = part_heads // 2
    part_cols = part_heads * (NOPE + VDIM)
    far = n_dp - 1
    lat_block = up_weight.shape[0]

    place = jnp.stack([core] + [dp ^ t for t in range(n_dp)] + [ctx]).astype(jnp.int32)

    crossed = exchange(up_weight, "ctx", 1)
    crossed, place, selected, offered, q_nope, q_rope, grad_out, log_total, kv_latent = (
        lax.optimization_barrier(
            (crossed, place, selected, offered, q_nope, q_rope, grad_out, log_total, kv_latent)
        )
    )
    chip_rows = weight_parts(place, up_weight, crossed, n_dp, far)
    own = [q_nope[0], q_rope[0], grad_out[0]]
    sibling = [exchange(array, "ctx", 1) for array in own]
    offered = offered[0]
    span = group_len + 16
    lists = selected[0].reshape(1, -1).astype(jnp.bfloat16)
    lists = jnp.pad(lists, ((0, 15), (0, LAT + ROPE - lists.shape[1])))
    bundle = after(jnp.concatenate([kv_latent[0], lists], axis=0), *sibling)
    bundles = [bundle, from_behind(bundle, "ctx", 2), from_behind(bundle, "ctx", 4)]
    own_bundles = stack(bundles, (((0, 0), (1, 0), (2, 0)),), LAT + ROPE)[0]
    sib_bundles = exchange(own_bundles, "ctx", 1)
    key_len = 2 * (group_len + len(partner_offsets) * BLOCK)
    shared = collect(place, offered, own_bundles, sib_bundles, key_len, lat_block)

    partners = halving_order(n_ctx)[::2]

    def over_chips(start):
        at_step = {0: start}
        for step in range(4, n_ctx, 4):
            at_step[step] = exchange(start, "ctx", step)
        at_step[2] = exchange(start, "ctx", 2)
        for step in range(4, n_ctx, 4):
            at_step[step + 2] = exchange(after(at_step[step], at_step[2]), "ctx", 2)
        return [at_step[partner] for partner in partners], at_step[n_ctx - 4]

    def joined(pieces):
        return stack(pieces, (tuple((index, 0) for index in range(len(pieces))),), part_cols)[0]

    near_pieces, last = over_chips(chip_rows[0])
    far_pieces, _ = over_chips(after(chip_rows[1], last))
    log_total = after(log_total, last)[0]
    sibling.append(exchange(log_total, "ctx", 1))
    own.append(log_total)
    for arrays in (own, sibling):
        arrays[3] = arrays[3].reshape(heads // 2, 2, group_len)

    weights = {0: joined([after(near_pieces[0], shared[0], sibling[3])] + near_pieces[1:])}
    for t in range(1, far):
        weights[t] = exchange(weights[0], "dp", t)
    earlier = None
    latents, ropes = [], []
    weight_grads = {t: ([], []) for t in range(n_dp)}
    bits = [1 << b for b in range(n_dp.bit_length() - 1)]
    orders = (bits, bits[::-1])
    first_sums = [{t: [] for t in range(n_dp) if t & order[0]} for order in orders]
    half_pairs = pairs // 2
    units = [(t, 0, pairs) for t in [far] + list(range(1, far - 1))]
    units += [(t, start, half_pairs) for t in (far - 1, 0) for start in (0, half_pairs)]
    for t, start, count in units:
        if t == far:
            weights[far] = joined(far_pieces)
        weight = weights[t]
        if t == 0 and start:
            there = [piece for sent in first_sums for u in sent for piece in sent[u]]
            weight = after(weight, latents[-1], *there)
        if t == 1 and not start:
            weight = after(weight, *[weights[near] for near in range(2, far)])
        if t == far - 1 and start:
            weight = after(weight, latents[-1], *[sent[far][0] for sent in first_sums])
        rest = chunk_backward(
            place,
            t,
            (start, count),
            own,
            sibling,
            weight,
            shared,
            earlier,
            (n_dp, pairs),
        )
        earlier = rest[:3]
        for side, sent in enumerate(first_sums):
            weight_grads[t][side].append(rest[3 + side])
            if t in sent:
                sent[t].append(exchange(rest[3 + side], "dp", orders[side][0]))
        latents.append(rest[5])
        ropes.append(rest[6])

    half_cols = part_cols // 2

    def columns(pieces, half):
        if len(pieces) == 2:
            return pieces[half]
        return pieces[0][:, half * half_cols : (half + 1) * half_cols]

    def total(addends, half):
        return functools.reduce(
            lambda left, right: left + right, [columns(pieces, half) for pieces in addends]
        )

    sums = []
    last_sums = first_sums[1][far - 1]
    for side, order in enumerate(orders):
        addends = {t: [weight_grads[t][side]] for t in weight_grads}
        arrived = {t ^ order[0]: pieces for t, pieces in first_sums[side].items()}
        addends = {t: addends[t] + [more] for t, more in arrived.items()}
        for bit in order[1:]:
            arrived = {}
            for t in sorted((t for t in addends if t & bit), reverse=True):
                leaving = [total(addends[t], half) for half in range(2)]
                if side == 0:
                    behind = [(last_sums[0],), (first_sums[0][order[0]][0], last_sums[-1], latents[-2])]
                else:
                    behind = [(weight_grads[far - 1][side][0],)] * 2
                leaving = [after(half, *there) for half, there in zip(leaving, behind)]
                arrived[t ^ bit] = [exchange(half, "dp", bit) for half in leaving]
            addends = {t: addends[t] + [more] for t, more in arrived.items()}
        sums.append(addends[0])

    q_full, rope_full, sib_grads = earlier
    received = exchange(sib_grads, "ctx", 1)
    grad_nope, grad_rope = place_columns(place, received, q_full, rope_full, n_dp)

    own_grads, sib_grads = spread(place, offered, latents, ropes, 3 * span, lat_block)
    swapped = exchange(sib_grads, "ctx", 1)
    grad_rows = own_grads + swapped
    ctx_bits = [1 << b for b in range(1, n_ctx.bit_length() - 1)]
    finished, arrived = [], None
    for half in range(2):
        if half:
            sums = [[[after(piece, arrived) for piece in pieces] for pieces in side] for side in sums]
        first, second = [total(side, half) for side in sums]
        arrived = exchange(after(second, sums[0][-1][half]), "ctx", ctx_bits[0])
        rows = first + arrived
        if half:
            rows = after(rows, received, swapped)
        for bit in ctx_bits[1:]:
            rows = halve(rows, "ctx", bit)
        kept, crossed = rows[:lat_block], exchange(rows[lat_block:], "ctx", 1)
        if half:
            kept = after(kept, *finished[0][1:])
        piece = join_cores(place, kept, crossed)
        finished.append([piece] + [exchange(piece, "dp", t) for t in range(1, n_dp)])

    grad_rows = after(grad_rows, rows)
    by_chip = [grad_rows[at * span : at * span + group_len] for at in range(3)]
    grad_rows = by_chip[0]
    for chips in (1, 2):
        grad_rows = grad_rows + from_behind(by_chip[chips], "ctx", -2 * chips)
    finished[0][0] = after(finished[0][0], grad_rows, grad_nope)
    grad_weight = lay_out(place, [piece for both in zip(*finished) for piece in both])
    return (grad_nope[None], grad_rope[None], grad_rows[None], grad_weight)


def solution(mesh):
    in_specs = (
        P("dp", "ctx", None),
        P("dp", "ctx", None),
        P("dp", "ctx", None),
        P("dp", None, "ctx"),
        P("dp", "ctx", None),
        P("ctx", None),
        P("dp", "ctx", None),
        P("dp", None, None),
    )
    out_specs = (P("dp", "ctx", None), P("dp", "ctx", None), P("dp", "ctx", None), P("ctx", None))
    return jax.shard_map(shards, mesh=mesh, in_specs=in_specs, out_specs=out_specs, check_vma=False)
```
